32 devices in a mesh: gz: 4 (over y, core), xy: 8 (over z, x).
Axes of the slice: x: 2, y: 2, z: 4, core: 2. Of those that a mesh axis runs over, the one named last changes fastest.
Arguments:
- density: float32 [32, 1024, 128], P('gz', 'xy'), may hold values from -96 to 96
- live_slices: int32 [4, 8], replicated, may hold values from 1 to 8, as said below
- shear_slopes: float32 [2], replicated, may hold values from -0.12 to 0.12
- palette: float32 [3], replicated, may hold values from 0.5 to 2
- depth_order: int32 [2, 4], replicated, may hold values from 0 to 3, each once within a row
- tile_owner: int32 [2, 4], replicated, may hold values from 0 to 3, each once within a row
Outputs:
- owned_tiles: float32 [2, 4, 4, 256, 128], P(None, None, 'gz', 'xy')
The draws below stay inside these ranges and needn't reach their ends.
Inputs may be any that keep to these rules, and one draw needn't show every extreme that they name: `live_slices`: some brick has all 8 slices live. `depth_order`: each row lists every slab once. `tile_owner`: each row names every index of gz once.
All inputs are finite; a program needn't handle non-finite values.
Results may differ from the reference program's by a relative error of at most 0.00042.
Values may be sent and summed in bfloat16 or wider, within the bound.
No kernel may reach another device: no remote copies, remote signals or barrier semaphores. Data moves between devices by JAX's collectives and lax.ppermute only.
A program may use at most 64 MiB of HBM per device.

```python
import math
from functools import partial
import jax
import jax.numpy as jnp
from jax import lax

CZ = 8
CY = 128
W = 128
NZ = 32
NY = 1024
TR = 32
N_GZ = 4
N_XY = 8


def draw_live_slices(key, part):
    spread = jax.random.randint(jax.random.fold_in(key, 11), (N_GZ, N_XY), 1, CZ + 1)
    chosen = jax.random.randint(jax.random.fold_in(key, 12), (), 0, N_GZ * N_XY)
    flat_index = jnp.arange(N_GZ * N_XY).reshape(N_GZ, N_XY)
    return jnp.where(flat_index == chosen, CZ, spread).astype(jnp.int32)


def draw_density(key, part):
    shape = (NZ, NY, W)
    return 16.0 * jax.random.truncated_normal(jax.random.fold_in(key, 23), -6.0, 6.0, shape, jnp.float32)


def setup_inputs(seed: int = 0) -> dict:
    keys = jax.random.split(jax.random.key(seed), 7)
    density = draw_density(jax.random.fold_in(keys[6], 71), 0)
    live_slices = draw_live_slices(jax.random.fold_in(keys[6], 71), 0)
    shear_slopes = jnp.clip(jax.random.uniform(keys[2], (2,), jnp.float32, -0.12, 0.12), -0.12, 0.12)
    palette = jnp.clip(jnp.exp(jax.random.uniform(keys[3], (3,), jnp.float32, math.log(0.5), math.log(2.0))), 0.5, 2.0)
    depth_order = jax.vmap(lambda own: jax.random.permutation(own, N_GZ))(jax.random.split(keys[4], 2)).reshape((2, N_GZ)).astype(jnp.int32)
    tile_owner = jax.vmap(lambda own: jax.random.permutation(own, N_GZ))(jax.random.split(keys[5], 2)).reshape((2, N_GZ)).astype(jnp.int32)
    return {"density": density, "live_slices": live_slices, "shear_slopes": shear_slopes, "palette": palette, "depth_order": depth_order, "tile_owner": tile_owner}


TAPS = (1.0 / 9,) * 9
LIGHT = (0.48, 0.6, 0.64)

def smooth_along(volume, along):
    extent = volume.shape[along] - 8
    total = TAPS[0] * lax.slice_in_dim(volume, 0, extent, axis=along)
    for offset in range(1, 9):
        total = total + TAPS[offset] * lax.slice_in_dim(volume, offset, offset + extent, axis=along)
    return total

def smooth_all(volume):
    return smooth_along(smooth_along(smooth_along(volume, 0), 1), 2)

def shade(padded, live_mask, palette, extinct, stack_axis):
    center = padded[1:-1, 1:-1, 1:-1]
    diff_depth = 0.5 * (padded[2:, 1:-1, 1:-1] - padded[:-2, 1:-1, 1:-1])
    diff_rows = 0.5 * (padded[1:-1, 2:, 1:-1] - padded[1:-1, :-2, 1:-1])
    diff_cols = 0.5 * (padded[1:-1, 1:-1, 2:] - padded[1:-1, 1:-1, :-2])
    magnitude = jnp.sqrt(diff_depth * diff_depth + diff_rows * diff_rows + diff_cols * diff_cols + 0.01)
    facing = jnp.maximum(0.0, LIGHT[0] * diff_depth + LIGHT[1] * diff_rows + LIGHT[2] * diff_cols) / magnitude
    opacity = jnp.where(live_mask, 1.0 - jnp.exp(-extinct * jax.nn.softplus(2.0 * center)), 0.0)
    bright = opacity * (0.25 + 0.75 * facing)
    stacked = jnp.stack([bright * palette[0], bright * palette[1], bright * palette[2], opacity], axis=stack_axis)
    return stacked.astype(jnp.bfloat16)

def shear_matrix(shear_slope, slice_depth, columns, total_depth):
    shift = shear_slope * (slice_depth + 0.5 - 0.5 * total_depth)
    shift = shift[..., None, None]
    source = lax.broadcasted_iota(jnp.float32, (columns, columns), 0)
    target = lax.broadcasted_iota(jnp.float32, (columns, columns), 1)
    return jnp.maximum(0.0, 1.0 - jnp.abs(source - target + shift)).astype(jnp.bfloat16)

def composite(fragments, order_row):
    ordered = jnp.take(fragments, order_row, axis=0)

    def blend(carry, fragment):
        shaded, transmit = carry
        return ((shaded + transmit * fragment[:3], transmit * (1.0 - fragment[3])), None)
    plane = fragments.shape[2:]
    init = (jnp.zeros((3,) + plane, jnp.float32), jnp.ones(plane, jnp.float32))
    (shaded, transmit), _ = lax.scan(blend, init, ordered)
    return jnp.concatenate([shaded, (1.0 - transmit)[None]], axis=0)

def render_column(column_index, padded_all, live_slices, shear_slopes, palette, depth_order):
    extinct = 3.0 / NZ
    start = (column_index * CY).astype(jnp.int32)
    zero = jnp.zeros((), jnp.int32)
    column_block = lax.dynamic_slice(padded_all, (zero, start, zero), (NZ + 10, CY + 10, W + 10))
    smoothed = smooth_all(column_block)
    depth_pos = lax.broadcasted_iota(jnp.int32, (NZ + 2, 1, 1), 0)
    row_pos = start - 1 + lax.broadcasted_iota(jnp.int32, (1, CY + 2, 1), 1)
    col_pos = lax.broadcasted_iota(jnp.int32, (1, 1, W + 2), 2)
    keep = (depth_pos >= 1) & (depth_pos <= NZ) & (row_pos >= 0) & (row_pos < NY) & (col_pos >= 1) & (col_pos <= W)
    padded = jnp.where(keep, smoothed, 0.0)
    live_column = lax.dynamic_index_in_dim(live_slices, column_index, axis=1, keepdims=False)
    local_depth = lax.broadcasted_iota(jnp.int32, (N_GZ, CZ), 1)
    live_mask = (local_depth < live_column[:, None]).reshape(NZ, 1, 1)
    rgba = shade(padded, live_mask, palette, extinct, 0)
    slabs = rgba.reshape(4, N_GZ, CZ, CY, W).transpose(2, 1, 0, 3, 4)
    slab_start = (lax.broadcasted_iota(jnp.int32, (N_GZ,), 0) * CZ).astype(jnp.float32)
    images = []
    for view_index in range(2):

        def march(carry, item):
            shaded, transmit = carry
            layer, local = item
            matrix = shear_matrix(shear_slopes[view_index], slab_start + local.astype(jnp.float32), W, NZ)
            sheared = jnp.einsum('gcyw,gwx->gcyx', layer.astype(jnp.float32), matrix.astype(jnp.float32), precision=lax.Precision.HIGHEST)
            return ((shaded + transmit[:, None] * sheared[:, :3], transmit * (1.0 - sheared[:, 3])), None)
        init = (jnp.zeros((N_GZ, 3, CY, W), jnp.float32), jnp.ones((N_GZ, CY, W), jnp.float32))
        depths = lax.broadcasted_iota(jnp.int32, (CZ,), 0)
        (shaded, transmit), _ = lax.scan(march, init, (slabs, depths), reverse=view_index == 1)
        fragments = jnp.concatenate([shaded, (1.0 - transmit)[:, None]], axis=1)
        images.append(composite(fragments, depth_order[view_index]))
    return jnp.stack(images)

def reference(density, live_slices, shear_slopes, palette, depth_order, tile_owner):
    padded_all = jnp.pad(density, 5)
    render = partial(render_column, padded_all=padded_all, live_slices=live_slices, shear_slopes=shear_slopes, palette=palette, depth_order=depth_order)
    images = lax.map(render, lax.broadcasted_iota(jnp.int32, (N_XY,), 0))
    tiles = images.reshape(N_XY, 2, 4, N_GZ, TR, W)
    ranks = lax.broadcasted_iota(jnp.int32, (N_GZ,), 0)
    inverse = lax.optimization_barrier(jnp.sum(ranks[None, None, :] * (tile_owner[:, None, :] == ranks[None, :, None]).astype(jnp.int32), axis=2))
    owned = []
    for view_index in range(2):
        picked = jnp.take(tiles[:, view_index], inverse[view_index], axis=2)
        owned.append(picked.transpose(1, 2, 0, 3, 4).reshape(4, N_GZ, N_XY * TR, W))
    return jnp.stack(owned)
```

```python
import jax
import jax.numpy as jnp
from jax import lax
from jax.experimental import pallas as pl
from jax.experimental.pallas import tpu as pltpu
from jax.sharding import PartitionSpec as P

LIGHT = (0.48, 0.6, 0.64)
REACH = 4
HALO = REACH + 1
TAPS = 2 * REACH + 1
ROW_TILE = 8
VIEWS = 2
VMEM_BYTES = 40 * 1024 * 1024


def column_matrix(columns):
    source = lax.broadcasted_iota(jnp.int32, (columns, columns), 0)
    target = lax.broadcasted_iota(jnp.int32, (columns, columns), 1)

    def band(shift):
        at = target + shift
        inside = (jnp.abs(source - at) <= REACH) & (at >= 0) & (at < columns)
        return jnp.where(inside, 1.0, 0.0).astype(jnp.float32)

    return jnp.concatenate([band(0), band(1) - band(-1)], axis=1).astype(jnp.bfloat16)


def shear_matrices(slopes_ref, slice_depth, columns, total_depth):
    source = lax.broadcasted_iota(jnp.int32, (columns, columns), 0)
    target = lax.broadcasted_iota(jnp.int32, (columns, columns), 1)
    distance = (source - target).astype(jnp.float32)
    parts = []
    for view in range(VIEWS):
        shift = slopes_ref[view] * (slice_depth + 0.5 - 0.5 * total_depth)
        parts.append(jnp.maximum(0.0, 1.0 - jnp.abs(distance + shift)))
    return jnp.concatenate(parts, axis=1).astype(jnp.bfloat16)


def window_sums(layers, taps):
    sums, width = layers, 1
    while 2 * width < taps:
        sums = [sums[i] + sums[i + width] for i in range(len(sums) - width)]
        width *= 2
    return [sums[i] + layers[i + width] for i in range(len(layers) - width)]


def make_render(n_depth, n_rows, depth_cells, row_cells, columns):
    total_depth = depth_cells * n_depth
    extinct = 3.0 / total_depth
    padded_rows = row_cells + 2 * ROW_TILE
    first, last = ROW_TILE, ROW_TILE + row_cells
    tile_rows = row_cells // n_depth
    cells = TAPS**3
    floor = 0.01 * (2.0 * cells) ** 2

    def kernel(
        live_ref, slopes_ref, palette_ref, owner_ref,
        own_ref, dlo_ref, dhi_ref, rlo_ref, rhi_ref, clo_ref, chi_ref,
        out_ref,
        deep, triple, smooth, across, sheared,
    ):
        depth_index = lax.axis_index("gz")
        row_index = lax.axis_index("xy")

        for chunk in range(padded_rows // ROW_TILE):
            if chunk == 0:
                low = [clo_ref[i] for i in range(HALO)]
                mid = [rlo_ref[i] for i in range(depth_cells)]
                high = [chi_ref[i] for i in range(HALO)]
            elif chunk == padded_rows // ROW_TILE - 1:
                low = [clo_ref[HALO + i] for i in range(HALO)]
                mid = [rhi_ref[i] for i in range(depth_cells)]
                high = [chi_ref[HALO + i] for i in range(HALO)]
            else:
                rows = pl.ds((chunk - 1) * ROW_TILE, ROW_TILE)
                low = [dlo_ref[i, rows] for i in range(HALO)]
                mid = [own_ref[i, rows] for i in range(depth_cells)]
                high = [dhi_ref[i, rows] for i in range(HALO)]
            for z, total in enumerate(window_sums(low + mid + high, TAPS)):
                deep[z, pl.ds(chunk * ROW_TILE, ROW_TILE)] = total

        band = column_matrix(columns)
        weights = jnp.concatenate([band, band, band], axis=0)
        for z in range(depth_cells + 2):
            lead = first - REACH
            span = row_cells + 2 * REACH
            triple[pl.ds(ROW_TILE, span)] = (
                deep[z, pl.ds(lead - 1, span)]
                + deep[z, pl.ds(lead, span)]
                + deep[z, pl.ds(lead + 1, span)]
            )
            base = ROW_TILE - lead
            total = (
                triple[pl.ds(base - 3, padded_rows)]
                + triple[pl.ds(base, padded_rows)]
                + triple[pl.ds(base + 3, padded_rows)]
            )
            hi = total.astype(jnp.bfloat16)
            rest = total - hi.astype(jnp.float32)
            mid = rest.astype(jnp.bfloat16)
            lo = (rest - mid.astype(jnp.float32)).astype(jnp.bfloat16)
            split = jnp.concatenate([hi, mid, lo], axis=1)
            if 1 <= z <= depth_cells:
                both = jnp.dot(split, weights, preferred_element_type=jnp.float32)
                smooth[z] = both[:, :columns]
                across[z - 1] = both[first:last, columns:]
            else:
                smooth[z] = jnp.dot(
                    split, weights[:, :columns], preferred_element_type=jnp.float32
                )

        @pl.when(row_index == 0)
        def _():
            smooth[:, first - 1 : first, :] = jnp.zeros(
                (depth_cells + 2, 1, columns), jnp.float32
            )

        @pl.when(row_index == n_rows - 1)
        def _():
            smooth[:, last : last + 1, :] = jnp.zeros((depth_cells + 2, 1, columns), jnp.float32)

        @pl.when(depth_index == 0)
        def _():
            smooth[0] = jnp.zeros((padded_rows, columns), jnp.float32)

        @pl.when(depth_index == n_depth - 1)
        def _():
            smooth[depth_cells + 1] = jnp.zeros((padded_rows, columns), jnp.float32)

        own_live = live_ref[depth_index, row_index]
        slab_start = (depth_index * depth_cells).astype(jnp.float32)
        for z in range(depth_cells):
            center = smooth[z + 1, pl.ds(first, row_cells)]
            diff_depth = (
                smooth[z + 2, pl.ds(first, row_cells)] - smooth[z, pl.ds(first, row_cells)]
            )
            diff_rows = (
                smooth[z + 1, pl.ds(first + 1, row_cells)]
                - smooth[z + 1, pl.ds(first - 1, row_cells)]
            )
            diff_cols = across[z]
            square = diff_depth * diff_depth + diff_rows * diff_rows + diff_cols * diff_cols
            toward = LIGHT[0] * diff_depth + LIGHT[1] * diff_rows + LIGHT[2] * diff_cols
            facing = jnp.maximum(0.0, toward) * lax.rsqrt(square + floor)
            twice = center * (2.0 / cells)
            small = jnp.exp(-jnp.abs(twice))
            log1p = jnp.where(small < 1e-4, small * (1.0 - 0.5 * small), jnp.log(1.0 + small))
            softplus = jnp.maximum(twice, 0.0) + log1p
            opacity = jnp.where(z < own_live, 1.0 - jnp.exp(-extinct * softplus), 0.0)
            bright = opacity * (0.25 + 0.75 * facing)
            rgba = jnp.concatenate(
                [(bright * palette_ref[c]).astype(jnp.bfloat16) for c in range(3)]
                + [opacity.astype(jnp.bfloat16)],
                axis=0,
            )
            matrix = shear_matrices(slopes_ref, slab_start + float(z), columns, total_depth)
            sheared[z] = jnp.dot(rgba, matrix, preferred_element_type=jnp.float32)

        for chunk in range(row_cells // ROW_TILE):
            tile = chunk * ROW_TILE // tile_rows
            inside = chunk * ROW_TILE - tile * tile_rows
            for view in range(VIEWS):
                lanes = pl.ds(view * columns, columns)
                colour, transmit = None, None
                for z in range(depth_cells):
                    part = [
                        sheared[z, pl.ds(c * row_cells + chunk * ROW_TILE, ROW_TILE), lanes]
                        for c in range(4)
                    ]
                    clear = 1.0 - part[3]
                    if z == 0:
                        colour, transmit = part[:3], clear
                    elif view == 0:
                        colour = [colour[c] + transmit * part[c] for c in range(3)]
                        transmit = transmit * clear
                    else:
                        colour = [part[c] + clear * colour[c] for c in range(3)]
                        transmit = transmit * clear
                place = owner_ref[view, tile]
                for c, value in enumerate(colour + [1.0 - transmit]):
                    out_ref[place, view, c, pl.ds(inside, ROW_TILE)] = value

    smem = pl.BlockSpec(memory_space=pltpu.SMEM)
    vmem = pl.BlockSpec(memory_space=pltpu.VMEM)
    return pl.pallas_call(
        kernel,
        out_shape=jax.ShapeDtypeStruct((n_depth, VIEWS, 4, tile_rows, columns), jnp.float32),
        in_specs=[smem] * 4 + [vmem] * 7,
        out_specs=vmem,
        scratch_shapes=[
            pltpu.VMEM((depth_cells + 2, padded_rows, columns), jnp.float32),
            pltpu.VMEM((padded_rows + 2 * ROW_TILE, columns), jnp.float32),
            pltpu.VMEM((depth_cells + 2, padded_rows, columns), jnp.float32),
            pltpu.VMEM((depth_cells, row_cells, columns), jnp.float32),
            pltpu.VMEM((depth_cells, 4 * row_cells, VIEWS * columns), jnp.float32),
        ],
        compiler_params=pltpu.CompilerParams(vmem_limit_bytes=VMEM_BYTES),
        name="render",
    )


def composite_kernel(order_ref, in_ref, out_ref):
    count = in_ref.shape[0]
    for view in range(VIEWS):
        colour, transmit = None, None
        for k in range(count):
            source = order_ref[view, k]
            part = [in_ref[source, view, c] for c in range(4)]
            clear = 1.0 - part[3]
            if k == 0:
                colour, transmit = part[:3], clear
            else:
                colour = [colour[c] + transmit * part[c] for c in range(3)]
                transmit = transmit * clear
        for c, value in enumerate(colour + [1.0 - transmit]):
            out_ref[view, c, 0] = value


def body(density, live_slices, shear_slopes, palette, depth_order, tile_owner):
    depth_cells, row_cells, columns = density.shape
    n_depth = lax.axis_size("gz")
    n_rows = lax.axis_size("xy")

    def both_ways(axis, to_next, to_previous):
        count = lax.axis_size(axis)
        forward = [(i, i + 1) for i in range(count - 1)]
        backward = [(target, source) for source, target in forward]
        return lax.ppermute(to_next, axis, forward), lax.ppermute(to_previous, axis, backward)

    dlo, dhi = both_ways("gz", density[depth_cells - HALO :], density[:HALO])
    rlo, rhi = both_ways("xy", density[:, row_cells - ROW_TILE :], density[:, :ROW_TILE])
    clo, chi = both_ways(
        "gz",
        jnp.concatenate([rlo[depth_cells - HALO :], rhi[depth_cells - HALO :]], axis=0),
        jnp.concatenate([rlo[:HALO], rhi[:HALO]], axis=0),
    )
    render = make_render(n_depth, n_rows, depth_cells, row_cells, columns)
    outgoing = render(
        live_slices, shear_slopes, palette, tile_owner,
        density, dlo, dhi, rlo, rhi, clo, chi,
    )
    incoming = lax.all_to_all(outgoing, "gz", split_axis=0, concat_axis=0, tiled=True)
    tile_rows = row_cells // n_depth
    return pl.pallas_call(
        composite_kernel,
        out_shape=jax.ShapeDtypeStruct((VIEWS, 4, 1, tile_rows, columns), jnp.float32),
        in_specs=[pl.BlockSpec(memory_space=pltpu.SMEM), pl.BlockSpec(memory_space=pltpu.VMEM)],
        out_specs=pl.BlockSpec(memory_space=pltpu.VMEM),
        compiler_params=pltpu.CompilerParams(vmem_limit_bytes=VMEM_BYTES),
        name="composite",
    )(depth_order, incoming)


def solution(mesh):
    placed = (P("gz", "xy", None), P(), P(), P(), P(), P())
    return jax.shard_map(
        body, mesh=mesh, in_specs=placed, out_specs=P(None, None, "gz", "xy", None), check_vma=False
    )
```

```python
import jax
import jax.numpy as jnp
from jax import lax
from jax.experimental import pallas as pl
from jax.experimental.pallas import tpu as pltpu
from jax.sharding import PartitionSpec as P

LIGHT = (0.48, 0.6, 0.64)
REACH = 4
HALO = REACH + 1
TAPS = 2 * REACH + 1
ROW_TILE = 8
VIEWS = 2
VMEM_BYTES = 40 * 1024 * 1024


def column_matrix(columns):
    source = lax.broadcasted_iota(jnp.int32, (columns, columns), 0)
    target = lax.broadcasted_iota(jnp.int32, (columns, columns), 1)

    def band(shift):
        at = target + shift
        inside = (jnp.abs(source - at) <= REACH) & (at >= 0) & (at < columns)
        return jnp.where(inside, 1.0, 0.0).astype(jnp.float32)

    return jnp.concatenate([band(0), band(1) - band(-1)], axis=1).astype(jnp.bfloat16)


def shear_matrices(slopes_ref, slice_depth, columns, total_depth):
    source = lax.broadcasted_iota(jnp.int32, (columns, columns), 0)
    target = lax.broadcasted_iota(jnp.int32, (columns, columns), 1)
    distance = (source - target).astype(jnp.float32)
    parts = []
    for view in range(VIEWS):
        shift = slopes_ref[view] * (slice_depth + 0.5 - 0.5 * total_depth)
        parts.append(jnp.maximum(0.0, 1.0 - jnp.abs(distance + shift)))
    return jnp.concatenate(parts, axis=1).astype(jnp.bfloat16)


def window_sums(layers, taps):
    sums, width = layers, 1
    while 2 * width < taps:
        sums = [sums[i] + sums[i + width] for i in range(len(sums) - width)]
        width *= 2
    return [sums[i] + layers[i + width] for i in range(len(layers) - width)]


def make_render(n_depth, n_rows, depth_cells, row_cells, columns):
    total_depth = depth_cells * n_depth
    extinct = 3.0 / total_depth
    padded_rows = row_cells + 2 * ROW_TILE
    first, last = ROW_TILE, ROW_TILE + row_cells
    tile_rows = row_cells // n_depth
    cells = TAPS**3
    floor = 0.01 * (2.0 * cells) ** 2

    def kernel(
        live_ref, slopes_ref, palette_ref, owner_ref,
        own_ref, dlo_ref, dhi_ref, rlo_ref, rhi_ref,
        out_ref,
        deep, triple, smooth, across, sheared,
    ):
        depth_index = lax.axis_index("gz")
        row_index = lax.axis_index("xy")

        for chunk in range(padded_rows // ROW_TILE):
            rows = pl.ds(chunk * ROW_TILE, ROW_TILE)
            low = [dlo_ref[i, rows] for i in range(HALO)]
            high = [dhi_ref[i, rows] for i in range(HALO)]
            if chunk == 0:
                mid = [rlo_ref[i] for i in range(depth_cells)]
            elif chunk == padded_rows // ROW_TILE - 1:
                mid = [rhi_ref[i] for i in range(depth_cells)]
            else:
                inner = pl.ds((chunk - 1) * ROW_TILE, ROW_TILE)
                mid = [own_ref[i, inner] for i in range(depth_cells)]
            for z, total in enumerate(window_sums(low + mid + high, TAPS)):
                deep[z, rows] = total

        band = column_matrix(columns)
        weights = jnp.concatenate([band, band, band], axis=0)
        for z in range(depth_cells + 2):
            lead = first - REACH
            span = row_cells + 2 * REACH
            triple[pl.ds(ROW_TILE, span)] = (
                deep[z, pl.ds(lead - 1, span)]
                + deep[z, pl.ds(lead, span)]
                + deep[z, pl.ds(lead + 1, span)]
            )
            base = ROW_TILE - lead
            total = (
                triple[pl.ds(base - 3, padded_rows)]
                + triple[pl.ds(base, padded_rows)]
                + triple[pl.ds(base + 3, padded_rows)]
            )
            hi = total.astype(jnp.bfloat16)
            rest = total - hi.astype(jnp.float32)
            mid = rest.astype(jnp.bfloat16)
            lo = (rest - mid.astype(jnp.float32)).astype(jnp.bfloat16)
            split = jnp.concatenate([hi, mid, lo], axis=1)
            if 1 <= z <= depth_cells:
                both = jnp.dot(split, weights, preferred_element_type=jnp.float32)
                smooth[z] = both[:, :columns]
                across[z - 1] = both[first:last, columns:]
            else:
                smooth[z] = jnp.dot(
                    split, weights[:, :columns], preferred_element_type=jnp.float32
                )

        @pl.when(row_index == 0)
        def _():
            smooth[:, first - 1 : first, :] = jnp.zeros(
                (depth_cells + 2, 1, columns), jnp.float32
            )

        @pl.when(row_index == n_rows - 1)
        def _():
            smooth[:, last : last + 1, :] = jnp.zeros((depth_cells + 2, 1, columns), jnp.float32)

        @pl.when(depth_index == 0)
        def _():
            smooth[0] = jnp.zeros((padded_rows, columns), jnp.float32)

        @pl.when(depth_index == n_depth - 1)
        def _():
            smooth[depth_cells + 1] = jnp.zeros((padded_rows, columns), jnp.float32)

        own_live = live_ref[depth_index, row_index]
        slab_start = (depth_index * depth_cells).astype(jnp.float32)
        for z in range(depth_cells):
            center = smooth[z + 1, pl.ds(first, row_cells)]
            diff_depth = (
                smooth[z + 2, pl.ds(first, row_cells)] - smooth[z, pl.ds(first, row_cells)]
            )
            diff_rows = (
                smooth[z + 1, pl.ds(first + 1, row_cells)]
                - smooth[z + 1, pl.ds(first - 1, row_cells)]
            )
            diff_cols = across[z]
            square = diff_depth * diff_depth + diff_rows * diff_rows + diff_cols * diff_cols
            toward = LIGHT[0] * diff_depth + LIGHT[1] * diff_rows + LIGHT[2] * diff_cols
            facing = jnp.maximum(0.0, toward) * lax.rsqrt(square + floor)
            twice = center * (2.0 / cells)
            small = jnp.exp(-jnp.abs(twice))
            log1p = jnp.where(small < 1e-4, small * (1.0 - 0.5 * small), jnp.log(1.0 + small))
            softplus = jnp.maximum(twice, 0.0) + log1p
            opacity = jnp.where(z < own_live, 1.0 - jnp.exp(-extinct * softplus), 0.0)
            bright = opacity * (0.25 + 0.75 * facing)
            rgba = jnp.concatenate(
                [(bright * palette_ref[c]).astype(jnp.bfloat16) for c in range(3)]
                + [opacity.astype(jnp.bfloat16)],
                axis=0,
            )
            matrix = shear_matrices(slopes_ref, slab_start + float(z), columns, total_depth)
            sheared[z] = jnp.dot(rgba, matrix, preferred_element_type=jnp.float32)

        for chunk in range(row_cells // ROW_TILE):
            tile = chunk * ROW_TILE // tile_rows
            inside = chunk * ROW_TILE - tile * tile_rows
            for view in range(VIEWS):
                lanes = pl.ds(view * columns, columns)
                colour, transmit = None, None
                for z in range(depth_cells):
                    part = [
                        sheared[z, pl.ds(c * row_cells + chunk * ROW_TILE, ROW_TILE), lanes]
                        for c in range(4)
                    ]
                    clear = 1.0 - part[3]
                    if z == 0:
                        colour, transmit = part[:3], clear
                    elif view == 0:
                        colour = [colour[c] + transmit * part[c] for c in range(3)]
                        transmit = transmit * clear
                    else:
                        colour = [part[c] + clear * colour[c] for c in range(3)]
                        transmit = transmit * clear
                place = owner_ref[view, tile]
                for c, value in enumerate(colour + [1.0 - transmit]):
                    out_ref[place, view, c, pl.ds(inside, ROW_TILE)] = value

    smem = pl.BlockSpec(memory_space=pltpu.SMEM)
    vmem = pl.BlockSpec(memory_space=pltpu.VMEM)
    return pl.pallas_call(
        kernel,
        out_shape=jax.ShapeDtypeStruct((n_depth, VIEWS, 4, tile_rows, columns), jnp.float32),
        in_specs=[smem] * 4 + [vmem] * 5,
        out_specs=vmem,
        scratch_shapes=[
            pltpu.VMEM((depth_cells + 2, padded_rows, columns), jnp.float32),
            pltpu.VMEM((padded_rows + 2 * ROW_TILE, columns), jnp.float32),
            pltpu.VMEM((depth_cells + 2, padded_rows, columns), jnp.float32),
            pltpu.VMEM((depth_cells, row_cells, columns), jnp.float32),
            pltpu.VMEM((depth_cells, 4 * row_cells, VIEWS * columns), jnp.float32),
        ],
        compiler_params=pltpu.CompilerParams(vmem_limit_bytes=VMEM_BYTES),
        name="render",
    )


def composite_kernel(order_ref, in_ref, out_ref):
    count = in_ref.shape[0]
    for view in range(VIEWS):
        colour, transmit = None, None
        for k in range(count):
            source = order_ref[view, k]
            part = [in_ref[source, view, c] for c in range(4)]
            clear = 1.0 - part[3]
            if k == 0:
                colour, transmit = part[:3], clear
            else:
                colour = [colour[c] + transmit * part[c] for c in range(3)]
                transmit = transmit * clear
        for c, value in enumerate(colour + [1.0 - transmit]):
            out_ref[view, c, 0] = value


def body(density, live_slices, shear_slopes, palette, depth_order, tile_owner):
    depth_cells, row_cells, columns = density.shape
    n_depth = lax.axis_size("gz")
    n_rows = lax.axis_size("xy")

    def both_ways(axis, to_next, to_previous):
        count = lax.axis_size(axis)
        forward = [(i, i + 1) for i in range(count - 1)]
        backward = [(target, source) for source, target in forward]
        return lax.ppermute(to_next, axis, forward), lax.ppermute(to_previous, axis, backward)

    rlo, rhi = both_ways("xy", density[:, row_cells - ROW_TILE :], density[:, :ROW_TILE])
    edge = depth_cells - HALO
    dlo, dhi = both_ways(
        "gz",
        jnp.concatenate([rlo[edge:], density[edge:], rhi[edge:]], axis=1),
        jnp.concatenate([rlo[:HALO], density[:HALO], rhi[:HALO]], axis=1),
    )
    render = make_render(n_depth, n_rows, depth_cells, row_cells, columns)
    outgoing = render(
        live_slices, shear_slopes, palette, tile_owner,
        density, dlo, dhi, rlo, rhi,
    )
    incoming = lax.all_to_all(outgoing, "gz", split_axis=0, concat_axis=0, tiled=True)
    tile_rows = row_cells // n_depth
    return pl.pallas_call(
        composite_kernel,
        out_shape=jax.ShapeDtypeStruct((VIEWS, 4, 1, tile_rows, columns), jnp.float32),
        in_specs=[pl.BlockSpec(memory_space=pltpu.SMEM), pl.BlockSpec(memory_space=pltpu.VMEM)],
        out_specs=pl.BlockSpec(memory_space=pltpu.VMEM),
        compiler_params=pltpu.CompilerParams(vmem_limit_bytes=VMEM_BYTES),
        name="composite",
    )(depth_order, incoming)


def solution(mesh):
    placed = (P("gz", "xy", None), P(), P(), P(), P(), P())
    return jax.shard_map(
        body, mesh=mesh, in_specs=placed, out_specs=P(None, None, "gz", "xy", None), check_vma=False
    )
```

```python
import jax
import jax.numpy as jnp
from jax import lax
from jax.experimental import pallas as pl
from jax.experimental.pallas import tpu as pltpu
from jax.sharding import PartitionSpec as P

LIGHT = (0.48, 0.6, 0.64)
REACH = 4
HALO = REACH + 1
TAPS = 2 * REACH + 1
ROW_TILE = 8
PACKED_ROWS = 16
VIEWS = 2
TOP = 2.2
STEPS = 65535.0
MIDDLE = 32768
VMEM_BYTES = 40 * 1024 * 1024


def column_matrix(columns):
    source = lax.broadcasted_iota(jnp.int32, (columns, columns), 0)
    target = lax.broadcasted_iota(jnp.int32, (columns, columns), 1)

    def band(shift):
        at = target + shift
        inside = (jnp.abs(source - at) <= REACH) & (at >= 0) & (at < columns)
        return jnp.where(inside, 1.0, 0.0).astype(jnp.float32)

    return jnp.concatenate([band(0), band(1) - band(-1)], axis=1).astype(jnp.bfloat16)


def shear_matrices(slopes_ref, slice_depth, columns, total_depth):
    source = lax.broadcasted_iota(jnp.int32, (columns, columns), 0)
    target = lax.broadcasted_iota(jnp.int32, (columns, columns), 1)
    distance = (source - target).astype(jnp.float32)
    parts = []
    for view in range(VIEWS):
        shift = slopes_ref[view] * (slice_depth + 0.5 - 0.5 * total_depth)
        parts.append(jnp.maximum(0.0, 1.0 - jnp.abs(distance + shift)))
    return jnp.concatenate(parts, axis=1).astype(jnp.bfloat16)


def window_sums(layers, taps):
    sums, width = layers, 1
    while 2 * width < taps:
        sums = [sums[i] + sums[i + width] for i in range(len(sums) - width)]
        width *= 2
    return [sums[i] + layers[i + width] for i in range(len(layers) - width)]


def encode(value):
    root = jnp.exp(0.125 * jnp.log(jnp.maximum(value, 1e-30) * (1.0 / TOP)))
    level = jnp.minimum(root * STEPS + 0.5, STEPS)
    return (level.astype(jnp.int32) - MIDDLE).astype(jnp.int16)


def decode(code):
    root = (code.astype(jnp.int32) + MIDDLE).astype(jnp.float32) * (TOP**0.125 / STEPS)
    square = root * root
    fourth = square * square
    return fourth * fourth


def make_render(n_depth, n_rows, depth_cells, row_cells, columns):
    total_depth = depth_cells * n_depth
    extinct = 3.0 / total_depth
    padded_rows = row_cells + 2 * ROW_TILE
    first, last = ROW_TILE, ROW_TILE + row_cells
    tile_rows = row_cells // n_depth
    step_rows = min(tile_rows, PACKED_ROWS)
    cells = TAPS**3
    floor = 0.01 * (2.0 * cells) ** 2

    def kernel(
        live_ref, slopes_ref, palette_ref, owner_ref,
        own_ref, dlo_ref, dhi_ref, rlo_ref, rhi_ref, clo_ref, chi_ref,
        out_ref,
        deep, triple, smooth, across, sheared,
    ):
        depth_index = lax.axis_index("gz")
        row_index = lax.axis_index("xy")

        for chunk in range(padded_rows // ROW_TILE):
            if chunk == 0:
                low = [clo_ref[i] for i in range(HALO)]
                mid = [rlo_ref[i] for i in range(depth_cells)]
                high = [chi_ref[i] for i in range(HALO)]
            elif chunk == padded_rows // ROW_TILE - 1:
                low = [clo_ref[HALO + i] for i in range(HALO)]
                mid = [rhi_ref[i] for i in range(depth_cells)]
                high = [chi_ref[HALO + i] for i in range(HALO)]
            else:
                rows = pl.ds((chunk - 1) * ROW_TILE, ROW_TILE)
                low = [dlo_ref[i, rows] for i in range(HALO)]
                mid = [own_ref[i, rows] for i in range(depth_cells)]
                high = [dhi_ref[i, rows] for i in range(HALO)]
            for z, total in enumerate(window_sums(low + mid + high, TAPS)):
                deep[z, pl.ds(chunk * ROW_TILE, ROW_TILE)] = total

        band = column_matrix(columns)
        weights = jnp.concatenate([band, band, band], axis=0)
        for z in range(depth_cells + 2):
            lead = first - REACH
            span = row_cells + 2 * REACH
            triple[pl.ds(ROW_TILE, span)] = (
                deep[z, pl.ds(lead - 1, span)]
                + deep[z, pl.ds(lead, span)]
                + deep[z, pl.ds(lead + 1, span)]
            )
            base = ROW_TILE - lead
            total = (
                triple[pl.ds(base - 3, padded_rows)]
                + triple[pl.ds(base, padded_rows)]
                + triple[pl.ds(base + 3, padded_rows)]
            )
            hi = total.astype(jnp.bfloat16)
            rest = total - hi.astype(jnp.float32)
            mid = rest.astype(jnp.bfloat16)
            lo = (rest - mid.astype(jnp.float32)).astype(jnp.bfloat16)
            split = jnp.concatenate([hi, mid, lo], axis=1)
            if 1 <= z <= depth_cells:
                both = jnp.dot(split, weights, preferred_element_type=jnp.float32)
                smooth[z] = both[:, :columns]
                across[z - 1] = both[first:last, columns:]
            else:
                smooth[z] = jnp.dot(
                    split, weights[:, :columns], preferred_element_type=jnp.float32
                )

        @pl.when(row_index == 0)
        def _():
            smooth[:, first - 1 : first, :] = jnp.zeros(
                (depth_cells + 2, 1, columns), jnp.float32
            )

        @pl.when(row_index == n_rows - 1)
        def _():
            smooth[:, last : last + 1, :] = jnp.zeros((depth_cells + 2, 1, columns), jnp.float32)

        @pl.when(depth_index == 0)
        def _():
            smooth[0] = jnp.zeros((padded_rows, columns), jnp.float32)

        @pl.when(depth_index == n_depth - 1)
        def _():
            smooth[depth_cells + 1] = jnp.zeros((padded_rows, columns), jnp.float32)

        own_live = live_ref[depth_index, row_index]
        slab_start = (depth_index * depth_cells).astype(jnp.float32)
        for z in range(depth_cells):
            center = smooth[z + 1, pl.ds(first, row_cells)]
            diff_depth = (
                smooth[z + 2, pl.ds(first, row_cells)] - smooth[z, pl.ds(first, row_cells)]
            )
            diff_rows = (
                smooth[z + 1, pl.ds(first + 1, row_cells)]
                - smooth[z + 1, pl.ds(first - 1, row_cells)]
            )
            diff_cols = across[z]
            square = diff_depth * diff_depth + diff_rows * diff_rows + diff_cols * diff_cols
            toward = LIGHT[0] * diff_depth + LIGHT[1] * diff_rows + LIGHT[2] * diff_cols
            facing = jnp.maximum(0.0, toward) * lax.rsqrt(square + floor)
            twice = center * (2.0 / cells)
            small = jnp.exp(-jnp.abs(twice))
            log1p = jnp.where(small < 1e-4, small * (1.0 - 0.5 * small), jnp.log(1.0 + small))
            softplus = jnp.maximum(twice, 0.0) + log1p
            opacity = jnp.where(z < own_live, 1.0 - jnp.exp(-extinct * softplus), 0.0)
            bright = opacity * (0.25 + 0.75 * facing)
            rgba = jnp.concatenate(
                [(bright * palette_ref[c]).astype(jnp.bfloat16) for c in range(3)]
                + [opacity.astype(jnp.bfloat16)],
                axis=0,
            )
            matrix = shear_matrices(slopes_ref, slab_start + float(z), columns, total_depth)
            sheared[z] = jnp.dot(rgba, matrix, preferred_element_type=jnp.float32)

        for tile in range(n_depth):
            place = [owner_ref[view, tile] for view in range(VIEWS)]
            for inside in range(0, tile_rows, step_rows):
                for view in range(VIEWS):
                    lanes = pl.ds(view * columns, columns)
                    colour, transmit = None, None
                    for z in range(depth_cells):
                        part = [
                            sheared[
                                z,
                                pl.ds(c * row_cells + tile * tile_rows + inside, step_rows),
                                lanes,
                            ]
                            for c in range(4)
                        ]
                        clear = 1.0 - part[3]
                        if z == 0:
                            colour, transmit = part[:3], clear
                        elif view == 0:
                            colour = [colour[c] + transmit * part[c] for c in range(3)]
                            transmit = transmit * clear
                        else:
                            colour = [part[c] + clear * colour[c] for c in range(3)]
                            transmit = transmit * clear
                    values = colour + [1.0 - transmit]
                    share = PACKED_ROWS // step_rows
                    for c in range(0, 4, share):
                        value = values[c] if share == 1 else jnp.concatenate(values[c : c + share])
                        rows = pl.ds(c * tile_rows + inside, PACKED_ROWS)
                        out_ref[place[view], view, rows] = encode(value)

    smem = pl.BlockSpec(memory_space=pltpu.SMEM)
    vmem = pl.BlockSpec(memory_space=pltpu.VMEM)
    return pl.pallas_call(
        kernel,
        out_shape=jax.ShapeDtypeStruct((n_depth, VIEWS, 4 * tile_rows, columns), jnp.int16),
        in_specs=[smem] * 4 + [vmem] * 7,
        out_specs=vmem,
        scratch_shapes=[
            pltpu.VMEM((depth_cells + 2, padded_rows, columns), jnp.float32),
            pltpu.VMEM((padded_rows + 2 * ROW_TILE, columns), jnp.float32),
            pltpu.VMEM((depth_cells + 2, padded_rows, columns), jnp.float32),
            pltpu.VMEM((depth_cells, row_cells, columns), jnp.float32),
            pltpu.VMEM((depth_cells, 4 * row_cells, VIEWS * columns), jnp.float32),
        ],
        compiler_params=pltpu.CompilerParams(vmem_limit_bytes=VMEM_BYTES),
        name="render",
    )


def composite_kernel(order_ref, in_ref, out_ref):
    count = in_ref.shape[0]
    rows = in_ref.shape[2] // 4
    for view in range(VIEWS):
        colour, transmit = None, None
        for k in range(count):
            source = order_ref[view, k]
            values = decode(in_ref[source, view])
            part = [values[c * rows : (c + 1) * rows] for c in range(4)]
            clear = 1.0 - part[3]
            if k == 0:
                colour, transmit = part[:3], clear
            else:
                colour = [colour[c] + transmit * part[c] for c in range(3)]
                transmit = transmit * clear
        for c, value in enumerate(colour + [1.0 - transmit]):
            out_ref[view, c, 0] = value


def body(density, live_slices, shear_slopes, palette, depth_order, tile_owner):
    depth_cells, row_cells, columns = density.shape
    n_depth = lax.axis_size("gz")
    n_rows = lax.axis_size("xy")

    def both_ways(axis, to_next, to_previous):
        count = lax.axis_size(axis)
        forward = [(i, i + 1) for i in range(count - 1)]
        backward = [(target, source) for source, target in forward]
        return lax.ppermute(to_next, axis, forward), lax.ppermute(to_previous, axis, backward)

    dlo, dhi = both_ways("gz", density[depth_cells - HALO :], density[:HALO])
    rlo, rhi = both_ways("xy", density[:, row_cells - ROW_TILE :], density[:, :ROW_TILE])
    clo, chi = both_ways(
        "gz",
        jnp.concatenate([rlo[depth_cells - HALO :], rhi[depth_cells - HALO :]], axis=0),
        jnp.concatenate([rlo[:HALO], rhi[:HALO]], axis=0),
    )
    render = make_render(n_depth, n_rows, depth_cells, row_cells, columns)
    outgoing = render(
        live_slices, shear_slopes, palette, tile_owner,
        density, dlo, dhi, rlo, rhi, clo, chi,
    )
    incoming = lax.all_to_all(outgoing, "gz", split_axis=0, concat_axis=0, tiled=True)
    tile_rows = row_cells // n_depth
    return pl.pallas_call(
        composite_kernel,
        out_shape=jax.ShapeDtypeStruct((VIEWS, 4, 1, tile_rows, columns), jnp.float32),
        in_specs=[pl.BlockSpec(memory_space=pltpu.SMEM), pl.BlockSpec(memory_space=pltpu.VMEM)],
        out_specs=pl.BlockSpec(memory_space=pltpu.VMEM),
        compiler_params=pltpu.CompilerParams(vmem_limit_bytes=VMEM_BYTES),
        name="composite",
    )(depth_order, incoming)


def solution(mesh):
    placed = (P("gz", "xy", None), P(), P(), P(), P(), P())
    return jax.shard_map(
        body, mesh=mesh, in_specs=placed, out_specs=P(None, None, "gz", "xy", None), check_vma=False
    )
```

```python
import jax
import jax.numpy as jnp
from jax import lax
from jax.experimental import pallas as pl
from jax.experimental.pallas import tpu as pltpu
from jax.sharding import PartitionSpec as P

LIGHT = (0.48, 0.6, 0.64)
REACH = 4
HALO = REACH + 1
TAPS = 2 * REACH + 1
ROW_TILE = 8
PACKED_ROWS = 16
VIEWS = 2
TOP = 2.2
STEPS = 65535.0
MIDDLE = 32768
VMEM_BYTES = 40 * 1024 * 1024


def column_matrix(columns):
    source = lax.broadcasted_iota(jnp.int32, (columns, columns), 0)
    target = lax.broadcasted_iota(jnp.int32, (columns, columns), 1)

    def band(shift):
        at = target + shift
        inside = (jnp.abs(source - at) <= REACH) & (at >= 0) & (at < columns)
        return jnp.where(inside, 1.0, 0.0).astype(jnp.float32)

    return jnp.concatenate([band(0), band(1) - band(-1)], axis=1).astype(jnp.bfloat16)


def shear_matrices(slopes_ref, slice_depth, columns, total_depth):
    source = lax.broadcasted_iota(jnp.int32, (columns, columns), 0)
    target = lax.broadcasted_iota(jnp.int32, (columns, columns), 1)
    distance = (source - target).astype(jnp.float32)
    parts = []
    for view in range(VIEWS):
        shift = slopes_ref[view] * (slice_depth + 0.5 - 0.5 * total_depth)
        parts.append(jnp.maximum(0.0, 1.0 - jnp.abs(distance + shift)))
    return jnp.concatenate(parts, axis=1).astype(jnp.bfloat16)


def window_sums(layers, taps):
    sums, width = layers, 1
    while 2 * width < taps:
        sums = [sums[i] + sums[i + width] for i in range(len(sums) - width)]
        width *= 2
    return [sums[i] + layers[i + width] for i in range(len(layers) - width)]


def encode(value):
    root = jnp.exp(0.125 * jnp.log(jnp.maximum(value, 1e-30) * (1.0 / TOP)))
    level = jnp.minimum(root * STEPS + 0.5, STEPS)
    return (level.astype(jnp.int32) - MIDDLE).astype(jnp.int16)


def decode(code):
    root = (code.astype(jnp.int32) + MIDDLE).astype(jnp.float32) * (TOP**0.125 / STEPS)
    square = root * root
    fourth = square * square
    return fourth * fourth


def make_render(n_depth, n_rows, depth_cells, row_cells, columns):
    total_depth = depth_cells * n_depth
    extinct = 3.0 / total_depth
    padded_rows = row_cells + 2 * ROW_TILE
    first, last = ROW_TILE, ROW_TILE + row_cells
    tile_rows = row_cells // n_depth
    step_rows = min(tile_rows, PACKED_ROWS)
    cells = TAPS**3
    floor = 0.01 * (2.0 * cells) ** 2

    def kernel(
        live_ref, slopes_ref, palette_ref, owner_ref,
        own_ref, even_ref, odd_ref, corner_ref, rlo_ref, rhi_ref,
        out_ref,
        deep, triple, smooth, across, sheared,
    ):
        depth_index = lax.axis_index("gz")
        row_index = lax.axis_index("xy")
        odd_depth = depth_index % 2 == 1

        for chunk in range(padded_rows // ROW_TILE):
            rows = pl.ds(chunk * ROW_TILE, ROW_TILE)
            inner = pl.ds((chunk - 1) * ROW_TILE, ROW_TILE)
            even = [even_ref[i, rows] for i in range(HALO)]
            if chunk == 0:
                odd = [corner_ref[i, pl.ds(0, ROW_TILE)] for i in range(HALO)]
                mid = [rlo_ref[i] for i in range(depth_cells)]
            elif chunk == padded_rows // ROW_TILE - 1:
                odd = [corner_ref[i, pl.ds(ROW_TILE, ROW_TILE)] for i in range(HALO)]
                mid = [rhi_ref[i] for i in range(depth_cells)]
            else:
                odd = [odd_ref[i, inner] for i in range(HALO)]
                mid = [own_ref[i, inner] for i in range(depth_cells)]
            low = [jnp.where(odd_depth, e, o) for e, o in zip(even, odd)]
            high = [jnp.where(odd_depth, o, e) for e, o in zip(even, odd)]
            for z, total in enumerate(window_sums(low + mid + high, TAPS)):
                deep[z, rows] = total

        band = column_matrix(columns)
        weights = jnp.concatenate([band, band, band], axis=0)
        for z in range(depth_cells + 2):
            lead = first - REACH
            span = row_cells + 2 * REACH
            triple[pl.ds(ROW_TILE, span)] = (
                deep[z, pl.ds(lead - 1, span)]
                + deep[z, pl.ds(lead, span)]
                + deep[z, pl.ds(lead + 1, span)]
            )
            base = ROW_TILE - lead
            total = (
                triple[pl.ds(base - 3, padded_rows)]
                + triple[pl.ds(base, padded_rows)]
                + triple[pl.ds(base + 3, padded_rows)]
            )
            hi = total.astype(jnp.bfloat16)
            rest = total - hi.astype(jnp.float32)
            mid = rest.astype(jnp.bfloat16)
            lo = (rest - mid.astype(jnp.float32)).astype(jnp.bfloat16)
            split = jnp.concatenate([hi, mid, lo], axis=1)
            if 1 <= z <= depth_cells:
                both = jnp.dot(split, weights, preferred_element_type=jnp.float32)
                smooth[z] = both[:, :columns]
                across[z - 1] = both[first:last, columns:]
            else:
                smooth[z] = jnp.dot(
                    split, weights[:, :columns], preferred_element_type=jnp.float32
                )

        @pl.when(row_index == 0)
        def _():
            smooth[:, first - 1 : first, :] = jnp.zeros(
                (depth_cells + 2, 1, columns), jnp.float32
            )

        @pl.when(row_index == n_rows - 1)
        def _():
            smooth[:, last : last + 1, :] = jnp.zeros((depth_cells + 2, 1, columns), jnp.float32)

        @pl.when(depth_index == 0)
        def _():
            smooth[0] = jnp.zeros((padded_rows, columns), jnp.float32)

        @pl.when(depth_index == n_depth - 1)
        def _():
            smooth[depth_cells + 1] = jnp.zeros((padded_rows, columns), jnp.float32)

        own_live = live_ref[depth_index, row_index]
        slab_start = (depth_index * depth_cells).astype(jnp.float32)
        for z in range(depth_cells):
            center = smooth[z + 1, pl.ds(first, row_cells)]
            diff_depth = (
                smooth[z + 2, pl.ds(first, row_cells)] - smooth[z, pl.ds(first, row_cells)]
            )
            diff_rows = (
                smooth[z + 1, pl.ds(first + 1, row_cells)]
                - smooth[z + 1, pl.ds(first - 1, row_cells)]
            )
            diff_cols = across[z]
            square = diff_depth * diff_depth + diff_rows * diff_rows + diff_cols * diff_cols
            toward = LIGHT[0] * diff_depth + LIGHT[1] * diff_rows + LIGHT[2] * diff_cols
            facing = jnp.maximum(0.0, toward) * lax.rsqrt(square + floor)
            twice = center * (2.0 / cells)
            small = jnp.exp(-jnp.abs(twice))
            log1p = jnp.where(small < 1e-4, small * (1.0 - 0.5 * small), jnp.log(1.0 + small))
            softplus = jnp.maximum(twice, 0.0) + log1p
            opacity = jnp.where(z < own_live, 1.0 - jnp.exp(-extinct * softplus), 0.0)
            bright = opacity * (0.25 + 0.75 * facing)
            rgba = jnp.concatenate(
                [(bright * palette_ref[c]).astype(jnp.bfloat16) for c in range(3)]
                + [opacity.astype(jnp.bfloat16)],
                axis=0,
            )
            matrix = shear_matrices(slopes_ref, slab_start + float(z), columns, total_depth)
            sheared[z] = jnp.dot(rgba, matrix, preferred_element_type=jnp.float32)

        for tile in range(n_depth):
            place = [owner_ref[view, tile] for view in range(VIEWS)]
            for inside in range(0, tile_rows, step_rows):
                for view in range(VIEWS):
                    lanes = pl.ds(view * columns, columns)
                    colour, transmit = None, None
                    for z in range(depth_cells):
                        part = [
                            sheared[
                                z,
                                pl.ds(c * row_cells + tile * tile_rows + inside, step_rows),
                                lanes,
                            ]
                            for c in range(4)
                        ]
                        clear = 1.0 - part[3]
                        if z == 0:
                            colour, transmit = part[:3], clear
                        elif view == 0:
                            colour = [colour[c] + transmit * part[c] for c in range(3)]
                            transmit = transmit * clear
                        else:
                            colour = [part[c] + clear * colour[c] for c in range(3)]
                            transmit = transmit * clear
                    values = colour + [1.0 - transmit]
                    share = PACKED_ROWS // step_rows
                    for c in range(0, 4, share):
                        value = values[c] if share == 1 else jnp.concatenate(values[c : c + share])
                        rows = pl.ds(c * tile_rows + inside, PACKED_ROWS)
                        out_ref[place[view], view, rows] = encode(value)

    smem = pl.BlockSpec(memory_space=pltpu.SMEM)
    vmem = pl.BlockSpec(memory_space=pltpu.VMEM)
    return pl.pallas_call(
        kernel,
        out_shape=jax.ShapeDtypeStruct((n_depth, VIEWS, 4 * tile_rows, columns), jnp.int16),
        in_specs=[smem] * 4 + [vmem] * 6,
        out_specs=vmem,
        scratch_shapes=[
            pltpu.VMEM((depth_cells + 2, padded_rows, columns), jnp.float32),
            pltpu.VMEM((padded_rows + 2 * ROW_TILE, columns), jnp.float32),
            pltpu.VMEM((depth_cells + 2, padded_rows, columns), jnp.float32),
            pltpu.VMEM((depth_cells, row_cells, columns), jnp.float32),
            pltpu.VMEM((depth_cells, 4 * row_cells, VIEWS * columns), jnp.float32),
        ],
        compiler_params=pltpu.CompilerParams(vmem_limit_bytes=VMEM_BYTES),
        name="render",
    )


def composite_kernel(order_ref, in_ref, out_ref):
    count = in_ref.shape[0]
    rows = in_ref.shape[2] // 4
    for view in range(VIEWS):
        colour, transmit = None, None
        for k in range(count):
            source = order_ref[view, k]
            values = decode(in_ref[source, view])
            part = [values[c * rows : (c + 1) * rows] for c in range(4)]
            clear = 1.0 - part[3]
            if k == 0:
                colour, transmit = part[:3], clear
            else:
                colour = [colour[c] + transmit * part[c] for c in range(3)]
                transmit = transmit * clear
        for c, value in enumerate(colour + [1.0 - transmit]):
            out_ref[view, c, 0] = value


def body(density, live_slices, shear_slopes, palette, depth_order, tile_owner):
    depth_cells, row_cells, columns = density.shape
    n_depth = lax.axis_size("gz")
    n_rows = lax.axis_size("xy")

    edge = depth_cells - HALO
    odd_depth = lax.axis_index("gz") % 2 == 1
    odd_row = lax.axis_index("xy") % 2 == 1

    def pairs(axis, first):
        count = lax.axis_size(axis)
        lower = range(first, count - 1, 2)
        return [(i, i + 1) for i in lower] + [(i + 1, i) for i in lower]

    low_rows, high_rows = density[:, :ROW_TILE], density[:, row_cells - ROW_TILE :]
    row_even = lax.ppermute(jnp.where(odd_row, low_rows, high_rows), "xy", pairs("xy", 0))
    row_odd = lax.ppermute(jnp.where(odd_row, high_rows, low_rows), "xy", pairs("xy", 1))
    low_deep, high_deep = density[:HALO], density[edge:]
    deep_odd = lax.ppermute(jnp.where(odd_depth, high_deep, low_deep), "gz", pairs("gz", 1))
    rlo = jnp.where(odd_row, row_even, row_odd)
    rhi = jnp.where(odd_row, row_odd, row_even)
    deep_even = lax.ppermute(
        jnp.where(
            odd_depth,
            jnp.concatenate([rlo[:HALO], low_deep, rhi[:HALO]], axis=1),
            jnp.concatenate([rlo[edge:], high_deep, rhi[edge:]], axis=1),
        ),
        "gz",
        pairs("gz", 0),
    )
    corner_odd = lax.ppermute(
        jnp.where(
            odd_depth,
            jnp.concatenate([rlo[edge:], rhi[edge:]], axis=1),
            jnp.concatenate([rlo[:HALO], rhi[:HALO]], axis=1),
        ),
        "gz",
        pairs("gz", 1),
    )
    render = make_render(n_depth, n_rows, depth_cells, row_cells, columns)
    outgoing = render(
        live_slices, shear_slopes, palette, tile_owner,
        density, deep_even, deep_odd, corner_odd, rlo, rhi,
    )
    incoming = lax.all_to_all(outgoing, "gz", split_axis=0, concat_axis=0, tiled=True)
    tile_rows = row_cells // n_depth
    return pl.pallas_call(
        composite_kernel,
        out_shape=jax.ShapeDtypeStruct((VIEWS, 4, 1, tile_rows, columns), jnp.float32),
        in_specs=[pl.BlockSpec(memory_space=pltpu.SMEM), pl.BlockSpec(memory_space=pltpu.VMEM)],
        out_specs=pl.BlockSpec(memory_space=pltpu.VMEM),
        compiler_params=pltpu.CompilerParams(vmem_limit_bytes=VMEM_BYTES),
        name="composite",
    )(depth_order, incoming)


def solution(mesh):
    placed = (P("gz", "xy", None), P(), P(), P(), P(), P())
    return jax.shard_map(
        body, mesh=mesh, in_specs=placed, out_specs=P(None, None, "gz", "xy", None), check_vma=False
    )
```

```python
import jax
import jax.numpy as jnp
from jax import lax
from jax.experimental import pallas as pl
from jax.experimental.pallas import tpu as pltpu
from jax.sharding import PartitionSpec as P

LIGHT = (0.48, 0.6, 0.64)
REACH = 4
HALO = REACH + 1
TAPS = 2 * REACH + 1
ROW_TILE = 8
PACKED_ROWS = 16
VIEWS = 2
TOP = 2.2
STEPS = 65535.0
MIDDLE = 32768
VMEM_BYTES = 40 * 1024 * 1024


def column_matrix(columns):
    source = lax.broadcasted_iota(jnp.int32, (columns, columns), 0)
    target = lax.broadcasted_iota(jnp.int32, (columns, columns), 1)

    def band(shift):
        at = target + shift
        inside = (jnp.abs(source - at) <= REACH) & (at >= 0) & (at < columns)
        return jnp.where(inside, 1.0, 0.0).astype(jnp.float32)

    return jnp.concatenate([band(0), band(1) - band(-1)], axis=1).astype(jnp.bfloat16)


def shear_matrices(slopes_ref, slice_depth, columns, total_depth):
    source = lax.broadcasted_iota(jnp.int32, (columns, columns), 0)
    target = lax.broadcasted_iota(jnp.int32, (columns, columns), 1)
    distance = (source - target).astype(jnp.float32)
    parts = []
    for view in range(VIEWS):
        shift = slopes_ref[view] * (slice_depth + 0.5 - 0.5 * total_depth)
        parts.append(jnp.maximum(0.0, 1.0 - jnp.abs(distance + shift)))
    return jnp.concatenate(parts, axis=1).astype(jnp.bfloat16)


def window_sums(layers, taps):
    sums, width = layers, 1
    while 2 * width < taps:
        sums = [sums[i] + sums[i + width] for i in range(len(sums) - width)]
        width *= 2
    return [sums[i] + layers[i + width] for i in range(len(layers) - width)]


def encode(value):
    root = jnp.exp(0.125 * jnp.log(jnp.maximum(value, 1e-30) * (1.0 / TOP)))
    level = jnp.minimum(root * STEPS + 0.5, STEPS)
    return (level.astype(jnp.int32) - MIDDLE).astype(jnp.int16)


def decode(code):
    root = (code.astype(jnp.int32) + MIDDLE).astype(jnp.float32) * (TOP**0.125 / STEPS)
    square = root * root
    fourth = square * square
    return fourth * fourth


def make_render(n_depth, n_rows, depth_cells, row_cells, columns):
    total_depth = depth_cells * n_depth
    extinct = 3.0 / total_depth
    padded_rows = row_cells + 2 * ROW_TILE
    first, last = ROW_TILE, ROW_TILE + row_cells
    tile_rows = row_cells // n_depth
    step_rows = min(tile_rows, PACKED_ROWS)
    cells = TAPS**3
    floor = 0.01 * (2.0 * cells) ** 2

    def kernel(
        live_ref, slopes_ref, palette_ref, owner_ref,
        own_ref, even_ref, odd_ref, row_even_ref, row_odd_ref,
        out_ref,
        deep, triple, smooth, across, sheared,
    ):
        depth_index = lax.axis_index("gz")
        row_index = lax.axis_index("xy")
        odd_depth = depth_index % 2 == 1
        odd_row = row_index % 2 == 1

        for chunk in range(padded_rows // ROW_TILE):
            rows = pl.ds(chunk * ROW_TILE, ROW_TILE)
            inner = pl.ds((chunk - 1) * ROW_TILE, ROW_TILE)
            if 0 < chunk < padded_rows // ROW_TILE - 1:
                even = [even_ref[i, inner] for i in range(HALO)]
                odd = [odd_ref[i, inner] for i in range(HALO)]
                low = [jnp.where(odd_depth, e, o) for e, o in zip(even, odd)]
                high = [jnp.where(odd_depth, o, e) for e, o in zip(even, odd)]
                layers = low + [own_ref[i, inner] for i in range(depth_cells)] + high
            else:
                take_even = odd_row if chunk == 0 else jnp.logical_not(odd_row)
                layers = [
                    jnp.where(take_even, row_even_ref[i], row_odd_ref[i])
                    for i in range(depth_cells + 2 * HALO)
                ]
            for z, total in enumerate(window_sums(layers, TAPS)):
                deep[z, rows] = total

        band = column_matrix(columns)
        weights = jnp.concatenate([band, band, band], axis=0)
        for z in range(depth_cells + 2):
            lead = first - REACH
            span = row_cells + 2 * REACH
            triple[pl.ds(ROW_TILE, span)] = (
                deep[z, pl.ds(lead - 1, span)]
                + deep[z, pl.ds(lead, span)]
                + deep[z, pl.ds(lead + 1, span)]
            )
            base = ROW_TILE - lead
            total = (
                triple[pl.ds(base - 3, padded_rows)]
                + triple[pl.ds(base, padded_rows)]
                + triple[pl.ds(base + 3, padded_rows)]
            )
            hi = total.astype(jnp.bfloat16)
            rest = total - hi.astype(jnp.float32)
            mid = rest.astype(jnp.bfloat16)
            lo = (rest - mid.astype(jnp.float32)).astype(jnp.bfloat16)
            split = jnp.concatenate([hi, mid, lo], axis=1)
            if 1 <= z <= depth_cells:
                both = jnp.dot(split, weights, preferred_element_type=jnp.float32)
                smooth[z] = both[:, :columns]
                across[z - 1] = both[first:last, columns:]
            else:
                smooth[z] = jnp.dot(
                    split, weights[:, :columns], preferred_element_type=jnp.float32
                )

        @pl.when(row_index == 0)
        def _():
            smooth[:, first - 1 : first, :] = jnp.zeros(
                (depth_cells + 2, 1, columns), jnp.float32
            )

        @pl.when(row_index == n_rows - 1)
        def _():
            smooth[:, last : last + 1, :] = jnp.zeros((depth_cells + 2, 1, columns), jnp.float32)

        @pl.when(depth_index == 0)
        def _():
            smooth[0] = jnp.zeros((padded_rows, columns), jnp.float32)

        @pl.when(depth_index == n_depth - 1)
        def _():
            smooth[depth_cells + 1] = jnp.zeros((padded_rows, columns), jnp.float32)

        own_live = live_ref[depth_index, row_index]
        slab_start = (depth_index * depth_cells).astype(jnp.float32)
        for z in range(depth_cells):
            center = smooth[z + 1, pl.ds(first, row_cells)]
            diff_depth = (
                smooth[z + 2, pl.ds(first, row_cells)] - smooth[z, pl.ds(first, row_cells)]
            )
            diff_rows = (
                smooth[z + 1, pl.ds(first + 1, row_cells)]
                - smooth[z + 1, pl.ds(first - 1, row_cells)]
            )
            diff_cols = across[z]
            square = diff_depth * diff_depth + diff_rows * diff_rows + diff_cols * diff_cols
            toward = LIGHT[0] * diff_depth + LIGHT[1] * diff_rows + LIGHT[2] * diff_cols
            facing = jnp.maximum(0.0, toward) * lax.rsqrt(square + floor)
            twice = center * (2.0 / cells)
            small = jnp.exp(-jnp.abs(twice))
            log1p = jnp.where(small < 1e-4, small * (1.0 - 0.5 * small), jnp.log(1.0 + small))
            softplus = jnp.maximum(twice, 0.0) + log1p
            opacity = jnp.where(z < own_live, 1.0 - jnp.exp(-extinct * softplus), 0.0)
            bright = opacity * (0.25 + 0.75 * facing)
            rgba = jnp.concatenate(
                [(bright * palette_ref[c]).astype(jnp.bfloat16) for c in range(3)]
                + [opacity.astype(jnp.bfloat16)],
                axis=0,
            )
            matrix = shear_matrices(slopes_ref, slab_start + float(z), columns, total_depth)
            sheared[z] = jnp.dot(rgba, matrix, preferred_element_type=jnp.float32)

        for tile in range(n_depth):
            place = [owner_ref[view, tile] for view in range(VIEWS)]
            for inside in range(0, tile_rows, step_rows):
                for view in range(VIEWS):
                    lanes = pl.ds(view * columns, columns)
                    colour, transmit = None, None
                    for z in range(depth_cells):
                        part = [
                            sheared[
                                z,
                                pl.ds(c * row_cells + tile * tile_rows + inside, step_rows),
                                lanes,
                            ]
                            for c in range(4)
                        ]
                        clear = 1.0 - part[3]
                        if z == 0:
                            colour, transmit = part[:3], clear
                        elif view == 0:
                            colour = [colour[c] + transmit * part[c] for c in range(3)]
                            transmit = transmit * clear
                        else:
                            colour = [part[c] + clear * colour[c] for c in range(3)]
                            transmit = transmit * clear
                    values = colour + [1.0 - transmit]
                    share = PACKED_ROWS // step_rows
                    for c in range(0, 4, share):
                        value = values[c] if share == 1 else jnp.concatenate(values[c : c + share])
                        rows = pl.ds(c * tile_rows + inside, PACKED_ROWS)
                        out_ref[place[view], view, rows] = encode(value)

    smem = pl.BlockSpec(memory_space=pltpu.SMEM)
    vmem = pl.BlockSpec(memory_space=pltpu.VMEM)
    return pl.pallas_call(
        kernel,
        out_shape=jax.ShapeDtypeStruct((n_depth, VIEWS, 4 * tile_rows, columns), jnp.int16),
        in_specs=[smem] * 4 + [vmem] * 5,
        out_specs=vmem,
        scratch_shapes=[
            pltpu.VMEM((depth_cells + 2, padded_rows, columns), jnp.float32),
            pltpu.VMEM((padded_rows + 2 * ROW_TILE, columns), jnp.float32),
            pltpu.VMEM((depth_cells + 2, padded_rows, columns), jnp.float32),
            pltpu.VMEM((depth_cells, row_cells, columns), jnp.float32),
            pltpu.VMEM((depth_cells, 4 * row_cells, VIEWS * columns), jnp.float32),
        ],
        compiler_params=pltpu.CompilerParams(vmem_limit_bytes=VMEM_BYTES),
        name="render",
    )


def composite_kernel(order_ref, in_ref, out_ref):
    count = in_ref.shape[0]
    rows = in_ref.shape[2] // 4
    for view in range(VIEWS):
        colour, transmit = None, None
        for k in range(count):
            source = order_ref[view, k]
            values = decode(in_ref[source, view])
            part = [values[c * rows : (c + 1) * rows] for c in range(4)]
            clear = 1.0 - part[3]
            if k == 0:
                colour, transmit = part[:3], clear
            else:
                colour = [colour[c] + transmit * part[c] for c in range(3)]
                transmit = transmit * clear
        for c, value in enumerate(colour + [1.0 - transmit]):
            out_ref[view, c, 0] = value


def body(density, live_slices, shear_slopes, palette, depth_order, tile_owner):
    depth_cells, row_cells, columns = density.shape
    n_depth = lax.axis_size("gz")
    n_rows = lax.axis_size("xy")

    edge = depth_cells - HALO
    odd_depth = lax.axis_index("gz") % 2 == 1
    odd_row = lax.axis_index("xy") % 2 == 1

    def pairs(axis, first):
        count = lax.axis_size(axis)
        lower = range(first, count - 1, 2)
        return [(i, i + 1) for i in lower] + [(i + 1, i) for i in lower]

    low_deep, high_deep = density[:HALO], density[edge:]
    deep_odd = lax.ppermute(jnp.where(odd_depth, high_deep, low_deep), "gz", pairs("gz", 1))
    deep_even = lax.ppermute(jnp.where(odd_depth, low_deep, high_deep), "gz", pairs("gz", 0))

    def rows_of(start):
        rows = slice(start, start + ROW_TILE)
        low = jnp.where(odd_depth, deep_even[:, rows], deep_odd[:, rows])
        high = jnp.where(odd_depth, deep_odd[:, rows], deep_even[:, rows])
        return jnp.concatenate([low, density[:, rows], high], axis=0)

    low_rows, high_rows = rows_of(0), rows_of(row_cells - ROW_TILE)
    row_odd = lax.ppermute(jnp.where(odd_row, high_rows, low_rows), "xy", pairs("xy", 1))
    row_even = lax.ppermute(jnp.where(odd_row, low_rows, high_rows), "xy", pairs("xy", 0))
    render = make_render(n_depth, n_rows, depth_cells, row_cells, columns)
    outgoing = render(
        live_slices, shear_slopes, palette, tile_owner,
        density, deep_even, deep_odd, row_even, row_odd,
    )
    incoming = lax.all_to_all(outgoing, "gz", split_axis=0, concat_axis=0, tiled=True)
    tile_rows = row_cells // n_depth
    return pl.pallas_call(
        composite_kernel,
        out_shape=jax.ShapeDtypeStruct((VIEWS, 4, 1, tile_rows, columns), jnp.float32),
        in_specs=[pl.BlockSpec(memory_space=pltpu.SMEM), pl.BlockSpec(memory_space=pltpu.VMEM)],
        out_specs=pl.BlockSpec(memory_space=pltpu.VMEM),
        compiler_params=pltpu.CompilerParams(vmem_limit_bytes=VMEM_BYTES),
        name="composite",
    )(depth_order, incoming)


def solution(mesh):
    placed = (P("gz", "xy", None), P(), P(), P(), P(), P())
    return jax.shard_map(
        body, mesh=mesh, in_specs=placed, out_specs=P(None, None, "gz", "xy", None), check_vma=False
    )
```

```python
import jax
import jax.numpy as jnp
from jax import lax
from jax.experimental import pallas as pl
from jax.experimental.pallas import tpu as pltpu
from jax.sharding import PartitionSpec as P

LIGHT = (0.48, 0.6, 0.64)
REACH = 4
HALO = REACH + 1
TAPS = 2 * REACH + 1
ROW_TILE = 8
PACKED_ROWS = 16
VIEWS = 2
TOP = 2.2
STEPS = 65535.0
MIDDLE = 32768
VMEM_BYTES = 40 * 1024 * 1024


def column_matrix(columns):
    source = lax.broadcasted_iota(jnp.int32, (columns, columns), 0)
    target = lax.broadcasted_iota(jnp.int32, (columns, columns), 1)

    def band(shift):
        at = target + shift
        inside = (jnp.abs(source - at) <= REACH) & (at >= 0) & (at < columns)
        return jnp.where(inside, 1.0, 0.0).astype(jnp.float32)

    return jnp.concatenate([band(0), band(1) - band(-1)], axis=1).astype(jnp.bfloat16)


def shear_matrices(slopes_ref, slice_depth, columns, total_depth):
    source = lax.broadcasted_iota(jnp.int32, (columns, columns), 0)
    target = lax.broadcasted_iota(jnp.int32, (columns, columns), 1)
    distance = (source - target).astype(jnp.float32)
    parts = []
    for view in range(VIEWS):
        shift = slopes_ref[view] * (slice_depth + 0.5 - 0.5 * total_depth)
        parts.append(jnp.maximum(0.0, 1.0 - jnp.abs(distance + shift)))
    return jnp.concatenate(parts, axis=1).astype(jnp.bfloat16)


def window_sums(layers, taps):
    sums, width = layers, 1
    while 2 * width < taps:
        sums = [sums[i] + sums[i + width] for i in range(len(sums) - width)]
        width *= 2
    return [sums[i] + layers[i + width] for i in range(len(layers) - width)]


def encode(value):
    root = jnp.exp(0.125 * jnp.log(jnp.maximum(value, 1e-30) * (1.0 / TOP)))
    level = jnp.minimum(root * STEPS + 0.5, STEPS)
    return (level.astype(jnp.int32) - MIDDLE).astype(jnp.int16)


def decode(code):
    root = (code.astype(jnp.int32) + MIDDLE).astype(jnp.float32) * (TOP**0.125 / STEPS)
    square = root * root
    fourth = square * square
    return fourth * fourth


def make_render(n_depth, n_rows, depth_cells, row_cells, columns):
    total_depth = depth_cells * n_depth
    extinct = 3.0 / total_depth
    padded_rows = row_cells + 2 * ROW_TILE
    first, last = ROW_TILE, ROW_TILE + row_cells
    tile_rows = row_cells // n_depth
    step_rows = min(tile_rows, PACKED_ROWS)
    cells = TAPS**3
    floor = 0.01 * (2.0 * cells) ** 2

    def kernel(
        live_ref, slopes_ref, palette_ref, owner_ref,
        own_ref, even_ref, odd_ref, corner_even_ref, corner_odd_ref, rlo_ref, rhi_ref,
        out_ref,
        deep, triple, smooth, across, sheared,
    ):
        depth_index = lax.axis_index("gz")
        row_index = lax.axis_index("xy")
        odd_depth = depth_index % 2 == 1

        for chunk in range(padded_rows // ROW_TILE):
            rows = pl.ds(chunk * ROW_TILE, ROW_TILE)
            inner = pl.ds((chunk - 1) * ROW_TILE, ROW_TILE)
            if chunk == 0:
                at, pair, mid_ref = pl.ds(0, ROW_TILE), (corner_even_ref, corner_odd_ref), rlo_ref
            elif chunk == padded_rows // ROW_TILE - 1:
                at = pl.ds(ROW_TILE, ROW_TILE)
                pair, mid_ref = (corner_even_ref, corner_odd_ref), rhi_ref
            else:
                at, pair, mid_ref = inner, (even_ref, odd_ref), own_ref
            mid_at = at if mid_ref is own_ref else pl.ds(0, ROW_TILE)
            even, odd = [[ref[i, at] for i in range(HALO)] for ref in pair]
            mid = [mid_ref[i, mid_at] for i in range(depth_cells)]
            low = [jnp.where(odd_depth, e, o) for e, o in zip(even, odd)]
            high = [jnp.where(odd_depth, o, e) for e, o in zip(even, odd)]
            for z, total in enumerate(window_sums(low + mid + high, TAPS)):
                deep[z, rows] = total

        band = column_matrix(columns)
        weights = jnp.concatenate([band, band, band], axis=0)
        for z in range(depth_cells + 2):
            lead = first - REACH
            span = row_cells + 2 * REACH
            triple[pl.ds(ROW_TILE, span)] = (
                deep[z, pl.ds(lead - 1, span)]
                + deep[z, pl.ds(lead, span)]
                + deep[z, pl.ds(lead + 1, span)]
            )
            base = ROW_TILE - lead
            total = (
                triple[pl.ds(base - 3, padded_rows)]
                + triple[pl.ds(base, padded_rows)]
                + triple[pl.ds(base + 3, padded_rows)]
            )
            hi = total.astype(jnp.bfloat16)
            rest = total - hi.astype(jnp.float32)
            mid = rest.astype(jnp.bfloat16)
            lo = (rest - mid.astype(jnp.float32)).astype(jnp.bfloat16)
            split = jnp.concatenate([hi, mid, lo], axis=1)
            if 1 <= z <= depth_cells:
                both = jnp.dot(split, weights, preferred_element_type=jnp.float32)
                smooth[z] = both[:, :columns]
                across[z - 1] = both[first:last, columns:]
            else:
                smooth[z] = jnp.dot(
                    split, weights[:, :columns], preferred_element_type=jnp.float32
                )

        @pl.when(row_index == 0)
        def _():
            smooth[:, first - 1 : first, :] = jnp.zeros(
                (depth_cells + 2, 1, columns), jnp.float32
            )

        @pl.when(row_index == n_rows - 1)
        def _():
            smooth[:, last : last + 1, :] = jnp.zeros((depth_cells + 2, 1, columns), jnp.float32)

        @pl.when(depth_index == 0)
        def _():
            smooth[0] = jnp.zeros((padded_rows, columns), jnp.float32)

        @pl.when(depth_index == n_depth - 1)
        def _():
            smooth[depth_cells + 1] = jnp.zeros((padded_rows, columns), jnp.float32)

        own_live = live_ref[depth_index, row_index]
        slab_start = (depth_index * depth_cells).astype(jnp.float32)
        for z in range(depth_cells):
            center = smooth[z + 1, pl.ds(first, row_cells)]
            diff_depth = (
                smooth[z + 2, pl.ds(first, row_cells)] - smooth[z, pl.ds(first, row_cells)]
            )
            diff_rows = (
                smooth[z + 1, pl.ds(first + 1, row_cells)]
                - smooth[z + 1, pl.ds(first - 1, row_cells)]
            )
            diff_cols = across[z]
            square = diff_depth * diff_depth + diff_rows * diff_rows + diff_cols * diff_cols
            toward = LIGHT[0] * diff_depth + LIGHT[1] * diff_rows + LIGHT[2] * diff_cols
            facing = jnp.maximum(0.0, toward) * lax.rsqrt(square + floor)
            twice = center * (2.0 / cells)
            small = jnp.exp(-jnp.abs(twice))
            log1p = jnp.where(small < 1e-4, small * (1.0 - 0.5 * small), jnp.log(1.0 + small))
            softplus = jnp.maximum(twice, 0.0) + log1p
            opacity = jnp.where(z < own_live, 1.0 - jnp.exp(-extinct * softplus), 0.0)
            bright = opacity * (0.25 + 0.75 * facing)
            rgba = jnp.concatenate(
                [(bright * palette_ref[c]).astype(jnp.bfloat16) for c in range(3)]
                + [opacity.astype(jnp.bfloat16)],
                axis=0,
            )
            matrix = shear_matrices(slopes_ref, slab_start + float(z), columns, total_depth)
            sheared[z] = jnp.dot(rgba, matrix, preferred_element_type=jnp.float32)

        for tile in range(n_depth):
            place = [owner_ref[view, tile] for view in range(VIEWS)]
            for inside in range(0, tile_rows, step_rows):
                for view in range(VIEWS):
                    lanes = pl.ds(view * columns, columns)
                    colour, transmit = None, None
                    for z in range(depth_cells):
                        part = [
                            sheared[
                                z,
                                pl.ds(c * row_cells + tile * tile_rows + inside, step_rows),
                                lanes,
                            ]
                            for c in range(4)
                        ]
                        clear = 1.0 - part[3]
                        if z == 0:
                            colour, transmit = part[:3], clear
                        elif view == 0:
                            colour = [colour[c] + transmit * part[c] for c in range(3)]
                            transmit = transmit * clear
                        else:
                            colour = [part[c] + clear * colour[c] for c in range(3)]
                            transmit = transmit * clear
                    values = colour + [1.0 - transmit]
                    share = PACKED_ROWS // step_rows
                    for c in range(0, 4, share):
                        value = values[c] if share == 1 else jnp.concatenate(values[c : c + share])
                        rows = pl.ds(c * tile_rows + inside, PACKED_ROWS)
                        out_ref[place[view], view, rows] = encode(value)

    smem = pl.BlockSpec(memory_space=pltpu.SMEM)
    vmem = pl.BlockSpec(memory_space=pltpu.VMEM)
    return pl.pallas_call(
        kernel,
        out_shape=jax.ShapeDtypeStruct((n_depth, VIEWS, 4 * tile_rows, columns), jnp.int16),
        in_specs=[smem] * 4 + [vmem] * 7,
        out_specs=vmem,
        scratch_shapes=[
            pltpu.VMEM((depth_cells + 2, padded_rows, columns), jnp.float32),
            pltpu.VMEM((padded_rows + 2 * ROW_TILE, columns), jnp.float32),
            pltpu.VMEM((depth_cells + 2, padded_rows, columns), jnp.float32),
            pltpu.VMEM((depth_cells, row_cells, columns), jnp.float32),
            pltpu.VMEM((depth_cells, 4 * row_cells, VIEWS * columns), jnp.float32),
        ],
        compiler_params=pltpu.CompilerParams(vmem_limit_bytes=VMEM_BYTES),
        name="render",
    )


def composite_kernel(order_ref, in_ref, out_ref):
    count = in_ref.shape[0]
    rows = in_ref.shape[2] // 4
    for view in range(VIEWS):
        colour, transmit = None, None
        for k in range(count):
            source = order_ref[view, k]
            values = decode(in_ref[source, view])
            part = [values[c * rows : (c + 1) * rows] for c in range(4)]
            clear = 1.0 - part[3]
            if k == 0:
                colour, transmit = part[:3], clear
            else:
                colour = [colour[c] + transmit * part[c] for c in range(3)]
                transmit = transmit * clear
        for c, value in enumerate(colour + [1.0 - transmit]):
            out_ref[view, c, 0] = value


def body(density, live_slices, shear_slopes, palette, depth_order, tile_owner):
    depth_cells, row_cells, columns = density.shape
    n_depth = lax.axis_size("gz")
    n_rows = lax.axis_size("xy")

    edge = depth_cells - HALO
    odd_depth = lax.axis_index("gz") % 2 == 1
    odd_row = lax.axis_index("xy") % 2 == 1

    def pairs(axis, first):
        count = lax.axis_size(axis)
        lower = range(first, count - 1, 2)
        return [(i, i + 1) for i in lower] + [(i + 1, i) for i in lower]

    low_rows, high_rows = density[:, :ROW_TILE], density[:, row_cells - ROW_TILE :]
    row_even = lax.ppermute(jnp.where(odd_row, low_rows, high_rows), "xy", pairs("xy", 0))
    row_odd = lax.ppermute(jnp.where(odd_row, high_rows, low_rows), "xy", pairs("xy", 1))
    low_deep, high_deep = density[:HALO], density[edge:]
    deep_odd = lax.ppermute(jnp.where(odd_depth, high_deep, low_deep), "gz", pairs("gz", 1))
    deep_even = lax.ppermute(jnp.where(odd_depth, low_deep, high_deep), "gz", pairs("gz", 0))
    rlo = jnp.where(odd_row, row_even, row_odd)
    rhi = jnp.where(odd_row, row_odd, row_even)
    low_corner = jnp.concatenate([rlo[:HALO], rhi[:HALO]], axis=1)
    high_corner = jnp.concatenate([rlo[edge:], rhi[edge:]], axis=1)
    corner_odd = lax.ppermute(
        jnp.where(odd_depth, high_corner, low_corner), "gz", pairs("gz", 1)
    )
    corner_even = lax.ppermute(
        jnp.where(odd_depth, low_corner, high_corner), "gz", pairs("gz", 0)
    )
    render = make_render(n_depth, n_rows, depth_cells, row_cells, columns)
    outgoing = render(
        live_slices, shear_slopes, palette, tile_owner,
        density, deep_even, deep_odd, corner_even, corner_odd, rlo, rhi,
    )
    incoming = lax.all_to_all(outgoing, "gz", split_axis=0, concat_axis=0, tiled=True)
    tile_rows = row_cells // n_depth
    return pl.pallas_call(
        composite_kernel,
        out_shape=jax.ShapeDtypeStruct((VIEWS, 4, 1, tile_rows, columns), jnp.float32),
        in_specs=[pl.BlockSpec(memory_space=pltpu.SMEM), pl.BlockSpec(memory_space=pltpu.VMEM)],
        out_specs=pl.BlockSpec(memory_space=pltpu.VMEM),
        compiler_params=pltpu.CompilerParams(vmem_limit_bytes=VMEM_BYTES),
        name="composite",
    )(depth_order, incoming)


def solution(mesh):
    placed = (P("gz", "xy", None), P(), P(), P(), P(), P())
    return jax.shard_map(
        body, mesh=mesh, in_specs=placed, out_specs=P(None, None, "gz", "xy", None), check_vma=False
    )
```

```python
import jax
import jax.numpy as jnp
from jax import lax
from jax.experimental import pallas as pl
from jax.experimental.pallas import tpu as pltpu
from jax.sharding import PartitionSpec as P

LIGHT = (0.48, 0.6, 0.64)
REACH = 4
HALO = REACH + 1
TAPS = 2 * REACH + 1
ROW_TILE = 8
PACKED_ROWS = 16
VIEWS = 2
TOP = 2.2
STEPS = 65535.0
MIDDLE = 32768
VMEM_BYTES = 40 * 1024 * 1024


def column_matrix(columns):
    source = lax.broadcasted_iota(jnp.int32, (columns, columns), 0)
    target = lax.broadcasted_iota(jnp.int32, (columns, columns), 1)

    def band(shift):
        at = target + shift
        inside = (jnp.abs(source - at) <= REACH) & (at >= 0) & (at < columns)
        return jnp.where(inside, 1.0, 0.0).astype(jnp.float32)

    return jnp.concatenate([band(0), band(1) - band(-1)], axis=1).astype(jnp.bfloat16)


def shear_matrices(slopes_ref, slice_depth, columns, total_depth):
    source = lax.broadcasted_iota(jnp.int32, (columns, columns), 0)
    target = lax.broadcasted_iota(jnp.int32, (columns, columns), 1)
    distance = (source - target).astype(jnp.float32)
    parts = []
    for view in range(VIEWS):
        shift = slopes_ref[view] * (slice_depth + 0.5 - 0.5 * total_depth)
        parts.append(jnp.maximum(0.0, 1.0 - jnp.abs(distance + shift)))
    return jnp.concatenate(parts, axis=1).astype(jnp.bfloat16)


def window_sums(layers, taps):
    sums, width = layers, 1
    while 2 * width < taps:
        sums = [sums[i] + sums[i + width] for i in range(len(sums) - width)]
        width *= 2
    return [sums[i] + layers[i + width] for i in range(len(layers) - width)]


def encode(value):
    root = jnp.exp(0.125 * jnp.log(jnp.maximum(value, 1e-30) * (1.0 / TOP)))
    level = jnp.minimum(root * STEPS + 0.5, STEPS)
    return (level.astype(jnp.int32) - MIDDLE).astype(jnp.int16)


def decode(code):
    root = (code.astype(jnp.int32) + MIDDLE).astype(jnp.float32) * (TOP**0.125 / STEPS)
    square = root * root
    fourth = square * square
    return fourth * fourth


def make_render(n_depth, n_rows, depth_cells, row_cells, columns):
    total_depth = depth_cells * n_depth
    extinct = 3.0 / total_depth
    padded_rows = row_cells + 2 * ROW_TILE
    first, last = ROW_TILE, ROW_TILE + row_cells
    tile_rows = row_cells // n_depth
    step_rows = min(tile_rows, PACKED_ROWS)
    cells = TAPS**3
    floor = 0.01 * (2.0 * cells) ** 2

    def kernel(
        live_ref, slopes_ref, palette_ref, owner_ref,
        own_ref, even_ref, odd_ref, corner_even_ref, corner_odd_ref, rlo_ref, rhi_ref,
        out_ref,
        deep, triple, smooth, across, sheared,
    ):
        depth_index = lax.axis_index("gz")
        row_index = lax.axis_index("xy")
        odd_depth = depth_index % 2 == 1

        for chunk in range(padded_rows // ROW_TILE):
            rows = pl.ds(chunk * ROW_TILE, ROW_TILE)
            inner = pl.ds((chunk - 1) * ROW_TILE, ROW_TILE)
            if chunk == 0:
                at, pair, mid_ref = pl.ds(0, ROW_TILE), (corner_even_ref, corner_odd_ref), rlo_ref
            elif chunk == padded_rows // ROW_TILE - 1:
                at = pl.ds(ROW_TILE, ROW_TILE)
                pair, mid_ref = (corner_even_ref, corner_odd_ref), rhi_ref
            else:
                at, pair, mid_ref = inner, (even_ref, odd_ref), own_ref
            mid_at = at if mid_ref is own_ref else pl.ds(0, ROW_TILE)
            even, odd = [[ref[i, at] for i in range(HALO)] for ref in pair]
            mid = [mid_ref[i, mid_at] for i in range(depth_cells)]
            low = [jnp.where(odd_depth, e, o) for e, o in zip(even, odd)]
            high = [jnp.where(odd_depth, o, e) for e, o in zip(even, odd)]
            for z, total in enumerate(window_sums(low + mid + high, TAPS)):
                deep[z, rows] = total

        band = column_matrix(columns)
        weights = jnp.concatenate([band, band, band], axis=0)
        for z in range(depth_cells + 2):
            lead = first - REACH
            span = row_cells + 2 * REACH
            triple[pl.ds(ROW_TILE, span)] = (
                deep[z, pl.ds(lead - 1, span)]
                + deep[z, pl.ds(lead, span)]
                + deep[z, pl.ds(lead + 1, span)]
            )
            base = ROW_TILE - lead
            total = (
                triple[pl.ds(base - 3, padded_rows)]
                + triple[pl.ds(base, padded_rows)]
                + triple[pl.ds(base + 3, padded_rows)]
            )
            hi = total.astype(jnp.bfloat16)
            rest = total - hi.astype(jnp.float32)
            mid = rest.astype(jnp.bfloat16)
            lo = (rest - mid.astype(jnp.float32)).astype(jnp.bfloat16)
            split = jnp.concatenate([hi, mid, lo], axis=1)
            if 1 <= z <= depth_cells:
                both = jnp.dot(split, weights, preferred_element_type=jnp.float32)
                smooth[z] = both[:, :columns]
                across[z - 1] = both[first:last, columns:]
            else:
                smooth[z] = jnp.dot(
                    split, weights[:, :columns], preferred_element_type=jnp.float32
                )

        @pl.when(row_index == 0)
        def _():
            smooth[:, first - 1 : first, :] = jnp.zeros(
                (depth_cells + 2, 1, columns), jnp.float32
            )

        @pl.when(row_index == n_rows - 1)
        def _():
            smooth[:, last : last + 1, :] = jnp.zeros((depth_cells + 2, 1, columns), jnp.float32)

        @pl.when(depth_index == 0)
        def _():
            smooth[0] = jnp.zeros((padded_rows, columns), jnp.float32)

        @pl.when(depth_index == n_depth - 1)
        def _():
            smooth[depth_cells + 1] = jnp.zeros((padded_rows, columns), jnp.float32)

        own_live = live_ref[depth_index, row_index]
        slab_start = (depth_index * depth_cells).astype(jnp.float32)
        for z in range(depth_cells):
            center = smooth[z + 1, pl.ds(first, row_cells)]
            diff_depth = (
                smooth[z + 2, pl.ds(first, row_cells)] - smooth[z, pl.ds(first, row_cells)]
            )
            diff_rows = (
                smooth[z + 1, pl.ds(first + 1, row_cells)]
                - smooth[z + 1, pl.ds(first - 1, row_cells)]
            )
            diff_cols = across[z]
            square = diff_depth * diff_depth + diff_rows * diff_rows + diff_cols * diff_cols
            toward = LIGHT[0] * diff_depth + LIGHT[1] * diff_rows + LIGHT[2] * diff_cols
            facing = jnp.maximum(0.0, toward) * lax.rsqrt(square + floor)
            twice = center * (2.0 / cells)
            small = jnp.exp(-jnp.abs(twice))
            log1p = jnp.where(small < 1e-4, small * (1.0 - 0.5 * small), jnp.log(1.0 + small))
            softplus = jnp.maximum(twice, 0.0) + log1p
            opacity = jnp.where(z < own_live, 1.0 - jnp.exp(-extinct * softplus), 0.0)
            bright = opacity * (0.25 + 0.75 * facing)
            rgba = jnp.concatenate(
                [(bright * palette_ref[c]).astype(jnp.bfloat16) for c in range(3)]
                + [opacity.astype(jnp.bfloat16)],
                axis=0,
            )
            matrix = shear_matrices(slopes_ref, slab_start + float(z), columns, total_depth)
            sheared[z] = jnp.dot(rgba, matrix, preferred_element_type=jnp.float32)

        for tile in range(n_depth):
            place = [owner_ref[view, tile] for view in range(VIEWS)]
            for inside in range(0, tile_rows, step_rows):
                for view in range(VIEWS):
                    lanes = pl.ds(view * columns, columns)
                    colour, transmit = None, None
                    for z in range(depth_cells):
                        part = [
                            sheared[
                                z,
                                pl.ds(c * row_cells + tile * tile_rows + inside, step_rows),
                                lanes,
                            ]
                            for c in range(4)
                        ]
                        clear = 1.0 - part[3]
                        if z == 0:
                            colour, transmit = part[:3], clear
                        elif view == 0:
                            colour = [colour[c] + transmit * part[c] for c in range(3)]
                            transmit = transmit * clear
                        else:
                            colour = [part[c] + clear * colour[c] for c in range(3)]
                            transmit = transmit * clear
                    values = colour + [1.0 - transmit]
                    share = PACKED_ROWS // step_rows
                    for c in range(0, 4, share):
                        value = values[c] if share == 1 else jnp.concatenate(values[c : c + share])
                        rows = pl.ds(c * tile_rows + inside, PACKED_ROWS)
                        out_ref[place[view], view, rows] = encode(value)

    smem = pl.BlockSpec(memory_space=pltpu.SMEM)
    vmem = pl.BlockSpec(memory_space=pltpu.VMEM)
    return pl.pallas_call(
        kernel,
        out_shape=jax.ShapeDtypeStruct((n_depth, VIEWS, 4 * tile_rows, columns), jnp.int16),
        in_specs=[smem] * 4 + [vmem] * 7,
        out_specs=vmem,
        scratch_shapes=[
            pltpu.VMEM((depth_cells + 2, padded_rows, columns), jnp.float32),
            pltpu.VMEM((padded_rows + 2 * ROW_TILE, columns), jnp.float32),
            pltpu.VMEM((depth_cells + 2, padded_rows, columns), jnp.float32),
            pltpu.VMEM((depth_cells, row_cells, columns), jnp.float32),
            pltpu.VMEM((depth_cells, 4 * row_cells, VIEWS * columns), jnp.float32),
        ],
        compiler_params=pltpu.CompilerParams(vmem_limit_bytes=VMEM_BYTES),
        name="render",
    )


def cut_edges(density):
    depth_cells, row_cells, columns = density.shape

    def kernel(density_ref, row_even_ref, row_odd_ref, deep_even_ref, deep_odd_ref, sems):
        row_bit = lax.axis_index("xy") % 2
        depth_bit = lax.axis_index("gz") % 2
        last_rows, last_deep = row_cells - ROW_TILE, depth_cells - HALO

        def rows(bit):
            return density_ref.at[:, pl.ds(pl.multiple_of(bit * last_rows, ROW_TILE), ROW_TILE)]

        def deep(bit):
            return density_ref.at[pl.ds(bit * last_deep, HALO)]

        copies = [
            pltpu.make_async_copy(deep(depth_bit), deep_odd_ref, sems.at[0]),
            pltpu.make_async_copy(deep(1 - depth_bit), deep_even_ref, sems.at[1]),
            pltpu.make_async_copy(rows(1 - row_bit), row_even_ref, sems.at[2]),
            pltpu.make_async_copy(rows(row_bit), row_odd_ref, sems.at[3]),
        ]
        for copy in copies:
            copy.start()
        for copy in copies:
            copy.wait()

    rows = jax.ShapeDtypeStruct((depth_cells, ROW_TILE, columns), jnp.float32)
    deep = jax.ShapeDtypeStruct((HALO, row_cells, columns), jnp.float32)
    return pl.pallas_call(
        kernel,
        out_shape=(rows, rows, deep, deep),
        in_specs=[pl.BlockSpec(memory_space=pltpu.HBM)],
        out_specs=(pl.BlockSpec(memory_space=pltpu.VMEM),) * 4,
        scratch_shapes=[pltpu.SemaphoreType.DMA((4,))],
        compiler_params=pltpu.CompilerParams(vmem_limit_bytes=VMEM_BYTES),
        name="cut_edges",
    )(density)


def composite_kernel(order_ref, in_ref, out_ref):
    count = in_ref.shape[0]
    rows = in_ref.shape[2] // 4
    for view in range(VIEWS):
        colour, transmit = None, None
        for k in range(count):
            source = order_ref[view, k]
            values = decode(in_ref[source, view])
            part = [values[c * rows : (c + 1) * rows] for c in range(4)]
            clear = 1.0 - part[3]
            if k == 0:
                colour, transmit = part[:3], clear
            else:
                colour = [colour[c] + transmit * part[c] for c in range(3)]
                transmit = transmit * clear
        for c, value in enumerate(colour + [1.0 - transmit]):
            out_ref[view, c, 0] = value


def body(density, live_slices, shear_slopes, palette, depth_order, tile_owner):
    depth_cells, row_cells, columns = density.shape
    n_depth = lax.axis_size("gz")
    n_rows = lax.axis_size("xy")

    edge = depth_cells - HALO
    odd_depth = lax.axis_index("gz") % 2 == 1
    odd_row = lax.axis_index("xy") % 2 == 1

    def pairs(axis, first):
        count = lax.axis_size(axis)
        lower = range(first, count - 1, 2)
        return [(i, i + 1) for i in lower] + [(i + 1, i) for i in lower]

    row_even, row_odd, deep_even, deep_odd = cut_edges(density)
    row_even = lax.ppermute(row_even, "xy", pairs("xy", 0))
    row_odd = lax.ppermute(row_odd, "xy", pairs("xy", 1))
    deep_odd = lax.ppermute(deep_odd, "gz", pairs("gz", 1))
    deep_even = lax.ppermute(deep_even, "gz", pairs("gz", 0))
    rlo = jnp.where(odd_row, row_even, row_odd)
    rhi = jnp.where(odd_row, row_odd, row_even)
    low_corner = jnp.concatenate([rlo[:HALO], rhi[:HALO]], axis=1)
    high_corner = jnp.concatenate([rlo[edge:], rhi[edge:]], axis=1)
    corner_odd = lax.ppermute(
        jnp.where(odd_depth, high_corner, low_corner), "gz", pairs("gz", 1)
    )
    corner_even = lax.ppermute(
        jnp.where(odd_depth, low_corner, high_corner), "gz", pairs("gz", 0)
    )
    render = make_render(n_depth, n_rows, depth_cells, row_cells, columns)
    outgoing = render(
        live_slices, shear_slopes, palette, tile_owner,
        density, deep_even, deep_odd, corner_even, corner_odd, rlo, rhi,
    )
    incoming = lax.all_to_all(outgoing, "gz", split_axis=0, concat_axis=0, tiled=True)
    tile_rows = row_cells // n_depth
    return pl.pallas_call(
        composite_kernel,
        out_shape=jax.ShapeDtypeStruct((VIEWS, 4, 1, tile_rows, columns), jnp.float32),
        in_specs=[pl.BlockSpec(memory_space=pltpu.SMEM), pl.BlockSpec(memory_space=pltpu.VMEM)],
        out_specs=pl.BlockSpec(memory_space=pltpu.VMEM),
        compiler_params=pltpu.CompilerParams(vmem_limit_bytes=VMEM_BYTES),
        name="composite",
    )(depth_order, incoming)


def solution(mesh):
    placed = (P("gz", "xy", None), P(), P(), P(), P(), P())
    return jax.shard_map(
        body, mesh=mesh, in_specs=placed, out_specs=P(None, None, "gz", "xy", None), check_vma=False
    )
```

```python
import jax
import jax.numpy as jnp
from jax import lax
from jax.experimental import pallas as pl
from jax.experimental.pallas import tpu as pltpu
from jax.sharding import PartitionSpec as P

LIGHT = (0.48, 0.6, 0.64)
REACH = 4
HALO = REACH + 1
TAPS = 2 * REACH + 1
ROW_TILE = 8
PACKED_ROWS = 16
VIEWS = 2
TOP = 2.2
STEPS = 65535.0
MIDDLE = 32768
VMEM_BYTES = 40 * 1024 * 1024


def column_matrix(columns):
    source = lax.broadcasted_iota(jnp.int32, (columns, columns), 0)
    target = lax.broadcasted_iota(jnp.int32, (columns, columns), 1)

    def band(shift):
        at = target + shift
        inside = (jnp.abs(source - at) <= REACH) & (at >= 0) & (at < columns)
        return jnp.where(inside, 1.0, 0.0).astype(jnp.float32)

    return jnp.concatenate([band(0), band(1) - band(-1)], axis=1).astype(jnp.bfloat16)


def shear_matrices(slopes_ref, slice_depth, columns, total_depth):
    source = lax.broadcasted_iota(jnp.int32, (columns, columns), 0)
    target = lax.broadcasted_iota(jnp.int32, (columns, columns), 1)
    distance = (source - target).astype(jnp.float32)
    parts = []
    for view in range(VIEWS):
        shift = slopes_ref[view] * (slice_depth + 0.5 - 0.5 * total_depth)
        parts.append(jnp.maximum(0.0, 1.0 - jnp.abs(distance + shift)))
    return jnp.concatenate(parts, axis=1).astype(jnp.bfloat16)


def window_sums(layers, taps):
    sums, width = layers, 1
    while 2 * width < taps:
        sums = [sums[i] + sums[i + width] for i in range(len(sums) - width)]
        width *= 2
    return [sums[i] + layers[i + width] for i in range(len(layers) - width)]


def depth_sums(even, middle, odd, odd_depth):
    low = [jnp.where(odd_depth, e, o) for e, o in zip(even, odd)]
    high = [jnp.where(odd_depth, o, e) for e, o in zip(even, odd)]
    return window_sums(low + middle + high, TAPS)


def prepare(shear_slopes, density, deep_even, deep_odd, n_depth):
    depth_cells, row_cells, columns = density.shape
    total_depth = depth_cells * n_depth

    def kernel(slopes_ref, own_ref, even_ref, odd_ref, deep_ref, shear_ref):
        depth_index = lax.axis_index("gz")
        odd_depth = depth_index % 2 == 1
        for start in range(0, row_cells, ROW_TILE):
            rows = pl.ds(start, ROW_TILE)
            even = [even_ref[i, rows] for i in range(HALO)]
            odd = [odd_ref[i, rows] for i in range(HALO)]
            middle = [own_ref[i, rows] for i in range(depth_cells)]
            for z, total in enumerate(depth_sums(even, middle, odd, odd_depth)):
                deep_ref[z, rows] = total
        slab_start = (depth_index * depth_cells).astype(jnp.float32)
        for z in range(depth_cells):
            shear_ref[z] = shear_matrices(
                slopes_ref, slab_start + float(z), columns, total_depth
            )

    smem = pl.BlockSpec(memory_space=pltpu.SMEM)
    vmem = pl.BlockSpec(memory_space=pltpu.VMEM)
    layers = depth_cells + 2
    plane = row_cells * columns
    return pl.pallas_call(
        kernel,
        out_shape=(
            jax.ShapeDtypeStruct((layers, row_cells, columns), jnp.float32),
            jax.ShapeDtypeStruct((depth_cells, columns, VIEWS * columns), jnp.bfloat16),
        ),
        in_specs=[smem] + [vmem] * 3,
        out_specs=(vmem, vmem),
        compiler_params=pltpu.CompilerParams(vmem_limit_bytes=VMEM_BYTES),
        cost_estimate=pl.CostEstimate(
            flops=6 * layers * plane,
            bytes_accessed=4 * plane * (2 * layers + 2 * HALO + depth_cells),
            transcendentals=0,
        ),
        name="prepare",
    )(shear_slopes, density, deep_even, deep_odd)


def encode(value):
    root = jnp.exp(0.125 * jnp.log(jnp.maximum(value, 1e-30) * (1.0 / TOP)))
    level = jnp.minimum(root * STEPS + 0.5, STEPS)
    return (level.astype(jnp.int32) - MIDDLE).astype(jnp.int16)


def decode(code):
    root = (code.astype(jnp.int32) + MIDDLE).astype(jnp.float32) * (TOP**0.125 / STEPS)
    square = root * root
    fourth = square * square
    return fourth * fourth


def make_render(n_depth, n_rows, depth_cells, row_cells, columns):
    total_depth = depth_cells * n_depth
    extinct = 3.0 / total_depth
    padded_rows = row_cells + 2 * ROW_TILE
    first, last = ROW_TILE, ROW_TILE + row_cells
    tile_rows = row_cells // n_depth
    step_rows = min(tile_rows, PACKED_ROWS)
    cells = TAPS**3
    floor = 0.01 * (2.0 * cells) ** 2

    def kernel(
        live_ref, palette_ref, owner_ref,
        deep_ref, shear_ref, corner_even_ref, corner_odd_ref, rlo_ref, rhi_ref,
        out_ref,
        deep, triple, smooth, across, sheared,
    ):
        depth_index = lax.axis_index("gz")
        row_index = lax.axis_index("xy")
        odd_depth = depth_index % 2 == 1

        deep[:, pl.ds(first, row_cells)] = deep_ref[...]
        for at, mid_ref in ((0, rlo_ref), (ROW_TILE, rhi_ref)):
            even = [corner_even_ref[i, pl.ds(at, ROW_TILE)] for i in range(HALO)]
            odd = [corner_odd_ref[i, pl.ds(at, ROW_TILE)] for i in range(HALO)]
            middle = [mid_ref[i] for i in range(depth_cells)]
            row = 0 if at == 0 else last
            for z, total in enumerate(depth_sums(even, middle, odd, odd_depth)):
                deep[z, pl.ds(row, ROW_TILE)] = total

        band = column_matrix(columns)
        weights = jnp.concatenate([band, band, band], axis=0)
        for z in range(depth_cells + 2):
            lead = first - REACH
            span = row_cells + 2 * REACH
            triple[pl.ds(ROW_TILE, span)] = (
                deep[z, pl.ds(lead - 1, span)]
                + deep[z, pl.ds(lead, span)]
                + deep[z, pl.ds(lead + 1, span)]
            )
            base = ROW_TILE - lead
            total = (
                triple[pl.ds(base - 3, padded_rows)]
                + triple[pl.ds(base, padded_rows)]
                + triple[pl.ds(base + 3, padded_rows)]
            )
            hi = total.astype(jnp.bfloat16)
            rest = total - hi.astype(jnp.float32)
            mid = rest.astype(jnp.bfloat16)
            lo = (rest - mid.astype(jnp.float32)).astype(jnp.bfloat16)
            split = jnp.concatenate([hi, mid, lo], axis=1)
            if 1 <= z <= depth_cells:
                both = jnp.dot(split, weights, preferred_element_type=jnp.float32)
                smooth[z] = both[:, :columns]
                across[z - 1] = both[first:last, columns:]
            else:
                smooth[z] = jnp.dot(
                    split, weights[:, :columns], preferred_element_type=jnp.float32
                )

        @pl.when(row_index == 0)
        def _():
            smooth[:, first - 1 : first, :] = jnp.zeros(
                (depth_cells + 2, 1, columns), jnp.float32
            )

        @pl.when(row_index == n_rows - 1)
        def _():
            smooth[:, last : last + 1, :] = jnp.zeros((depth_cells + 2, 1, columns), jnp.float32)

        @pl.when(depth_index == 0)
        def _():
            smooth[0] = jnp.zeros((padded_rows, columns), jnp.float32)

        @pl.when(depth_index == n_depth - 1)
        def _():
            smooth[depth_cells + 1] = jnp.zeros((padded_rows, columns), jnp.float32)

        own_live = live_ref[depth_index, row_index]
        for z in range(depth_cells):
            center = smooth[z + 1, pl.ds(first, row_cells)]
            diff_depth = (
                smooth[z + 2, pl.ds(first, row_cells)] - smooth[z, pl.ds(first, row_cells)]
            )
            diff_rows = (
                smooth[z + 1, pl.ds(first + 1, row_cells)]
                - smooth[z + 1, pl.ds(first - 1, row_cells)]
            )
            diff_cols = across[z]
            square = diff_depth * diff_depth + diff_rows * diff_rows + diff_cols * diff_cols
            toward = LIGHT[0] * diff_depth + LIGHT[1] * diff_rows + LIGHT[2] * diff_cols
            facing = jnp.maximum(0.0, toward) * lax.rsqrt(square + floor)
            twice = center * (2.0 / cells)
            small = jnp.exp(-jnp.abs(twice))
            log1p = jnp.where(small < 1e-4, small * (1.0 - 0.5 * small), jnp.log(1.0 + small))
            softplus = jnp.maximum(twice, 0.0) + log1p
            opacity = jnp.where(z < own_live, 1.0 - jnp.exp(-extinct * softplus), 0.0)
            bright = opacity * (0.25 + 0.75 * facing)
            rgba = jnp.concatenate(
                [(bright * palette_ref[c]).astype(jnp.bfloat16) for c in range(3)]
                + [opacity.astype(jnp.bfloat16)],
                axis=0,
            )
            sheared[z] = jnp.dot(rgba, shear_ref[z], preferred_element_type=jnp.float32)

        for tile in range(n_depth):
            place = [owner_ref[view, tile] for view in range(VIEWS)]
            for inside in range(0, tile_rows, step_rows):
                for view in range(VIEWS):
                    lanes = pl.ds(view * columns, columns)
                    colour, transmit = None, None
                    for z in range(depth_cells):
                        part = [
                            sheared[
                                z,
                                pl.ds(c * row_cells + tile * tile_rows + inside, step_rows),
                                lanes,
                            ]
                            for c in range(4)
                        ]
                        clear = 1.0 - part[3]
                        if z == 0:
                            colour, transmit = part[:3], clear
                        elif view == 0:
                            colour = [colour[c] + transmit * part[c] for c in range(3)]
                            transmit = transmit * clear
                        else:
                            colour = [part[c] + clear * colour[c] for c in range(3)]
                            transmit = transmit * clear
                    values = colour + [1.0 - transmit]
                    share = PACKED_ROWS // step_rows
                    for c in range(0, 4, share):
                        value = values[c] if share == 1 else jnp.concatenate(values[c : c + share])
                        rows = pl.ds(c * tile_rows + inside, PACKED_ROWS)
                        out_ref[place[view], view, rows] = encode(value)

    smem = pl.BlockSpec(memory_space=pltpu.SMEM)
    vmem = pl.BlockSpec(memory_space=pltpu.VMEM)
    return pl.pallas_call(
        kernel,
        out_shape=jax.ShapeDtypeStruct((n_depth, VIEWS, 4 * tile_rows, columns), jnp.int16),
        in_specs=[smem] * 3 + [vmem] * 6,
        out_specs=vmem,
        scratch_shapes=[
            pltpu.VMEM((depth_cells + 2, padded_rows, columns), jnp.float32),
            pltpu.VMEM((padded_rows + 2 * ROW_TILE, columns), jnp.float32),
            pltpu.VMEM((depth_cells + 2, padded_rows, columns), jnp.float32),
            pltpu.VMEM((depth_cells, row_cells, columns), jnp.float32),
            pltpu.VMEM((depth_cells, 4 * row_cells, VIEWS * columns), jnp.float32),
        ],
        compiler_params=pltpu.CompilerParams(vmem_limit_bytes=VMEM_BYTES),
        name="render",
    )


def cut_edges(density):
    depth_cells, row_cells, columns = density.shape

    def kernel(density_ref, row_even_ref, row_odd_ref, deep_even_ref, deep_odd_ref, sems):
        row_bit = lax.axis_index("xy") % 2
        depth_bit = lax.axis_index("gz") % 2
        last_rows, last_deep = row_cells - ROW_TILE, depth_cells - HALO

        def rows(bit):
            return density_ref.at[:, pl.ds(pl.multiple_of(bit * last_rows, ROW_TILE), ROW_TILE)]

        def deep(bit):
            return density_ref.at[pl.ds(bit * last_deep, HALO)]

        copies = [
            pltpu.make_async_copy(deep(depth_bit), deep_odd_ref, sems.at[0]),
            pltpu.make_async_copy(deep(1 - depth_bit), deep_even_ref, sems.at[1]),
            pltpu.make_async_copy(rows(1 - row_bit), row_even_ref, sems.at[2]),
            pltpu.make_async_copy(rows(row_bit), row_odd_ref, sems.at[3]),
        ]
        for copy in copies:
            copy.start()
        for copy in copies:
            copy.wait()

    rows = jax.ShapeDtypeStruct((depth_cells, ROW_TILE, columns), jnp.float32)
    deep = jax.ShapeDtypeStruct((HALO, row_cells, columns), jnp.float32)
    return pl.pallas_call(
        kernel,
        out_shape=(rows, rows, deep, deep),
        in_specs=[pl.BlockSpec(memory_space=pltpu.HBM)],
        out_specs=(pl.BlockSpec(memory_space=pltpu.VMEM),) * 4,
        scratch_shapes=[pltpu.SemaphoreType.DMA((4,))],
        compiler_params=pltpu.CompilerParams(vmem_limit_bytes=VMEM_BYTES),
        name="cut_edges",
    )(density)


def composite_kernel(order_ref, in_ref, out_ref):
    count = in_ref.shape[0]
    rows = in_ref.shape[2] // 4
    for view in range(VIEWS):
        colour, transmit = None, None
        for k in range(count):
            source = order_ref[view, k]
            values = decode(in_ref[source, view])
            part = [values[c * rows : (c + 1) * rows] for c in range(4)]
            clear = 1.0 - part[3]
            if k == 0:
                colour, transmit = part[:3], clear
            else:
                colour = [colour[c] + transmit * part[c] for c in range(3)]
                transmit = transmit * clear
        for c, value in enumerate(colour + [1.0 - transmit]):
            out_ref[view, c, 0] = value


def body(density, live_slices, shear_slopes, palette, depth_order, tile_owner):
    depth_cells, row_cells, columns = density.shape
    n_depth = lax.axis_size("gz")
    n_rows = lax.axis_size("xy")

    edge = depth_cells - HALO
    odd_depth = lax.axis_index("gz") % 2 == 1
    odd_row = lax.axis_index("xy") % 2 == 1

    def pairs(axis, first):
        count = lax.axis_size(axis)
        lower = range(first, count - 1, 2)
        return [(i, i + 1) for i in lower] + [(i + 1, i) for i in lower]

    row_even, row_odd, deep_even, deep_odd = cut_edges(density)
    row_even = lax.ppermute(row_even, "xy", pairs("xy", 0))
    row_odd = lax.ppermute(row_odd, "xy", pairs("xy", 1))
    deep_odd = lax.ppermute(deep_odd, "gz", pairs("gz", 1))
    deep_even = lax.ppermute(deep_even, "gz", pairs("gz", 0))
    rlo = jnp.where(odd_row, row_even, row_odd)
    rhi = jnp.where(odd_row, row_odd, row_even)
    low_corner = jnp.concatenate([rlo[:HALO], rhi[:HALO]], axis=1)
    high_corner = jnp.concatenate([rlo[edge:], rhi[edge:]], axis=1)
    corner_odd = lax.ppermute(
        jnp.where(odd_depth, high_corner, low_corner), "gz", pairs("gz", 1)
    )
    corner_even = lax.ppermute(
        jnp.where(odd_depth, low_corner, high_corner), "gz", pairs("gz", 0)
    )
    render = make_render(n_depth, n_rows, depth_cells, row_cells, columns)
    deep, shear = prepare(shear_slopes, density, deep_even, deep_odd, n_depth)
    outgoing = render(
        live_slices, palette, tile_owner, deep, shear, corner_even, corner_odd, rlo, rhi
    )
    incoming = lax.all_to_all(outgoing, "gz", split_axis=0, concat_axis=0, tiled=True)
    tile_rows = row_cells // n_depth
    return pl.pallas_call(
        composite_kernel,
        out_shape=jax.ShapeDtypeStruct((VIEWS, 4, 1, tile_rows, columns), jnp.float32),
        in_specs=[pl.BlockSpec(memory_space=pltpu.SMEM), pl.BlockSpec(memory_space=pltpu.VMEM)],
        out_specs=pl.BlockSpec(memory_space=pltpu.VMEM),
        compiler_params=pltpu.CompilerParams(vmem_limit_bytes=VMEM_BYTES),
        name="composite",
    )(depth_order, incoming)


def solution(mesh):
    placed = (P("gz", "xy", None), P(), P(), P(), P(), P())
    return jax.shard_map(
        body, mesh=mesh, in_specs=placed, out_specs=P(None, None, "gz", "xy", None), check_vma=False
    )
```

```python
import jax
import jax.numpy as jnp
from jax import lax
from jax.experimental import pallas as pl
from jax.experimental.pallas import tpu as pltpu
from jax.sharding import PartitionSpec as P

LIGHT = (0.48, 0.6, 0.64)
REACH = 4
HALO = REACH + 1
TAPS = 2 * REACH + 1
ROW_TILE = 8
PACKED_ROWS = 16
VIEWS = 2
TOP = 2.2
STEPS = 65535.0
MIDDLE = 32768
VMEM_BYTES = 40 * 1024 * 1024


def column_matrix(columns):
    source = lax.broadcasted_iota(jnp.int32, (columns, columns), 0)
    target = lax.broadcasted_iota(jnp.int32, (columns, columns), 1)

    def band(shift):
        at = target + shift
        inside = (jnp.abs(source - at) <= REACH) & (at >= 0) & (at < columns)
        return jnp.where(inside, 1.0, 0.0).astype(jnp.float32)

    return jnp.concatenate([band(0), band(1) - band(-1)], axis=1).astype(jnp.bfloat16)


def shear_matrices(slopes_ref, slice_depth, columns, total_depth):
    source = lax.broadcasted_iota(jnp.int32, (columns, columns), 0)
    target = lax.broadcasted_iota(jnp.int32, (columns, columns), 1)
    distance = (source - target).astype(jnp.float32)
    parts = []
    for view in range(VIEWS):
        shift = slopes_ref[view] * (slice_depth + 0.5 - 0.5 * total_depth)
        parts.append(jnp.maximum(0.0, 1.0 - jnp.abs(distance + shift)))
    return jnp.concatenate(parts, axis=1).astype(jnp.bfloat16)


def window_sums(layers, taps):
    sums, width = layers, 1
    while 2 * width < taps:
        sums = [sums[i] + sums[i + width] for i in range(len(sums) - width)]
        width *= 2
    return [sums[i] + layers[i + width] for i in range(len(layers) - width)]


def encode(value):
    root = jnp.exp(0.125 * jnp.log(jnp.maximum(value, 1e-30) * (1.0 / TOP)))
    level = jnp.minimum(root * STEPS + 0.5, STEPS)
    return (level.astype(jnp.int32) - MIDDLE).astype(jnp.int16)


def decode(code):
    root = (code.astype(jnp.int32) + MIDDLE).astype(jnp.float32) * (TOP**0.125 / STEPS)
    square = root * root
    fourth = square * square
    return fourth * fourth


def make_render(n_depth, n_rows, depth_cells, row_cells, columns):
    total_depth = depth_cells * n_depth
    extinct = 3.0 / total_depth
    padded_rows = row_cells + 2 * ROW_TILE
    first, last = ROW_TILE, ROW_TILE + row_cells
    tile_rows = row_cells // n_depth
    step_rows = min(tile_rows, PACKED_ROWS)
    cells = TAPS**3
    floor = 0.01 * (2.0 * cells) ** 2

    def kernel(
        live_ref, slopes_ref, palette_ref, owner_ref,
        own_ref, odd_ref, even_ref, corner_odd_ref, corner_even_ref, rlo_ref, rhi_ref,
        out_ref,
        deep, triple, smooth, across, sheared,
    ):
        depth_index = lax.axis_index("gz")
        row_index = lax.axis_index("xy")
        odd_depth = depth_index % 2 == 1

        for chunk in range(padded_rows // ROW_TILE):
            rows = pl.ds(chunk * ROW_TILE, ROW_TILE)
            inner = pl.ds((chunk - 1) * ROW_TILE, ROW_TILE)
            if chunk == 0:
                at, pair, mid_ref = pl.ds(0, ROW_TILE), (corner_even_ref, corner_odd_ref), rlo_ref
            elif chunk == padded_rows // ROW_TILE - 1:
                at = pl.ds(ROW_TILE, ROW_TILE)
                pair, mid_ref = (corner_even_ref, corner_odd_ref), rhi_ref
            else:
                at, pair, mid_ref = inner, (even_ref, odd_ref), own_ref
            mid_at = at if mid_ref is own_ref else pl.ds(0, ROW_TILE)
            even, odd = [[ref[i, at] for i in range(HALO)] for ref in pair]
            mid = [mid_ref[i, mid_at] for i in range(depth_cells)]
            low = [jnp.where(odd_depth, e, o) for e, o in zip(even, odd)]
            high = [jnp.where(odd_depth, o, e) for e, o in zip(even, odd)]
            for z, total in enumerate(window_sums(low + mid + high, TAPS)):
                deep[z, rows] = total

        band = column_matrix(columns)
        weights = jnp.concatenate([band, band, band], axis=0)
        for z in range(depth_cells + 2):
            lead = first - REACH
            span = row_cells + 2 * REACH
            triple[pl.ds(ROW_TILE, span)] = (
                deep[z, pl.ds(lead - 1, span)]
                + deep[z, pl.ds(lead, span)]
                + deep[z, pl.ds(lead + 1, span)]
            )
            base = ROW_TILE - lead
            total = (
                triple[pl.ds(base - 3, padded_rows)]
                + triple[pl.ds(base, padded_rows)]
                + triple[pl.ds(base + 3, padded_rows)]
            )
            hi = total.astype(jnp.bfloat16)
            rest = total - hi.astype(jnp.float32)
            mid = rest.astype(jnp.bfloat16)
            lo = (rest - mid.astype(jnp.float32)).astype(jnp.bfloat16)
            split = jnp.concatenate([hi, mid, lo], axis=1)
            if 1 <= z <= depth_cells:
                both = jnp.dot(split, weights, preferred_element_type=jnp.float32)
                smooth[z] = both[:, :columns]
                across[z - 1] = both[first:last, columns:]
            else:
                smooth[z] = jnp.dot(
                    split, weights[:, :columns], preferred_element_type=jnp.float32
                )

        @pl.when(row_index == 0)
        def _():
            smooth[:, first - 1 : first, :] = jnp.zeros(
                (depth_cells + 2, 1, columns), jnp.float32
            )

        @pl.when(row_index == n_rows - 1)
        def _():
            smooth[:, last : last + 1, :] = jnp.zeros((depth_cells + 2, 1, columns), jnp.float32)

        @pl.when(depth_index == 0)
        def _():
            smooth[0] = jnp.zeros((padded_rows, columns), jnp.float32)

        @pl.when(depth_index == n_depth - 1)
        def _():
            smooth[depth_cells + 1] = jnp.zeros((padded_rows, columns), jnp.float32)

        own_live = live_ref[depth_index, row_index]
        slab_start = (depth_index * depth_cells).astype(jnp.float32)
        for z in range(depth_cells):
            center = smooth[z + 1, pl.ds(first, row_cells)]
            diff_depth = (
                smooth[z + 2, pl.ds(first, row_cells)] - smooth[z, pl.ds(first, row_cells)]
            )
            diff_rows = (
                smooth[z + 1, pl.ds(first + 1, row_cells)]
                - smooth[z + 1, pl.ds(first - 1, row_cells)]
            )
            diff_cols = across[z]
            square = diff_depth * diff_depth + diff_rows * diff_rows + diff_cols * diff_cols
            toward = LIGHT[0] * diff_depth + LIGHT[1] * diff_rows + LIGHT[2] * diff_cols
            facing = jnp.maximum(0.0, toward) * lax.rsqrt(square + floor)
            twice = center * (2.0 / cells)
            small = jnp.exp(-jnp.abs(twice))
            log1p = jnp.where(small < 1e-4, small * (1.0 - 0.5 * small), jnp.log(1.0 + small))
            softplus = jnp.maximum(twice, 0.0) + log1p
            opacity = jnp.where(z < own_live, 1.0 - jnp.exp(-extinct * softplus), 0.0)
            bright = opacity * (0.25 + 0.75 * facing)
            rgba = jnp.concatenate(
                [(bright * palette_ref[c]).astype(jnp.bfloat16) for c in range(3)]
                + [opacity.astype(jnp.bfloat16)],
                axis=0,
            )
            matrix = shear_matrices(slopes_ref, slab_start + float(z), columns, total_depth)
            sheared[z] = jnp.dot(rgba, matrix, preferred_element_type=jnp.float32)

        for tile in range(n_depth):
            place = [owner_ref[view, tile] for view in range(VIEWS)]
            for inside in range(0, tile_rows, step_rows):
                for view in range(VIEWS):
                    lanes = pl.ds(view * columns, columns)
                    colour, transmit = None, None
                    for z in range(depth_cells):
                        part = [
                            sheared[
                                z,
                                pl.ds(c * row_cells + tile * tile_rows + inside, step_rows),
                                lanes,
                            ]
                            for c in range(4)
                        ]
                        clear = 1.0 - part[3]
                        if z == 0:
                            colour, transmit = part[:3], clear
                        elif view == 0:
                            colour = [colour[c] + transmit * part[c] for c in range(3)]
                            transmit = transmit * clear
                        else:
                            colour = [part[c] + clear * colour[c] for c in range(3)]
                            transmit = transmit * clear
                    values = colour + [1.0 - transmit]
                    share = PACKED_ROWS // step_rows
                    for c in range(0, 4, share):
                        value = values[c] if share == 1 else jnp.concatenate(values[c : c + share])
                        rows = pl.ds(c * tile_rows + inside, PACKED_ROWS)
                        out_ref[place[view], view, rows] = encode(value)

    smem = pl.BlockSpec(memory_space=pltpu.SMEM)
    vmem = pl.BlockSpec(memory_space=pltpu.VMEM)
    return pl.pallas_call(
        kernel,
        out_shape=jax.ShapeDtypeStruct((n_depth, VIEWS, 4 * tile_rows, columns), jnp.int16),
        in_specs=[smem] * 4 + [vmem] * 7,
        out_specs=vmem,
        scratch_shapes=[
            pltpu.VMEM((depth_cells + 2, padded_rows, columns), jnp.float32),
            pltpu.VMEM((padded_rows + 2 * ROW_TILE, columns), jnp.float32),
            pltpu.VMEM((depth_cells + 2, padded_rows, columns), jnp.float32),
            pltpu.VMEM((depth_cells, row_cells, columns), jnp.float32),
            pltpu.VMEM((depth_cells, 4 * row_cells, VIEWS * columns), jnp.float32),
        ],
        compiler_params=pltpu.CompilerParams(vmem_limit_bytes=VMEM_BYTES),
        name="render",
    )


def cut_edges(density):
    depth_cells, row_cells, columns = density.shape

    def kernel(density_ref, row_even_ref, row_odd_ref, deep_even_ref, deep_odd_ref, sems):
        row_bit = lax.axis_index("xy") % 2
        depth_bit = lax.axis_index("gz") % 2
        last_rows, last_deep = row_cells - ROW_TILE, depth_cells - HALO

        def rows(bit):
            return density_ref.at[:, pl.ds(pl.multiple_of(bit * last_rows, ROW_TILE), ROW_TILE)]

        def deep(bit):
            return density_ref.at[pl.ds(bit * last_deep, HALO)]

        copies = [
            pltpu.make_async_copy(deep(depth_bit), deep_odd_ref, sems.at[0]),
            pltpu.make_async_copy(deep(1 - depth_bit), deep_even_ref, sems.at[1]),
            pltpu.make_async_copy(rows(1 - row_bit), row_even_ref, sems.at[2]),
            pltpu.make_async_copy(rows(row_bit), row_odd_ref, sems.at[3]),
        ]
        for copy in copies:
            copy.start()
        for copy in copies:
            copy.wait()

    rows = jax.ShapeDtypeStruct((depth_cells, ROW_TILE, columns), jnp.float32)
    deep = jax.ShapeDtypeStruct((HALO, row_cells, columns), jnp.float32)
    return pl.pallas_call(
        kernel,
        out_shape=(rows, rows, deep, deep),
        in_specs=[pl.BlockSpec(memory_space=pltpu.HBM)],
        out_specs=(pl.BlockSpec(memory_space=pltpu.VMEM),) * 4,
        scratch_shapes=[pltpu.SemaphoreType.DMA((4,))],
        compiler_params=pltpu.CompilerParams(vmem_limit_bytes=VMEM_BYTES),
        name="cut_edges",
    )(density)


def composite_kernel(order_ref, in_ref, out_ref):
    count = in_ref.shape[0]
    rows = in_ref.shape[2] // 4
    for view in range(VIEWS):
        colour, transmit = None, None
        for k in range(count):
            source = order_ref[view, k]
            values = decode(in_ref[source, view])
            part = [values[c * rows : (c + 1) * rows] for c in range(4)]
            clear = 1.0 - part[3]
            if k == 0:
                colour, transmit = part[:3], clear
            else:
                colour = [colour[c] + transmit * part[c] for c in range(3)]
                transmit = transmit * clear
        for c, value in enumerate(colour + [1.0 - transmit]):
            out_ref[view, c, 0] = value


def body(density, live_slices, shear_slopes, palette, depth_order, tile_owner):
    depth_cells, row_cells, columns = density.shape
    n_depth = lax.axis_size("gz")
    n_rows = lax.axis_size("xy")

    edge = depth_cells - HALO
    odd_depth = lax.axis_index("gz") % 2 == 1
    odd_row = lax.axis_index("xy") % 2 == 1

    def pairs(axis, first):
        count = lax.axis_size(axis)
        lower = range(first, count - 1, 2)
        return [(i, i + 1) for i in lower] + [(i + 1, i) for i in lower]

    row_even, row_odd, deep_even, deep_odd = cut_edges(density)
    row_even = lax.ppermute(row_even, "xy", pairs("xy", 0))
    row_odd = lax.ppermute(row_odd, "xy", pairs("xy", 1))
    deep_odd = lax.ppermute(deep_odd, "gz", pairs("gz", 1))
    deep_even = lax.ppermute(deep_even, "gz", pairs("gz", 0))
    rlo = jnp.where(odd_row, row_even, row_odd)
    rhi = jnp.where(odd_row, row_odd, row_even)
    low_corner = jnp.concatenate([rlo[:HALO], rhi[:HALO]], axis=1)
    high_corner = jnp.concatenate([rlo[edge:], rhi[edge:]], axis=1)
    corner_odd = lax.ppermute(
        jnp.where(odd_depth, high_corner, low_corner), "gz", pairs("gz", 1)
    )
    corner_even = lax.ppermute(
        jnp.where(odd_depth, low_corner, high_corner), "gz", pairs("gz", 0)
    )
    render = make_render(n_depth, n_rows, depth_cells, row_cells, columns)
    outgoing = render(
        live_slices, shear_slopes, palette, tile_owner,
        density, deep_odd, deep_even, corner_odd, corner_even, rlo, rhi,
    )
    incoming = lax.all_to_all(outgoing, "gz", split_axis=0, concat_axis=0, tiled=True)
    tile_rows = row_cells // n_depth
    return pl.pallas_call(
        composite_kernel,
        out_shape=jax.ShapeDtypeStruct((VIEWS, 4, 1, tile_rows, columns), jnp.float32),
        in_specs=[pl.BlockSpec(memory_space=pltpu.SMEM), pl.BlockSpec(memory_space=pltpu.VMEM)],
        out_specs=pl.BlockSpec(memory_space=pltpu.VMEM),
        compiler_params=pltpu.CompilerParams(vmem_limit_bytes=VMEM_BYTES),
        name="composite",
    )(depth_order, incoming)


def solution(mesh):
    placed = (P("gz", "xy", None), P(), P(), P(), P(), P())
    return jax.shard_map(
        body, mesh=mesh, in_specs=placed, out_specs=P(None, None, "gz", "xy", None), check_vma=False
    )
```

```python
import jax
import jax.numpy as jnp
from jax import lax
from jax.experimental import pallas as pl
from jax.experimental.pallas import tpu as pltpu
from jax.sharding import PartitionSpec as P

LIGHT = (0.48, 0.6, 0.64)
REACH = 4
HALO = REACH + 1
TAPS = 2 * REACH + 1
ROW_TILE = 8
PACKED_ROWS = 16
VIEWS = 2
TOP = 2.2
STEPS = 65535.0
MIDDLE = 32768
VMEM_BYTES = 40 * 1024 * 1024


def column_matrix(columns):
    source = lax.broadcasted_iota(jnp.int32, (columns, columns), 0)
    target = lax.broadcasted_iota(jnp.int32, (columns, columns), 1)

    def band(shift):
        at = target + shift
        inside = (jnp.abs(source - at) <= REACH) & (at >= 0) & (at < columns)
        return jnp.where(inside, 1.0, 0.0).astype(jnp.float32)

    return jnp.concatenate([band(0), band(1) - band(-1)], axis=1).astype(jnp.bfloat16)


def shear_matrices(slopes_ref, slice_depth, columns, total_depth):
    source = lax.broadcasted_iota(jnp.int32, (columns, columns), 0)
    target = lax.broadcasted_iota(jnp.int32, (columns, columns), 1)
    distance = (source - target).astype(jnp.float32)
    parts = []
    for view in range(VIEWS):
        shift = slopes_ref[view] * (slice_depth + 0.5 - 0.5 * total_depth)
        parts.append(jnp.maximum(0.0, 1.0 - jnp.abs(distance + shift)))
    return jnp.concatenate(parts, axis=1).astype(jnp.bfloat16)


def window_sums(layers, taps):
    sums, width = layers, 1
    while 2 * width < taps:
        sums = [sums[i] + sums[i + width] for i in range(len(sums) - width)]
        width *= 2
    return [sums[i] + layers[i + width] for i in range(len(layers) - width)]


def encode(value):
    root = jnp.exp(0.125 * jnp.log(jnp.maximum(value, 1e-30) * (1.0 / TOP)))
    level = jnp.minimum(root * STEPS + 0.5, STEPS)
    return (level.astype(jnp.int32) - MIDDLE).astype(jnp.int16)


def decode(code):
    root = (code.astype(jnp.int32) + MIDDLE).astype(jnp.float32) * (TOP**0.125 / STEPS)
    square = root * root
    fourth = square * square
    return fourth * fourth


def make_render(n_depth, n_rows, depth_cells, row_cells, columns):
    total_depth = depth_cells * n_depth
    extinct = 3.0 / total_depth
    padded_rows = row_cells + 2 * ROW_TILE
    first, last = ROW_TILE, ROW_TILE + row_cells
    tile_rows = row_cells // n_depth
    step_rows = min(tile_rows, PACKED_ROWS)
    cells = TAPS**3
    floor = 0.01 * (2.0 * cells) ** 2

    def kernel(
        live_ref, slopes_ref, palette_ref, owner_ref,
        own_ref, odd_first_ref, odd_second_ref, even_ref, corner_odd_ref, corner_even_ref, rlo_ref, rhi_ref,
        out_ref,
        deep, triple, smooth, across, sheared,
    ):
        depth_index = lax.axis_index("gz")
        row_index = lax.axis_index("xy")
        odd_depth = depth_index % 2 == 1

        for chunk in range(padded_rows // ROW_TILE):
            rows = pl.ds(chunk * ROW_TILE, ROW_TILE)
            inner = pl.ds((chunk - 1) * ROW_TILE, ROW_TILE)
            if chunk == 0:
                at, pair, mid_ref = pl.ds(0, ROW_TILE), (corner_even_ref, corner_odd_ref), rlo_ref
            elif chunk == padded_rows // ROW_TILE - 1:
                at = pl.ds(ROW_TILE, ROW_TILE)
                pair, mid_ref = (corner_even_ref, corner_odd_ref), rhi_ref
            else:
                at, pair, mid_ref = inner, (even_ref, None), own_ref
            mid_at = at if mid_ref is own_ref else pl.ds(0, ROW_TILE)
            even = [pair[0][i, at] for i in range(HALO)]
            if pair[1] is None:
                start = (chunk - 1) * ROW_TILE
                odd_ref = odd_first_ref if start < row_cells // 2 else odd_second_ref
                part = pl.ds(start % (row_cells // 2), ROW_TILE)
                odd = [odd_ref[i, part] for i in range(HALO)]
            else:
                odd = [pair[1][i, at] for i in range(HALO)]
            mid = [mid_ref[i, mid_at] for i in range(depth_cells)]
            low = [jnp.where(odd_depth, e, o) for e, o in zip(even, odd)]
            high = [jnp.where(odd_depth, o, e) for e, o in zip(even, odd)]
            for z, total in enumerate(window_sums(low + mid + high, TAPS)):
                deep[z, rows] = total

        band = column_matrix(columns)
        weights = jnp.concatenate([band, band, band], axis=0)
        for z in range(depth_cells + 2):
            lead = first - REACH
            span = row_cells + 2 * REACH
            triple[pl.ds(ROW_TILE, span)] = (
                deep[z, pl.ds(lead - 1, span)]
                + deep[z, pl.ds(lead, span)]
                + deep[z, pl.ds(lead + 1, span)]
            )
            base = ROW_TILE - lead
            total = (
                triple[pl.ds(base - 3, padded_rows)]
                + triple[pl.ds(base, padded_rows)]
                + triple[pl.ds(base + 3, padded_rows)]
            )
            hi = total.astype(jnp.bfloat16)
            rest = total - hi.astype(jnp.float32)
            mid = rest.astype(jnp.bfloat16)
            lo = (rest - mid.astype(jnp.float32)).astype(jnp.bfloat16)
            split = jnp.concatenate([hi, mid, lo], axis=1)
            if 1 <= z <= depth_cells:
                both = jnp.dot(split, weights, preferred_element_type=jnp.float32)
                smooth[z] = both[:, :columns]
                across[z - 1] = both[first:last, columns:]
            else:
                smooth[z] = jnp.dot(
                    split, weights[:, :columns], preferred_element_type=jnp.float32
                )

        @pl.when(row_index == 0)
        def _():
            smooth[:, first - 1 : first, :] = jnp.zeros(
                (depth_cells + 2, 1, columns), jnp.float32
            )

        @pl.when(row_index == n_rows - 1)
        def _():
            smooth[:, last : last + 1, :] = jnp.zeros((depth_cells + 2, 1, columns), jnp.float32)

        @pl.when(depth_index == 0)
        def _():
            smooth[0] = jnp.zeros((padded_rows, columns), jnp.float32)

        @pl.when(depth_index == n_depth - 1)
        def _():
            smooth[depth_cells + 1] = jnp.zeros((padded_rows, columns), jnp.float32)

        own_live = live_ref[depth_index, row_index]
        slab_start = (depth_index * depth_cells).astype(jnp.float32)
        for z in range(depth_cells):
            center = smooth[z + 1, pl.ds(first, row_cells)]
            diff_depth = (
                smooth[z + 2, pl.ds(first, row_cells)] - smooth[z, pl.ds(first, row_cells)]
            )
            diff_rows = (
                smooth[z + 1, pl.ds(first + 1, row_cells)]
                - smooth[z + 1, pl.ds(first - 1, row_cells)]
            )
            diff_cols = across[z]
            square = diff_depth * diff_depth + diff_rows * diff_rows + diff_cols * diff_cols
            toward = LIGHT[0] * diff_depth + LIGHT[1] * diff_rows + LIGHT[2] * diff_cols
            facing = jnp.maximum(0.0, toward) * lax.rsqrt(square + floor)
            twice = center * (2.0 / cells)
            small = jnp.exp(-jnp.abs(twice))
            log1p = jnp.where(small < 1e-4, small * (1.0 - 0.5 * small), jnp.log(1.0 + small))
            softplus = jnp.maximum(twice, 0.0) + log1p
            opacity = jnp.where(z < own_live, 1.0 - jnp.exp(-extinct * softplus), 0.0)
            bright = opacity * (0.25 + 0.75 * facing)
            rgba = jnp.concatenate(
                [(bright * palette_ref[c]).astype(jnp.bfloat16) for c in range(3)]
                + [opacity.astype(jnp.bfloat16)],
                axis=0,
            )
            matrix = shear_matrices(slopes_ref, slab_start + float(z), columns, total_depth)
            sheared[z] = jnp.dot(rgba, matrix, preferred_element_type=jnp.float32)

        for tile in range(n_depth):
            place = [owner_ref[view, tile] for view in range(VIEWS)]
            for inside in range(0, tile_rows, step_rows):
                for view in range(VIEWS):
                    lanes = pl.ds(view * columns, columns)
                    colour, transmit = None, None
                    for z in range(depth_cells):
                        part = [
                            sheared[
                                z,
                                pl.ds(c * row_cells + tile * tile_rows + inside, step_rows),
                                lanes,
                            ]
                            for c in range(4)
                        ]
                        clear = 1.0 - part[3]
                        if z == 0:
                            colour, transmit = part[:3], clear
                        elif view == 0:
                            colour = [colour[c] + transmit * part[c] for c in range(3)]
                            transmit = transmit * clear
                        else:
                            colour = [part[c] + clear * colour[c] for c in range(3)]
                            transmit = transmit * clear
                    values = colour + [1.0 - transmit]
                    share = PACKED_ROWS // step_rows
                    for c in range(0, 4, share):
                        value = values[c] if share == 1 else jnp.concatenate(values[c : c + share])
                        rows = pl.ds(c * tile_rows + inside, PACKED_ROWS)
                        out_ref[place[view], view, rows] = encode(value)

    smem = pl.BlockSpec(memory_space=pltpu.SMEM)
    vmem = pl.BlockSpec(memory_space=pltpu.VMEM)
    return pl.pallas_call(
        kernel,
        out_shape=jax.ShapeDtypeStruct((n_depth, VIEWS, 4 * tile_rows, columns), jnp.int16),
        in_specs=[smem] * 4 + [vmem] * 8,
        out_specs=vmem,
        scratch_shapes=[
            pltpu.VMEM((depth_cells + 2, padded_rows, columns), jnp.float32),
            pltpu.VMEM((padded_rows + 2 * ROW_TILE, columns), jnp.float32),
            pltpu.VMEM((depth_cells + 2, padded_rows, columns), jnp.float32),
            pltpu.VMEM((depth_cells, row_cells, columns), jnp.float32),
            pltpu.VMEM((depth_cells, 4 * row_cells, VIEWS * columns), jnp.float32),
        ],
        compiler_params=pltpu.CompilerParams(vmem_limit_bytes=VMEM_BYTES),
        name="render",
    )


def cut_edges(density):
    depth_cells, row_cells, columns = density.shape

    half = row_cells // 2

    def kernel(density_ref, row_even_ref, row_odd_ref, deep_even_ref, first_ref, second_ref, sems):
        row_bit = lax.axis_index("xy") % 2
        depth_bit = lax.axis_index("gz") % 2
        last_rows, last_deep = row_cells - ROW_TILE, depth_cells - HALO

        def rows(bit):
            return density_ref.at[:, pl.ds(pl.multiple_of(bit * last_rows, ROW_TILE), ROW_TILE)]

        def deep(bit, start, size):
            return density_ref.at[pl.ds(bit * last_deep, HALO), pl.ds(start, size)]

        copies = [
            pltpu.make_async_copy(deep(depth_bit, 0, half), first_ref, sems.at[0]),
            pltpu.make_async_copy(deep(depth_bit, half, half), second_ref, sems.at[4]),
            pltpu.make_async_copy(deep(1 - depth_bit, 0, row_cells), deep_even_ref, sems.at[1]),
            pltpu.make_async_copy(rows(1 - row_bit), row_even_ref, sems.at[2]),
            pltpu.make_async_copy(rows(row_bit), row_odd_ref, sems.at[3]),
        ]
        for copy in copies:
            copy.start()
        for copy in copies:
            copy.wait()

    rows = jax.ShapeDtypeStruct((depth_cells, ROW_TILE, columns), jnp.float32)
    deep = jax.ShapeDtypeStruct((HALO, row_cells, columns), jnp.float32)
    part = jax.ShapeDtypeStruct((HALO, half, columns), jnp.float32)
    return pl.pallas_call(
        kernel,
        out_shape=(rows, rows, deep, part, part),
        in_specs=[pl.BlockSpec(memory_space=pltpu.HBM)],
        out_specs=(pl.BlockSpec(memory_space=pltpu.VMEM),) * 5,
        scratch_shapes=[pltpu.SemaphoreType.DMA((5,))],
        compiler_params=pltpu.CompilerParams(vmem_limit_bytes=VMEM_BYTES),
        name="cut_edges",
    )(density)


def composite_kernel(order_ref, in_ref, out_ref):
    count = in_ref.shape[0]
    rows = in_ref.shape[2] // 4
    for view in range(VIEWS):
        colour, transmit = None, None
        for k in range(count):
            source = order_ref[view, k]
            values = decode(in_ref[source, view])
            part = [values[c * rows : (c + 1) * rows] for c in range(4)]
            clear = 1.0 - part[3]
            if k == 0:
                colour, transmit = part[:3], clear
            else:
                colour = [colour[c] + transmit * part[c] for c in range(3)]
                transmit = transmit * clear
        for c, value in enumerate(colour + [1.0 - transmit]):
            out_ref[view, c, 0] = value


def body(density, live_slices, shear_slopes, palette, depth_order, tile_owner):
    depth_cells, row_cells, columns = density.shape
    n_depth = lax.axis_size("gz")
    n_rows = lax.axis_size("xy")

    edge = depth_cells - HALO
    odd_depth = lax.axis_index("gz") % 2 == 1
    odd_row = lax.axis_index("xy") % 2 == 1

    def pairs(axis, first):
        count = lax.axis_size(axis)
        lower = range(first, count - 1, 2)
        return [(i, i + 1) for i in lower] + [(i + 1, i) for i in lower]

    row_even, row_odd, deep_even, *deep_odd = cut_edges(density)
    row_even = lax.ppermute(row_even, "xy", pairs("xy", 0))
    row_odd = lax.ppermute(row_odd, "xy", pairs("xy", 1))
    deep_odd = [lax.ppermute(part, "gz", pairs("gz", 1)) for part in deep_odd]
    deep_even = lax.ppermute(deep_even, "gz", pairs("gz", 0))
    rlo = jnp.where(odd_row, row_even, row_odd)
    rhi = jnp.where(odd_row, row_odd, row_even)
    low_corner = jnp.concatenate([rlo[:HALO], rhi[:HALO]], axis=1)
    high_corner = jnp.concatenate([rlo[edge:], rhi[edge:]], axis=1)
    corner_odd = lax.ppermute(
        jnp.where(odd_depth, high_corner, low_corner), "gz", pairs("gz", 1)
    )
    corner_even = lax.ppermute(
        jnp.where(odd_depth, low_corner, high_corner), "gz", pairs("gz", 0)
    )
    render = make_render(n_depth, n_rows, depth_cells, row_cells, columns)
    outgoing = render(
        live_slices, shear_slopes, palette, tile_owner,
        density, *deep_odd, deep_even, corner_odd, corner_even, rlo, rhi,
    )
    incoming = lax.all_to_all(outgoing, "gz", split_axis=0, concat_axis=0, tiled=True)
    tile_rows = row_cells // n_depth
    return pl.pallas_call(
        composite_kernel,
        out_shape=jax.ShapeDtypeStruct((VIEWS, 4, 1, tile_rows, columns), jnp.float32),
        in_specs=[pl.BlockSpec(memory_space=pltpu.SMEM), pl.BlockSpec(memory_space=pltpu.VMEM)],
        out_specs=pl.BlockSpec(memory_space=pltpu.VMEM),
        compiler_params=pltpu.CompilerParams(vmem_limit_bytes=VMEM_BYTES),
        name="composite",
    )(depth_order, incoming)


def solution(mesh):
    placed = (P("gz", "xy", None), P(), P(), P(), P(), P())
    return jax.shard_map(
        body, mesh=mesh, in_specs=placed, out_specs=P(None, None, "gz", "xy", None), check_vma=False
    )
```

```python
import jax
import jax.numpy as jnp
from jax import lax
from jax.experimental import pallas as pl
from jax.experimental.pallas import tpu as pltpu
from jax.sharding import PartitionSpec as P

LIGHT = (0.48, 0.6, 0.64)
REACH = 4
HALO = REACH + 1
TAPS = 2 * REACH + 1
ROW_TILE = 8
PACKED_ROWS = 16
VIEWS = 2
TOP = 2.2
STEPS = 65535.0
MIDDLE = 32768
LEVELS_PER_UNIT = 5461.0
ZERO_LEVEL = 1 << 19
GROUP, WORDS = 8, 5
VMEM_BYTES = 40 * 1024 * 1024


def column_matrix(columns):
    source = lax.broadcasted_iota(jnp.int32, (columns, columns), 0)
    target = lax.broadcasted_iota(jnp.int32, (columns, columns), 1)

    def band(shift):
        at = target + shift
        inside = (jnp.abs(source - at) <= REACH) & (at >= 0) & (at < columns)
        return jnp.where(inside, 1.0, 0.0).astype(jnp.float32)

    return jnp.concatenate([band(0), band(1) - band(-1)], axis=1).astype(jnp.bfloat16)


def shear_matrices(slopes_ref, slice_depth, columns, total_depth):
    source = lax.broadcasted_iota(jnp.int32, (columns, columns), 0)
    target = lax.broadcasted_iota(jnp.int32, (columns, columns), 1)
    distance = (source - target).astype(jnp.float32)
    parts = []
    for view in range(VIEWS):
        shift = slopes_ref[view] * (slice_depth + 0.5 - 0.5 * total_depth)
        parts.append(jnp.maximum(0.0, 1.0 - jnp.abs(distance + shift)))
    return jnp.concatenate(parts, axis=1).astype(jnp.bfloat16)


def window_sums(layers, taps):
    sums, width = layers, 1
    while 2 * width < taps:
        sums = [sums[i] + sums[i + width] for i in range(len(sums) - width)]
        width *= 2
    return [sums[i] + layers[i + width] for i in range(len(layers) - width)]


def pack(values):
    v = [(x * LEVELS_PER_UNIT + (ZERO_LEVEL + 0.5)).astype(jnp.int32) for x in values]
    v = [(x - ZERO_LEVEL) & 0xFFFFF for x in v]
    upper = [
        v[5] & 0xFFF,
        (v[5] >> 12) | ((v[6] & 0xF) << 8),
        (v[6] >> 4) & 0xFFF,
        (v[6] >> 16) | ((v[7] & 0xFF) << 4),
        v[7] >> 8,
    ]
    return [v[i] | (upper[i] << 20) for i in range(WORDS)]


def unpack(words):
    upper = [lax.shift_right_logical(w, jnp.full_like(w, 20)) for w in words]
    levels = words + [
        upper[0] | ((upper[1] & 0xFF) << 12),
        (upper[1] >> 8) | (upper[2] << 4) | ((upper[3] & 0xF) << 16),
        (upper[3] >> 4) | (upper[4] << 8),
    ]
    levels = [(x << 12) >> 12 for x in levels]
    return [x.astype(jnp.float32) * (1.0 / LEVELS_PER_UNIT) for x in levels]


def encode(value):
    root = jnp.exp(0.125 * jnp.log(jnp.maximum(value, 1e-30) * (1.0 / TOP)))
    level = jnp.minimum(root * STEPS + 0.5, STEPS)
    return (level.astype(jnp.int32) - MIDDLE).astype(jnp.int16)


def decode(code):
    root = (code.astype(jnp.int32) + MIDDLE).astype(jnp.float32) * (TOP**0.125 / STEPS)
    square = root * root
    fourth = square * square
    return fourth * fourth


def make_render(n_depth, n_rows, depth_cells, row_cells, columns):
    total_depth = depth_cells * n_depth
    extinct = 3.0 / total_depth
    padded_rows = row_cells + 2 * ROW_TILE
    first, last = ROW_TILE, ROW_TILE + row_cells
    tile_rows = row_cells // n_depth
    step_rows = min(tile_rows, PACKED_ROWS)
    cells = TAPS**3
    floor = 0.01 * (2.0 * cells) ** 2

    def kernel(
        live_ref, slopes_ref, palette_ref, owner_ref,
        own_ref, odd_ref, even_ref, corner_odd_ref, corner_even_ref, rlo_ref, rhi_ref,
        out_ref,
        deep, triple, smooth, across, sheared,
    ):
        depth_index = lax.axis_index("gz")
        row_index = lax.axis_index("xy")
        odd_depth = depth_index % 2 == 1

        for at, mid_ref in ((0, rlo_ref), (ROW_TILE, rhi_ref)):
            even = [corner_even_ref[i, pl.ds(at, ROW_TILE)] for i in range(HALO)]
            odd = [corner_odd_ref[i, pl.ds(at, ROW_TILE)] for i in range(HALO)]
            low = [jnp.where(odd_depth, e, o) for e, o in zip(even, odd)]
            high = [jnp.where(odd_depth, o, e) for e, o in zip(even, odd)]
            layers = low + [mid_ref[i] for i in range(depth_cells)] + high
            for z, total in enumerate(window_sums(layers, TAPS)):
                deep[z, pl.ds(0 if at == 0 else last, ROW_TILE)] = total
        low, high, word = [], [], 0
        for start in range(0, row_cells, ROW_TILE):
            while len(low) < HALO:
                even = [even_ref[word + k] for k in range(WORDS)]
                odd = [odd_ref[word + k] for k in range(WORDS)]
                low += unpack([jnp.where(odd_depth, e, o) for e, o in zip(even, odd)])
                high += unpack([jnp.where(odd_depth, o, e) for e, o in zip(even, odd)])
                word += WORDS
            own = [own_ref[i, pl.ds(start, ROW_TILE)] for i in range(depth_cells)]
            for z, total in enumerate(window_sums(low[:HALO] + own + high[:HALO], TAPS)):
                deep[z, pl.ds(first + start, ROW_TILE)] = total
            low, high = low[HALO:], high[HALO:]

        band = column_matrix(columns)
        weights = jnp.concatenate([band, band, band], axis=0)
        for z in range(depth_cells + 2):
            lead = first - REACH
            span = row_cells + 2 * REACH
            triple[pl.ds(ROW_TILE, span)] = (
                deep[z, pl.ds(lead - 1, span)]
                + deep[z, pl.ds(lead, span)]
                + deep[z, pl.ds(lead + 1, span)]
            )
            base = ROW_TILE - lead
            total = (
                triple[pl.ds(base - 3, padded_rows)]
                + triple[pl.ds(base, padded_rows)]
                + triple[pl.ds(base + 3, padded_rows)]
            )
            hi = total.astype(jnp.bfloat16)
            rest = total - hi.astype(jnp.float32)
            mid = rest.astype(jnp.bfloat16)
            lo = (rest - mid.astype(jnp.float32)).astype(jnp.bfloat16)
            split = jnp.concatenate([hi, mid, lo], axis=1)
            if 1 <= z <= depth_cells:
                both = jnp.dot(split, weights, preferred_element_type=jnp.float32)
                smooth[z] = both[:, :columns]
                across[z - 1] = both[first:last, columns:]
            else:
                smooth[z] = jnp.dot(
                    split, weights[:, :columns], preferred_element_type=jnp.float32
                )

        @pl.when(row_index == 0)
        def _():
            smooth[:, first - 1 : first, :] = jnp.zeros(
                (depth_cells + 2, 1, columns), jnp.float32
            )

        @pl.when(row_index == n_rows - 1)
        def _():
            smooth[:, last : last + 1, :] = jnp.zeros((depth_cells + 2, 1, columns), jnp.float32)

        @pl.when(depth_index == 0)
        def _():
            smooth[0] = jnp.zeros((padded_rows, columns), jnp.float32)

        @pl.when(depth_index == n_depth - 1)
        def _():
            smooth[depth_cells + 1] = jnp.zeros((padded_rows, columns), jnp.float32)

        own_live = live_ref[depth_index, row_index]
        slab_start = (depth_index * depth_cells).astype(jnp.float32)
        for z in range(depth_cells):
            center = smooth[z + 1, pl.ds(first, row_cells)]
            diff_depth = (
                smooth[z + 2, pl.ds(first, row_cells)] - smooth[z, pl.ds(first, row_cells)]
            )
            diff_rows = (
                smooth[z + 1, pl.ds(first + 1, row_cells)]
                - smooth[z + 1, pl.ds(first - 1, row_cells)]
            )
            diff_cols = across[z]
            square = diff_depth * diff_depth + diff_rows * diff_rows + diff_cols * diff_cols
            toward = LIGHT[0] * diff_depth + LIGHT[1] * diff_rows + LIGHT[2] * diff_cols
            facing = jnp.maximum(0.0, toward) * lax.rsqrt(square + floor)
            twice = center * (2.0 / cells)
            small = jnp.exp(-jnp.abs(twice))
            log1p = jnp.where(small < 1e-4, small * (1.0 - 0.5 * small), jnp.log(1.0 + small))
            softplus = jnp.maximum(twice, 0.0) + log1p
            opacity = jnp.where(z < own_live, 1.0 - jnp.exp(-extinct * softplus), 0.0)
            bright = opacity * (0.25 + 0.75 * facing)
            rgba = jnp.concatenate(
                [(bright * palette_ref[c]).astype(jnp.bfloat16) for c in range(3)]
                + [opacity.astype(jnp.bfloat16)],
                axis=0,
            )
            matrix = shear_matrices(slopes_ref, slab_start + float(z), columns, total_depth)
            sheared[z] = jnp.dot(rgba, matrix, preferred_element_type=jnp.float32)

        for tile in range(n_depth):
            place = [owner_ref[view, tile] for view in range(VIEWS)]
            for inside in range(0, tile_rows, step_rows):
                for view in range(VIEWS):
                    lanes = pl.ds(view * columns, columns)
                    colour, transmit = None, None
                    for z in range(depth_cells):
                        part = [
                            sheared[
                                z,
                                pl.ds(c * row_cells + tile * tile_rows + inside, step_rows),
                                lanes,
                            ]
                            for c in range(4)
                        ]
                        clear = 1.0 - part[3]
                        if z == 0:
                            colour, transmit = part[:3], clear
                        elif view == 0:
                            colour = [colour[c] + transmit * part[c] for c in range(3)]
                            transmit = transmit * clear
                        else:
                            colour = [part[c] + clear * colour[c] for c in range(3)]
                            transmit = transmit * clear
                    values = colour + [1.0 - transmit]
                    share = PACKED_ROWS // step_rows
                    for c in range(0, 4, share):
                        value = values[c] if share == 1 else jnp.concatenate(values[c : c + share])
                        rows = pl.ds(c * tile_rows + inside, PACKED_ROWS)
                        out_ref[place[view], view, rows] = encode(value)

    smem = pl.BlockSpec(memory_space=pltpu.SMEM)
    vmem = pl.BlockSpec(memory_space=pltpu.VMEM)
    return pl.pallas_call(
        kernel,
        out_shape=jax.ShapeDtypeStruct((n_depth, VIEWS, 4 * tile_rows, columns), jnp.int16),
        in_specs=[smem] * 4 + [vmem] * 7,
        out_specs=vmem,
        scratch_shapes=[
            pltpu.VMEM((depth_cells + 2, padded_rows, columns), jnp.float32),
            pltpu.VMEM((padded_rows + 2 * ROW_TILE, columns), jnp.float32),
            pltpu.VMEM((depth_cells + 2, padded_rows, columns), jnp.float32),
            pltpu.VMEM((depth_cells, row_cells, columns), jnp.float32),
            pltpu.VMEM((depth_cells, 4 * row_cells, VIEWS * columns), jnp.float32),
        ],
        compiler_params=pltpu.CompilerParams(vmem_limit_bytes=VMEM_BYTES),
        name="render",
    )


def cut_edges(density):
    depth_cells, row_cells, columns = density.shape

    places = [(i, start) for start in range(0, row_cells, ROW_TILE) for i in range(HALO)]
    words = len(places) // GROUP * WORDS

    def kernel(density_ref, row_even_ref, row_odd_ref, deep_even_ref, deep_odd_ref):
        row_bit = lax.axis_index("xy") % 2
        depth_bit = lax.axis_index("gz") % 2
        last_rows, last_deep = row_cells - ROW_TILE, depth_cells - HALO
        for ref, bit in ((deep_odd_ref, depth_bit), (deep_even_ref, 1 - depth_bit)):
            for group in range(len(places) // GROUP):
                values = [
                    density_ref[bit * last_deep + i, pl.ds(start, ROW_TILE)]
                    for i, start in places[group * GROUP : (group + 1) * GROUP]
                ]
                for k, word in enumerate(pack(values)):
                    ref[group * WORDS + k] = word
        for ref, bit in ((row_even_ref, 1 - row_bit), (row_odd_ref, row_bit)):
            start = pl.multiple_of(bit * last_rows, ROW_TILE)
            ref[...] = density_ref[:, pl.ds(start, ROW_TILE)]

    rows = jax.ShapeDtypeStruct((depth_cells, ROW_TILE, columns), jnp.float32)
    deep = jax.ShapeDtypeStruct((words, ROW_TILE, columns), jnp.int32)
    vmem = pl.BlockSpec(memory_space=pltpu.VMEM)
    return pl.pallas_call(
        kernel,
        out_shape=(rows, rows, deep, deep),
        in_specs=[vmem],
        out_specs=(vmem,) * 4,
        compiler_params=pltpu.CompilerParams(vmem_limit_bytes=VMEM_BYTES),
        name="cut_edges",
    )(density)


def composite_kernel(order_ref, in_ref, out_ref):
    count = in_ref.shape[0]
    rows = in_ref.shape[2] // 4
    for view in range(VIEWS):
        colour, transmit = None, None
        for k in range(count):
            source = order_ref[view, k]
            values = decode(in_ref[source, view])
            part = [values[c * rows : (c + 1) * rows] for c in range(4)]
            clear = 1.0 - part[3]
            if k == 0:
                colour, transmit = part[:3], clear
            else:
                colour = [colour[c] + transmit * part[c] for c in range(3)]
                transmit = transmit * clear
        for c, value in enumerate(colour + [1.0 - transmit]):
            out_ref[view, c, 0] = value


def body(density, live_slices, shear_slopes, palette, depth_order, tile_owner):
    depth_cells, row_cells, columns = density.shape
    n_depth = lax.axis_size("gz")
    n_rows = lax.axis_size("xy")

    edge = depth_cells - HALO
    odd_depth = lax.axis_index("gz") % 2 == 1
    odd_row = lax.axis_index("xy") % 2 == 1

    def pairs(axis, first):
        count = lax.axis_size(axis)
        lower = range(first, count - 1, 2)
        return [(i, i + 1) for i in lower] + [(i + 1, i) for i in lower]

    row_even, row_odd, deep_even, deep_odd = cut_edges(density)
    row_even = lax.ppermute(row_even, "xy", pairs("xy", 0))
    row_odd = lax.ppermute(row_odd, "xy", pairs("xy", 1))
    deep_odd = lax.ppermute(deep_odd, "gz", pairs("gz", 1))
    deep_even = lax.ppermute(deep_even, "gz", pairs("gz", 0))
    rlo = jnp.where(odd_row, row_even, row_odd)
    rhi = jnp.where(odd_row, row_odd, row_even)
    low_corner = jnp.concatenate([rlo[:HALO], rhi[:HALO]], axis=1)
    high_corner = jnp.concatenate([rlo[edge:], rhi[edge:]], axis=1)
    corner_odd = lax.ppermute(
        jnp.where(odd_depth, high_corner, low_corner), "gz", pairs("gz", 1)
    )
    corner_even = lax.ppermute(
        jnp.where(odd_depth, low_corner, high_corner), "gz", pairs("gz", 0)
    )
    render = make_render(n_depth, n_rows, depth_cells, row_cells, columns)
    outgoing = render(
        live_slices, shear_slopes, palette, tile_owner,
        density, deep_odd, deep_even, corner_odd, corner_even, rlo, rhi,
    )
    incoming = lax.all_to_all(outgoing, "gz", split_axis=0, concat_axis=0, tiled=True)
    tile_rows = row_cells // n_depth
    return pl.pallas_call(
        composite_kernel,
        out_shape=jax.ShapeDtypeStruct((VIEWS, 4, 1, tile_rows, columns), jnp.float32),
        in_specs=[pl.BlockSpec(memory_space=pltpu.SMEM), pl.BlockSpec(memory_space=pltpu.VMEM)],
        out_specs=pl.BlockSpec(memory_space=pltpu.VMEM),
        compiler_params=pltpu.CompilerParams(vmem_limit_bytes=VMEM_BYTES),
        name="composite",
    )(depth_order, incoming)


def solution(mesh):
    placed = (P("gz", "xy", None), P(), P(), P(), P(), P())
    return jax.shard_map(
        body, mesh=mesh, in_specs=placed, out_specs=P(None, None, "gz", "xy", None), check_vma=False
    )
```

```python
import jax
import jax.numpy as jnp
from jax import lax
from jax.experimental import pallas as pl
from jax.experimental.pallas import tpu as pltpu
from jax.sharding import PartitionSpec as P

LIGHT = (0.48, 0.6, 0.64)
REACH = 4
HALO = REACH + 1
TAPS = 2 * REACH + 1
ROW_TILE = 8
PACKED_ROWS = 16
VIEWS = 2
TOP = 2.2
STEPS = 65535.0
MIDDLE = 32768
LEVELS_PER_UNIT = 5461.0
ZERO_LEVEL = 1 << 19
GROUP, WORDS = 8, 5
VMEM_BYTES = 40 * 1024 * 1024


def column_matrix(columns):
    source = lax.broadcasted_iota(jnp.int32, (columns, columns), 0)
    target = lax.broadcasted_iota(jnp.int32, (columns, columns), 1)

    def band(shift):
        at = target + shift
        inside = (jnp.abs(source - at) <= REACH) & (at >= 0) & (at < columns)
        return jnp.where(inside, 1.0, 0.0).astype(jnp.float32)

    return jnp.concatenate([band(0), band(1) - band(-1)], axis=1).astype(jnp.bfloat16)


def shear_matrices(slopes_ref, slice_depth, columns, total_depth):
    source = lax.broadcasted_iota(jnp.int32, (columns, columns), 0)
    target = lax.broadcasted_iota(jnp.int32, (columns, columns), 1)
    distance = (source - target).astype(jnp.float32)
    parts = []
    for view in range(VIEWS):
        shift = slopes_ref[view] * (slice_depth + 0.5 - 0.5 * total_depth)
        parts.append(jnp.maximum(0.0, 1.0 - jnp.abs(distance + shift)))
    return jnp.concatenate(parts, axis=1).astype(jnp.bfloat16)


def window_sums(layers, taps):
    sums, width = layers, 1
    while 2 * width < taps:
        sums = [sums[i] + sums[i + width] for i in range(len(sums) - width)]
        width *= 2
    return [sums[i] + layers[i + width] for i in range(len(layers) - width)]


def pack(values):
    v = [(x * LEVELS_PER_UNIT + (ZERO_LEVEL + 0.5)).astype(jnp.int32) for x in values]
    v = [(x - ZERO_LEVEL) & 0xFFFFF for x in v]
    upper = [
        v[5] & 0xFFF,
        (v[5] >> 12) | ((v[6] & 0xF) << 8),
        (v[6] >> 4) & 0xFFF,
        (v[6] >> 16) | ((v[7] & 0xFF) << 4),
        v[7] >> 8,
    ]
    return [v[i] | (upper[i] << 20) for i in range(WORDS)]


def unpack(words):
    upper = [lax.shift_right_logical(w, jnp.full_like(w, 20)) for w in words]
    levels = words + [
        upper[0] | ((upper[1] & 0xFF) << 12),
        (upper[1] >> 8) | (upper[2] << 4) | ((upper[3] & 0xF) << 16),
        (upper[3] >> 4) | (upper[4] << 8),
    ]
    levels = [(x << 12) >> 12 for x in levels]
    return [x.astype(jnp.float32) * (1.0 / LEVELS_PER_UNIT) for x in levels]


def encode(value):
    root = jnp.exp(0.125 * jnp.log(jnp.maximum(value, 1e-30) * (1.0 / TOP)))
    level = jnp.minimum(root * STEPS + 0.5, STEPS)
    return (level.astype(jnp.int32) - MIDDLE).astype(jnp.int16)


def decode(code):
    root = (code.astype(jnp.int32) + MIDDLE).astype(jnp.float32) * (TOP**0.125 / STEPS)
    square = root * root
    fourth = square * square
    return fourth * fourth


def make_render(n_depth, n_rows, depth_cells, row_cells, columns):
    total_depth = depth_cells * n_depth
    extinct = 3.0 / total_depth
    padded_rows = row_cells + 2 * ROW_TILE
    first, last = ROW_TILE, ROW_TILE + row_cells
    tile_rows = row_cells // n_depth
    step_rows = min(tile_rows, PACKED_ROWS)
    cells = TAPS**3
    floor = 0.01 * (2.0 * cells) ** 2

    def kernel(
        live_ref, slopes_ref, palette_ref, owner_ref,
        own_ref, odd_ref, even_ref, row_even_ref, row_odd_ref,
        out_ref,
        deep, triple, smooth, across, sheared,
    ):
        depth_index = lax.axis_index("gz")
        row_index = lax.axis_index("xy")
        odd_depth = depth_index % 2 == 1
        odd_row = row_index % 2 == 1

        chunks = padded_rows // ROW_TILE
        low, high, word = [], [], 0
        for chunk in range(chunks):
            while len(low) < HALO:
                even = [even_ref[word + k] for k in range(WORDS)]
                odd = [odd_ref[word + k] for k in range(WORDS)]
                low += unpack([jnp.where(odd_depth, e, o) for e, o in zip(even, odd)])
                high += unpack([jnp.where(odd_depth, o, e) for e, o in zip(even, odd)])
                word += WORDS
            own = [
                layer_rows(own_ref, row_even_ref, row_odd_ref, odd_row, i, chunk, chunks)
                for i in range(depth_cells)
            ]
            for z, total in enumerate(window_sums(low[:HALO] + own + high[:HALO], TAPS)):
                deep[z, pl.ds(chunk * ROW_TILE, ROW_TILE)] = total
            low, high = low[HALO:], high[HALO:]

        band = column_matrix(columns)
        weights = jnp.concatenate([band, band, band], axis=0)
        for z in range(depth_cells + 2):
            lead = first - REACH
            span = row_cells + 2 * REACH
            triple[pl.ds(ROW_TILE, span)] = (
                deep[z, pl.ds(lead - 1, span)]
                + deep[z, pl.ds(lead, span)]
                + deep[z, pl.ds(lead + 1, span)]
            )
            base = ROW_TILE - lead
            total = (
                triple[pl.ds(base - 3, padded_rows)]
                + triple[pl.ds(base, padded_rows)]
                + triple[pl.ds(base + 3, padded_rows)]
            )
            hi = total.astype(jnp.bfloat16)
            rest = total - hi.astype(jnp.float32)
            mid = rest.astype(jnp.bfloat16)
            lo = (rest - mid.astype(jnp.float32)).astype(jnp.bfloat16)
            split = jnp.concatenate([hi, mid, lo], axis=1)
            if 1 <= z <= depth_cells:
                both = jnp.dot(split, weights, preferred_element_type=jnp.float32)
                smooth[z] = both[:, :columns]
                across[z - 1] = both[first:last, columns:]
            else:
                smooth[z] = jnp.dot(
                    split, weights[:, :columns], preferred_element_type=jnp.float32
                )

        @pl.when(row_index == 0)
        def _():
            smooth[:, first - 1 : first, :] = jnp.zeros(
                (depth_cells + 2, 1, columns), jnp.float32
            )

        @pl.when(row_index == n_rows - 1)
        def _():
            smooth[:, last : last + 1, :] = jnp.zeros((depth_cells + 2, 1, columns), jnp.float32)

        @pl.when(depth_index == 0)
        def _():
            smooth[0] = jnp.zeros((padded_rows, columns), jnp.float32)

        @pl.when(depth_index == n_depth - 1)
        def _():
            smooth[depth_cells + 1] = jnp.zeros((padded_rows, columns), jnp.float32)

        own_live = live_ref[depth_index, row_index]
        slab_start = (depth_index * depth_cells).astype(jnp.float32)
        for z in range(depth_cells):
            center = smooth[z + 1, pl.ds(first, row_cells)]
            diff_depth = (
                smooth[z + 2, pl.ds(first, row_cells)] - smooth[z, pl.ds(first, row_cells)]
            )
            diff_rows = (
                smooth[z + 1, pl.ds(first + 1, row_cells)]
                - smooth[z + 1, pl.ds(first - 1, row_cells)]
            )
            diff_cols = across[z]
            square = diff_depth * diff_depth + diff_rows * diff_rows + diff_cols * diff_cols
            toward = LIGHT[0] * diff_depth + LIGHT[1] * diff_rows + LIGHT[2] * diff_cols
            facing = jnp.maximum(0.0, toward) * lax.rsqrt(square + floor)
            twice = center * (2.0 / cells)
            small = jnp.exp(-jnp.abs(twice))
            log1p = jnp.where(small < 1e-4, small * (1.0 - 0.5 * small), jnp.log(1.0 + small))
            softplus = jnp.maximum(twice, 0.0) + log1p
            opacity = jnp.where(z < own_live, 1.0 - jnp.exp(-extinct * softplus), 0.0)
            bright = opacity * (0.25 + 0.75 * facing)
            rgba = jnp.concatenate(
                [(bright * palette_ref[c]).astype(jnp.bfloat16) for c in range(3)]
                + [opacity.astype(jnp.bfloat16)],
                axis=0,
            )
            matrix = shear_matrices(slopes_ref, slab_start + float(z), columns, total_depth)
            sheared[z] = jnp.dot(rgba, matrix, preferred_element_type=jnp.float32)

        for tile in range(n_depth):
            place = [owner_ref[view, tile] for view in range(VIEWS)]
            for inside in range(0, tile_rows, step_rows):
                for view in range(VIEWS):
                    lanes = pl.ds(view * columns, columns)
                    colour, transmit = None, None
                    for z in range(depth_cells):
                        part = [
                            sheared[
                                z,
                                pl.ds(c * row_cells + tile * tile_rows + inside, step_rows),
                                lanes,
                            ]
                            for c in range(4)
                        ]
                        clear = 1.0 - part[3]
                        if z == 0:
                            colour, transmit = part[:3], clear
                        elif view == 0:
                            colour = [colour[c] + transmit * part[c] for c in range(3)]
                            transmit = transmit * clear
                        else:
                            colour = [part[c] + clear * colour[c] for c in range(3)]
                            transmit = transmit * clear
                    values = colour + [1.0 - transmit]
                    share = PACKED_ROWS // step_rows
                    for c in range(0, 4, share):
                        value = values[c] if share == 1 else jnp.concatenate(values[c : c + share])
                        rows = pl.ds(c * tile_rows + inside, PACKED_ROWS)
                        out_ref[place[view], view, rows] = encode(value)

    smem = pl.BlockSpec(memory_space=pltpu.SMEM)
    vmem = pl.BlockSpec(memory_space=pltpu.VMEM)
    return pl.pallas_call(
        kernel,
        out_shape=jax.ShapeDtypeStruct((n_depth, VIEWS, 4 * tile_rows, columns), jnp.int16),
        in_specs=[smem] * 4 + [vmem] * 5,
        out_specs=vmem,
        scratch_shapes=[
            pltpu.VMEM((depth_cells + 2, padded_rows, columns), jnp.float32),
            pltpu.VMEM((padded_rows + 2 * ROW_TILE, columns), jnp.float32),
            pltpu.VMEM((depth_cells + 2, padded_rows, columns), jnp.float32),
            pltpu.VMEM((depth_cells, row_cells, columns), jnp.float32),
            pltpu.VMEM((depth_cells, 4 * row_cells, VIEWS * columns), jnp.float32),
        ],
        compiler_params=pltpu.CompilerParams(vmem_limit_bytes=VMEM_BYTES),
        name="render",
    )


def layer_rows(own_ref, row_even_ref, row_odd_ref, odd_row, layer, chunk, chunks):
    if 0 < chunk < chunks - 1:
        return own_ref[layer, pl.ds((chunk - 1) * ROW_TILE, ROW_TILE)]
    take_even = odd_row if chunk == 0 else jnp.logical_not(odd_row)
    return jnp.where(take_even, row_even_ref[layer], row_odd_ref[layer])


def cut_layers(density, row_even, row_odd):
    depth_cells, row_cells, columns = density.shape
    chunks = row_cells // ROW_TILE + 2
    places = [(i, chunk) for chunk in range(chunks) for i in range(HALO)]
    groups = pl.cdiv(len(places), GROUP)

    def kernel(own_ref, row_even_ref, row_odd_ref, deep_even_ref, deep_odd_ref):
        odd_row = lax.axis_index("xy") % 2 == 1
        depth_bit = lax.axis_index("gz") % 2
        last_deep = depth_cells - HALO
        for ref, bit in ((deep_odd_ref, depth_bit), (deep_even_ref, 1 - depth_bit)):
            for group in range(groups):
                values = [
                    layer_rows(
                        own_ref, row_even_ref, row_odd_ref, odd_row,
                        bit * last_deep + i, chunk, chunks,
                    )
                    for i, chunk in places[group * GROUP : (group + 1) * GROUP]
                ]
                values += [jnp.zeros_like(values[0])] * (GROUP - len(values))
                for k, word in enumerate(pack(values)):
                    ref[group * WORDS + k] = word

    deep = jax.ShapeDtypeStruct((groups * WORDS, ROW_TILE, columns), jnp.int32)
    vmem = pl.BlockSpec(memory_space=pltpu.VMEM)
    return pl.pallas_call(
        kernel,
        out_shape=(deep, deep),
        in_specs=[vmem] * 3,
        out_specs=(vmem,) * 2,
        compiler_params=pltpu.CompilerParams(vmem_limit_bytes=VMEM_BYTES),
        name="cut_layers",
    )(density, row_even, row_odd)


def composite_kernel(order_ref, in_ref, out_ref):
    count = in_ref.shape[0]
    rows = in_ref.shape[2] // 4
    for view in range(VIEWS):
        colour, transmit = None, None
        for k in range(count):
            source = order_ref[view, k]
            values = decode(in_ref[source, view])
            part = [values[c * rows : (c + 1) * rows] for c in range(4)]
            clear = 1.0 - part[3]
            if k == 0:
                colour, transmit = part[:3], clear
            else:
                colour = [colour[c] + transmit * part[c] for c in range(3)]
                transmit = transmit * clear
        for c, value in enumerate(colour + [1.0 - transmit]):
            out_ref[view, c, 0] = value


def body(density, live_slices, shear_slopes, palette, depth_order, tile_owner):
    depth_cells, row_cells, columns = density.shape
    n_depth = lax.axis_size("gz")
    n_rows = lax.axis_size("xy")

    odd_row = lax.axis_index("xy") % 2 == 1

    def pairs(axis, first):
        count = lax.axis_size(axis)
        lower = range(first, count - 1, 2)
        return [(i, i + 1) for i in lower] + [(i + 1, i) for i in lower]

    low_rows, high_rows = density[:, :ROW_TILE], density[:, row_cells - ROW_TILE :]
    row_even = lax.ppermute(jnp.where(odd_row, low_rows, high_rows), "xy", pairs("xy", 0))
    row_odd = lax.ppermute(jnp.where(odd_row, high_rows, low_rows), "xy", pairs("xy", 1))
    deep_even, deep_odd = cut_layers(density, row_even, row_odd)
    deep_odd = lax.ppermute(deep_odd, "gz", pairs("gz", 1))
    deep_even = lax.ppermute(deep_even, "gz", pairs("gz", 0))
    render = make_render(n_depth, n_rows, depth_cells, row_cells, columns)
    outgoing = render(
        live_slices, shear_slopes, palette, tile_owner,
        density, deep_odd, deep_even, row_even, row_odd,
    )
    incoming = lax.all_to_all(outgoing, "gz", split_axis=0, concat_axis=0, tiled=True)
    tile_rows = row_cells // n_depth
    return pl.pallas_call(
        composite_kernel,
        out_shape=jax.ShapeDtypeStruct((VIEWS, 4, 1, tile_rows, columns), jnp.float32),
        in_specs=[pl.BlockSpec(memory_space=pltpu.SMEM), pl.BlockSpec(memory_space=pltpu.VMEM)],
        out_specs=pl.BlockSpec(memory_space=pltpu.VMEM),
        compiler_params=pltpu.CompilerParams(vmem_limit_bytes=VMEM_BYTES),
        name="composite",
    )(depth_order, incoming)


def solution(mesh):
    placed = (P("gz", "xy", None), P(), P(), P(), P(), P())
    return jax.shard_map(
        body, mesh=mesh, in_specs=placed, out_specs=P(None, None, "gz", "xy", None), check_vma=False
    )
```

```python
import jax
import jax.numpy as jnp
from jax import lax
from jax.experimental import pallas as pl
from jax.experimental.pallas import tpu as pltpu
from jax.sharding import PartitionSpec as P

LIGHT = (0.48, 0.6, 0.64)
REACH = 4
HALO = REACH + 1
TAPS = 2 * REACH + 1
ROW_TILE = 8
PACKED_ROWS = 16
EDGE = 16
VIEWS = 2
TOP = 2.2
STEPS = 65535.0
MIDDLE = 32768
LEVELS_PER_UNIT = 5461.0
ZERO_LEVEL = 1 << 19
GROUP, WORDS = 8, 5
VMEM_BYTES = 40 * 1024 * 1024


def column_matrix(columns):
    source = lax.broadcasted_iota(jnp.int32, (columns, columns), 0)
    target = lax.broadcasted_iota(jnp.int32, (columns, columns), 1)

    def band(shift):
        at = target + shift
        inside = (jnp.abs(source - at) <= REACH) & (at >= 0) & (at < columns)
        return jnp.where(inside, 1.0, 0.0).astype(jnp.float32)

    return jnp.concatenate([band(0), band(1) - band(-1)], axis=1).astype(jnp.bfloat16)


def shear_matrices(slopes_ref, slice_depth, columns, total_depth):
    source = lax.broadcasted_iota(jnp.int32, (columns, columns), 0)
    target = lax.broadcasted_iota(jnp.int32, (columns, columns), 1)
    distance = (source - target).astype(jnp.float32)
    parts = []
    for view in range(VIEWS):
        shift = slopes_ref[view] * (slice_depth + 0.5 - 0.5 * total_depth)
        parts.append(jnp.maximum(0.0, 1.0 - jnp.abs(distance + shift)))
    return jnp.concatenate(parts, axis=1).astype(jnp.bfloat16)


def window_sums(layers, taps):
    sums, width = layers, 1
    while 2 * width < taps:
        sums = [sums[i] + sums[i + width] for i in range(len(sums) - width)]
        width *= 2
    return [sums[i] + layers[i + width] for i in range(len(layers) - width)]


def pack(values):
    v = [(x * LEVELS_PER_UNIT + (ZERO_LEVEL + 0.5)).astype(jnp.int32) for x in values]
    v = [(x - ZERO_LEVEL) & 0xFFFFF for x in v]
    upper = [
        v[5] & 0xFFF,
        (v[5] >> 12) | ((v[6] & 0xF) << 8),
        (v[6] >> 4) & 0xFFF,
        (v[6] >> 16) | ((v[7] & 0xFF) << 4),
        v[7] >> 8,
    ]
    return [v[i] | (upper[i] << 20) for i in range(WORDS)]


def unpack(words):
    upper = [lax.shift_right_logical(w, jnp.full_like(w, 20)) for w in words]
    levels = words + [
        upper[0] | ((upper[1] & 0xFF) << 12),
        (upper[1] >> 8) | (upper[2] << 4) | ((upper[3] & 0xF) << 16),
        (upper[3] >> 4) | (upper[4] << 8),
    ]
    levels = [(x << 12) >> 12 for x in levels]
    return [x.astype(jnp.float32) * (1.0 / LEVELS_PER_UNIT) for x in levels]


def encode(value):
    root = jnp.exp(0.125 * jnp.log(jnp.maximum(value, 1e-30) * (1.0 / TOP)))
    level = jnp.minimum(root * STEPS + 0.5, STEPS)
    return (level.astype(jnp.int32) - MIDDLE).astype(jnp.int16)


def decode(code):
    root = (code.astype(jnp.int32) + MIDDLE).astype(jnp.float32) * (TOP**0.125 / STEPS)
    square = root * root
    fourth = square * square
    return fourth * fourth


def column_sums(total, weights):
    hi = total.astype(jnp.bfloat16)
    rest = total - hi.astype(jnp.float32)
    mid = rest.astype(jnp.bfloat16)
    lo = (rest - mid.astype(jnp.float32)).astype(jnp.bfloat16)
    split = jnp.concatenate([hi, mid, lo], axis=1)
    return jnp.dot(split, weights, preferred_element_type=jnp.float32)


def column_weights(columns):
    band = column_matrix(columns)
    return jnp.concatenate([band, band, band], axis=0)


def shade(center, diff_depth, diff_rows, diff_cols, live, palette_ref, extinct):
    cells = TAPS**3
    floor = 0.01 * (2.0 * cells) ** 2
    square = diff_depth * diff_depth + diff_rows * diff_rows + diff_cols * diff_cols
    toward = LIGHT[0] * diff_depth + LIGHT[1] * diff_rows + LIGHT[2] * diff_cols
    facing = jnp.maximum(0.0, toward) * lax.rsqrt(square + floor)
    twice = center * (2.0 / cells)
    small = jnp.exp(-jnp.abs(twice))
    log1p = jnp.where(small < 1e-4, small * (1.0 - 0.5 * small), jnp.log(1.0 + small))
    softplus = jnp.maximum(twice, 0.0) + log1p
    opacity = jnp.where(live, 1.0 - jnp.exp(-extinct * softplus), 0.0)
    bright = opacity * (0.25 + 0.75 * facing)
    channels = [bright * palette_ref[c] for c in range(3)] + [opacity]
    return [channel.astype(jnp.bfloat16) for channel in channels]


def march(layer, depth_cells, view):
    colour, transmit = None, None
    for z in range(depth_cells):
        part = [layer(z, c) for c in range(4)]
        clear = 1.0 - part[3]
        if z == 0:
            colour, transmit = part[:3], clear
        elif view == 0:
            colour = [colour[c] + transmit * part[c] for c in range(3)]
            transmit = transmit * clear
        else:
            colour = [part[c] + clear * colour[c] for c in range(3)]
            transmit = transmit * clear
    return colour + [1.0 - transmit]


def march_rows(sheared, out_ref, owner_ref, rows, base, height, depth_cells, tile_rows, columns):
    step = min(tile_rows, PACKED_ROWS)
    share = PACKED_ROWS // step
    for row in range(rows.start, rows.stop, step):
        tile, inside = row // tile_rows, row % tile_rows
        at = row - rows.start + base
        for view in range(VIEWS):
            place = owner_ref[view, tile]
            lanes = pl.ds(view * columns, columns)
            values = march(
                lambda z, c: sheared[z, pl.ds(c * height + at, step), lanes], depth_cells, view
            )
            for c in range(0, 4, share):
                value = values[c] if share == 1 else jnp.concatenate(values[c : c + share])
                at_rows = pl.ds(c * tile_rows + inside, PACKED_ROWS)
                out_ref[place, view, at_rows] = encode(value)


def zero_outside(smooth, depth_index, n_depth, layers):
    @pl.when(depth_index == 0)
    def _():
        smooth[0] = jnp.zeros_like(smooth[0])

    @pl.when(depth_index == n_depth - 1)
    def _():
        smooth[layers - 1] = jnp.zeros_like(smooth[layers - 1])


def render_inner(live_slices, slopes, palette, owner, density, deep_odd, deep_even, n_depth):
    depth_cells, row_cells, columns = density.shape
    total_depth = depth_cells * n_depth
    extinct = 3.0 / total_depth
    tile_rows = row_cells // n_depth
    layers = depth_cells + 2
    rows = range(EDGE, row_cells - EDGE)
    height = len(rows)
    lead, span = EDGE - ROW_TILE, height + 2 * ROW_TILE

    def kernel(
        live_ref, slopes_ref, palette_ref, owner_ref, own_ref, odd_ref, even_ref,
        out_ref, deep, shear_ref, triple, smooth, across, sheared,
    ):
        depth_index = lax.axis_index("gz")
        row_index = lax.axis_index("xy")
        odd_depth = depth_index % 2 == 1

        low, high, word = [], [], 0
        for start in range(0, row_cells, ROW_TILE):
            while len(low) < HALO:
                even = [even_ref[word + k] for k in range(WORDS)]
                odd = [odd_ref[word + k] for k in range(WORDS)]
                low += unpack([jnp.where(odd_depth, e, o) for e, o in zip(even, odd)])
                high += unpack([jnp.where(odd_depth, o, e) for e, o in zip(even, odd)])
                word += WORDS
            own = [own_ref[i, pl.ds(start, ROW_TILE)] for i in range(depth_cells)]
            for z, total in enumerate(window_sums(low[:HALO] + own + high[:HALO], TAPS)):
                deep[z, pl.ds(start, ROW_TILE)] = total
            low, high = low[HALO:], high[HALO:]

        slab_start = (depth_index * depth_cells).astype(jnp.float32)
        for z in range(depth_cells):
            shear_ref[z] = shear_matrices(slopes_ref, slab_start + float(z), columns, total_depth)

        weights = column_weights(columns)
        for z in range(layers):
            triple[...] = (
                deep[z, pl.ds(lead - 4, span + ROW_TILE)]
                + deep[z, pl.ds(lead - 3, span + ROW_TILE)]
                + deep[z, pl.ds(lead - 2, span + ROW_TILE)]
            )
            total = triple[pl.ds(0, span)] + triple[pl.ds(3, span)] + triple[pl.ds(6, span)]
            if 1 <= z <= depth_cells:
                both = column_sums(total, weights)
                smooth[z] = both[:, :columns]
                across[z - 1] = both[ROW_TILE : ROW_TILE + height, columns:]
            else:
                smooth[z] = column_sums(total, weights[:, :columns])
        zero_outside(smooth, depth_index, n_depth, layers)

        own_live = live_ref[depth_index, row_index]
        middle = pl.ds(ROW_TILE, height)
        for z in range(depth_cells):
            channels = shade(
                smooth[z + 1, middle],
                smooth[z + 2, middle] - smooth[z, middle],
                smooth[z + 1, pl.ds(ROW_TILE + 1, height)]
                - smooth[z + 1, pl.ds(ROW_TILE - 1, height)],
                across[z],
                z < own_live,
                palette_ref,
                extinct,
            )
            sheared[z] = jnp.dot(
                jnp.concatenate(channels), shear_ref[z], preferred_element_type=jnp.float32
            )
        march_rows(sheared, out_ref, owner_ref, rows, 0, height, depth_cells, tile_rows, columns)

    smem = pl.BlockSpec(memory_space=pltpu.SMEM)
    vmem = pl.BlockSpec(memory_space=pltpu.VMEM)
    return pl.pallas_call(
        kernel,
        out_shape=(
            jax.ShapeDtypeStruct((n_depth, VIEWS, 4 * tile_rows, columns), jnp.int16),
            jax.ShapeDtypeStruct((layers, row_cells, columns), jnp.float32),
            jax.ShapeDtypeStruct((depth_cells, columns, VIEWS * columns), jnp.bfloat16),
        ),
        in_specs=[smem] * 4 + [vmem] * 3,
        out_specs=(vmem,) * 3,
        scratch_shapes=[
            pltpu.VMEM((span + ROW_TILE, columns), jnp.float32),
            pltpu.VMEM((layers, span, columns), jnp.float32),
            pltpu.VMEM((depth_cells, height, columns), jnp.float32),
            pltpu.VMEM((depth_cells, 4 * height, VIEWS * columns), jnp.float32),
        ],
        compiler_params=pltpu.CompilerParams(vmem_limit_bytes=VMEM_BYTES),
        cost_estimate=pl.CostEstimate(
            flops=100 * depth_cells * row_cells * columns,
            bytes_accessed=16 * 4 * depth_cells * row_cells * columns,
            transcendentals=4 * depth_cells * row_cells * columns,
        ),
        name="render_inner",
    )(live_slices, slopes, palette, owner, density, deep_odd, deep_even)


def render_edges(
    live_slices, palette, owner, inner, deep, shear, corner_odd, corner_even, rlo, rhi, n_depth
):
    layers, row_cells, columns = deep.shape
    depth_cells = layers - 2
    n_rows = lax.axis_size("xy")
    extinct = 3.0 / (depth_cells * n_depth)
    tile_rows = row_cells // n_depth
    band = EDGE + 2 * ROW_TILE
    height = 2 * EDGE

    def kernel(
        live_ref, palette_ref, owner_ref, inner_ref, deep_ref, shear_ref,
        corner_odd_ref, corner_even_ref, rlo_ref, rhi_ref,
        out_ref, halo, triple, split_sums, smooth, across, sheared,
    ):
        depth_index = lax.axis_index("gz")
        row_index = lax.axis_index("xy")
        odd_depth = depth_index % 2 == 1

        for side, mid_ref in ((0, rlo_ref), (1, rhi_ref)):
            at = pl.ds(side * ROW_TILE, ROW_TILE)
            even = [corner_even_ref[i, at] for i in range(HALO)]
            odd = [corner_odd_ref[i, at] for i in range(HALO)]
            low = [jnp.where(odd_depth, e, o) for e, o in zip(even, odd)]
            high = [jnp.where(odd_depth, o, e) for e, o in zip(even, odd)]
            outer = 0 if side == 0 else band - ROW_TILE
            inner_at = ROW_TILE if side == 0 else 0
            own_at = 0 if side == 0 else row_cells - (band - ROW_TILE)
            sums = window_sums(low + [mid_ref[i] for i in range(depth_cells)] + high, TAPS)
            for z in range(layers):
                halo[z, side, pl.ds(outer, ROW_TILE)] = sums[z]
                halo[z, side, pl.ds(inner_at, band - ROW_TILE)] = deep_ref[
                    z, pl.ds(own_at, band - ROW_TILE)
                ]

        span = band - ROW_TILE
        for z in range(layers):
            for side in range(2):
                triple[pl.ds(0, span)] = (
                    halo[z, side, pl.ds(3, span)]
                    + halo[z, side, pl.ds(4, span)]
                    + halo[z, side, pl.ds(5, span)]
                )
                split_sums[z, side] = (
                    triple[pl.ds(0, band)] + triple[pl.ds(3, band)] + triple[pl.ds(6, band)]
                )
        both = column_sums(
            split_sums[...].reshape(layers * 2 * band, columns), column_weights(columns)
        ).reshape(layers, 2, band, 2 * columns)
        smooth[...] = both[..., :columns]
        across[...] = both[1:-1, :, :, columns:]

        @pl.when(row_index == 0)
        def _():
            smooth[:, 0, :1] = jnp.zeros((layers, 1, columns), jnp.float32)

        @pl.when(row_index == n_rows - 1)
        def _():
            smooth[:, 1, EDGE + 1 : EDGE + 2] = jnp.zeros((layers, 1, columns), jnp.float32)

        zero_outside(smooth, depth_index, n_depth, layers)

        own_live = live_ref[depth_index, row_index]
        middle = pl.ds(1, EDGE)
        for z in range(depth_cells):
            sides = [
                shade(
                    smooth[z + 1, side, middle],
                    smooth[z + 2, side, middle] - smooth[z, side, middle],
                    smooth[z + 1, side, pl.ds(2, EDGE)] - smooth[z + 1, side, pl.ds(0, EDGE)],
                    across[z, side, middle],
                    z < own_live,
                    palette_ref,
                    extinct,
                )
                for side in range(2)
            ]
            rgba = jnp.concatenate([side[c] for c in range(4) for side in sides])
            sheared[z] = jnp.dot(rgba, shear_ref[z], preferred_element_type=jnp.float32)
        out_ref[...] = inner_ref[...]
        for side, rows in enumerate((range(EDGE), range(row_cells - EDGE, row_cells))):
            march_rows(
                sheared, out_ref, owner_ref, rows, side * EDGE, height,
                depth_cells, tile_rows, columns,
            )

    smem = pl.BlockSpec(memory_space=pltpu.SMEM)
    vmem = pl.BlockSpec(memory_space=pltpu.VMEM)
    return pl.pallas_call(
        kernel,
        out_shape=jax.ShapeDtypeStruct(inner.shape, inner.dtype),
        in_specs=[smem] * 3 + [vmem] * 7,
        out_specs=vmem,
        scratch_shapes=[
            pltpu.VMEM((layers, 2, band, columns), jnp.float32),
            pltpu.VMEM((band + ROW_TILE, columns), jnp.float32),
            pltpu.VMEM((layers, 2, band, columns), jnp.float32),
            pltpu.VMEM((layers, 2, band, columns), jnp.float32),
            pltpu.VMEM((depth_cells, 2, band, columns), jnp.float32),
            pltpu.VMEM((depth_cells, 4 * height, VIEWS * columns), jnp.float32),
        ],
        compiler_params=pltpu.CompilerParams(vmem_limit_bytes=VMEM_BYTES),
        name="render_edges",
    )(live_slices, palette, owner, inner, deep, shear, corner_odd, corner_even, rlo, rhi)


def cut_edges(density):
    depth_cells, row_cells, columns = density.shape

    places = [(i, start) for start in range(0, row_cells, ROW_TILE) for i in range(HALO)]
    words = len(places) // GROUP * WORDS

    def kernel(density_ref, row_even_ref, row_odd_ref, deep_even_ref, deep_odd_ref):
        row_bit = lax.axis_index("xy") % 2
        depth_bit = lax.axis_index("gz") % 2
        last_rows, last_deep = row_cells - ROW_TILE, depth_cells - HALO
        for ref, bit in ((deep_odd_ref, depth_bit), (deep_even_ref, 1 - depth_bit)):
            for group in range(len(places) // GROUP):
                values = [
                    density_ref[bit * last_deep + i, pl.ds(start, ROW_TILE)]
                    for i, start in places[group * GROUP : (group + 1) * GROUP]
                ]
                for k, word in enumerate(pack(values)):
                    ref[group * WORDS + k] = word
        for ref, bit in ((row_even_ref, 1 - row_bit), (row_odd_ref, row_bit)):
            start = pl.multiple_of(bit * last_rows, ROW_TILE)
            ref[...] = density_ref[:, pl.ds(start, ROW_TILE)]

    rows = jax.ShapeDtypeStruct((depth_cells, ROW_TILE, columns), jnp.float32)
    deep = jax.ShapeDtypeStruct((words, ROW_TILE, columns), jnp.int32)
    vmem = pl.BlockSpec(memory_space=pltpu.VMEM)
    return pl.pallas_call(
        kernel,
        out_shape=(rows, rows, deep, deep),
        in_specs=[vmem],
        out_specs=(vmem,) * 4,
        compiler_params=pltpu.CompilerParams(vmem_limit_bytes=VMEM_BYTES),
        name="cut_edges",
    )(density)


def composite_kernel(order_ref, in_ref, out_ref):
    count = in_ref.shape[0]
    rows = in_ref.shape[2] // 4
    for view in range(VIEWS):
        colour, transmit = None, None
        for k in range(count):
            source = order_ref[view, k]
            values = decode(in_ref[source, view])
            part = [values[c * rows : (c + 1) * rows] for c in range(4)]
            clear = 1.0 - part[3]
            if k == 0:
                colour, transmit = part[:3], clear
            else:
                colour = [colour[c] + transmit * part[c] for c in range(3)]
                transmit = transmit * clear
        for c, value in enumerate(colour + [1.0 - transmit]):
            out_ref[view, c, 0] = value


def body(density, live_slices, shear_slopes, palette, depth_order, tile_owner):
    depth_cells, row_cells, columns = density.shape
    n_depth = lax.axis_size("gz")
    edge = depth_cells - HALO
    odd_depth = lax.axis_index("gz") % 2 == 1
    odd_row = lax.axis_index("xy") % 2 == 1

    def pairs(axis, first):
        count = lax.axis_size(axis)
        lower = range(first, count - 1, 2)
        return [(i, i + 1) for i in lower] + [(i + 1, i) for i in lower]

    row_even, row_odd, deep_even, deep_odd = cut_edges(density)
    row_even = lax.ppermute(row_even, "xy", pairs("xy", 0))
    row_odd = lax.ppermute(row_odd, "xy", pairs("xy", 1))
    deep_odd = lax.ppermute(deep_odd, "gz", pairs("gz", 1))
    deep_even = lax.ppermute(deep_even, "gz", pairs("gz", 0))
    rlo = jnp.where(odd_row, row_even, row_odd)
    rhi = jnp.where(odd_row, row_odd, row_even)
    low_corner = jnp.concatenate([rlo[:HALO], rhi[:HALO]], axis=1)
    high_corner = jnp.concatenate([rlo[edge:], rhi[edge:]], axis=1)
    corner_odd = lax.ppermute(
        jnp.where(odd_depth, high_corner, low_corner), "gz", pairs("gz", 1)
    )
    corner_even = lax.ppermute(
        jnp.where(odd_depth, low_corner, high_corner), "gz", pairs("gz", 0)
    )
    inner, deep, shear = render_inner(
        live_slices, shear_slopes, palette, tile_owner, density, deep_odd, deep_even, n_depth
    )
    outgoing = render_edges(
        live_slices, palette, tile_owner, inner, deep, shear,
        corner_odd, corner_even, rlo, rhi, n_depth,
    )
    incoming = lax.all_to_all(outgoing, "gz", split_axis=0, concat_axis=0, tiled=True)
    tile_rows = row_cells // n_depth
    return pl.pallas_call(
        composite_kernel,
        out_shape=jax.ShapeDtypeStruct((VIEWS, 4, 1, tile_rows, columns), jnp.float32),
        in_specs=[pl.BlockSpec(memory_space=pltpu.SMEM), pl.BlockSpec(memory_space=pltpu.VMEM)],
        out_specs=pl.BlockSpec(memory_space=pltpu.VMEM),
        compiler_params=pltpu.CompilerParams(vmem_limit_bytes=VMEM_BYTES),
        name="composite",
    )(depth_order, incoming)


def solution(mesh):
    placed = (P("gz", "xy", None), P(), P(), P(), P(), P())
    return jax.shard_map(
        body, mesh=mesh, in_specs=placed, out_specs=P(None, None, "gz", "xy", None), check_vma=False
    )
```

```python
import jax
import jax.numpy as jnp
from jax import lax
from jax.experimental import pallas as pl
from jax.experimental.pallas import tpu as pltpu
from jax.sharding import PartitionSpec as P

LIGHT = (0.48, 0.6, 0.64)
REACH = 4
HALO = REACH + 1
TAPS = 2 * REACH + 1
ROW_TILE = 8
PACKED_ROWS = 16
EDGE = 16
VIEWS = 2
TOP = 2.2
STEPS = 65535.0
MIDDLE = 32768
LEVELS_PER_UNIT = 5461.0
ZERO_LEVEL = 1 << 19
GROUP, WORDS = 8, 5
VMEM_BYTES = 40 * 1024 * 1024


def column_matrix(columns):
    source = lax.broadcasted_iota(jnp.int32, (columns, columns), 0)
    target = lax.broadcasted_iota(jnp.int32, (columns, columns), 1)

    def band(shift):
        at = target + shift
        inside = (jnp.abs(source - at) <= REACH) & (at >= 0) & (at < columns)
        return jnp.where(inside, 1.0, 0.0).astype(jnp.float32)

    return jnp.concatenate([band(0), band(1) - band(-1)], axis=1).astype(jnp.bfloat16)


def shear_matrices(slopes_ref, slice_depth, columns, total_depth):
    source = lax.broadcasted_iota(jnp.int32, (columns, columns), 0)
    target = lax.broadcasted_iota(jnp.int32, (columns, columns), 1)
    distance = (source - target).astype(jnp.float32)
    parts = []
    for view in range(VIEWS):
        shift = slopes_ref[view] * (slice_depth + 0.5 - 0.5 * total_depth)
        parts.append(jnp.maximum(0.0, 1.0 - jnp.abs(distance + shift)))
    return jnp.concatenate(parts, axis=1).astype(jnp.bfloat16)


def window_sums(layers, taps):
    sums, width = layers, 1
    while 2 * width < taps:
        sums = [sums[i] + sums[i + width] for i in range(len(sums) - width)]
        width *= 2
    return [sums[i] + layers[i + width] for i in range(len(layers) - width)]


def pack(values):
    v = [(x * LEVELS_PER_UNIT + (ZERO_LEVEL + 0.5)).astype(jnp.int32) for x in values]
    v = [(x - ZERO_LEVEL) & 0xFFFFF for x in v]
    upper = [
        v[5] & 0xFFF,
        (v[5] >> 12) | ((v[6] & 0xF) << 8),
        (v[6] >> 4) & 0xFFF,
        (v[6] >> 16) | ((v[7] & 0xFF) << 4),
        v[7] >> 8,
    ]
    return [v[i] | (upper[i] << 20) for i in range(WORDS)]


def unpack(words):
    upper = [lax.shift_right_logical(w, jnp.full_like(w, 20)) for w in words]
    levels = words + [
        upper[0] | ((upper[1] & 0xFF) << 12),
        (upper[1] >> 8) | (upper[2] << 4) | ((upper[3] & 0xF) << 16),
        (upper[3] >> 4) | (upper[4] << 8),
    ]
    levels = [(x << 12) >> 12 for x in levels]
    return [x.astype(jnp.float32) * (1.0 / LEVELS_PER_UNIT) for x in levels]


def encode(value):
    root = jnp.exp(0.125 * jnp.log(jnp.maximum(value, 1e-30) * (1.0 / TOP)))
    level = jnp.minimum(root * STEPS + 0.5, STEPS)
    return (level.astype(jnp.int32) - MIDDLE).astype(jnp.int16)


def decode(code):
    root = (code.astype(jnp.int32) + MIDDLE).astype(jnp.float32) * (TOP**0.125 / STEPS)
    square = root * root
    fourth = square * square
    return fourth * fourth


def split_parts(total):
    hi = total.astype(jnp.bfloat16)
    rest = total - hi.astype(jnp.float32)
    mid = rest.astype(jnp.bfloat16)
    lo = (rest - mid.astype(jnp.float32)).astype(jnp.bfloat16)
    return jnp.concatenate([hi, mid, lo], axis=1)


def column_sums(split, columns):
    band = column_matrix(columns)
    weights = jnp.concatenate([band, band, band], axis=0)
    return jnp.dot(split, weights, preferred_element_type=jnp.float32)


def shear_tables(slopes, depth_cells, columns, n_depth):
    def kernel(slopes_ref, shear_ref):
        slab_start = (lax.axis_index("gz") * depth_cells).astype(jnp.float32)
        for z in range(depth_cells):
            shear_ref[z] = shear_matrices(
                slopes_ref, slab_start + float(z), columns, depth_cells * n_depth
            )

    return pl.pallas_call(
        kernel,
        out_shape=jax.ShapeDtypeStruct((depth_cells, columns, VIEWS * columns), jnp.bfloat16),
        in_specs=[pl.BlockSpec(memory_space=pltpu.SMEM)],
        out_specs=pl.BlockSpec(memory_space=pltpu.VMEM),
        compiler_params=pltpu.CompilerParams(vmem_limit_bytes=VMEM_BYTES),
        name="shear_tables",
    )(slopes)


def shade(center, diff_depth, diff_rows, diff_cols, live, palette_ref, extinct):
    cells = TAPS**3
    floor = 0.01 * (2.0 * cells) ** 2
    square = diff_depth * diff_depth + diff_rows * diff_rows + diff_cols * diff_cols
    toward = LIGHT[0] * diff_depth + LIGHT[1] * diff_rows + LIGHT[2] * diff_cols
    facing = jnp.maximum(0.0, toward) * lax.rsqrt(square + floor)
    twice = center * (2.0 / cells)
    small = jnp.exp(-jnp.abs(twice))
    log1p = jnp.where(small < 1e-4, small * (1.0 - 0.5 * small), jnp.log(1.0 + small))
    softplus = jnp.maximum(twice, 0.0) + log1p
    opacity = jnp.where(live, 1.0 - jnp.exp(-extinct * softplus), 0.0)
    bright = opacity * (0.25 + 0.75 * facing)
    channels = [bright * palette_ref[c] for c in range(3)] + [opacity]
    return [channel.astype(jnp.bfloat16) for channel in channels]


def march(layer, depth_cells, view):
    colour, transmit = None, None
    for z in range(depth_cells):
        part = [layer(z, c) for c in range(4)]
        clear = 1.0 - part[3]
        if z == 0:
            colour, transmit = part[:3], clear
        elif view == 0:
            colour = [colour[c] + transmit * part[c] for c in range(3)]
            transmit = transmit * clear
        else:
            colour = [part[c] + clear * colour[c] for c in range(3)]
            transmit = transmit * clear
    return colour + [1.0 - transmit]


def march_rows(sheared, out_ref, owner_ref, rows, base, height, depth_cells, tile_rows, columns):
    step = min(tile_rows, PACKED_ROWS)
    share = PACKED_ROWS // step
    for row in range(rows.start, rows.stop, step):
        tile, inside = row // tile_rows, row % tile_rows
        at = row - rows.start + base
        for view in range(VIEWS):
            place = owner_ref[view, tile]
            lanes = pl.ds(view * columns, columns)
            values = march(
                lambda z, c: sheared[z, pl.ds(c * height + at, step), lanes], depth_cells, view
            )
            for c in range(0, 4, share):
                value = values[c] if share == 1 else jnp.concatenate(values[c : c + share])
                at_rows = pl.ds(c * tile_rows + inside, PACKED_ROWS)
                out_ref[place, view, at_rows] = encode(value)


def zero_outside(smooth, depth_index, n_depth, layers):
    @pl.when(depth_index == 0)
    def _():
        smooth[0] = jnp.zeros_like(smooth[0])

    @pl.when(depth_index == n_depth - 1)
    def _():
        smooth[layers - 1] = jnp.zeros_like(smooth[layers - 1])


def render_inner(live_slices, palette, owner, shear, density, deep_odd, deep_even, n_depth):
    depth_cells, row_cells, columns = density.shape
    extinct = 3.0 / (depth_cells * n_depth)
    tile_rows = row_cells // n_depth
    layers = depth_cells + 2
    rows = range(EDGE, row_cells - EDGE)
    height = len(rows)
    lead, span = EDGE - ROW_TILE, height + 2 * ROW_TILE

    def kernel(
        live_ref, palette_ref, owner_ref, shear_ref, own_ref, odd_ref, even_ref,
        out_ref, deep, triple, split, smooth, across, sheared,
    ):
        depth_index = lax.axis_index("gz")
        row_index = lax.axis_index("xy")
        odd_depth = depth_index % 2 == 1

        low, high, word = [], [], 0
        for start in range(0, row_cells, ROW_TILE):
            while len(low) < HALO:
                even = [even_ref[word + k] for k in range(WORDS)]
                odd = [odd_ref[word + k] for k in range(WORDS)]
                low += unpack([jnp.where(odd_depth, e, o) for e, o in zip(even, odd)])
                high += unpack([jnp.where(odd_depth, o, e) for e, o in zip(even, odd)])
                word += WORDS
            own = [own_ref[i, pl.ds(start, ROW_TILE)] for i in range(depth_cells)]
            for z, total in enumerate(window_sums(low[:HALO] + own + high[:HALO], TAPS)):
                deep[z, pl.ds(start, ROW_TILE)] = total
            low, high = low[HALO:], high[HALO:]

        for z in range(layers):
            triple[...] = (
                deep[z, pl.ds(lead - 4, span + ROW_TILE)]
                + deep[z, pl.ds(lead - 3, span + ROW_TILE)]
                + deep[z, pl.ds(lead - 2, span + ROW_TILE)]
            )
            split[pl.ds(z * span, span)] = split_parts(
                triple[pl.ds(0, span)] + triple[pl.ds(3, span)] + triple[pl.ds(6, span)]
            )
        both = column_sums(split[...], columns).reshape(layers, span, 2 * columns)
        smooth[...] = both[..., :columns]
        across[...] = both[1:-1, ROW_TILE : ROW_TILE + height, columns:]
        zero_outside(smooth, depth_index, n_depth, layers)

        own_live = live_ref[depth_index, row_index]
        middle = pl.ds(ROW_TILE, height)
        for z in range(depth_cells):
            channels = shade(
                smooth[z + 1, middle],
                smooth[z + 2, middle] - smooth[z, middle],
                smooth[z + 1, pl.ds(ROW_TILE + 1, height)]
                - smooth[z + 1, pl.ds(ROW_TILE - 1, height)],
                across[z],
                z < own_live,
                palette_ref,
                extinct,
            )
            sheared[z] = jnp.dot(
                jnp.concatenate(channels), shear_ref[z], preferred_element_type=jnp.float32
            )
        march_rows(sheared, out_ref, owner_ref, rows, 0, height, depth_cells, tile_rows, columns)

    smem = pl.BlockSpec(memory_space=pltpu.SMEM)
    vmem = pl.BlockSpec(memory_space=pltpu.VMEM)
    return pl.pallas_call(
        kernel,
        out_shape=(
            jax.ShapeDtypeStruct((n_depth, VIEWS, 4 * tile_rows, columns), jnp.int16),
            jax.ShapeDtypeStruct((layers, row_cells, columns), jnp.float32),
        ),
        in_specs=[smem] * 3 + [vmem] * 4,
        out_specs=(vmem,) * 2,
        scratch_shapes=[
            pltpu.VMEM((span + ROW_TILE, columns), jnp.float32),
            pltpu.VMEM((layers * span, 3 * columns), jnp.bfloat16),
            pltpu.VMEM((layers, span, columns), jnp.float32),
            pltpu.VMEM((depth_cells, height, columns), jnp.float32),
            pltpu.VMEM((depth_cells, 4 * height, VIEWS * columns), jnp.float32),
        ],
        compiler_params=pltpu.CompilerParams(vmem_limit_bytes=VMEM_BYTES),
        cost_estimate=pl.CostEstimate(
            flops=100 * depth_cells * row_cells * columns,
            bytes_accessed=16 * 4 * depth_cells * row_cells * columns,
            transcendentals=4 * depth_cells * row_cells * columns,
        ),
        name="render_inner",
    )(live_slices, palette, owner, shear, density, deep_odd, deep_even)


def render_edges(
    live_slices, palette, owner, inner, deep, shear, corner_odd, corner_even, rlo, rhi, n_depth
):
    layers, row_cells, columns = deep.shape
    depth_cells = layers - 2
    n_rows = lax.axis_size("xy")
    extinct = 3.0 / (depth_cells * n_depth)
    tile_rows = row_cells // n_depth
    band = EDGE + 2 * ROW_TILE
    height = 2 * EDGE

    def kernel(
        live_ref, palette_ref, owner_ref, inner_ref, deep_ref, shear_ref,
        corner_odd_ref, corner_even_ref, rlo_ref, rhi_ref,
        out_ref, halo, triple, split, smooth, across, sheared,
    ):
        depth_index = lax.axis_index("gz")
        row_index = lax.axis_index("xy")
        odd_depth = depth_index % 2 == 1

        for side, mid_ref in ((0, rlo_ref), (1, rhi_ref)):
            at = pl.ds(side * ROW_TILE, ROW_TILE)
            even = [corner_even_ref[i, at] for i in range(HALO)]
            odd = [corner_odd_ref[i, at] for i in range(HALO)]
            low = [jnp.where(odd_depth, e, o) for e, o in zip(even, odd)]
            high = [jnp.where(odd_depth, o, e) for e, o in zip(even, odd)]
            outer = 0 if side == 0 else band - ROW_TILE
            inner_at = ROW_TILE if side == 0 else 0
            own_at = 0 if side == 0 else row_cells - (band - ROW_TILE)
            sums = window_sums(low + [mid_ref[i] for i in range(depth_cells)] + high, TAPS)
            for z in range(layers):
                halo[z, side, pl.ds(outer, ROW_TILE)] = sums[z]
                halo[z, side, pl.ds(inner_at, band - ROW_TILE)] = deep_ref[
                    z, pl.ds(own_at, band - ROW_TILE)
                ]

        span = band - ROW_TILE
        for z in range(layers):
            for side in range(2):
                triple[pl.ds(0, span)] = (
                    halo[z, side, pl.ds(3, span)]
                    + halo[z, side, pl.ds(4, span)]
                    + halo[z, side, pl.ds(5, span)]
                )
                split[pl.ds((2 * z + side) * band, band)] = split_parts(
                    triple[pl.ds(0, band)] + triple[pl.ds(3, band)] + triple[pl.ds(6, band)]
                )
        both = column_sums(split[...], columns).reshape(layers, 2, band, 2 * columns)
        smooth[...] = both[..., :columns]
        across[...] = both[1:-1, :, :, columns:]

        @pl.when(row_index == 0)
        def _():
            smooth[:, 0, :1] = jnp.zeros((layers, 1, columns), jnp.float32)

        @pl.when(row_index == n_rows - 1)
        def _():
            smooth[:, 1, EDGE + 1 : EDGE + 2] = jnp.zeros((layers, 1, columns), jnp.float32)

        zero_outside(smooth, depth_index, n_depth, layers)

        own_live = live_ref[depth_index, row_index]
        middle = pl.ds(1, EDGE)
        for z in range(depth_cells):
            sides = [
                shade(
                    smooth[z + 1, side, middle],
                    smooth[z + 2, side, middle] - smooth[z, side, middle],
                    smooth[z + 1, side, pl.ds(2, EDGE)] - smooth[z + 1, side, pl.ds(0, EDGE)],
                    across[z, side, middle],
                    z < own_live,
                    palette_ref,
                    extinct,
                )
                for side in range(2)
            ]
            rgba = jnp.concatenate([side[c] for c in range(4) for side in sides])
            sheared[z] = jnp.dot(rgba, shear_ref[z], preferred_element_type=jnp.float32)
        out_ref[...] = inner_ref[...]
        for side, rows in enumerate((range(EDGE), range(row_cells - EDGE, row_cells))):
            march_rows(
                sheared, out_ref, owner_ref, rows, side * EDGE, height,
                depth_cells, tile_rows, columns,
            )

    smem = pl.BlockSpec(memory_space=pltpu.SMEM)
    vmem = pl.BlockSpec(memory_space=pltpu.VMEM)
    return pl.pallas_call(
        kernel,
        out_shape=jax.ShapeDtypeStruct(inner.shape, inner.dtype),
        in_specs=[smem] * 3 + [vmem] * 7,
        out_specs=vmem,
        scratch_shapes=[
            pltpu.VMEM((layers, 2, band, columns), jnp.float32),
            pltpu.VMEM((band + ROW_TILE, columns), jnp.float32),
            pltpu.VMEM((layers * 2 * band, 3 * columns), jnp.bfloat16),
            pltpu.VMEM((layers, 2, band, columns), jnp.float32),
            pltpu.VMEM((depth_cells, 2, band, columns), jnp.float32),
            pltpu.VMEM((depth_cells, 4 * height, VIEWS * columns), jnp.float32),
        ],
        compiler_params=pltpu.CompilerParams(vmem_limit_bytes=VMEM_BYTES),
        name="render_edges",
    )(live_slices, palette, owner, inner, deep, shear, corner_odd, corner_even, rlo, rhi)


def cut_edges(density):
    depth_cells, row_cells, columns = density.shape

    places = [(i, start) for start in range(0, row_cells, ROW_TILE) for i in range(HALO)]
    words = len(places) // GROUP * WORDS

    def kernel(density_ref, row_even_ref, row_odd_ref, deep_even_ref, deep_odd_ref):
        row_bit = lax.axis_index("xy") % 2
        depth_bit = lax.axis_index("gz") % 2
        last_rows, last_deep = row_cells - ROW_TILE, depth_cells - HALO
        for ref, bit in ((deep_odd_ref, depth_bit), (deep_even_ref, 1 - depth_bit)):
            for group in range(len(places) // GROUP):
                values = [
                    density_ref[bit * last_deep + i, pl.ds(start, ROW_TILE)]
                    for i, start in places[group * GROUP : (group + 1) * GROUP]
                ]
                for k, word in enumerate(pack(values)):
                    ref[group * WORDS + k] = word
        for ref, bit in ((row_even_ref, 1 - row_bit), (row_odd_ref, row_bit)):
            start = pl.multiple_of(bit * last_rows, ROW_TILE)
            ref[...] = density_ref[:, pl.ds(start, ROW_TILE)]

    rows = jax.ShapeDtypeStruct((depth_cells, ROW_TILE, columns), jnp.float32)
    deep = jax.ShapeDtypeStruct((words, ROW_TILE, columns), jnp.int32)
    vmem = pl.BlockSpec(memory_space=pltpu.VMEM)
    return pl.pallas_call(
        kernel,
        out_shape=(rows, rows, deep, deep),
        in_specs=[vmem],
        out_specs=(vmem,) * 4,
        compiler_params=pltpu.CompilerParams(vmem_limit_bytes=VMEM_BYTES),
        name="cut_edges",
    )(density)


def composite_kernel(order_ref, in_ref, out_ref):
    count = in_ref.shape[0]
    rows = in_ref.shape[2] // 4
    for view in range(VIEWS):
        colour, transmit = None, None
        for k in range(count):
            source = order_ref[view, k]
            values = decode(in_ref[source, view])
            part = [values[c * rows : (c + 1) * rows] for c in range(4)]
            clear = 1.0 - part[3]
            if k == 0:
                colour, transmit = part[:3], clear
            else:
                colour = [colour[c] + transmit * part[c] for c in range(3)]
                transmit = transmit * clear
        for c, value in enumerate(colour + [1.0 - transmit]):
            out_ref[view, c, 0] = value


def body(density, live_slices, shear_slopes, palette, depth_order, tile_owner):
    depth_cells, row_cells, columns = density.shape
    n_depth = lax.axis_size("gz")
    edge = depth_cells - HALO
    odd_depth = lax.axis_index("gz") % 2 == 1
    odd_row = lax.axis_index("xy") % 2 == 1

    def pairs(axis, first):
        count = lax.axis_size(axis)
        lower = range(first, count - 1, 2)
        return [(i, i + 1) for i in lower] + [(i + 1, i) for i in lower]

    row_even, row_odd, deep_even, deep_odd = cut_edges(density)
    row_even = lax.ppermute(row_even, "xy", pairs("xy", 0))
    row_odd = lax.ppermute(row_odd, "xy", pairs("xy", 1))
    deep_odd = lax.ppermute(deep_odd, "gz", pairs("gz", 1))
    deep_even = lax.ppermute(deep_even, "gz", pairs("gz", 0))
    rlo = jnp.where(odd_row, row_even, row_odd)
    rhi = jnp.where(odd_row, row_odd, row_even)
    low_corner = jnp.concatenate([rlo[:HALO], rhi[:HALO]], axis=1)
    high_corner = jnp.concatenate([rlo[edge:], rhi[edge:]], axis=1)
    corner_odd = lax.ppermute(
        jnp.where(odd_depth, high_corner, low_corner), "gz", pairs("gz", 1)
    )
    corner_even = lax.ppermute(
        jnp.where(odd_depth, low_corner, high_corner), "gz", pairs("gz", 0)
    )
    shear = shear_tables(shear_slopes, depth_cells, columns, n_depth)
    inner, deep = render_inner(
        live_slices, palette, tile_owner, shear, density, deep_odd, deep_even, n_depth
    )
    outgoing = render_edges(
        live_slices, palette, tile_owner, inner, deep, shear,
        corner_odd, corner_even, rlo, rhi, n_depth,
    )
    incoming = lax.all_to_all(outgoing, "gz", split_axis=0, concat_axis=0, tiled=True)
    tile_rows = row_cells // n_depth
    return pl.pallas_call(
        composite_kernel,
        out_shape=jax.ShapeDtypeStruct((VIEWS, 4, 1, tile_rows, columns), jnp.float32),
        in_specs=[pl.BlockSpec(memory_space=pltpu.SMEM), pl.BlockSpec(memory_space=pltpu.VMEM)],
        out_specs=pl.BlockSpec(memory_space=pltpu.VMEM),
        compiler_params=pltpu.CompilerParams(vmem_limit_bytes=VMEM_BYTES),
        name="composite",
    )(depth_order, incoming)


def solution(mesh):
    placed = (P("gz", "xy", None), P(), P(), P(), P(), P())
    return jax.shard_map(
        body, mesh=mesh, in_specs=placed, out_specs=P(None, None, "gz", "xy", None), check_vma=False
    )
```

```python
import jax
import jax.numpy as jnp
from jax import lax
from jax.experimental import pallas as pl
from jax.experimental.pallas import tpu as pltpu
from jax.sharding import PartitionSpec as P

LIGHT = (0.48, 0.6, 0.64)
REACH = 4
HALO = REACH + 1
TAPS = 2 * REACH + 1
ROW_TILE = 8
PACKED_ROWS = 16
EDGE = 16
VIEWS = 2
TOP = 2.2
STEPS = 65535.0
MIDDLE = 32768
LEVELS_PER_UNIT = 5461.0
ZERO_LEVEL = 1 << 19
GROUP, WORDS = 8, 5
VMEM_BYTES = 40 * 1024 * 1024


def column_matrix(columns):
    source = lax.broadcasted_iota(jnp.int32, (columns, columns), 0)
    target = lax.broadcasted_iota(jnp.int32, (columns, columns), 1)

    def band(shift):
        at = target + shift
        inside = (jnp.abs(source - at) <= REACH) & (at >= 0) & (at < columns)
        return jnp.where(inside, 1.0, 0.0).astype(jnp.float32)

    return jnp.concatenate([band(0), band(1) - band(-1)], axis=1).astype(jnp.bfloat16)


def shear_matrices(slopes_ref, slice_depth, columns, total_depth):
    source = lax.broadcasted_iota(jnp.int32, (columns, columns), 0)
    target = lax.broadcasted_iota(jnp.int32, (columns, columns), 1)
    distance = (source - target).astype(jnp.float32)
    parts = []
    for view in range(VIEWS):
        shift = slopes_ref[view] * (slice_depth + 0.5 - 0.5 * total_depth)
        parts.append(jnp.maximum(0.0, 1.0 - jnp.abs(distance + shift)))
    return jnp.concatenate(parts, axis=1).astype(jnp.bfloat16)


def window_sums(layers, taps):
    sums, width = layers, 1
    while 2 * width < taps:
        sums = [sums[i] + sums[i + width] for i in range(len(sums) - width)]
        width *= 2
    return [sums[i] + layers[i + width] for i in range(len(layers) - width)]


def pack(values):
    v = [(x * LEVELS_PER_UNIT + (ZERO_LEVEL + 0.5)).astype(jnp.int32) for x in values]
    v = [(x - ZERO_LEVEL) & 0xFFFFF for x in v]
    upper = [
        v[5] & 0xFFF,
        (v[5] >> 12) | ((v[6] & 0xF) << 8),
        (v[6] >> 4) & 0xFFF,
        (v[6] >> 16) | ((v[7] & 0xFF) << 4),
        v[7] >> 8,
    ]
    return [v[i] | (upper[i] << 20) for i in range(WORDS)]


def unpack(words):
    upper = [lax.shift_right_logical(w, jnp.full_like(w, 20)) for w in words]
    levels = words + [
        upper[0] | ((upper[1] & 0xFF) << 12),
        (upper[1] >> 8) | (upper[2] << 4) | ((upper[3] & 0xF) << 16),
        (upper[3] >> 4) | (upper[4] << 8),
    ]
    levels = [(x << 12) >> 12 for x in levels]
    return [x.astype(jnp.float32) * (1.0 / LEVELS_PER_UNIT) for x in levels]


def encode(value):
    root = jnp.exp(0.125 * jnp.log(jnp.maximum(value, 1e-30) * (1.0 / TOP)))
    level = jnp.minimum(root * STEPS + 0.5, STEPS)
    return (level.astype(jnp.int32) - MIDDLE).astype(jnp.int16)


def decode(code):
    root = (code.astype(jnp.int32) + MIDDLE).astype(jnp.float32) * (TOP**0.125 / STEPS)
    square = root * root
    fourth = square * square
    return fourth * fourth


def column_sums(total, weights):
    hi = total.astype(jnp.bfloat16)
    rest = total - hi.astype(jnp.float32)
    mid = rest.astype(jnp.bfloat16)
    lo = (rest - mid.astype(jnp.float32)).astype(jnp.bfloat16)
    split = jnp.concatenate([hi, mid, lo], axis=1)
    return jnp.dot(split, weights, preferred_element_type=jnp.float32)


def column_weights(columns):
    band = column_matrix(columns)
    return jnp.concatenate([band, band, band], axis=0)


def shade(center, diff_depth, diff_rows, diff_cols, live, palette_ref, extinct):
    cells = TAPS**3
    floor = 0.01 * (2.0 * cells) ** 2
    square = diff_depth * diff_depth + diff_rows * diff_rows + diff_cols * diff_cols
    toward = LIGHT[0] * diff_depth + LIGHT[1] * diff_rows + LIGHT[2] * diff_cols
    facing = jnp.maximum(0.0, toward) * lax.rsqrt(square + floor)
    twice = center * (2.0 / cells)
    small = jnp.exp(-jnp.abs(twice))
    log1p = jnp.where(small < 1e-4, small * (1.0 - 0.5 * small), jnp.log(1.0 + small))
    softplus = jnp.maximum(twice, 0.0) + log1p
    opacity = jnp.where(live, 1.0 - jnp.exp(-extinct * softplus), 0.0)
    bright = opacity * (0.25 + 0.75 * facing)
    channels = [bright * palette_ref[c] for c in range(3)] + [opacity]
    return [channel.astype(jnp.bfloat16) for channel in channels]


def march(layer, depth_cells, view):
    colour, transmit = None, None
    for z in range(depth_cells):
        part = [layer(z, c) for c in range(4)]
        clear = 1.0 - part[3]
        if z == 0:
            colour, transmit = part[:3], clear
        elif view == 0:
            colour = [colour[c] + transmit * part[c] for c in range(3)]
            transmit = transmit * clear
        else:
            colour = [part[c] + clear * colour[c] for c in range(3)]
            transmit = transmit * clear
    return colour + [1.0 - transmit]


def march_rows(sheared, out_ref, owner_ref, rows, base, height, depth_cells, tile_rows, columns):
    step = min(tile_rows, PACKED_ROWS)
    share = PACKED_ROWS // step
    for row in range(rows.start, rows.stop, step):
        tile, inside = row // tile_rows, row % tile_rows
        at = row - rows.start + base
        for view in range(VIEWS):
            place = owner_ref[view, tile]
            lanes = pl.ds(view * columns, columns)
            values = march(
                lambda z, c: sheared[z, pl.ds(c * height + at, step), lanes], depth_cells, view
            )
            for c in range(0, 4, share):
                value = values[c] if share == 1 else jnp.concatenate(values[c : c + share])
                at_rows = pl.ds(c * tile_rows + inside, PACKED_ROWS)
                out_ref[place, view, at_rows] = encode(value)


def zero_outside(smooth, depth_index, n_depth, layers):
    @pl.when(depth_index == 0)
    def _():
        smooth[0] = jnp.zeros_like(smooth[0])

    @pl.when(depth_index == n_depth - 1)
    def _():
        smooth[layers - 1] = jnp.zeros_like(smooth[layers - 1])


def render_inner(live_slices, slopes, palette, owner, density, deep_odd, deep_even, n_depth):
    depth_cells, row_cells, columns = density.shape
    total_depth = depth_cells * n_depth
    extinct = 3.0 / total_depth
    tile_rows = row_cells // n_depth
    layers = depth_cells + 2
    rows = range(EDGE, row_cells - EDGE)
    height = len(rows)
    lead, span = EDGE - ROW_TILE, height + 2 * ROW_TILE

    def kernel(
        live_ref, slopes_ref, palette_ref, owner_ref, own_ref, odd_ref, even_ref,
        out_ref, deep, shear_ref, triple, smooth, across, sheared,
    ):
        depth_index = lax.axis_index("gz")
        row_index = lax.axis_index("xy")
        odd_depth = depth_index % 2 == 1

        low, high, word = [], [], 0
        for start in range(0, row_cells, ROW_TILE):
            while len(low) < HALO:
                even = [even_ref[word + k] for k in range(WORDS)]
                odd = [odd_ref[word + k] for k in range(WORDS)]
                low += unpack([jnp.where(odd_depth, e, o) for e, o in zip(even, odd)])
                high += unpack([jnp.where(odd_depth, o, e) for e, o in zip(even, odd)])
                word += WORDS
            own = [own_ref[i, pl.ds(start, ROW_TILE)] for i in range(depth_cells)]
            for z, total in enumerate(window_sums(low[:HALO] + own + high[:HALO], TAPS)):
                deep[z, pl.ds(start, ROW_TILE)] = total
            low, high = low[HALO:], high[HALO:]

        slab_start = (depth_index * depth_cells).astype(jnp.float32)
        for z in range(depth_cells):
            shear_ref[z] = shear_matrices(slopes_ref, slab_start + float(z), columns, total_depth)

        weights = column_weights(columns)
        for z in range(layers):
            triple[...] = (
                deep[z, pl.ds(lead - 4, span + ROW_TILE)]
                + deep[z, pl.ds(lead - 3, span + ROW_TILE)]
                + deep[z, pl.ds(lead - 2, span + ROW_TILE)]
            )
            total = triple[pl.ds(0, span)] + triple[pl.ds(3, span)] + triple[pl.ds(6, span)]
            if 1 <= z <= depth_cells:
                both = column_sums(total, weights)
                smooth[z] = both[:, :columns]
                across[z - 1] = both[ROW_TILE : ROW_TILE + height, columns:]
            else:
                smooth[z] = column_sums(total, weights[:, :columns])
        zero_outside(smooth, depth_index, n_depth, layers)

        own_live = live_ref[depth_index, row_index]
        middle = pl.ds(ROW_TILE, height)
        for z in range(depth_cells):
            channels = shade(
                smooth[z + 1, middle],
                smooth[z + 2, middle] - smooth[z, middle],
                smooth[z + 1, pl.ds(ROW_TILE + 1, height)]
                - smooth[z + 1, pl.ds(ROW_TILE - 1, height)],
                across[z],
                z < own_live,
                palette_ref,
                extinct,
            )
            sheared[z] = jnp.dot(
                jnp.concatenate(channels), shear_ref[z], preferred_element_type=jnp.float32
            )
        march_rows(sheared, out_ref, owner_ref, rows, 0, height, depth_cells, tile_rows, columns)

    smem = pl.BlockSpec(memory_space=pltpu.SMEM)
    vmem = pl.BlockSpec(memory_space=pltpu.VMEM)
    return pl.pallas_call(
        kernel,
        out_shape=(
            jax.ShapeDtypeStruct((n_depth, VIEWS, 4 * tile_rows, columns), jnp.int16),
            jax.ShapeDtypeStruct((layers, row_cells, columns), jnp.float32),
            jax.ShapeDtypeStruct((depth_cells, columns, VIEWS * columns), jnp.bfloat16),
        ),
        in_specs=[smem] * 4 + [vmem] * 3,
        out_specs=(vmem,) * 3,
        scratch_shapes=[
            pltpu.VMEM((span + ROW_TILE, columns), jnp.float32),
            pltpu.VMEM((layers, span, columns), jnp.float32),
            pltpu.VMEM((depth_cells, height, columns), jnp.float32),
            pltpu.VMEM((depth_cells, 4 * height, VIEWS * columns), jnp.float32),
        ],
        compiler_params=pltpu.CompilerParams(vmem_limit_bytes=VMEM_BYTES),
        cost_estimate=pl.CostEstimate(
            flops=100 * depth_cells * row_cells * columns,
            bytes_accessed=16 * 4 * depth_cells * row_cells * columns,
            transcendentals=4 * depth_cells * row_cells * columns,
        ),
        name="render_inner",
    )(live_slices, slopes, palette, owner, density, deep_odd, deep_even)


def render_edges(
    live_slices, palette, owner, inner, deep, shear, corner_odd, corner_even, rlo, rhi, n_depth
):
    layers, row_cells, columns = deep.shape
    depth_cells = layers - 2
    n_rows = lax.axis_size("xy")
    extinct = 3.0 / (depth_cells * n_depth)
    tile_rows = row_cells // n_depth
    band = EDGE + 2 * ROW_TILE
    height = 2 * EDGE

    def kernel(
        live_ref, palette_ref, owner_ref, inner_ref, deep_ref, shear_ref,
        corner_odd_ref, corner_even_ref, rlo_ref, rhi_ref,
        out_ref, halo, triple, split_sums, smooth, across, sheared,
    ):
        depth_index = lax.axis_index("gz")
        row_index = lax.axis_index("xy")
        odd_depth = depth_index % 2 == 1

        for side, mid_ref in ((0, rlo_ref), (1, rhi_ref)):
            at = pl.ds(side * ROW_TILE, ROW_TILE)
            even = [corner_even_ref[i, at] for i in range(HALO)]
            odd = [corner_odd_ref[i, at] for i in range(HALO)]
            low = [jnp.where(odd_depth, e, o) for e, o in zip(even, odd)]
            high = [jnp.where(odd_depth, o, e) for e, o in zip(even, odd)]
            outer = 0 if side == 0 else band - ROW_TILE
            inner_at = ROW_TILE if side == 0 else 0
            own_at = 0 if side == 0 else row_cells - (band - ROW_TILE)
            sums = window_sums(low + [mid_ref[i] for i in range(depth_cells)] + high, TAPS)
            for z in range(layers):
                halo[z, side, pl.ds(outer, ROW_TILE)] = sums[z]
                halo[z, side, pl.ds(inner_at, band - ROW_TILE)] = deep_ref[
                    z, pl.ds(own_at, band - ROW_TILE)
                ]

        span = band - ROW_TILE
        for z in range(layers):
            for side in range(2):
                triple[pl.ds(0, span)] = (
                    halo[z, side, pl.ds(3, span)]
                    + halo[z, side, pl.ds(4, span)]
                    + halo[z, side, pl.ds(5, span)]
                )
                split_sums[z, side] = (
                    triple[pl.ds(0, band)] + triple[pl.ds(3, band)] + triple[pl.ds(6, band)]
                )
        both = column_sums(
            split_sums[...].reshape(layers * 2 * band, columns), column_weights(columns)
        ).reshape(layers, 2, band, 2 * columns)
        smooth[...] = both[..., :columns]
        across[...] = both[1:-1, :, :, columns:]

        @pl.when(row_index == 0)
        def _():
            smooth[:, 0, :1] = jnp.zeros((layers, 1, columns), jnp.float32)

        @pl.when(row_index == n_rows - 1)
        def _():
            smooth[:, 1, EDGE + 1 : EDGE + 2] = jnp.zeros((layers, 1, columns), jnp.float32)

        zero_outside(smooth, depth_index, n_depth, layers)

        own_live = live_ref[depth_index, row_index]
        middle = pl.ds(1, EDGE)
        for z in range(depth_cells):
            sides = [
                shade(
                    smooth[z + 1, side, middle],
                    smooth[z + 2, side, middle] - smooth[z, side, middle],
                    smooth[z + 1, side, pl.ds(2, EDGE)] - smooth[z + 1, side, pl.ds(0, EDGE)],
                    across[z, side, middle],
                    z < own_live,
                    palette_ref,
                    extinct,
                )
                for side in range(2)
            ]
            rgba = jnp.concatenate([side[c] for c in range(4) for side in sides])
            sheared[z] = jnp.dot(rgba, shear_ref[z], preferred_element_type=jnp.float32)
        out_ref[...] = inner_ref[...]
        for side, rows in enumerate((range(EDGE), range(row_cells - EDGE, row_cells))):
            march_rows(
                sheared, out_ref, owner_ref, rows, side * EDGE, height,
                depth_cells, tile_rows, columns,
            )

    smem = pl.BlockSpec(memory_space=pltpu.SMEM)
    vmem = pl.BlockSpec(memory_space=pltpu.VMEM)
    return pl.pallas_call(
        kernel,
        out_shape=jax.ShapeDtypeStruct(inner.shape, inner.dtype),
        in_specs=[smem] * 3 + [vmem] * 7,
        out_specs=vmem,
        scratch_shapes=[
            pltpu.VMEM((layers, 2, band, columns), jnp.float32),
            pltpu.VMEM((band + ROW_TILE, columns), jnp.float32),
            pltpu.VMEM((layers, 2, band, columns), jnp.float32),
            pltpu.VMEM((layers, 2, band, columns), jnp.float32),
            pltpu.VMEM((depth_cells, 2, band, columns), jnp.float32),
            pltpu.VMEM((depth_cells, 4 * height, VIEWS * columns), jnp.float32),
        ],
        compiler_params=pltpu.CompilerParams(vmem_limit_bytes=VMEM_BYTES),
        name="render_edges",
    )(live_slices, palette, owner, inner, deep, shear, corner_odd, corner_even, rlo, rhi)


def cut_edges(density):
    depth_cells, row_cells, columns = density.shape

    places = [(i, start) for start in range(0, row_cells, ROW_TILE) for i in range(HALO)]
    words = len(places) // GROUP * WORDS

    def kernel(density_ref, row_even_ref, row_odd_ref, deep_even_ref, deep_odd_ref):
        row_bit = lax.axis_index("xy") % 2
        depth_bit = lax.axis_index("gz") % 2
        last_rows, last_deep = row_cells - ROW_TILE, depth_cells - HALO
        for ref, bit in ((deep_odd_ref, depth_bit), (deep_even_ref, 1 - depth_bit)):
            for group in range(len(places) // GROUP):
                values = [
                    density_ref[bit * last_deep + i, pl.ds(start, ROW_TILE)]
                    for i, start in places[group * GROUP : (group + 1) * GROUP]
                ]
                for k, word in enumerate(pack(values)):
                    ref[group * WORDS + k] = word
        for ref, bit in ((row_even_ref, 1 - row_bit), (row_odd_ref, row_bit)):
            start = pl.multiple_of(bit * last_rows, ROW_TILE)
            ref[...] = density_ref[:, pl.ds(start, ROW_TILE)]

    rows = jax.ShapeDtypeStruct((depth_cells, ROW_TILE, columns), jnp.float32)
    deep = jax.ShapeDtypeStruct((words, ROW_TILE, columns), jnp.int32)
    vmem = pl.BlockSpec(memory_space=pltpu.VMEM)
    return pl.pallas_call(
        kernel,
        out_shape=(rows, rows, deep, deep),
        in_specs=[vmem],
        out_specs=(vmem,) * 4,
        compiler_params=pltpu.CompilerParams(vmem_limit_bytes=VMEM_BYTES),
        name="cut_edges",
    )(density)


def composite_kernel(order_ref, in_ref, out_ref):
    count = in_ref.shape[0]
    rows = in_ref.shape[2] // 4
    for view in range(VIEWS):
        colour, transmit = None, None
        for k in range(count):
            source = order_ref[view, k]
            values = decode(in_ref[source, view])
            part = [values[c * rows : (c + 1) * rows] for c in range(4)]
            clear = 1.0 - part[3]
            if k == 0:
                colour, transmit = part[:3], clear
            else:
                colour = [colour[c] + transmit * part[c] for c in range(3)]
                transmit = transmit * clear
        for c, value in enumerate(colour + [1.0 - transmit]):
            out_ref[view, c, 0] = value


def body(density, live_slices, shear_slopes, palette, depth_order, tile_owner):
    depth_cells, row_cells, columns = density.shape
    n_depth = lax.axis_size("gz")
    edge = depth_cells - HALO
    odd_depth = lax.axis_index("gz") % 2 == 1
    odd_row = lax.axis_index("xy") % 2 == 1

    def pairs(axis, first):
        count = lax.axis_size(axis)
        lower = range(first, count - 1, 2)
        return [(i, i + 1) for i in lower] + [(i + 1, i) for i in lower]

    row_even, row_odd, deep_even, deep_odd = cut_edges(density)
    deep_odd = lax.ppermute(deep_odd, "gz", pairs("gz", 1))
    deep_even = lax.ppermute(deep_even, "gz", pairs("gz", 0))

    def exchange_rows(even, odd):
        return lax.ppermute(even, "xy", pairs("xy", 0)), lax.ppermute(odd, "xy", pairs("xy", 1))

    row_even, row_odd = lax.cond(
        lax.axis_index("gz") < 0, lambda even, odd: (even, odd), exchange_rows, row_even, row_odd
    )
    rlo = jnp.where(odd_row, row_even, row_odd)
    rhi = jnp.where(odd_row, row_odd, row_even)
    low_corner = jnp.concatenate([rlo[:HALO], rhi[:HALO]], axis=1)
    high_corner = jnp.concatenate([rlo[edge:], rhi[edge:]], axis=1)
    corner_odd = lax.ppermute(
        jnp.where(odd_depth, high_corner, low_corner), "gz", pairs("gz", 1)
    )
    corner_even = lax.ppermute(
        jnp.where(odd_depth, low_corner, high_corner), "gz", pairs("gz", 0)
    )
    inner, deep, shear = render_inner(
        live_slices, shear_slopes, palette, tile_owner, density, deep_odd, deep_even, n_depth
    )
    outgoing = render_edges(
        live_slices, palette, tile_owner, inner, deep, shear,
        corner_odd, corner_even, rlo, rhi, n_depth,
    )
    incoming = lax.all_to_all(outgoing, "gz", split_axis=0, concat_axis=0, tiled=True)
    tile_rows = row_cells // n_depth
    return pl.pallas_call(
        composite_kernel,
        out_shape=jax.ShapeDtypeStruct((VIEWS, 4, 1, tile_rows, columns), jnp.float32),
        in_specs=[pl.BlockSpec(memory_space=pltpu.SMEM), pl.BlockSpec(memory_space=pltpu.VMEM)],
        out_specs=pl.BlockSpec(memory_space=pltpu.VMEM),
        compiler_params=pltpu.CompilerParams(vmem_limit_bytes=VMEM_BYTES),
        name="composite",
    )(depth_order, incoming)


def solution(mesh):
    placed = (P("gz", "xy", None), P(), P(), P(), P(), P())
    return jax.shard_map(
        body, mesh=mesh, in_specs=placed, out_specs=P(None, None, "gz", "xy", None), check_vma=False
    )
```

```python
import math

import jax
import jax.numpy as jnp
from jax import lax
from jax.experimental import pallas as pl
from jax.experimental.pallas import tpu as pltpu
from jax.sharding import PartitionSpec as P

LIGHT = (0.48, 0.6, 0.64)
REACH = 4
HALO = REACH + 1
TAPS = 2 * REACH + 1
ROW_TILE = 8
PACKED_ROWS = 16
EDGE = 16
VIEWS = 2
TOP = 2.2
STEPS = 65535.0
MIDDLE = 32768
LEVELS_PER_UNIT = 5461.0
ZERO_LEVEL = 1 << 19
GROUP, WORDS = 8, 5
VMEM_BYTES = 40 * 1024 * 1024


def column_matrix(columns):
    source = lax.broadcasted_iota(jnp.int32, (columns, columns), 0)
    target = lax.broadcasted_iota(jnp.int32, (columns, columns), 1)

    def band(shift):
        at = target + shift
        inside = (jnp.abs(source - at) <= REACH) & (at >= 0) & (at < columns)
        return jnp.where(inside, 1.0, 0.0).astype(jnp.float32)

    return jnp.concatenate([band(0), band(1) - band(-1)], axis=1).astype(jnp.bfloat16)


def shear_matrices(slopes_ref, slice_depth, columns, total_depth):
    source = lax.broadcasted_iota(jnp.int32, (columns, columns), 0)
    target = lax.broadcasted_iota(jnp.int32, (columns, columns), 1)
    distance = (source - target).astype(jnp.float32)
    parts = []
    for view in range(VIEWS):
        shift = slopes_ref[view] * (slice_depth + 0.5 - 0.5 * total_depth)
        parts.append(jnp.maximum(0.0, 1.0 - jnp.abs(distance + shift)))
    return jnp.concatenate(parts, axis=1).astype(jnp.bfloat16)


def window_sums(layers, taps):
    sums, width = layers, 1
    while 2 * width < taps:
        sums = [sums[i] + sums[i + width] for i in range(len(sums) - width)]
        width *= 2
    return [sums[i] + layers[i + width] for i in range(len(layers) - width)]


def pack(values):
    v = [(x * LEVELS_PER_UNIT + (ZERO_LEVEL + 0.5)).astype(jnp.int32) for x in values]
    v = [(x - ZERO_LEVEL) & 0xFFFFF for x in v]
    upper = [
        v[5] & 0xFFF,
        (v[5] >> 12) | ((v[6] & 0xF) << 8),
        (v[6] >> 4) & 0xFFF,
        (v[6] >> 16) | ((v[7] & 0xFF) << 4),
        v[7] >> 8,
    ]
    return [v[i] | (upper[i] << 20) for i in range(WORDS)]


def unpack(words):
    upper = [lax.shift_right_logical(w, jnp.full_like(w, 20)) for w in words]
    levels = words + [
        upper[0] | ((upper[1] & 0xFF) << 12),
        (upper[1] >> 8) | (upper[2] << 4) | ((upper[3] & 0xF) << 16),
        (upper[3] >> 4) | (upper[4] << 8),
    ]
    levels = [(x << 12) >> 12 for x in levels]
    return [x.astype(jnp.float32) * (1.0 / LEVELS_PER_UNIT) for x in levels]


def encode(value):
    scale = math.log2(STEPS) - 0.125 * math.log2(TOP)
    root = jnp.exp2(0.125 * jnp.log2(jnp.maximum(value, 1e-30)) + scale)
    return ((root + 0.5).astype(jnp.int32) - MIDDLE).astype(jnp.int16)


def decode(code):
    root = (code.astype(jnp.int32) + MIDDLE).astype(jnp.float32) * (TOP**0.125 / STEPS)
    square = root * root
    fourth = square * square
    return fourth * fourth


def column_sums(total, weights):
    hi = total.astype(jnp.bfloat16)
    rest = total - hi.astype(jnp.float32)
    mid = rest.astype(jnp.bfloat16)
    lo = (rest - mid.astype(jnp.float32)).astype(jnp.bfloat16)
    split = jnp.concatenate([hi, mid, lo], axis=1)
    return jnp.dot(split, weights, preferred_element_type=jnp.float32)


def column_weights(columns):
    band = column_matrix(columns)
    return jnp.concatenate([band, band, band], axis=0)


def shade(center, diff_depth, diff_rows, diff_cols, live, palette_ref, extinct):
    cells = TAPS**3
    floor = 0.01 * (2.0 * cells) ** 2
    square = diff_depth * diff_depth + diff_rows * diff_rows + diff_cols * diff_cols + floor
    light = [0.75 * part for part in LIGHT]
    toward = light[0] * diff_depth + light[1] * diff_rows + light[2] * diff_cols
    facing = jnp.maximum(0.0, toward) * lax.rsqrt(square)
    t = center * (2.0 * math.log2(math.e) / cells)
    softplus = jnp.maximum(t, 0.0) + jnp.log2(1.0 + jnp.exp2(-jnp.abs(t)))
    opacity = 1.0 - jnp.exp2(jnp.where(live, -extinct, 0.0) * softplus)
    bright = opacity * (0.25 + facing)
    channels = [bright * palette_ref[c] for c in range(3)] + [opacity]
    return [channel.astype(jnp.bfloat16) for channel in channels]


def march(layer, depth_cells, view):
    colour, transmit = None, None
    for z in range(depth_cells):
        part = [layer(z, c) for c in range(4)]
        clear = 1.0 - part[3]
        if z == 0:
            colour, transmit = part[:3], clear
        elif view == 0:
            colour = [colour[c] + transmit * part[c] for c in range(3)]
            transmit = transmit * clear
        else:
            colour = [part[c] + clear * colour[c] for c in range(3)]
            transmit = transmit * clear
    return colour + [1.0 - transmit]


def march_rows(sheared, out_ref, owner_ref, rows, base, height, depth_cells, tile_rows, columns):
    step = min(tile_rows, PACKED_ROWS)
    share = PACKED_ROWS // step
    for row in range(rows.start, rows.stop, step):
        tile, inside = row // tile_rows, row % tile_rows
        at = row - rows.start + base
        for view in range(VIEWS):
            place = owner_ref[view, tile]
            lanes = pl.ds(view * columns, columns)
            values = march(
                lambda z, c: sheared[z, pl.ds(c * height + at, step), lanes], depth_cells, view
            )
            for c in range(0, 4, share):
                value = values[c] if share == 1 else jnp.concatenate(values[c : c + share])
                at_rows = pl.ds(c * tile_rows + inside, PACKED_ROWS)
                out_ref[place, view, at_rows] = encode(value)


def zero_outside(smooth, depth_index, n_depth, layers):
    @pl.when(depth_index == 0)
    def _():
        smooth[0] = jnp.zeros_like(smooth[0])

    @pl.when(depth_index == n_depth - 1)
    def _():
        smooth[layers - 1] = jnp.zeros_like(smooth[layers - 1])


def render_inner(live_slices, slopes, palette, owner, density, deep_odd, deep_even, n_depth):
    depth_cells, row_cells, columns = density.shape
    total_depth = depth_cells * n_depth
    extinct = 3.0 / total_depth
    tile_rows = row_cells // n_depth
    layers = depth_cells + 2
    rows = range(EDGE, row_cells - EDGE)
    height = len(rows)
    lead, span = EDGE - ROW_TILE, height + 2 * ROW_TILE

    def kernel(
        live_ref, slopes_ref, palette_ref, owner_ref, own_ref, odd_ref, even_ref,
        out_ref, deep, shear_ref, triple, smooth, across, sheared,
    ):
        depth_index = lax.axis_index("gz")
        row_index = lax.axis_index("xy")
        odd_depth = depth_index % 2 == 1

        low, high, word = [], [], 0
        for start in range(0, row_cells, ROW_TILE):
            while len(low) < HALO:
                even = [even_ref[word + k] for k in range(WORDS)]
                odd = [odd_ref[word + k] for k in range(WORDS)]
                low += unpack([jnp.where(odd_depth, e, o) for e, o in zip(even, odd)])
                high += unpack([jnp.where(odd_depth, o, e) for e, o in zip(even, odd)])
                word += WORDS
            own = [own_ref[i, pl.ds(start, ROW_TILE)] for i in range(depth_cells)]
            for z, total in enumerate(window_sums(low[:HALO] + own + high[:HALO], TAPS)):
                deep[z, pl.ds(start, ROW_TILE)] = total
            low, high = low[HALO:], high[HALO:]

        slab_start = (depth_index * depth_cells).astype(jnp.float32)
        for z in range(depth_cells):
            shear_ref[z] = shear_matrices(slopes_ref, slab_start + float(z), columns, total_depth)

        weights = column_weights(columns)
        for z in range(layers):
            triple[...] = (
                deep[z, pl.ds(lead - 4, span + ROW_TILE)]
                + deep[z, pl.ds(lead - 3, span + ROW_TILE)]
                + deep[z, pl.ds(lead - 2, span + ROW_TILE)]
            )
            total = triple[pl.ds(0, span)] + triple[pl.ds(3, span)] + triple[pl.ds(6, span)]
            if 1 <= z <= depth_cells:
                both = column_sums(total, weights)
                smooth[z] = both[:, :columns]
                across[z - 1] = both[ROW_TILE : ROW_TILE + height, columns:]
            else:
                smooth[z] = column_sums(total, weights[:, :columns])
        zero_outside(smooth, depth_index, n_depth, layers)

        own_live = live_ref[depth_index, row_index]
        middle = pl.ds(ROW_TILE, height)
        for z in range(depth_cells):
            channels = shade(
                smooth[z + 1, middle],
                smooth[z + 2, middle] - smooth[z, middle],
                smooth[z + 1, pl.ds(ROW_TILE + 1, height)]
                - smooth[z + 1, pl.ds(ROW_TILE - 1, height)],
                across[z],
                z < own_live,
                palette_ref,
                extinct,
            )
            sheared[z] = jnp.dot(
                jnp.concatenate(channels), shear_ref[z], preferred_element_type=jnp.float32
            )
        march_rows(sheared, out_ref, owner_ref, rows, 0, height, depth_cells, tile_rows, columns)

    smem = pl.BlockSpec(memory_space=pltpu.SMEM)
    vmem = pl.BlockSpec(memory_space=pltpu.VMEM)
    return pl.pallas_call(
        kernel,
        out_shape=(
            jax.ShapeDtypeStruct((n_depth, VIEWS, 4 * tile_rows, columns), jnp.int16),
            jax.ShapeDtypeStruct((layers, row_cells, columns), jnp.float32),
            jax.ShapeDtypeStruct((depth_cells, columns, VIEWS * columns), jnp.bfloat16),
        ),
        in_specs=[smem] * 4 + [vmem] * 3,
        out_specs=(vmem,) * 3,
        scratch_shapes=[
            pltpu.VMEM((span + ROW_TILE, columns), jnp.float32),
            pltpu.VMEM((layers, span, columns), jnp.float32),
            pltpu.VMEM((depth_cells, height, columns), jnp.float32),
            pltpu.VMEM((depth_cells, 4 * height, VIEWS * columns), jnp.float32),
        ],
        compiler_params=pltpu.CompilerParams(vmem_limit_bytes=VMEM_BYTES),
        cost_estimate=pl.CostEstimate(
            flops=100 * depth_cells * row_cells * columns,
            bytes_accessed=16 * 4 * depth_cells * row_cells * columns,
            transcendentals=4 * depth_cells * row_cells * columns,
        ),
        name="render_inner",
    )(live_slices, slopes, palette, owner, density, deep_odd, deep_even)


def render_edges(
    live_slices, palette, owner, inner, deep, shear, corner_odd, corner_even, rlo, rhi, n_depth
):
    layers, row_cells, columns = deep.shape
    depth_cells = layers - 2
    n_rows = lax.axis_size("xy")
    extinct = 3.0 / (depth_cells * n_depth)
    tile_rows = row_cells // n_depth
    band = EDGE + 2 * ROW_TILE
    height = 2 * EDGE

    def kernel(
        live_ref, palette_ref, owner_ref, inner_ref, deep_ref, shear_ref,
        corner_odd_ref, corner_even_ref, rlo_ref, rhi_ref,
        out_ref, halo, triple, split_sums, smooth, across, sheared,
    ):
        depth_index = lax.axis_index("gz")
        row_index = lax.axis_index("xy")
        odd_depth = depth_index % 2 == 1

        for side, mid_ref in ((0, rlo_ref), (1, rhi_ref)):
            at = pl.ds(side * ROW_TILE, ROW_TILE)
            even = [corner_even_ref[i, at] for i in range(HALO)]
            odd = [corner_odd_ref[i, at] for i in range(HALO)]
            low = [jnp.where(odd_depth, e, o) for e, o in zip(even, odd)]
            high = [jnp.where(odd_depth, o, e) for e, o in zip(even, odd)]
            outer = 0 if side == 0 else band - ROW_TILE
            inner_at = ROW_TILE if side == 0 else 0
            own_at = 0 if side == 0 else row_cells - (band - ROW_TILE)
            sums = window_sums(low + [mid_ref[i] for i in range(depth_cells)] + high, TAPS)
            for z in range(layers):
                halo[z, side, pl.ds(outer, ROW_TILE)] = sums[z]
                halo[z, side, pl.ds(inner_at, band - ROW_TILE)] = deep_ref[
                    z, pl.ds(own_at, band - ROW_TILE)
                ]

        span = band - ROW_TILE
        for z in range(layers):
            for side in range(2):
                triple[pl.ds(0, span)] = (
                    halo[z, side, pl.ds(3, span)]
                    + halo[z, side, pl.ds(4, span)]
                    + halo[z, side, pl.ds(5, span)]
                )
                split_sums[z, side] = (
                    triple[pl.ds(0, band)] + triple[pl.ds(3, band)] + triple[pl.ds(6, band)]
                )
        both = column_sums(
            split_sums[...].reshape(layers * 2 * band, columns), column_weights(columns)
        ).reshape(layers, 2, band, 2 * columns)
        smooth[...] = both[..., :columns]
        across[...] = both[1:-1, :, :, columns:]

        @pl.when(row_index == 0)
        def _():
            smooth[:, 0, :1] = jnp.zeros((layers, 1, columns), jnp.float32)

        @pl.when(row_index == n_rows - 1)
        def _():
            smooth[:, 1, EDGE + 1 : EDGE + 2] = jnp.zeros((layers, 1, columns), jnp.float32)

        zero_outside(smooth, depth_index, n_depth, layers)

        own_live = live_ref[depth_index, row_index]
        middle = pl.ds(1, EDGE)
        for z in range(depth_cells):
            sides = [
                shade(
                    smooth[z + 1, side, middle],
                    smooth[z + 2, side, middle] - smooth[z, side, middle],
                    smooth[z + 1, side, pl.ds(2, EDGE)] - smooth[z + 1, side, pl.ds(0, EDGE)],
                    across[z, side, middle],
                    z < own_live,
                    palette_ref,
                    extinct,
                )
                for side in range(2)
            ]
            rgba = jnp.concatenate([side[c] for c in range(4) for side in sides])
            sheared[z] = jnp.dot(rgba, shear_ref[z], preferred_element_type=jnp.float32)
        out_ref[...] = inner_ref[...]
        for side, rows in enumerate((range(EDGE), range(row_cells - EDGE, row_cells))):
            march_rows(
                sheared, out_ref, owner_ref, rows, side * EDGE, height,
                depth_cells, tile_rows, columns,
            )

    smem = pl.BlockSpec(memory_space=pltpu.SMEM)
    vmem = pl.BlockSpec(memory_space=pltpu.VMEM)
    return pl.pallas_call(
        kernel,
        out_shape=jax.ShapeDtypeStruct(inner.shape, inner.dtype),
        in_specs=[smem] * 3 + [vmem] * 7,
        out_specs=vmem,
        scratch_shapes=[
            pltpu.VMEM((layers, 2, band, columns), jnp.float32),
            pltpu.VMEM((band + ROW_TILE, columns), jnp.float32),
            pltpu.VMEM((layers, 2, band, columns), jnp.float32),
            pltpu.VMEM((layers, 2, band, columns), jnp.float32),
            pltpu.VMEM((depth_cells, 2, band, columns), jnp.float32),
            pltpu.VMEM((depth_cells, 4 * height, VIEWS * columns), jnp.float32),
        ],
        compiler_params=pltpu.CompilerParams(vmem_limit_bytes=VMEM_BYTES),
        name="render_edges",
    )(live_slices, palette, owner, inner, deep, shear, corner_odd, corner_even, rlo, rhi)


def cut_edges(density):
    depth_cells, row_cells, columns = density.shape

    places = [(i, start) for start in range(0, row_cells, ROW_TILE) for i in range(HALO)]
    words = len(places) // GROUP * WORDS

    def kernel(density_ref, row_even_ref, row_odd_ref, deep_even_ref, deep_odd_ref):
        row_bit = lax.axis_index("xy") % 2
        depth_bit = lax.axis_index("gz") % 2
        last_rows, last_deep = row_cells - ROW_TILE, depth_cells - HALO
        for ref, bit in ((deep_odd_ref, depth_bit), (deep_even_ref, 1 - depth_bit)):
            for group in range(len(places) // GROUP):
                values = [
                    density_ref[bit * last_deep + i, pl.ds(start, ROW_TILE)]
                    for i, start in places[group * GROUP : (group + 1) * GROUP]
                ]
                for k, word in enumerate(pack(values)):
                    ref[group * WORDS + k] = word
        for ref, bit in ((row_even_ref, 1 - row_bit), (row_odd_ref, row_bit)):
            start = pl.multiple_of(bit * last_rows, ROW_TILE)
            ref[...] = density_ref[:, pl.ds(start, ROW_TILE)]

    rows = jax.ShapeDtypeStruct((depth_cells, ROW_TILE, columns), jnp.float32)
    deep = jax.ShapeDtypeStruct((words, ROW_TILE, columns), jnp.int32)
    vmem = pl.BlockSpec(memory_space=pltpu.VMEM)
    return pl.pallas_call(
        kernel,
        out_shape=(rows, rows, deep, deep),
        in_specs=[vmem],
        out_specs=(vmem,) * 4,
        compiler_params=pltpu.CompilerParams(vmem_limit_bytes=VMEM_BYTES),
        name="cut_edges",
    )(density)


def composite_kernel(order_ref, in_ref, out_ref):
    count = in_ref.shape[0]
    rows = in_ref.shape[2] // 4
    for view in range(VIEWS):
        colour, transmit = None, None
        for k in range(count):
            source = order_ref[view, k]
            values = decode(in_ref[source, view])
            part = [values[c * rows : (c + 1) * rows] for c in range(4)]
            clear = 1.0 - part[3]
            if k == 0:
                colour, transmit = part[:3], clear
            else:
                colour = [colour[c] + transmit * part[c] for c in range(3)]
                transmit = transmit * clear
        for c, value in enumerate(colour + [1.0 - transmit]):
            out_ref[view, c, 0] = value


def body(density, live_slices, shear_slopes, palette, depth_order, tile_owner):
    depth_cells, row_cells, columns = density.shape
    n_depth = lax.axis_size("gz")
    edge = depth_cells - HALO
    odd_depth = lax.axis_index("gz") % 2 == 1
    odd_row = lax.axis_index("xy") % 2 == 1

    def pairs(axis, first):
        count = lax.axis_size(axis)
        lower = range(first, count - 1, 2)
        return [(i, i + 1) for i in lower] + [(i + 1, i) for i in lower]

    row_even, row_odd, deep_even, deep_odd = cut_edges(density)
    row_even = lax.ppermute(row_even, "xy", pairs("xy", 0))
    row_odd = lax.ppermute(row_odd, "xy", pairs("xy", 1))
    deep_odd = lax.ppermute(deep_odd, "gz", pairs("gz", 1))
    deep_even = lax.ppermute(deep_even, "gz", pairs("gz", 0))
    rlo = jnp.where(odd_row, row_even, row_odd)
    rhi = jnp.where(odd_row, row_odd, row_even)
    low_corner = jnp.concatenate([rlo[:HALO], rhi[:HALO]], axis=1)
    high_corner = jnp.concatenate([rlo[edge:], rhi[edge:]], axis=1)
    corner_odd = lax.ppermute(
        jnp.where(odd_depth, high_corner, low_corner), "gz", pairs("gz", 1)
    )
    corner_even = lax.ppermute(
        jnp.where(odd_depth, low_corner, high_corner), "gz", pairs("gz", 0)
    )
    inner, deep, shear = render_inner(
        live_slices, shear_slopes, palette, tile_owner, density, deep_odd, deep_even, n_depth
    )
    outgoing = render_edges(
        live_slices, palette, tile_owner, inner, deep, shear,
        corner_odd, corner_even, rlo, rhi, n_depth,
    )
    incoming = lax.all_to_all(outgoing, "gz", split_axis=0, concat_axis=0, tiled=True)
    tile_rows = row_cells // n_depth
    return pl.pallas_call(
        composite_kernel,
        out_shape=jax.ShapeDtypeStruct((VIEWS, 4, 1, tile_rows, columns), jnp.float32),
        in_specs=[pl.BlockSpec(memory_space=pltpu.SMEM), pl.BlockSpec(memory_space=pltpu.VMEM)],
        out_specs=pl.BlockSpec(memory_space=pltpu.VMEM),
        compiler_params=pltpu.CompilerParams(vmem_limit_bytes=VMEM_BYTES),
        name="composite",
    )(depth_order, incoming)


def solution(mesh):
    placed = (P("gz", "xy", None), P(), P(), P(), P(), P())
    return jax.shard_map(
        body, mesh=mesh, in_specs=placed, out_specs=P(None, None, "gz", "xy", None), check_vma=False
    )
```

```python
import math

import jax
import jax.numpy as jnp
from jax import lax
from jax.experimental import pallas as pl
from jax.experimental.pallas import tpu as pltpu
from jax.sharding import PartitionSpec as P

LIGHT = (0.48, 0.6, 0.64)
REACH = 4
HALO = REACH + 1
TAPS = 2 * REACH + 1
ROW_TILE = 8
PACKED_ROWS = 16
EDGE = 16
VIEWS = 2
TOP = 2.2
STEPS = 65535.0
MIDDLE = 32768
LEVELS_PER_UNIT = 5461.0
ZERO_LEVEL = 1 << 19
GROUP, WORDS = 8, 5
VMEM_BYTES = 40 * 1024 * 1024


def column_matrix(columns):
    source = lax.broadcasted_iota(jnp.int32, (columns, columns), 0)
    target = lax.broadcasted_iota(jnp.int32, (columns, columns), 1)

    def band(shift):
        at = target + shift
        inside = (jnp.abs(source - at) <= REACH) & (at >= 0) & (at < columns)
        return jnp.where(inside, 1.0, 0.0).astype(jnp.float32)

    return jnp.concatenate([band(0), band(1) - band(-1)], axis=1).astype(jnp.bfloat16)


def shear_matrices(slopes_ref, slice_depth, columns, total_depth):
    source = lax.broadcasted_iota(jnp.int32, (columns, columns), 0)
    target = lax.broadcasted_iota(jnp.int32, (columns, columns), 1)
    distance = (source - target).astype(jnp.float32)
    parts = []
    for view in range(VIEWS):
        shift = slopes_ref[view] * (slice_depth + 0.5 - 0.5 * total_depth)
        parts.append(jnp.maximum(0.0, 1.0 - jnp.abs(distance + shift)))
    return jnp.concatenate(parts, axis=1).astype(jnp.bfloat16)


def window_sums(layers, taps):
    sums, width = layers, 1
    while 2 * width < taps:
        sums = [sums[i] + sums[i + width] for i in range(len(sums) - width)]
        width *= 2
    return [sums[i] + layers[i + width] for i in range(len(layers) - width)]


def pack(values):
    v = [(x * LEVELS_PER_UNIT + (ZERO_LEVEL + 0.5)).astype(jnp.int32) for x in values]
    v = [(x - ZERO_LEVEL) & 0xFFFFF for x in v]
    upper = [
        v[5] & 0xFFF,
        (v[5] >> 12) | ((v[6] & 0xF) << 8),
        (v[6] >> 4) & 0xFFF,
        (v[6] >> 16) | ((v[7] & 0xFF) << 4),
        v[7] >> 8,
    ]
    return [v[i] | (upper[i] << 20) for i in range(WORDS)]


def unpack(words):
    upper = [lax.shift_right_logical(w, jnp.full_like(w, 20)) for w in words]
    levels = words + [
        upper[0] | ((upper[1] & 0xFF) << 12),
        (upper[1] >> 8) | (upper[2] << 4) | ((upper[3] & 0xF) << 16),
        (upper[3] >> 4) | (upper[4] << 8),
    ]
    levels = [(x << 12) >> 12 for x in levels]
    return [x.astype(jnp.float32) * (1.0 / LEVELS_PER_UNIT) for x in levels]


def encode(value):
    scale = math.log2(STEPS) - 0.125 * math.log2(TOP)
    root = jnp.exp2(0.125 * jnp.log2(jnp.maximum(value, 1e-30)) + scale)
    return ((root + 0.5).astype(jnp.int32) - MIDDLE).astype(jnp.int16)


def decode(code):
    root = (code.astype(jnp.int32) + MIDDLE).astype(jnp.float32) * (TOP**0.125 / STEPS)
    square = root * root
    fourth = square * square
    return fourth * fourth


def column_sums(total, weights):
    hi = total.astype(jnp.bfloat16)
    rest = total - hi.astype(jnp.float32)
    mid = rest.astype(jnp.bfloat16)
    lo = (rest - mid.astype(jnp.float32)).astype(jnp.bfloat16)
    split = jnp.concatenate([hi, mid, lo], axis=1)
    return jnp.dot(split, weights, preferred_element_type=jnp.float32)


def shade(center, diff_depth, diff_rows, diff_cols, live, palette_ref, extinct):
    cells = TAPS**3
    floor = 0.01 * (2.0 * cells) ** 2
    square = diff_depth * diff_depth + diff_rows * diff_rows + diff_cols * diff_cols + floor
    light = [0.75 * part for part in LIGHT]
    toward = light[0] * diff_depth + light[1] * diff_rows + light[2] * diff_cols
    facing = jnp.maximum(0.0, toward) * lax.rsqrt(square)
    t = center * (2.0 * math.log2(math.e) / cells)
    softplus = jnp.maximum(t, 0.0) + jnp.log2(1.0 + jnp.exp2(-jnp.abs(t)))
    opacity = 1.0 - jnp.exp2(jnp.where(live, -extinct, 0.0) * softplus)
    bright = opacity * (0.25 + facing)
    channels = [bright * palette_ref[c] for c in range(3)] + [opacity]
    return [channel.astype(jnp.bfloat16) for channel in channels]


def march(layer, depth_cells, view):
    colour, transmit = None, None
    for z in range(depth_cells):
        part = [layer(z, c) for c in range(4)]
        clear = 1.0 - part[3]
        if z == 0:
            colour, transmit = part[:3], clear
        elif view == 0:
            colour = [colour[c] + transmit * part[c] for c in range(3)]
            transmit = transmit * clear
        else:
            colour = [part[c] + clear * colour[c] for c in range(3)]
            transmit = transmit * clear
    return colour + [1.0 - transmit]


def march_rows(sheared, out_ref, owner_ref, rows, base, height, depth_cells, tile_rows, columns):
    step = min(tile_rows, PACKED_ROWS)
    share = PACKED_ROWS // step
    for row in range(rows.start, rows.stop, step):
        tile, inside = row // tile_rows, row % tile_rows
        at = row - rows.start + base
        for view in range(VIEWS):
            place = owner_ref[view, tile]
            lanes = pl.ds(view * columns, columns)
            values = march(
                lambda z, c: sheared[z, pl.ds(c * height + at, step), lanes], depth_cells, view
            )
            for c in range(0, 4, share):
                value = values[c] if share == 1 else jnp.concatenate(values[c : c + share])
                at_rows = pl.ds(c * tile_rows + inside, PACKED_ROWS)
                out_ref[place, view, at_rows] = encode(value)


def zero_outside(smooth, depth_index, n_depth, layers):
    @pl.when(depth_index == 0)
    def _():
        smooth[0] = jnp.zeros_like(smooth[0])

    @pl.when(depth_index == n_depth - 1)
    def _():
        smooth[layers - 1] = jnp.zeros_like(smooth[layers - 1])


def render_inner(live_slices, slopes, palette, owner, density, deep_odd, deep_even, n_depth):
    depth_cells, row_cells, columns = density.shape
    total_depth = depth_cells * n_depth
    extinct = 3.0 / total_depth
    tile_rows = row_cells // n_depth
    layers = depth_cells + 2
    rows = range(EDGE, row_cells - EDGE)
    height = len(rows)
    lead, span = EDGE - ROW_TILE, height + 2 * ROW_TILE

    def kernel(
        live_ref, slopes_ref, palette_ref, owner_ref, own_ref, odd_ref, even_ref,
        out_ref, deep, shear_ref, band_ref, triple, smooth, across, sheared,
    ):
        depth_index = lax.axis_index("gz")
        row_index = lax.axis_index("xy")
        odd_depth = depth_index % 2 == 1

        low, high, word = [], [], 0
        for start in range(0, row_cells, ROW_TILE):
            while len(low) < HALO:
                even = [even_ref[word + k] for k in range(WORDS)]
                odd = [odd_ref[word + k] for k in range(WORDS)]
                low += unpack([jnp.where(odd_depth, e, o) for e, o in zip(even, odd)])
                high += unpack([jnp.where(odd_depth, o, e) for e, o in zip(even, odd)])
                word += WORDS
            own = [own_ref[i, pl.ds(start, ROW_TILE)] for i in range(depth_cells)]
            for z, total in enumerate(window_sums(low[:HALO] + own + high[:HALO], TAPS)):
                deep[z, pl.ds(start, ROW_TILE)] = total
            low, high = low[HALO:], high[HALO:]

        slab_start = (depth_index * depth_cells).astype(jnp.float32)
        for z in range(depth_cells):
            shear_ref[z] = shear_matrices(slopes_ref, slab_start + float(z), columns, total_depth)

        band = column_matrix(columns)
        band_ref[...] = band
        weights = jnp.concatenate([band, band, band], axis=0)
        for z in range(layers):
            triple[z] = (
                deep[z, pl.ds(lead - 4, span + ROW_TILE)]
                + deep[z, pl.ds(lead - 3, span + ROW_TILE)]
                + deep[z, pl.ds(lead - 2, span + ROW_TILE)]
            )
            total = (
                triple[z, pl.ds(0, span)] + triple[z, pl.ds(3, span)] + triple[z, pl.ds(6, span)]
            )
            if 1 <= z <= depth_cells:
                both = column_sums(total, weights)
                smooth[z] = both[:, :columns]
                across[z - 1] = both[ROW_TILE : ROW_TILE + height, columns:]
            else:
                smooth[z] = column_sums(total, weights[:, :columns])
        zero_outside(smooth, depth_index, n_depth, layers)

        own_live = live_ref[depth_index, row_index]
        middle = pl.ds(ROW_TILE, height)
        for z in range(depth_cells):
            channels = shade(
                smooth[z + 1, middle],
                smooth[z + 2, middle] - smooth[z, middle],
                smooth[z + 1, pl.ds(ROW_TILE + 1, height)]
                - smooth[z + 1, pl.ds(ROW_TILE - 1, height)],
                across[z],
                z < own_live,
                palette_ref,
                extinct,
            )
            sheared[z] = jnp.dot(
                jnp.concatenate(channels), shear_ref[z], preferred_element_type=jnp.float32
            )
        march_rows(sheared, out_ref, owner_ref, rows, 0, height, depth_cells, tile_rows, columns)

    smem = pl.BlockSpec(memory_space=pltpu.SMEM)
    vmem = pl.BlockSpec(memory_space=pltpu.VMEM)
    return pl.pallas_call(
        kernel,
        out_shape=(
            jax.ShapeDtypeStruct((n_depth, VIEWS, 4 * tile_rows, columns), jnp.int16),
            jax.ShapeDtypeStruct((layers, row_cells, columns), jnp.float32),
            jax.ShapeDtypeStruct((depth_cells, columns, VIEWS * columns), jnp.bfloat16),
            jax.ShapeDtypeStruct((columns, 2 * columns), jnp.bfloat16),
        ),
        in_specs=[smem] * 4 + [vmem] * 3,
        out_specs=(vmem,) * 4,
        scratch_shapes=[
            pltpu.VMEM((layers, span + ROW_TILE, columns), jnp.float32),
            pltpu.VMEM((layers, span, columns), jnp.float32),
            pltpu.VMEM((depth_cells, height, columns), jnp.float32),
            pltpu.VMEM((depth_cells, 4 * height, VIEWS * columns), jnp.float32),
        ],
        compiler_params=pltpu.CompilerParams(vmem_limit_bytes=VMEM_BYTES),
        cost_estimate=pl.CostEstimate(
            flops=100 * depth_cells * row_cells * columns,
            bytes_accessed=16 * 4 * depth_cells * row_cells * columns,
            transcendentals=4 * depth_cells * row_cells * columns,
        ),
        name="render_inner",
    )(live_slices, slopes, palette, owner, density, deep_odd, deep_even)


def render_edges(
    live_slices, palette, owner, inner, deep, shear, band_weights,
    corner_odd, corner_even, rlo, rhi, n_depth,
):
    layers, row_cells, columns = deep.shape
    depth_cells = layers - 2
    n_rows = lax.axis_size("xy")
    extinct = 3.0 / (depth_cells * n_depth)
    tile_rows = row_cells // n_depth
    band = EDGE + 2 * ROW_TILE
    height = 2 * EDGE

    def kernel(
        live_ref, palette_ref, owner_ref, inner_ref, deep_ref, shear_ref, band_ref,
        corner_odd_ref, corner_even_ref, rlo_ref, rhi_ref,
        out_ref, halo, triple, split_sums, smooth, across, sheared,
    ):
        depth_index = lax.axis_index("gz")
        row_index = lax.axis_index("xy")
        odd_depth = depth_index % 2 == 1

        for side, mid_ref in ((0, rlo_ref), (1, rhi_ref)):
            at = pl.ds(side * ROW_TILE, ROW_TILE)
            even = [corner_even_ref[i, at] for i in range(HALO)]
            odd = [corner_odd_ref[i, at] for i in range(HALO)]
            low = [jnp.where(odd_depth, e, o) for e, o in zip(even, odd)]
            high = [jnp.where(odd_depth, o, e) for e, o in zip(even, odd)]
            outer = 0 if side == 0 else band - ROW_TILE
            inner_at = ROW_TILE if side == 0 else 0
            own_at = 0 if side == 0 else row_cells - (band - ROW_TILE)
            sums = window_sums(low + [mid_ref[i] for i in range(depth_cells)] + high, TAPS)
            for z in range(layers):
                halo[z, side, pl.ds(outer, ROW_TILE)] = sums[z]
                halo[z, side, pl.ds(inner_at, band - ROW_TILE)] = deep_ref[
                    z, pl.ds(own_at, band - ROW_TILE)
                ]

        span = band - ROW_TILE
        for z in range(layers):
            for side in range(2):
                triple[z, side, pl.ds(0, span)] = (
                    halo[z, side, pl.ds(3, span)]
                    + halo[z, side, pl.ds(4, span)]
                    + halo[z, side, pl.ds(5, span)]
                )
                split_sums[z, side] = (
                    triple[z, side, pl.ds(0, band)]
                    + triple[z, side, pl.ds(3, band)]
                    + triple[z, side, pl.ds(6, band)]
                )
        weights = jnp.concatenate([band_ref[...]] * 3, axis=0)
        both = column_sums(split_sums[...].reshape(layers * 2 * band, columns), weights)
        both = both.reshape(layers, 2, band, 2 * columns)
        smooth[...] = both[..., :columns]
        across[...] = both[1:-1, :, :, columns:]

        @pl.when(row_index == 0)
        def _():
            smooth[:, 0, :1] = jnp.zeros((layers, 1, columns), jnp.float32)

        @pl.when(row_index == n_rows - 1)
        def _():
            smooth[:, 1, EDGE + 1 : EDGE + 2] = jnp.zeros((layers, 1, columns), jnp.float32)

        zero_outside(smooth, depth_index, n_depth, layers)

        own_live = live_ref[depth_index, row_index]
        middle = pl.ds(1, EDGE)
        for z in range(depth_cells):
            sides = [
                shade(
                    smooth[z + 1, side, middle],
                    smooth[z + 2, side, middle] - smooth[z, side, middle],
                    smooth[z + 1, side, pl.ds(2, EDGE)] - smooth[z + 1, side, pl.ds(0, EDGE)],
                    across[z, side, middle],
                    z < own_live,
                    palette_ref,
                    extinct,
                )
                for side in range(2)
            ]
            rgba = jnp.concatenate([side[c] for c in range(4) for side in sides])
            sheared[z] = jnp.dot(rgba, shear_ref[z], preferred_element_type=jnp.float32)
        out_ref[...] = inner_ref[...]
        for side, rows in enumerate((range(EDGE), range(row_cells - EDGE, row_cells))):
            march_rows(
                sheared, out_ref, owner_ref, rows, side * EDGE, height,
                depth_cells, tile_rows, columns,
            )

    smem = pl.BlockSpec(memory_space=pltpu.SMEM)
    vmem = pl.BlockSpec(memory_space=pltpu.VMEM)
    return pl.pallas_call(
        kernel,
        out_shape=jax.ShapeDtypeStruct(inner.shape, inner.dtype),
        in_specs=[smem] * 3 + [vmem] * 8,
        out_specs=vmem,
        scratch_shapes=[
            pltpu.VMEM((layers, 2, band, columns), jnp.float32),
            pltpu.VMEM((layers, 2, band + ROW_TILE, columns), jnp.float32),
            pltpu.VMEM((layers, 2, band, columns), jnp.float32),
            pltpu.VMEM((layers, 2, band, columns), jnp.float32),
            pltpu.VMEM((depth_cells, 2, band, columns), jnp.float32),
            pltpu.VMEM((depth_cells, 4 * height, VIEWS * columns), jnp.float32),
        ],
        compiler_params=pltpu.CompilerParams(vmem_limit_bytes=VMEM_BYTES),
        name="render_edges",
    )(
        live_slices, palette, owner, inner, deep, shear, band_weights,
        corner_odd, corner_even, rlo, rhi,
    )


def cut_edges(density):
    depth_cells, row_cells, columns = density.shape

    places = [(i, start) for start in range(0, row_cells, ROW_TILE) for i in range(HALO)]
    words = len(places) // GROUP * WORDS

    def kernel(density_ref, row_even_ref, row_odd_ref, deep_even_ref, deep_odd_ref):
        row_bit = lax.axis_index("xy") % 2
        depth_bit = lax.axis_index("gz") % 2
        last_rows, last_deep = row_cells - ROW_TILE, depth_cells - HALO
        for ref, bit in ((deep_odd_ref, depth_bit), (deep_even_ref, 1 - depth_bit)):
            for group in range(len(places) // GROUP):
                values = [
                    density_ref[bit * last_deep + i, pl.ds(start, ROW_TILE)]
                    for i, start in places[group * GROUP : (group + 1) * GROUP]
                ]
                for k, word in enumerate(pack(values)):
                    ref[group * WORDS + k] = word
        for ref, bit in ((row_even_ref, 1 - row_bit), (row_odd_ref, row_bit)):
            start = pl.multiple_of(bit * last_rows, ROW_TILE)
            ref[...] = density_ref[:, pl.ds(start, ROW_TILE)]

    rows = jax.ShapeDtypeStruct((depth_cells, ROW_TILE, columns), jnp.float32)
    deep = jax.ShapeDtypeStruct((words, ROW_TILE, columns), jnp.int32)
    vmem = pl.BlockSpec(memory_space=pltpu.VMEM)
    return pl.pallas_call(
        kernel,
        out_shape=(rows, rows, deep, deep),
        in_specs=[vmem],
        out_specs=(vmem,) * 4,
        compiler_params=pltpu.CompilerParams(vmem_limit_bytes=VMEM_BYTES),
        name="cut_edges",
    )(density)


def composite_kernel(order_ref, in_ref, out_ref):
    count = in_ref.shape[0]
    rows = in_ref.shape[2] // 4
    for view in range(VIEWS):
        colour, transmit = None, None
        for k in range(count):
            source = order_ref[view, k]
            values = decode(in_ref[source, view])
            part = [values[c * rows : (c + 1) * rows] for c in range(4)]
            clear = 1.0 - part[3]
            if k == 0:
                colour, transmit = part[:3], clear
            else:
                colour = [colour[c] + transmit * part[c] for c in range(3)]
                transmit = transmit * clear
        for c, value in enumerate(colour + [1.0 - transmit]):
            out_ref[view, c, 0] = value


def body(density, live_slices, shear_slopes, palette, depth_order, tile_owner):
    depth_cells, row_cells, columns = density.shape
    n_depth = lax.axis_size("gz")
    edge = depth_cells - HALO
    odd_depth = lax.axis_index("gz") % 2 == 1
    odd_row = lax.axis_index("xy") % 2 == 1

    def pairs(axis, first):
        count = lax.axis_size(axis)
        lower = range(first, count - 1, 2)
        return [(i, i + 1) for i in lower] + [(i + 1, i) for i in lower]

    row_even, row_odd, deep_even, deep_odd = cut_edges(density)
    row_even = lax.ppermute(row_even, "xy", pairs("xy", 0))
    row_odd = lax.ppermute(row_odd, "xy", pairs("xy", 1))
    deep_odd = lax.ppermute(deep_odd, "gz", pairs("gz", 1))
    deep_even = lax.ppermute(deep_even, "gz", pairs("gz", 0))
    rlo = jnp.where(odd_row, row_even, row_odd)
    rhi = jnp.where(odd_row, row_odd, row_even)
    low_corner = jnp.concatenate([rlo[:HALO], rhi[:HALO]], axis=1)
    high_corner = jnp.concatenate([rlo[edge:], rhi[edge:]], axis=1)
    corner_odd = lax.ppermute(
        jnp.where(odd_depth, high_corner, low_corner), "gz", pairs("gz", 1)
    )
    corner_even = lax.ppermute(
        jnp.where(odd_depth, low_corner, high_corner), "gz", pairs("gz", 0)
    )
    inner, deep, shear, band_weights = render_inner(
        live_slices, shear_slopes, palette, tile_owner, density, deep_odd, deep_even, n_depth
    )
    outgoing = render_edges(
        live_slices, palette, tile_owner, inner, deep, shear, band_weights,
        corner_odd, corner_even, rlo, rhi, n_depth,
    )
    incoming = lax.all_to_all(outgoing, "gz", split_axis=0, concat_axis=0, tiled=True)
    tile_rows = row_cells // n_depth
    return pl.pallas_call(
        composite_kernel,
        out_shape=jax.ShapeDtypeStruct((VIEWS, 4, 1, tile_rows, columns), jnp.float32),
        in_specs=[pl.BlockSpec(memory_space=pltpu.SMEM), pl.BlockSpec(memory_space=pltpu.VMEM)],
        out_specs=pl.BlockSpec(memory_space=pltpu.VMEM),
        compiler_params=pltpu.CompilerParams(vmem_limit_bytes=VMEM_BYTES),
        name="composite",
    )(depth_order, incoming)


def solution(mesh):
    placed = (P("gz", "xy", None), P(), P(), P(), P(), P())
    return jax.shard_map(
        body, mesh=mesh, in_specs=placed, out_specs=P(None, None, "gz", "xy", None), check_vma=False
    )
```

```python
import math

import jax
import jax.numpy as jnp
from jax import lax
from jax.experimental import pallas as pl
from jax.experimental.pallas import tpu as pltpu
from jax.sharding import PartitionSpec as P

LIGHT = (0.48, 0.6, 0.64)
REACH = 4
HALO = REACH + 1
TAPS = 2 * REACH + 1
ROW_TILE = 8
PACKED_ROWS = 16
EDGE = 16
VIEWS = 2
TOP = 2.2
STEPS = 65535.0
MIDDLE = 32768
LEVELS_PER_UNIT = 5461.0
ZERO_LEVEL = 1 << 19
GROUP, WORDS = 8, 5
VMEM_BYTES = 40 * 1024 * 1024


def column_matrix(columns):
    source = lax.broadcasted_iota(jnp.int32, (columns, columns), 0)
    target = lax.broadcasted_iota(jnp.int32, (columns, columns), 1)

    def band(shift):
        at = target + shift
        inside = (jnp.abs(source - at) <= REACH) & (at >= 0) & (at < columns)
        return jnp.where(inside, 1.0, 0.0).astype(jnp.float32)

    return jnp.concatenate([band(0), band(1) - band(-1)], axis=1).astype(jnp.bfloat16)


def shear_matrices(slopes_ref, slice_depth, columns, total_depth):
    source = lax.broadcasted_iota(jnp.int32, (columns, columns), 0)
    target = lax.broadcasted_iota(jnp.int32, (columns, columns), 1)
    distance = (source - target).astype(jnp.float32)
    parts = []
    for view in range(VIEWS):
        shift = slopes_ref[view] * (slice_depth + 0.5 - 0.5 * total_depth)
        parts.append(jnp.maximum(0.0, 1.0 - jnp.abs(distance + shift)))
    return jnp.concatenate(parts, axis=1).astype(jnp.bfloat16)


def window_sums(layers, taps):
    sums, width = layers, 1
    while 2 * width < taps:
        sums = [sums[i] + sums[i + width] for i in range(len(sums) - width)]
        width *= 2
    return [sums[i] + layers[i + width] for i in range(len(layers) - width)]


def pack(values):
    v = [(x * LEVELS_PER_UNIT + (ZERO_LEVEL + 0.5)).astype(jnp.int32) for x in values]
    v = [(x - ZERO_LEVEL) & 0xFFFFF for x in v]
    upper = [
        v[5] & 0xFFF,
        (v[5] >> 12) | ((v[6] & 0xF) << 8),
        (v[6] >> 4) & 0xFFF,
        (v[6] >> 16) | ((v[7] & 0xFF) << 4),
        v[7] >> 8,
    ]
    return [v[i] | (upper[i] << 20) for i in range(WORDS)]


def unpack(words):
    upper = [lax.shift_right_logical(w, jnp.full_like(w, 20)) for w in words]
    levels = words + [
        upper[0] | ((upper[1] & 0xFF) << 12),
        (upper[1] >> 8) | (upper[2] << 4) | ((upper[3] & 0xF) << 16),
        (upper[3] >> 4) | (upper[4] << 8),
    ]
    levels = [(x << 12) >> 12 for x in levels]
    return [x.astype(jnp.float32) * (1.0 / LEVELS_PER_UNIT) for x in levels]


def encode(value):
    scale = math.log2(STEPS) - 0.125 * math.log2(TOP)
    root = jnp.exp2(0.125 * jnp.log2(jnp.maximum(value, 1e-30)) + scale)
    return ((root + 0.5).astype(jnp.int32) - MIDDLE).astype(jnp.int16)


def decode(code):
    root = (code.astype(jnp.int32) + MIDDLE).astype(jnp.float32) * (TOP**0.125 / STEPS)
    square = root * root
    fourth = square * square
    return fourth * fourth


def column_sums(total, weights):
    hi = total.astype(jnp.bfloat16)
    rest = total - hi.astype(jnp.float32)
    mid = rest.astype(jnp.bfloat16)
    lo = (rest - mid.astype(jnp.float32)).astype(jnp.bfloat16)
    split = jnp.concatenate([hi, mid, lo], axis=1)
    return jnp.dot(split, weights, preferred_element_type=jnp.float32)


def shade(center, diff_depth, diff_rows, diff_cols, live, palette_ref, extinct):
    cells = TAPS**3
    floor = 0.01 * (2.0 * cells) ** 2
    square = diff_depth * diff_depth + diff_rows * diff_rows + diff_cols * diff_cols + floor
    light = [0.75 * part for part in LIGHT]
    toward = light[0] * diff_depth + light[1] * diff_rows + light[2] * diff_cols
    facing = jnp.maximum(0.0, toward) * lax.rsqrt(square)
    t = center * (2.0 * math.log2(math.e) / cells)
    softplus = jnp.maximum(t, 0.0) + jnp.log2(1.0 + jnp.exp2(-jnp.abs(t)))
    opacity = 1.0 - jnp.exp2(jnp.where(live, -extinct, 0.0) * softplus)
    bright = opacity * (0.25 + facing)
    channels = [bright * palette_ref[c] for c in range(3)] + [opacity]
    return [channel.astype(jnp.bfloat16) for channel in channels]


def march(layer, depth_cells, view):
    colour, transmit = None, None
    for z in range(depth_cells):
        part = [layer(z, c) for c in range(4)]
        clear = 1.0 - part[3]
        if z == 0:
            colour, transmit = part[:3], clear
        elif view == 0:
            colour = [colour[c] + transmit * part[c] for c in range(3)]
            transmit = transmit * clear
        else:
            colour = [part[c] + clear * colour[c] for c in range(3)]
            transmit = transmit * clear
    return colour + [1.0 - transmit]


def march_rows(sheared, out_ref, owner_ref, rows, base, height, depth_cells, tile_rows, columns):
    step = min(tile_rows, PACKED_ROWS)
    share = PACKED_ROWS // step
    for row in range(rows.start, rows.stop, step):
        tile, inside = row // tile_rows, row % tile_rows
        at = row - rows.start + base
        for view in range(VIEWS):
            place = owner_ref[view, tile]
            lanes = pl.ds(view * columns, columns)
            values = march(
                lambda z, c: sheared[z, pl.ds(c * height + at, step), lanes], depth_cells, view
            )
            for c in range(0, 4, share):
                value = values[c] if share == 1 else jnp.concatenate(values[c : c + share])
                at_rows = pl.ds(c * tile_rows + inside, PACKED_ROWS)
                out_ref[place, view, at_rows] = encode(value)


def zero_outside(smooth, depth_index, n_depth, layers):
    @pl.when(depth_index == 0)
    def _():
        smooth[0] = jnp.zeros_like(smooth[0])

    @pl.when(depth_index == n_depth - 1)
    def _():
        smooth[layers - 1] = jnp.zeros_like(smooth[layers - 1])


def render_inner(live_slices, slopes, palette, owner, density, deep_odd, deep_even, n_depth):
    depth_cells, row_cells, columns = density.shape
    total_depth = depth_cells * n_depth
    extinct = 3.0 / total_depth
    tile_rows = row_cells // n_depth
    layers = depth_cells + 2
    rows = range(EDGE, row_cells - EDGE)
    height = len(rows)
    lead, span = EDGE - ROW_TILE, height + 2 * ROW_TILE

    def kernel(
        live_ref, slopes_ref, palette_ref, owner_ref, own_ref, odd_ref, even_ref,
        out_ref, deep, shear_ref, band_ref, triple, smooth, across, sheared,
    ):
        depth_index = lax.axis_index("gz")
        row_index = lax.axis_index("xy")
        odd_depth = depth_index % 2 == 1

        below = jnp.where(depth_index > 0, -1, 0)
        above = jnp.where(depth_index < n_depth - 1, -1, 0)
        low, high, word = [], [], 0
        for start in range(0, row_cells, ROW_TILE):
            while len(low) < HALO:
                even = [even_ref[word + k] for k in range(WORDS)]
                odd = [odd_ref[word + k] for k in range(WORDS)]
                low += unpack([jnp.where(odd_depth, e, o) & below for e, o in zip(even, odd)])
                high += unpack([jnp.where(odd_depth, o, e) & above for e, o in zip(even, odd)])
                word += WORDS
            own = [own_ref[i, pl.ds(start, ROW_TILE)] for i in range(depth_cells)]
            for z, total in enumerate(window_sums(low[:HALO] + own + high[:HALO], TAPS)):
                deep[z, pl.ds(start, ROW_TILE)] = total
            low, high = low[HALO:], high[HALO:]

        slab_start = (depth_index * depth_cells).astype(jnp.float32)
        for z in range(depth_cells):
            shear_ref[z] = shear_matrices(slopes_ref, slab_start + float(z), columns, total_depth)

        band = column_matrix(columns)
        band_ref[...] = band
        weights = jnp.concatenate([band, band, band], axis=0)
        for z in range(layers):
            triple[z] = (
                deep[z, pl.ds(lead - 4, span + ROW_TILE)]
                + deep[z, pl.ds(lead - 3, span + ROW_TILE)]
                + deep[z, pl.ds(lead - 2, span + ROW_TILE)]
            )
            total = (
                triple[z, pl.ds(0, span)] + triple[z, pl.ds(3, span)] + triple[z, pl.ds(6, span)]
            )
            if 1 <= z <= depth_cells:
                both = column_sums(total, weights)
                smooth[z] = both[:, :columns]
                across[z - 1] = both[ROW_TILE : ROW_TILE + height, columns:]
            else:
                smooth[z] = column_sums(total, weights[:, :columns])
        zero_outside(smooth, depth_index, n_depth, layers)

        own_live = live_ref[depth_index, row_index]
        middle = pl.ds(ROW_TILE, height)
        for z in range(depth_cells):
            channels = shade(
                smooth[z + 1, middle],
                smooth[z + 2, middle] - smooth[z, middle],
                smooth[z + 1, pl.ds(ROW_TILE + 1, height)]
                - smooth[z + 1, pl.ds(ROW_TILE - 1, height)],
                across[z],
                z < own_live,
                palette_ref,
                extinct,
            )
            sheared[z] = jnp.dot(
                jnp.concatenate(channels), shear_ref[z], preferred_element_type=jnp.float32
            )
        march_rows(sheared, out_ref, owner_ref, rows, 0, height, depth_cells, tile_rows, columns)

    smem = pl.BlockSpec(memory_space=pltpu.SMEM)
    vmem = pl.BlockSpec(memory_space=pltpu.VMEM)
    return pl.pallas_call(
        kernel,
        out_shape=(
            jax.ShapeDtypeStruct((n_depth, VIEWS, 4 * tile_rows, columns), jnp.int16),
            jax.ShapeDtypeStruct((layers, row_cells, columns), jnp.float32),
            jax.ShapeDtypeStruct((depth_cells, columns, VIEWS * columns), jnp.bfloat16),
            jax.ShapeDtypeStruct((columns, 2 * columns), jnp.bfloat16),
        ),
        in_specs=[smem] * 4 + [vmem] * 3,
        out_specs=(vmem,) * 4,
        scratch_shapes=[
            pltpu.VMEM((layers, span + ROW_TILE, columns), jnp.float32),
            pltpu.VMEM((layers, span, columns), jnp.float32),
            pltpu.VMEM((depth_cells, height, columns), jnp.float32),
            pltpu.VMEM((depth_cells, 4 * height, VIEWS * columns), jnp.float32),
        ],
        compiler_params=pltpu.CompilerParams(vmem_limit_bytes=VMEM_BYTES),
        cost_estimate=pl.CostEstimate(
            flops=100 * depth_cells * row_cells * columns,
            bytes_accessed=16 * 4 * depth_cells * row_cells * columns,
            transcendentals=4 * depth_cells * row_cells * columns,
        ),
        name="render_inner",
    )(live_slices, slopes, palette, owner, density, deep_odd, deep_even)


def render_edges(
    live_slices, palette, owner, inner, deep, shear, band_weights,
    corner_odd, corner_even, rlo, rhi, n_depth,
):
    layers, row_cells, columns = deep.shape
    depth_cells = layers - 2
    n_rows = lax.axis_size("xy")
    extinct = 3.0 / (depth_cells * n_depth)
    tile_rows = row_cells // n_depth
    band = EDGE + 2 * ROW_TILE
    height = 2 * EDGE

    def kernel(
        live_ref, palette_ref, owner_ref, inner_ref, deep_ref, shear_ref, band_ref,
        corner_odd_ref, corner_even_ref, rlo_ref, rhi_ref,
        out_ref, halo, triple, split_sums, smooth, across, sheared,
    ):
        depth_index = lax.axis_index("gz")
        row_index = lax.axis_index("xy")
        odd_depth = depth_index % 2 == 1

        below = jnp.where(depth_index > 0, 1.0, 0.0)
        above = jnp.where(depth_index < n_depth - 1, 1.0, 0.0)
        for side, mid_ref in ((0, rlo_ref), (1, rhi_ref)):
            at = pl.ds(side * ROW_TILE, ROW_TILE)
            even = [corner_even_ref[i, at] for i in range(HALO)]
            odd = [corner_odd_ref[i, at] for i in range(HALO)]
            low = [jnp.where(odd_depth, e, o) * below for e, o in zip(even, odd)]
            high = [jnp.where(odd_depth, o, e) * above for e, o in zip(even, odd)]
            outer = 0 if side == 0 else band - ROW_TILE
            inner_at = ROW_TILE if side == 0 else 0
            own_at = 0 if side == 0 else row_cells - (band - ROW_TILE)
            sums = window_sums(low + [mid_ref[i] for i in range(depth_cells)] + high, TAPS)
            for z in range(layers):
                halo[z, side, pl.ds(outer, ROW_TILE)] = sums[z]
                halo[z, side, pl.ds(inner_at, band - ROW_TILE)] = deep_ref[
                    z, pl.ds(own_at, band - ROW_TILE)
                ]

        span = band - ROW_TILE
        for z in range(layers):
            for side in range(2):
                triple[z, side, pl.ds(0, span)] = (
                    halo[z, side, pl.ds(3, span)]
                    + halo[z, side, pl.ds(4, span)]
                    + halo[z, side, pl.ds(5, span)]
                )
                split_sums[z, side] = (
                    triple[z, side, pl.ds(0, band)]
                    + triple[z, side, pl.ds(3, band)]
                    + triple[z, side, pl.ds(6, band)]
                )
        weights = jnp.concatenate([band_ref[...]] * 3, axis=0)
        both = column_sums(split_sums[...].reshape(layers * 2 * band, columns), weights)
        both = both.reshape(layers, 2, band, 2 * columns)
        smooth[...] = both[..., :columns]
        across[...] = both[1:-1, :, :, columns:]

        @pl.when(row_index == 0)
        def _():
            smooth[:, 0, :1] = jnp.zeros((layers, 1, columns), jnp.float32)

        @pl.when(row_index == n_rows - 1)
        def _():
            smooth[:, 1, EDGE + 1 : EDGE + 2] = jnp.zeros((layers, 1, columns), jnp.float32)

        zero_outside(smooth, depth_index, n_depth, layers)

        own_live = live_ref[depth_index, row_index]
        middle = pl.ds(1, EDGE)
        for z in range(depth_cells):
            sides = [
                shade(
                    smooth[z + 1, side, middle],
                    smooth[z + 2, side, middle] - smooth[z, side, middle],
                    smooth[z + 1, side, pl.ds(2, EDGE)] - smooth[z + 1, side, pl.ds(0, EDGE)],
                    across[z, side, middle],
                    z < own_live,
                    palette_ref,
                    extinct,
                )
                for side in range(2)
            ]
            rgba = jnp.concatenate([side[c] for c in range(4) for side in sides])
            sheared[z] = jnp.dot(rgba, shear_ref[z], preferred_element_type=jnp.float32)
        out_ref[...] = inner_ref[...]
        for side, rows in enumerate((range(EDGE), range(row_cells - EDGE, row_cells))):
            march_rows(
                sheared, out_ref, owner_ref, rows, side * EDGE, height,
                depth_cells, tile_rows, columns,
            )

    smem = pl.BlockSpec(memory_space=pltpu.SMEM)
    vmem = pl.BlockSpec(memory_space=pltpu.VMEM)
    return pl.pallas_call(
        kernel,
        out_shape=jax.ShapeDtypeStruct(inner.shape, inner.dtype),
        in_specs=[smem] * 3 + [vmem] * 8,
        out_specs=vmem,
        scratch_shapes=[
            pltpu.VMEM((layers, 2, band, columns), jnp.float32),
            pltpu.VMEM((layers, 2, band + ROW_TILE, columns), jnp.float32),
            pltpu.VMEM((layers, 2, band, columns), jnp.float32),
            pltpu.VMEM((layers, 2, band, columns), jnp.float32),
            pltpu.VMEM((depth_cells, 2, band, columns), jnp.float32),
            pltpu.VMEM((depth_cells, 4 * height, VIEWS * columns), jnp.float32),
        ],
        compiler_params=pltpu.CompilerParams(vmem_limit_bytes=VMEM_BYTES),
        name="render_edges",
    )(
        live_slices, palette, owner, inner, deep, shear, band_weights,
        corner_odd, corner_even, rlo, rhi,
    )


def cut_edges(density):
    depth_cells, row_cells, columns = density.shape

    places = [(i, start) for start in range(0, row_cells, ROW_TILE) for i in range(HALO)]
    words = len(places) // GROUP * WORDS

    def kernel(density_ref, row_even_ref, row_odd_ref, deep_even_ref, deep_odd_ref):
        row_bit = lax.axis_index("xy") % 2
        depth_bit = lax.axis_index("gz") % 2
        last_rows, last_deep = row_cells - ROW_TILE, depth_cells - HALO
        for ref, bit in ((deep_odd_ref, depth_bit), (deep_even_ref, 1 - depth_bit)):
            for group in range(len(places) // GROUP):
                values = [
                    density_ref[bit * last_deep + i, pl.ds(start, ROW_TILE)]
                    for i, start in places[group * GROUP : (group + 1) * GROUP]
                ]
                for k, word in enumerate(pack(values)):
                    ref[group * WORDS + k] = word
        for ref, bit in ((row_even_ref, 1 - row_bit), (row_odd_ref, row_bit)):
            start = pl.multiple_of(bit * last_rows, ROW_TILE)
            ref[...] = density_ref[:, pl.ds(start, ROW_TILE)]

    rows = jax.ShapeDtypeStruct((depth_cells, ROW_TILE, columns), jnp.float32)
    deep = jax.ShapeDtypeStruct((words, ROW_TILE, columns), jnp.int32)
    vmem = pl.BlockSpec(memory_space=pltpu.VMEM)
    return pl.pallas_call(
        kernel,
        out_shape=(rows, rows, deep, deep),
        in_specs=[vmem],
        out_specs=(vmem,) * 4,
        compiler_params=pltpu.CompilerParams(vmem_limit_bytes=VMEM_BYTES),
        name="cut_edges",
    )(density)


def composite_kernel(order_ref, in_ref, out_ref):
    count = in_ref.shape[0]
    rows = in_ref.shape[2] // 4
    for view in range(VIEWS):
        colour, transmit = None, None
        for k in range(count):
            source = order_ref[view, k]
            values = decode(in_ref[source, view])
            part = [values[c * rows : (c + 1) * rows] for c in range(4)]
            clear = 1.0 - part[3]
            if k == 0:
                colour, transmit = part[:3], clear
            else:
                colour = [colour[c] + transmit * part[c] for c in range(3)]
                transmit = transmit * clear
        for c, value in enumerate(colour + [1.0 - transmit]):
            out_ref[view, c, 0] = value


def body(density, live_slices, shear_slopes, palette, depth_order, tile_owner):
    depth_cells, row_cells, columns = density.shape
    n_depth = lax.axis_size("gz")
    edge = depth_cells - HALO
    odd_depth = lax.axis_index("gz") % 2 == 1
    odd_row = lax.axis_index("xy") % 2 == 1

    def pairs(axis, first):
        count = lax.axis_size(axis)
        lower = range(first, count - 1, 2)
        met = [(i, i + 1) for i in lower] + [(i + 1, i) for i in lower]
        alone = set(range(count)) - {source for source, _ in met}
        return met + [(i, i) for i in sorted(alone)]

    row_even, row_odd, deep_even, deep_odd = cut_edges(density)
    row_even = lax.ppermute(row_even, "xy", pairs("xy", 0))
    row_odd = lax.ppermute(row_odd, "xy", pairs("xy", 1))
    deep_odd = lax.ppermute(deep_odd, "gz", pairs("gz", 1))
    deep_even = lax.ppermute(deep_even, "gz", pairs("gz", 0))
    row_index, n_rows = lax.axis_index("xy"), lax.axis_size("xy")
    rlo = jnp.where(row_index > 0, jnp.where(odd_row, row_even, row_odd), 0.0)
    rhi = jnp.where(row_index < n_rows - 1, jnp.where(odd_row, row_odd, row_even), 0.0)
    low_corner = jnp.concatenate([rlo[:HALO], rhi[:HALO]], axis=1)
    high_corner = jnp.concatenate([rlo[edge:], rhi[edge:]], axis=1)
    corner_odd = lax.ppermute(
        jnp.where(odd_depth, high_corner, low_corner), "gz", pairs("gz", 1)
    )
    corner_even = lax.ppermute(
        jnp.where(odd_depth, low_corner, high_corner), "gz", pairs("gz", 0)
    )
    inner, deep, shear, band_weights = render_inner(
        live_slices, shear_slopes, palette, tile_owner, density, deep_odd, deep_even, n_depth
    )
    outgoing = render_edges(
        live_slices, palette, tile_owner, inner, deep, shear, band_weights,
        corner_odd, corner_even, rlo, rhi, n_depth,
    )
    incoming = lax.all_to_all(outgoing, "gz", split_axis=0, concat_axis=0, tiled=True)
    tile_rows = row_cells // n_depth
    return pl.pallas_call(
        composite_kernel,
        out_shape=jax.ShapeDtypeStruct((VIEWS, 4, 1, tile_rows, columns), jnp.float32),
        in_specs=[pl.BlockSpec(memory_space=pltpu.SMEM), pl.BlockSpec(memory_space=pltpu.VMEM)],
        out_specs=pl.BlockSpec(memory_space=pltpu.VMEM),
        compiler_params=pltpu.CompilerParams(vmem_limit_bytes=VMEM_BYTES),
        name="composite",
    )(depth_order, incoming)


def solution(mesh):
    placed = (P("gz", "xy", None), P(), P(), P(), P(), P())
    return jax.shard_map(
        body, mesh=mesh, in_specs=placed, out_specs=P(None, None, "gz", "xy", None), check_vma=False
    )
```

```python
import math

import jax
import jax.numpy as jnp
from jax import lax
from jax.experimental import pallas as pl
from jax.experimental.pallas import tpu as pltpu
from jax.sharding import PartitionSpec as P

LIGHT = (0.48, 0.6, 0.64)
REACH = 4
HALO = REACH + 1
TAPS = 2 * REACH + 1
ROW_TILE = 8
PACKED_ROWS = 16
EDGE = 8
VIEWS = 2
TOP = 2.2
STEPS = 65535.0
MIDDLE = 32768
LEVELS_PER_UNIT = 5461.0
ZERO_LEVEL = 1 << 19
GROUP, WORDS = 8, 5
VMEM_BYTES = 40 * 1024 * 1024


def column_matrix(columns):
    source = lax.broadcasted_iota(jnp.int32, (columns, columns), 0)
    target = lax.broadcasted_iota(jnp.int32, (columns, columns), 1)

    def band(shift):
        at = target + shift
        inside = (jnp.abs(source - at) <= REACH) & (at >= 0) & (at < columns)
        return jnp.where(inside, 1.0, 0.0).astype(jnp.float32)

    return jnp.concatenate([band(0), band(1) - band(-1)], axis=1).astype(jnp.bfloat16)


def shear_matrices(slopes_ref, slice_depth, columns, total_depth):
    source = lax.broadcasted_iota(jnp.int32, (columns, columns), 0)
    target = lax.broadcasted_iota(jnp.int32, (columns, columns), 1)
    distance = (source - target).astype(jnp.float32)
    parts = []
    for view in range(VIEWS):
        shift = slopes_ref[view] * (slice_depth + 0.5 - 0.5 * total_depth)
        parts.append(jnp.maximum(0.0, 1.0 - jnp.abs(distance + shift)))
    return jnp.concatenate(parts, axis=1).astype(jnp.bfloat16)


def window_sums(layers, taps):
    sums, width = layers, 1
    while 2 * width < taps:
        sums = [sums[i] + sums[i + width] for i in range(len(sums) - width)]
        width *= 2
    return [sums[i] + layers[i + width] for i in range(len(layers) - width)]


def pack(values):
    v = [(x * LEVELS_PER_UNIT + (ZERO_LEVEL + 0.5)).astype(jnp.int32) for x in values]
    v = [(x - ZERO_LEVEL) & 0xFFFFF for x in v]
    upper = [
        v[5] & 0xFFF,
        (v[5] >> 12) | ((v[6] & 0xF) << 8),
        (v[6] >> 4) & 0xFFF,
        (v[6] >> 16) | ((v[7] & 0xFF) << 4),
        v[7] >> 8,
    ]
    return [v[i] | (upper[i] << 20) for i in range(WORDS)]


def unpack(words):
    upper = [lax.shift_right_logical(w, jnp.full_like(w, 20)) for w in words]
    levels = words + [
        upper[0] | ((upper[1] & 0xFF) << 12),
        (upper[1] >> 8) | (upper[2] << 4) | ((upper[3] & 0xF) << 16),
        (upper[3] >> 4) | (upper[4] << 8),
    ]
    levels = [(x << 12) >> 12 for x in levels]
    return [x.astype(jnp.float32) * (1.0 / LEVELS_PER_UNIT) for x in levels]


def encode(value):
    scale = math.log2(STEPS) - 0.125 * math.log2(TOP)
    root = jnp.exp2(0.125 * jnp.log2(jnp.maximum(value, 1e-30)) + scale)
    return (root + 0.5).astype(jnp.int32) - MIDDLE


def decode(code):
    root = (code.astype(jnp.int32) + MIDDLE).astype(jnp.float32) * (TOP**0.125 / STEPS)
    square = root * root
    fourth = square * square
    return fourth * fourth


def column_sums(total, weights):
    hi = total.astype(jnp.bfloat16)
    rest = total - hi.astype(jnp.float32)
    mid = rest.astype(jnp.bfloat16)
    lo = (rest - mid.astype(jnp.float32)).astype(jnp.bfloat16)
    split = jnp.concatenate([hi, mid, lo], axis=1)
    return jnp.dot(split, weights, preferred_element_type=jnp.float32)


def shade(center, diff_depth, diff_rows, diff_cols, live, palette_ref, extinct):
    cells = TAPS**3
    floor = 0.01 * (2.0 * cells) ** 2
    square = diff_depth * diff_depth + diff_rows * diff_rows + diff_cols * diff_cols + floor
    light = [0.75 * part for part in LIGHT]
    toward = light[0] * diff_depth + light[1] * diff_rows + light[2] * diff_cols
    facing = jnp.maximum(0.0, toward) * lax.rsqrt(square)
    t = center * (2.0 * math.log2(math.e) / cells)
    softplus = jnp.maximum(t, 0.0) + jnp.log2(1.0 + jnp.exp2(-jnp.abs(t)))
    opacity = 1.0 - jnp.exp2(jnp.where(live, -extinct, 0.0) * softplus)
    bright = opacity * (0.25 + facing)
    channels = [bright * palette_ref[c] for c in range(3)] + [opacity]
    return [channel.astype(jnp.bfloat16) for channel in channels]


def march(layer, depth_cells, view):
    colour, transmit = None, None
    for z in range(depth_cells):
        part = [layer(z, c) for c in range(4)]
        clear = 1.0 - part[3]
        if z == 0:
            colour, transmit = part[:3], clear
        elif view == 0:
            colour = [colour[c] + transmit * part[c] for c in range(3)]
            transmit = transmit * clear
        else:
            colour = [part[c] + clear * colour[c] for c in range(3)]
            transmit = transmit * clear
    return colour + [1.0 - transmit]


def store_codes(out_ref, place, view, codes, row, tile_rows, other=None):
    if tile_rows < PACKED_ROWS:
        for c in range(0, 4, 2):
            pair = jnp.concatenate(codes[c : c + 2])
            out_ref[place, view, pl.ds(c * tile_rows, PACKED_ROWS)] = pair.astype(jnp.int16)
        return
    for c in range(4):
        at = pl.ds(c * tile_rows + row // PACKED_ROWS * PACKED_ROWS, PACKED_ROWS)
        code = codes[c]
        if code.shape[0] < PACKED_ROWS:
            half = row % PACKED_ROWS
            rest = jnp.zeros_like(code)
            if other is not None:
                rest = other[place, view, at].astype(jnp.int32)
                rest = rest[ROW_TILE:] if half == 0 else rest[:ROW_TILE]
            code = jnp.concatenate([code, rest] if half == 0 else [rest, code])
        out_ref[place, view, at] = code.astype(jnp.int16)


def zero_outside(smooth, depth_index, n_depth, layers):
    @pl.when(depth_index == 0)
    def _():
        smooth[0] = jnp.zeros_like(smooth[0])

    @pl.when(depth_index == n_depth - 1)
    def _():
        smooth[layers - 1] = jnp.zeros_like(smooth[layers - 1])


def render_inner(live_slices, slopes, palette, owner, density, deep_odd, deep_even, n_depth):
    depth_cells, row_cells, columns = density.shape
    total_depth = depth_cells * n_depth
    extinct = 3.0 / total_depth
    tile_rows = row_cells // n_depth
    layers = depth_cells + 2
    rows = range(EDGE, row_cells - EDGE)
    height = len(rows)
    lead, span = EDGE, height + 2 * ROW_TILE

    def kernel(
        live_ref, slopes_ref, palette_ref, owner_ref, own_ref, odd_ref, even_ref,
        out_ref, deep, shear_ref, band_ref, triple, smooth, across, sheared,
    ):
        depth_index = lax.axis_index("gz")
        row_index = lax.axis_index("xy")
        odd_depth = depth_index % 2 == 1

        low, high, word = [], [], 0
        for start in range(0, row_cells, ROW_TILE):
            while len(low) < HALO:
                even = [even_ref[word + k] for k in range(WORDS)]
                odd = [odd_ref[word + k] for k in range(WORDS)]
                low += unpack([jnp.where(odd_depth, e, o) for e, o in zip(even, odd)])
                high += unpack([jnp.where(odd_depth, o, e) for e, o in zip(even, odd)])
                word += WORDS
            own = [own_ref[i, pl.ds(start, ROW_TILE)] for i in range(depth_cells)]
            for z, total in enumerate(window_sums(low[:HALO] + own + high[:HALO], TAPS)):
                deep[z, pl.ds(ROW_TILE + start, ROW_TILE)] = total
            low, high = low[HALO:], high[HALO:]

        slab_start = (depth_index * depth_cells).astype(jnp.float32)
        for z in range(depth_cells):
            shear_ref[z] = shear_matrices(slopes_ref, slab_start + float(z), columns, total_depth)

        band = column_matrix(columns)
        band_ref[...] = band
        weights = jnp.concatenate([band, band, band], axis=0)
        for z in range(layers):
            triple[z] = (
                deep[z, pl.ds(lead - 4, span + ROW_TILE)]
                + deep[z, pl.ds(lead - 3, span + ROW_TILE)]
                + deep[z, pl.ds(lead - 2, span + ROW_TILE)]
            )
            total = (
                triple[z, pl.ds(0, span)] + triple[z, pl.ds(3, span)] + triple[z, pl.ds(6, span)]
            )
            if 1 <= z <= depth_cells:
                both = column_sums(total, weights)
                smooth[z] = both[:, :columns]
                across[z - 1] = both[ROW_TILE : ROW_TILE + height, columns:]
            else:
                smooth[z] = column_sums(total, weights[:, :columns])
        zero_outside(smooth, depth_index, n_depth, layers)

        own_live = live_ref[depth_index, row_index]
        middle = pl.ds(ROW_TILE, height)
        for z in range(depth_cells):
            channels = shade(
                smooth[z + 1, middle],
                smooth[z + 2, middle] - smooth[z, middle],
                smooth[z + 1, pl.ds(ROW_TILE + 1, height)]
                - smooth[z + 1, pl.ds(ROW_TILE - 1, height)],
                across[z],
                z < own_live,
                palette_ref,
                extinct,
            )
            sheared[z] = jnp.dot(
                jnp.concatenate(channels), shear_ref[z], preferred_element_type=jnp.float32
            )
        row = rows.start
        while row < rows.stop:
            whole = tile_rows >= PACKED_ROWS and row % PACKED_ROWS == 0
            count = PACKED_ROWS if whole and row + PACKED_ROWS <= rows.stop else ROW_TILE
            at = row - rows.start
            for view in range(VIEWS):
                lanes = pl.ds(view * columns, columns)
                values = march(
                    lambda z, c: sheared[z, pl.ds(c * height + at, count), lanes],
                    depth_cells,
                    view,
                )
                place = owner_ref[view, row // tile_rows]
                codes = [encode(value) for value in values]
                store_codes(out_ref, place, view, codes, row % tile_rows, tile_rows)
            row += count

    smem = pl.BlockSpec(memory_space=pltpu.SMEM)
    vmem = pl.BlockSpec(memory_space=pltpu.VMEM)
    return pl.pallas_call(
        kernel,
        out_shape=(
            jax.ShapeDtypeStruct((n_depth, VIEWS, 4 * tile_rows, columns), jnp.int16),
            jax.ShapeDtypeStruct((layers, row_cells + 2 * ROW_TILE, columns), jnp.float32),
            jax.ShapeDtypeStruct((depth_cells, columns, VIEWS * columns), jnp.bfloat16),
            jax.ShapeDtypeStruct((columns, 2 * columns), jnp.bfloat16),
        ),
        in_specs=[smem] * 4 + [vmem] * 3,
        out_specs=(vmem,) * 4,
        scratch_shapes=[
            pltpu.VMEM((layers, span + ROW_TILE, columns), jnp.float32),
            pltpu.VMEM((layers, span, columns), jnp.float32),
            pltpu.VMEM((depth_cells, height, columns), jnp.float32),
            pltpu.VMEM((depth_cells, 4 * height, VIEWS * columns), jnp.float32),
        ],
        compiler_params=pltpu.CompilerParams(vmem_limit_bytes=VMEM_BYTES),
        cost_estimate=pl.CostEstimate(
            flops=100 * depth_cells * row_cells * columns,
            bytes_accessed=16 * 4 * depth_cells * row_cells * columns,
            transcendentals=4 * depth_cells * row_cells * columns,
        ),
        name="render_inner",
    )(live_slices, slopes, palette, owner, density, deep_odd, deep_even)


def render_edges(
    live_slices, palette, owner, inner, deep, shear, band_weights,
    corner_odd, corner_even, rlo, rhi, n_depth,
):
    layers, padded_rows, columns = deep.shape
    row_cells = padded_rows - 2 * ROW_TILE
    depth_cells = layers - 2
    n_rows = lax.axis_size("xy")
    extinct = 3.0 / (depth_cells * n_depth)
    tile_rows = row_cells // n_depth
    band = EDGE + 2 * ROW_TILE
    piece = 2 * ROW_TILE
    height = 2 * EDGE

    def kernel(
        live_ref, palette_ref, owner_ref, inner_ref, deep_ref, shear_ref, band_ref,
        corner_odd_ref, corner_even_ref, rlo_ref, rhi_ref,
        out_ref, halo, triple, split_sums, smooth, across, sheared,
    ):
        depth_index = lax.axis_index("gz")
        row_index = lax.axis_index("xy")
        odd_depth = depth_index % 2 == 1

        for side, mid_ref in ((0, rlo_ref), (1, rhi_ref)):
            at = pl.ds(side * ROW_TILE, ROW_TILE)
            even = [corner_even_ref[i, at] for i in range(HALO)]
            odd = [corner_odd_ref[i, at] for i in range(HALO)]
            low = [jnp.where(odd_depth, e, o) for e, o in zip(even, odd)]
            high = [jnp.where(odd_depth, o, e) for e, o in zip(even, odd)]
            outer = 0 if side == 0 else band - ROW_TILE
            inner_at = ROW_TILE if side == 0 else 0
            own_at = ROW_TILE if side == 0 else padded_rows - band
            sums = window_sums(low + [mid_ref[i] for i in range(depth_cells)] + high, TAPS)
            for z in range(layers):
                halo[z, side, pl.ds(outer, ROW_TILE)] = sums[z]
                halo[z, side, pl.ds(inner_at, band - ROW_TILE)] = deep_ref[
                    z, pl.ds(own_at, band - ROW_TILE)
                ]

        span = band - ROW_TILE
        for z in range(layers):
            for side in range(2):
                triple[z, side, pl.ds(0, span)] = (
                    halo[z, side, pl.ds(3, span)]
                    + halo[z, side, pl.ds(4, span)]
                    + halo[z, side, pl.ds(5, span)]
                )
                split_sums[z, side] = (
                    triple[z, side, pl.ds(0, piece)]
                    + triple[z, side, pl.ds(3, piece)]
                    + triple[z, side, pl.ds(6, piece)]
                )
        weights = jnp.concatenate([band_ref[...]] * 3, axis=0)
        both = column_sums(split_sums[...].reshape(layers * 2 * piece, columns), weights)
        both = both.reshape(layers, 2, piece, 2 * columns)
        smooth[...] = both[..., :columns]
        across[...] = both[1:-1, :, :, columns:]

        @pl.when(row_index == 0)
        def _():
            smooth[:, 0, :1] = jnp.zeros((layers, 1, columns), jnp.float32)

        @pl.when(row_index == n_rows - 1)
        def _():
            smooth[:, 1, EDGE + 1 : EDGE + 2] = jnp.zeros((layers, 1, columns), jnp.float32)

        zero_outside(smooth, depth_index, n_depth, layers)

        own_live = live_ref[depth_index, row_index]

        def both_sides(ref, z, start):
            return ref[z, :, pl.ds(start, EDGE)].reshape(height, columns)

        for z in range(depth_cells):
            channels = shade(
                both_sides(smooth, z + 1, 1),
                both_sides(smooth, z + 2, 1) - both_sides(smooth, z, 1),
                both_sides(smooth, z + 1, 2) - both_sides(smooth, z + 1, 0),
                both_sides(across, z, 1),
                z < own_live,
                palette_ref,
                extinct,
            )
            sheared[z] = jnp.dot(
                jnp.concatenate(channels), shear_ref[z], preferred_element_type=jnp.float32
            )
        out_ref[...] = inner_ref[...]
        for view in range(VIEWS):
            lanes = pl.ds(view * columns, columns)
            values = march(
                lambda z, c: sheared[z, pl.ds(c * height, height), lanes], depth_cells, view
            )
            codes = [encode(value) for value in values]
            for side, row in enumerate((0, row_cells - EDGE)):
                place = owner_ref[view, row // tile_rows]
                part = [code[side * EDGE : (side + 1) * EDGE] for code in codes]
                store_codes(out_ref, place, view, part, row % tile_rows, tile_rows, inner_ref)

    smem = pl.BlockSpec(memory_space=pltpu.SMEM)
    vmem = pl.BlockSpec(memory_space=pltpu.VMEM)
    return pl.pallas_call(
        kernel,
        out_shape=jax.ShapeDtypeStruct(inner.shape, inner.dtype),
        in_specs=[smem] * 3 + [vmem] * 8,
        out_specs=vmem,
        scratch_shapes=[
            pltpu.VMEM((layers, 2, band, columns), jnp.float32),
            pltpu.VMEM((layers, 2, piece + ROW_TILE, columns), jnp.float32),
            pltpu.VMEM((layers, 2, piece, columns), jnp.float32),
            pltpu.VMEM((layers, 2, piece, columns), jnp.float32),
            pltpu.VMEM((depth_cells, 2, piece, columns), jnp.float32),
            pltpu.VMEM((depth_cells, 4 * height, VIEWS * columns), jnp.float32),
        ],
        compiler_params=pltpu.CompilerParams(vmem_limit_bytes=VMEM_BYTES),
        name="render_edges",
    )(
        live_slices, palette, owner, inner, deep, shear, band_weights,
        corner_odd, corner_even, rlo, rhi,
    )


def cut_edges(density):
    depth_cells, row_cells, columns = density.shape

    places = [(i, start) for start in range(0, row_cells, ROW_TILE) for i in range(HALO)]
    words = len(places) // GROUP * WORDS

    def kernel(density_ref, row_even_ref, row_odd_ref, deep_even_ref, deep_odd_ref):
        row_bit = lax.axis_index("xy") % 2
        depth_bit = lax.axis_index("gz") % 2
        last_rows, last_deep = row_cells - ROW_TILE, depth_cells - HALO
        for ref, bit in ((deep_odd_ref, depth_bit), (deep_even_ref, 1 - depth_bit)):
            for group in range(len(places) // GROUP):
                values = [
                    density_ref[bit * last_deep + i, pl.ds(start, ROW_TILE)]
                    for i, start in places[group * GROUP : (group + 1) * GROUP]
                ]
                for k, word in enumerate(pack(values)):
                    ref[group * WORDS + k] = word
        for ref, bit in ((row_even_ref, 1 - row_bit), (row_odd_ref, row_bit)):
            start = pl.multiple_of(bit * last_rows, ROW_TILE)
            ref[...] = density_ref[:, pl.ds(start, ROW_TILE)]

    rows = jax.ShapeDtypeStruct((depth_cells, ROW_TILE, columns), jnp.float32)
    deep = jax.ShapeDtypeStruct((words, ROW_TILE, columns), jnp.int32)
    vmem = pl.BlockSpec(memory_space=pltpu.VMEM)
    return pl.pallas_call(
        kernel,
        out_shape=(rows, rows, deep, deep),
        in_specs=[vmem],
        out_specs=(vmem,) * 4,
        compiler_params=pltpu.CompilerParams(vmem_limit_bytes=VMEM_BYTES),
        name="cut_edges",
    )(density)


def composite_kernel(order_ref, in_ref, out_ref):
    count = in_ref.shape[0]
    rows = in_ref.shape[2] // 4
    for view in range(VIEWS):
        colour, transmit = None, None
        for k in range(count):
            source = order_ref[view, k]
            values = decode(in_ref[source, view])
            part = [values[c * rows : (c + 1) * rows] for c in range(4)]
            clear = 1.0 - part[3]
            if k == 0:
                colour, transmit = part[:3], clear
            else:
                colour = [colour[c] + transmit * part[c] for c in range(3)]
                transmit = transmit * clear
        for c, value in enumerate(colour + [1.0 - transmit]):
            out_ref[view, c, 0] = value


def body(density, live_slices, shear_slopes, palette, depth_order, tile_owner):
    depth_cells, row_cells, columns = density.shape
    n_depth = lax.axis_size("gz")
    edge = depth_cells - HALO
    odd_depth = lax.axis_index("gz") % 2 == 1
    odd_row = lax.axis_index("xy") % 2 == 1

    def pairs(axis, first):
        count = lax.axis_size(axis)
        lower = range(first, count - 1, 2)
        return [(i, i + 1) for i in lower] + [(i + 1, i) for i in lower]

    row_even, row_odd, deep_even, deep_odd = cut_edges(density)
    row_even = lax.ppermute(row_even, "xy", pairs("xy", 0))
    row_odd = lax.ppermute(row_odd, "xy", pairs("xy", 1))
    deep_odd = lax.ppermute(deep_odd, "gz", pairs("gz", 1))
    deep_even = lax.ppermute(deep_even, "gz", pairs("gz", 0))
    rlo = jnp.where(odd_row, row_even, row_odd)
    rhi = jnp.where(odd_row, row_odd, row_even)
    low_corner = jnp.concatenate([rlo[:HALO], rhi[:HALO]], axis=1)
    high_corner = jnp.concatenate([rlo[edge:], rhi[edge:]], axis=1)
    corner_odd = lax.ppermute(
        jnp.where(odd_depth, high_corner, low_corner), "gz", pairs("gz", 1)
    )
    corner_even = lax.ppermute(
        jnp.where(odd_depth, low_corner, high_corner), "gz", pairs("gz", 0)
    )
    inner, deep, shear, band_weights = render_inner(
        live_slices, shear_slopes, palette, tile_owner, density, deep_odd, deep_even, n_depth
    )
    outgoing = render_edges(
        live_slices, palette, tile_owner, inner, deep, shear, band_weights,
        corner_odd, corner_even, rlo, rhi, n_depth,
    )
    incoming = lax.all_to_all(outgoing, "gz", split_axis=0, concat_axis=0, tiled=True)
    tile_rows = row_cells // n_depth
    return pl.pallas_call(
        composite_kernel,
        out_shape=jax.ShapeDtypeStruct((VIEWS, 4, 1, tile_rows, columns), jnp.float32),
        in_specs=[pl.BlockSpec(memory_space=pltpu.SMEM), pl.BlockSpec(memory_space=pltpu.VMEM)],
        out_specs=pl.BlockSpec(memory_space=pltpu.VMEM),
        compiler_params=pltpu.CompilerParams(vmem_limit_bytes=VMEM_BYTES),
        name="composite",
    )(depth_order, incoming)


def solution(mesh):
    placed = (P("gz", "xy", None), P(), P(), P(), P(), P())
    return jax.shard_map(
        body, mesh=mesh, in_specs=placed, out_specs=P(None, None, "gz", "xy", None), check_vma=False
    )
```

```python
import math

import jax
import jax.numpy as jnp
from jax import lax
from jax.experimental import pallas as pl
from jax.experimental.pallas import tpu as pltpu
from jax.sharding import PartitionSpec as P

LIGHT = (0.48, 0.6, 0.64)
REACH = 4
HALO = REACH + 1
TAPS = 2 * REACH + 1
ROW_TILE = 8
PACKED_ROWS = 16
EDGE = 8
VIEWS = 2
TOP = 2.2
STEPS = 65535.0
MIDDLE = 32768
LEVELS_PER_UNIT = 5461.0
ZERO_LEVEL = 1 << 19
GROUP, WORDS = 8, 5
VMEM_BYTES = 40 * 1024 * 1024


def column_matrix(columns):
    source = lax.broadcasted_iota(jnp.int32, (columns, columns), 0)
    target = lax.broadcasted_iota(jnp.int32, (columns, columns), 1)

    def band(shift):
        at = target + shift
        inside = (jnp.abs(source - at) <= REACH) & (at >= 0) & (at < columns)
        return jnp.where(inside, 1.0, 0.0).astype(jnp.float32)

    return jnp.concatenate([band(0), band(1) - band(-1)], axis=1).astype(jnp.bfloat16)


def shear_matrices(slopes_ref, slice_depth, columns, total_depth):
    source = lax.broadcasted_iota(jnp.int32, (columns, columns), 0)
    target = lax.broadcasted_iota(jnp.int32, (columns, columns), 1)
    distance = (source - target).astype(jnp.float32)
    parts = []
    for view in range(VIEWS):
        shift = slopes_ref[view] * (slice_depth + 0.5 - 0.5 * total_depth)
        parts.append(jnp.maximum(0.0, 1.0 - jnp.abs(distance + shift)))
    return jnp.concatenate(parts, axis=1).astype(jnp.bfloat16)


def window_sums(layers, taps):
    sums, width = layers, 1
    while 2 * width < taps:
        sums = [sums[i] + sums[i + width] for i in range(len(sums) - width)]
        width *= 2
    return [sums[i] + layers[i + width] for i in range(len(layers) - width)]


def pack(values):
    v = [(x * LEVELS_PER_UNIT + (ZERO_LEVEL + 0.5)).astype(jnp.int32) for x in values]
    v = [(x - ZERO_LEVEL) & 0xFFFFF for x in v]
    upper = [
        v[5] & 0xFFF,
        (v[5] >> 12) | ((v[6] & 0xF) << 8),
        (v[6] >> 4) & 0xFFF,
        (v[6] >> 16) | ((v[7] & 0xFF) << 4),
        v[7] >> 8,
    ]
    return [v[i] | (upper[i] << 20) for i in range(WORDS)]


def unpack(words):
    upper = [lax.shift_right_logical(w, jnp.full_like(w, 20)) for w in words]
    levels = words + [
        upper[0] | ((upper[1] & 0xFF) << 12),
        (upper[1] >> 8) | (upper[2] << 4) | ((upper[3] & 0xF) << 16),
        (upper[3] >> 4) | (upper[4] << 8),
    ]
    levels = [(x << 12) >> 12 for x in levels]
    return [x.astype(jnp.float32) * (1.0 / LEVELS_PER_UNIT) for x in levels]


def encode(value):
    scale = math.log2(STEPS) - 0.125 * math.log2(TOP)
    root = jnp.exp2(0.125 * jnp.log2(jnp.maximum(value, 1e-30)) + scale)
    return (root + 0.5).astype(jnp.int32) - MIDDLE


def decode(code):
    root = (code.astype(jnp.int32) + MIDDLE).astype(jnp.float32) * (TOP**0.125 / STEPS)
    square = root * root
    fourth = square * square
    return fourth * fourth


def column_sums(total, weights):
    hi = total.astype(jnp.bfloat16)
    rest = total - hi.astype(jnp.float32)
    mid = rest.astype(jnp.bfloat16)
    lo = (rest - mid.astype(jnp.float32)).astype(jnp.bfloat16)
    split = jnp.concatenate([hi, mid, lo], axis=1)
    return jnp.dot(split, weights, preferred_element_type=jnp.float32)


def shade(center, diff_depth, diff_rows, diff_cols, live, palette_ref, extinct):
    cells = TAPS**3
    floor = 0.01 * (2.0 * cells) ** 2
    square = diff_depth * diff_depth + diff_rows * diff_rows + diff_cols * diff_cols + floor
    light = [0.75 * part for part in LIGHT]
    toward = light[0] * diff_depth + light[1] * diff_rows + light[2] * diff_cols
    facing = jnp.maximum(0.0, toward) * lax.rsqrt(square)
    t = center * (2.0 * math.log2(math.e) / cells)
    softplus = jnp.maximum(t, 0.0) + jnp.log2(1.0 + jnp.exp2(-jnp.abs(t)))
    opacity = 1.0 - jnp.exp2(jnp.where(live, -extinct, 0.0) * softplus)
    bright = opacity * (0.25 + facing)
    channels = [bright * palette_ref[c] for c in range(3)] + [opacity]
    return [channel.astype(jnp.bfloat16) for channel in channels]


def march(layer, depth_cells, view):
    colour, transmit = None, None
    for z in range(depth_cells):
        part = [layer(z, c) for c in range(4)]
        clear = 1.0 - part[3]
        if z == 0:
            colour, transmit = part[:3], clear
        elif view == 0:
            colour = [colour[c] + transmit * part[c] for c in range(3)]
            transmit = transmit * clear
        else:
            colour = [part[c] + clear * colour[c] for c in range(3)]
            transmit = transmit * clear
    return colour + [1.0 - transmit]


def store_codes(out_ref, place, view, codes, row, tile_rows, other=None):
    if tile_rows < PACKED_ROWS:
        for c in range(0, 4, 2):
            pair = jnp.concatenate(codes[c : c + 2])
            out_ref[place, view, pl.ds(c * tile_rows, PACKED_ROWS)] = pair.astype(jnp.int16)
        return
    for c in range(4):
        at = pl.ds(c * tile_rows + row // PACKED_ROWS * PACKED_ROWS, PACKED_ROWS)
        code = codes[c]
        if code.shape[0] < PACKED_ROWS:
            half = row % PACKED_ROWS
            rest = jnp.zeros_like(code)
            if other is not None:
                rest = other[place, view, at].astype(jnp.int32)
                rest = rest[ROW_TILE:] if half == 0 else rest[:ROW_TILE]
            code = jnp.concatenate([code, rest] if half == 0 else [rest, code])
        out_ref[place, view, at] = code.astype(jnp.int16)


def fetch_scalars(pairs, sems):
    copies = [
        pltpu.make_async_copy(source, target, sems.at[i]) for i, (source, target) in enumerate(pairs)
    ]
    for copy in copies:
        copy.start()

    def wait():
        for copy in copies:
            copy.wait()

    return wait


def zero_outside(smooth, depth_index, n_depth, layers):
    @pl.when(depth_index == 0)
    def _():
        smooth[0] = jnp.zeros_like(smooth[0])

    @pl.when(depth_index == n_depth - 1)
    def _():
        smooth[layers - 1] = jnp.zeros_like(smooth[layers - 1])


def render_inner(live_slices, slopes, palette, owner, density, deep_odd, deep_even, n_depth):
    depth_cells, row_cells, columns = density.shape
    total_depth = depth_cells * n_depth
    extinct = 3.0 / total_depth
    tile_rows = row_cells // n_depth
    layers = depth_cells + 2
    rows = range(EDGE, row_cells - EDGE)
    height = len(rows)
    lead, span = EDGE, height + 2 * ROW_TILE

    def kernel(
        live_in, slopes_in, palette_in, owner_in, own_ref, odd_ref, even_ref,
        out_ref, deep, shear_ref, band_ref, triple, smooth, across, sheared,
        live_ref, slopes_ref, palette_ref, owner_ref, sems,
    ):
        wait_scalars = fetch_scalars(
            [
                (live_in, live_ref),
                (slopes_in, slopes_ref),
                (palette_in, palette_ref),
                (owner_in, owner_ref),
            ],
            sems,
        )
        depth_index = lax.axis_index("gz")
        row_index = lax.axis_index("xy")
        odd_depth = depth_index % 2 == 1

        low, high, word = [], [], 0
        for start in range(0, row_cells, ROW_TILE):
            while len(low) < HALO:
                even = [even_ref[word + k] for k in range(WORDS)]
                odd = [odd_ref[word + k] for k in range(WORDS)]
                low += unpack([jnp.where(odd_depth, e, o) for e, o in zip(even, odd)])
                high += unpack([jnp.where(odd_depth, o, e) for e, o in zip(even, odd)])
                word += WORDS
            own = [own_ref[i, pl.ds(start, ROW_TILE)] for i in range(depth_cells)]
            for z, total in enumerate(window_sums(low[:HALO] + own + high[:HALO], TAPS)):
                deep[z, pl.ds(ROW_TILE + start, ROW_TILE)] = total
            low, high = low[HALO:], high[HALO:]

        band = column_matrix(columns)
        band_ref[...] = band
        weights = jnp.concatenate([band, band, band], axis=0)
        for z in range(layers):
            triple[z] = (
                deep[z, pl.ds(lead - 4, span + ROW_TILE)]
                + deep[z, pl.ds(lead - 3, span + ROW_TILE)]
                + deep[z, pl.ds(lead - 2, span + ROW_TILE)]
            )
            total = (
                triple[z, pl.ds(0, span)] + triple[z, pl.ds(3, span)] + triple[z, pl.ds(6, span)]
            )
            if 1 <= z <= depth_cells:
                both = column_sums(total, weights)
                smooth[z] = both[:, :columns]
                across[z - 1] = both[ROW_TILE : ROW_TILE + height, columns:]
            else:
                smooth[z] = column_sums(total, weights[:, :columns])
        zero_outside(smooth, depth_index, n_depth, layers)

        wait_scalars()
        slab_start = (depth_index * depth_cells).astype(jnp.float32)
        for z in range(depth_cells):
            shear_ref[z] = shear_matrices(slopes_ref, slab_start + float(z), columns, total_depth)

        own_live = live_ref[depth_index, row_index]
        middle = pl.ds(ROW_TILE, height)
        for z in range(depth_cells):
            channels = shade(
                smooth[z + 1, middle],
                smooth[z + 2, middle] - smooth[z, middle],
                smooth[z + 1, pl.ds(ROW_TILE + 1, height)]
                - smooth[z + 1, pl.ds(ROW_TILE - 1, height)],
                across[z],
                z < own_live,
                palette_ref,
                extinct,
            )
            sheared[z] = jnp.dot(
                jnp.concatenate(channels), shear_ref[z], preferred_element_type=jnp.float32
            )
        row = rows.start
        while row < rows.stop:
            whole = tile_rows >= PACKED_ROWS and row % PACKED_ROWS == 0
            count = PACKED_ROWS if whole and row + PACKED_ROWS <= rows.stop else ROW_TILE
            at = row - rows.start
            for view in range(VIEWS):
                lanes = pl.ds(view * columns, columns)
                values = march(
                    lambda z, c: sheared[z, pl.ds(c * height + at, count), lanes],
                    depth_cells,
                    view,
                )
                place = owner_ref[view, row // tile_rows]
                codes = [encode(value) for value in values]
                store_codes(out_ref, place, view, codes, row % tile_rows, tile_rows)
            row += count

    vmem = pl.BlockSpec(memory_space=pltpu.VMEM)
    return pl.pallas_call(
        kernel,
        out_shape=(
            jax.ShapeDtypeStruct((n_depth, VIEWS, 4 * tile_rows, columns), jnp.int16),
            jax.ShapeDtypeStruct((layers, row_cells + 2 * ROW_TILE, columns), jnp.float32),
            jax.ShapeDtypeStruct((depth_cells, columns, VIEWS * columns), jnp.bfloat16),
            jax.ShapeDtypeStruct((columns, 2 * columns), jnp.bfloat16),
        ),
        in_specs=[vmem] * 7,
        out_specs=(vmem,) * 4,
        scratch_shapes=[
            pltpu.VMEM((layers, span + ROW_TILE, columns), jnp.float32),
            pltpu.VMEM((layers, span, columns), jnp.float32),
            pltpu.VMEM((depth_cells, height, columns), jnp.float32),
            pltpu.VMEM((depth_cells, 4 * height, VIEWS * columns), jnp.float32),
            pltpu.SMEM(live_slices.shape, jnp.int32),
            pltpu.SMEM(slopes.shape, jnp.float32),
            pltpu.SMEM(palette.shape, jnp.float32),
            pltpu.SMEM(owner.shape, jnp.int32),
            pltpu.SemaphoreType.DMA((4,)),
        ],
        compiler_params=pltpu.CompilerParams(vmem_limit_bytes=VMEM_BYTES),
        cost_estimate=pl.CostEstimate(
            flops=100 * depth_cells * row_cells * columns,
            bytes_accessed=16 * 4 * depth_cells * row_cells * columns,
            transcendentals=4 * depth_cells * row_cells * columns,
        ),
        name="render_inner",
    )(live_slices, slopes, palette, owner, density, deep_odd, deep_even)


def render_edges(
    live_slices, palette, owner, inner, deep, shear, band_weights,
    corner_odd, corner_even, rlo, rhi, n_depth,
):
    layers, padded_rows, columns = deep.shape
    row_cells = padded_rows - 2 * ROW_TILE
    depth_cells = layers - 2
    n_rows = lax.axis_size("xy")
    extinct = 3.0 / (depth_cells * n_depth)
    tile_rows = row_cells // n_depth
    band = EDGE + 2 * ROW_TILE
    piece = 2 * ROW_TILE
    height = 2 * EDGE

    def kernel(
        live_in, palette_in, owner_in, inner_ref, deep_ref, shear_ref, band_ref,
        corner_odd_ref, corner_even_ref, rlo_ref, rhi_ref,
        out_ref, halo, triple, split_sums, smooth, across, sheared,
        live_ref, palette_ref, owner_ref, sems,
    ):
        wait_scalars = fetch_scalars(
            [(live_in, live_ref), (palette_in, palette_ref), (owner_in, owner_ref)], sems
        )
        depth_index = lax.axis_index("gz")
        row_index = lax.axis_index("xy")
        odd_depth = depth_index % 2 == 1

        for side, mid_ref in ((0, rlo_ref), (1, rhi_ref)):
            at = pl.ds(side * ROW_TILE, ROW_TILE)
            even = [corner_even_ref[i, at] for i in range(HALO)]
            odd = [corner_odd_ref[i, at] for i in range(HALO)]
            low = [jnp.where(odd_depth, e, o) for e, o in zip(even, odd)]
            high = [jnp.where(odd_depth, o, e) for e, o in zip(even, odd)]
            outer = 0 if side == 0 else band - ROW_TILE
            inner_at = ROW_TILE if side == 0 else 0
            own_at = ROW_TILE if side == 0 else padded_rows - band
            sums = window_sums(low + [mid_ref[i] for i in range(depth_cells)] + high, TAPS)
            for z in range(layers):
                halo[z, side, pl.ds(outer, ROW_TILE)] = sums[z]
                halo[z, side, pl.ds(inner_at, band - ROW_TILE)] = deep_ref[
                    z, pl.ds(own_at, band - ROW_TILE)
                ]

        span = band - ROW_TILE
        for z in range(layers):
            for side in range(2):
                triple[z, side, pl.ds(0, span)] = (
                    halo[z, side, pl.ds(3, span)]
                    + halo[z, side, pl.ds(4, span)]
                    + halo[z, side, pl.ds(5, span)]
                )
                split_sums[z, side] = (
                    triple[z, side, pl.ds(0, piece)]
                    + triple[z, side, pl.ds(3, piece)]
                    + triple[z, side, pl.ds(6, piece)]
                )
        weights = jnp.concatenate([band_ref[...]] * 3, axis=0)
        both = column_sums(split_sums[...].reshape(layers * 2 * piece, columns), weights)
        both = both.reshape(layers, 2, piece, 2 * columns)
        smooth[...] = both[..., :columns]
        across[...] = both[1:-1, :, :, columns:]

        @pl.when(row_index == 0)
        def _():
            smooth[:, 0, :1] = jnp.zeros((layers, 1, columns), jnp.float32)

        @pl.when(row_index == n_rows - 1)
        def _():
            smooth[:, 1, EDGE + 1 : EDGE + 2] = jnp.zeros((layers, 1, columns), jnp.float32)

        zero_outside(smooth, depth_index, n_depth, layers)

        wait_scalars()
        own_live = live_ref[depth_index, row_index]

        def both_sides(ref, z, start):
            return ref[z, :, pl.ds(start, EDGE)].reshape(height, columns)

        for z in range(depth_cells):
            channels = shade(
                both_sides(smooth, z + 1, 1),
                both_sides(smooth, z + 2, 1) - both_sides(smooth, z, 1),
                both_sides(smooth, z + 1, 2) - both_sides(smooth, z + 1, 0),
                both_sides(across, z, 1),
                z < own_live,
                palette_ref,
                extinct,
            )
            sheared[z] = jnp.dot(
                jnp.concatenate(channels), shear_ref[z], preferred_element_type=jnp.float32
            )
        out_ref[...] = inner_ref[...]
        for view in range(VIEWS):
            lanes = pl.ds(view * columns, columns)
            values = march(
                lambda z, c: sheared[z, pl.ds(c * height, height), lanes], depth_cells, view
            )
            codes = [encode(value) for value in values]
            for side, row in enumerate((0, row_cells - EDGE)):
                place = owner_ref[view, row // tile_rows]
                part = [code[side * EDGE : (side + 1) * EDGE] for code in codes]
                store_codes(out_ref, place, view, part, row % tile_rows, tile_rows, inner_ref)

    vmem = pl.BlockSpec(memory_space=pltpu.VMEM)
    return pl.pallas_call(
        kernel,
        out_shape=jax.ShapeDtypeStruct(inner.shape, inner.dtype),
        in_specs=[vmem] * 11,
        out_specs=vmem,
        scratch_shapes=[
            pltpu.VMEM((layers, 2, band, columns), jnp.float32),
            pltpu.VMEM((layers, 2, piece + ROW_TILE, columns), jnp.float32),
            pltpu.VMEM((layers, 2, piece, columns), jnp.float32),
            pltpu.VMEM((layers, 2, piece, columns), jnp.float32),
            pltpu.VMEM((depth_cells, 2, piece, columns), jnp.float32),
            pltpu.VMEM((depth_cells, 4 * height, VIEWS * columns), jnp.float32),
            pltpu.SMEM(live_slices.shape, jnp.int32),
            pltpu.SMEM(palette.shape, jnp.float32),
            pltpu.SMEM(owner.shape, jnp.int32),
            pltpu.SemaphoreType.DMA((3,)),
        ],
        compiler_params=pltpu.CompilerParams(vmem_limit_bytes=VMEM_BYTES),
        name="render_edges",
    )(
        live_slices, palette, owner, inner, deep, shear, band_weights,
        corner_odd, corner_even, rlo, rhi,
    )


def cut_edges(density):
    depth_cells, row_cells, columns = density.shape

    places = [(i, start) for start in range(0, row_cells, ROW_TILE) for i in range(HALO)]
    words = len(places) // GROUP * WORDS

    def kernel(density_ref, row_even_ref, row_odd_ref, deep_even_ref, deep_odd_ref):
        row_bit = lax.axis_index("xy") % 2
        depth_bit = lax.axis_index("gz") % 2
        last_rows, last_deep = row_cells - ROW_TILE, depth_cells - HALO
        for ref, bit in ((deep_odd_ref, depth_bit), (deep_even_ref, 1 - depth_bit)):
            for group in range(len(places) // GROUP):
                values = [
                    density_ref[bit * last_deep + i, pl.ds(start, ROW_TILE)]
                    for i, start in places[group * GROUP : (group + 1) * GROUP]
                ]
                for k, word in enumerate(pack(values)):
                    ref[group * WORDS + k] = word
        for ref, bit in ((row_even_ref, 1 - row_bit), (row_odd_ref, row_bit)):
            start = pl.multiple_of(bit * last_rows, ROW_TILE)
            ref[...] = density_ref[:, pl.ds(start, ROW_TILE)]

    rows = jax.ShapeDtypeStruct((depth_cells, ROW_TILE, columns), jnp.float32)
    deep = jax.ShapeDtypeStruct((words, ROW_TILE, columns), jnp.int32)
    vmem = pl.BlockSpec(memory_space=pltpu.VMEM)
    return pl.pallas_call(
        kernel,
        out_shape=(rows, rows, deep, deep),
        in_specs=[vmem],
        out_specs=(vmem,) * 4,
        compiler_params=pltpu.CompilerParams(vmem_limit_bytes=VMEM_BYTES),
        name="cut_edges",
    )(density)


def composite_kernel(order_in, in_ref, out_ref, values, order_ref, sems):
    wait_scalars = fetch_scalars([(order_in, order_ref)], sems)
    count = in_ref.shape[0]
    rows = in_ref.shape[2] // 4
    for source in range(count):
        for view in range(VIEWS):
            values[source, view] = decode(in_ref[source, view])
    wait_scalars()
    for view in range(VIEWS):
        colour, transmit = None, None
        for k in range(count):
            source = order_ref[view, k]
            part = [values[source, view, pl.ds(c * rows, rows)] for c in range(4)]
            clear = 1.0 - part[3]
            if k == 0:
                colour, transmit = part[:3], clear
            else:
                colour = [colour[c] + transmit * part[c] for c in range(3)]
                transmit = transmit * clear
        for c, value in enumerate(colour + [1.0 - transmit]):
            out_ref[view, c, 0] = value


def body(density, live_slices, shear_slopes, palette, depth_order, tile_owner):
    depth_cells, row_cells, columns = density.shape
    n_depth = lax.axis_size("gz")
    edge = depth_cells - HALO
    odd_depth = lax.axis_index("gz") % 2 == 1
    odd_row = lax.axis_index("xy") % 2 == 1

    def pairs(axis, first):
        count = lax.axis_size(axis)
        lower = range(first, count - 1, 2)
        return [(i, i + 1) for i in lower] + [(i + 1, i) for i in lower]

    row_even, row_odd, deep_even, deep_odd = cut_edges(density)
    row_even = lax.ppermute(row_even, "xy", pairs("xy", 0))
    row_odd = lax.ppermute(row_odd, "xy", pairs("xy", 1))
    deep_odd = lax.ppermute(deep_odd, "gz", pairs("gz", 1))
    deep_even = lax.ppermute(deep_even, "gz", pairs("gz", 0))
    rlo = jnp.where(odd_row, row_even, row_odd)
    rhi = jnp.where(odd_row, row_odd, row_even)
    low_corner = jnp.concatenate([rlo[:HALO], rhi[:HALO]], axis=1)
    high_corner = jnp.concatenate([rlo[edge:], rhi[edge:]], axis=1)
    corner_odd = lax.ppermute(
        jnp.where(odd_depth, high_corner, low_corner), "gz", pairs("gz", 1)
    )
    corner_even = lax.ppermute(
        jnp.where(odd_depth, low_corner, high_corner), "gz", pairs("gz", 0)
    )
    inner, deep, shear, band_weights = render_inner(
        live_slices, shear_slopes, palette, tile_owner, density, deep_odd, deep_even, n_depth
    )
    outgoing = render_edges(
        live_slices, palette, tile_owner, inner, deep, shear, band_weights,
        corner_odd, corner_even, rlo, rhi, n_depth,
    )
    incoming = lax.all_to_all(outgoing, "gz", split_axis=0, concat_axis=0, tiled=True)
    tile_rows = row_cells // n_depth
    return pl.pallas_call(
        composite_kernel,
        out_shape=jax.ShapeDtypeStruct((VIEWS, 4, 1, tile_rows, columns), jnp.float32),
        in_specs=[pl.BlockSpec(memory_space=pltpu.VMEM)] * 2,
        out_specs=pl.BlockSpec(memory_space=pltpu.VMEM),
        scratch_shapes=[
            pltpu.VMEM(incoming.shape, jnp.float32),
            pltpu.SMEM(depth_order.shape, jnp.int32),
            pltpu.SemaphoreType.DMA((1,)),
        ],
        compiler_params=pltpu.CompilerParams(vmem_limit_bytes=VMEM_BYTES),
        name="composite",
    )(depth_order, incoming)


def solution(mesh):
    placed = (P("gz", "xy", None), P(), P(), P(), P(), P())
    return jax.shard_map(
        body, mesh=mesh, in_specs=placed, out_specs=P(None, None, "gz", "xy", None), check_vma=False
    )
```

```python
import math

import jax
import jax.numpy as jnp
from jax import lax
from jax.experimental import pallas as pl
from jax.experimental.pallas import tpu as pltpu
from jax.sharding import PartitionSpec as P

LIGHT = (0.48, 0.6, 0.64)
REACH = 4
HALO = REACH + 1
TAPS = 2 * REACH + 1
ROW_TILE = 8
PACKED_ROWS = 16
EDGE = 8
VIEWS = 2
TOP = 2.2
STEPS = 65535.0
MIDDLE = 32768
LEVELS_PER_UNIT = 5461.0
ZERO_LEVEL = 1 << 19
GROUP, WORDS = 8, 5
VMEM_BYTES = 40 * 1024 * 1024


def column_matrix(columns):
    source = lax.broadcasted_iota(jnp.int32, (columns, columns), 0)
    target = lax.broadcasted_iota(jnp.int32, (columns, columns), 1)

    def band(shift):
        at = target + shift
        inside = (jnp.abs(source - at) <= REACH) & (at >= 0) & (at < columns)
        return jnp.where(inside, 1.0, 0.0).astype(jnp.float32)

    return jnp.concatenate([band(0), band(1) - band(-1)], axis=1).astype(jnp.bfloat16)


def shear_matrices(slopes_ref, slice_depth, columns, total_depth):
    source = lax.broadcasted_iota(jnp.int32, (columns, columns), 0)
    target = lax.broadcasted_iota(jnp.int32, (columns, columns), 1)
    distance = (source - target).astype(jnp.float32)
    parts = []
    for view in range(VIEWS):
        shift = slopes_ref[view] * (slice_depth + 0.5 - 0.5 * total_depth)
        parts.append(jnp.maximum(0.0, 1.0 - jnp.abs(distance + shift)))
    return jnp.concatenate(parts, axis=1).astype(jnp.bfloat16)


def window_sums(layers, taps):
    sums, width = layers, 1
    while 2 * width < taps:
        sums = [sums[i] + sums[i + width] for i in range(len(sums) - width)]
        width *= 2
    return [sums[i] + layers[i + width] for i in range(len(layers) - width)]


def pack(values):
    v = [(x * LEVELS_PER_UNIT + (ZERO_LEVEL + 0.5)).astype(jnp.int32) for x in values]
    v = [(x - ZERO_LEVEL) & 0xFFFFF for x in v]
    upper = [
        v[5] & 0xFFF,
        (v[5] >> 12) | ((v[6] & 0xF) << 8),
        (v[6] >> 4) & 0xFFF,
        (v[6] >> 16) | ((v[7] & 0xFF) << 4),
        v[7] >> 8,
    ]
    return [v[i] | (upper[i] << 20) for i in range(WORDS)]


def unpack(words):
    upper = [lax.shift_right_logical(w, jnp.full_like(w, 20)) for w in words]
    levels = words + [
        upper[0] | ((upper[1] & 0xFF) << 12),
        (upper[1] >> 8) | (upper[2] << 4) | ((upper[3] & 0xF) << 16),
        (upper[3] >> 4) | (upper[4] << 8),
    ]
    levels = [(x << 12) >> 12 for x in levels]
    return [x.astype(jnp.float32) * (1.0 / LEVELS_PER_UNIT) for x in levels]


def encode(value):
    scale = math.log2(STEPS) - 0.125 * math.log2(TOP)
    root = jnp.exp2(0.125 * jnp.log2(jnp.maximum(value, 1e-30)) + scale)
    return (root + 0.5).astype(jnp.int32) - MIDDLE


def decode(code):
    root = (code.astype(jnp.int32) + MIDDLE).astype(jnp.float32) * (TOP**0.125 / STEPS)
    square = root * root
    fourth = square * square
    return fourth * fourth


def column_sums(total, weights):
    hi = total.astype(jnp.bfloat16)
    rest = total - hi.astype(jnp.float32)
    mid = rest.astype(jnp.bfloat16)
    lo = (rest - mid.astype(jnp.float32)).astype(jnp.bfloat16)
    split = jnp.concatenate([hi, mid, lo], axis=1)
    return jnp.dot(split, weights, preferred_element_type=jnp.float32)


def shade(center, diff_depth, diff_rows, diff_cols, live, palette_ref, extinct):
    cells = TAPS**3
    floor = 0.01 * (2.0 * cells) ** 2
    square = diff_depth * diff_depth + diff_rows * diff_rows + diff_cols * diff_cols + floor
    light = [0.75 * part for part in LIGHT]
    toward = light[0] * diff_depth + light[1] * diff_rows + light[2] * diff_cols
    facing = jnp.maximum(0.0, toward) * lax.rsqrt(square)
    t = center * (2.0 * math.log2(math.e) / cells)
    softplus = jnp.maximum(t, 0.0) + jnp.log2(1.0 + jnp.exp2(-jnp.abs(t)))
    opacity = 1.0 - jnp.exp2(jnp.where(live, -extinct, 0.0) * softplus)
    bright = opacity * (0.25 + facing)
    channels = [bright * palette_ref[c] for c in range(3)] + [opacity]
    return [channel.astype(jnp.bfloat16) for channel in channels]


def march(layer, depth_cells, view):
    colour, transmit = None, None
    for z in range(depth_cells):
        part = [layer(z, c) for c in range(4)]
        clear = 1.0 - part[3]
        if z == 0:
            colour, transmit = part[:3], clear
        elif view == 0:
            colour = [colour[c] + transmit * part[c] for c in range(3)]
            transmit = transmit * clear
        else:
            colour = [part[c] + clear * colour[c] for c in range(3)]
            transmit = transmit * clear
    return colour + [1.0 - transmit]


def store_codes(out_ref, place, view, codes, row, tile_rows, other=None):
    if tile_rows < PACKED_ROWS:
        for c in range(0, 4, 2):
            pair = jnp.concatenate(codes[c : c + 2])
            out_ref[place, view, pl.ds(c * tile_rows, PACKED_ROWS)] = pair.astype(jnp.int16)
        return
    for c in range(4):
        at = pl.ds(c * tile_rows + row // PACKED_ROWS * PACKED_ROWS, PACKED_ROWS)
        code = codes[c]
        if code.shape[0] < PACKED_ROWS:
            half = row % PACKED_ROWS
            rest = jnp.zeros_like(code)
            if other is not None:
                rest = other[place, view, at].astype(jnp.int32)
                rest = rest[ROW_TILE:] if half == 0 else rest[:ROW_TILE]
            code = jnp.concatenate([code, rest] if half == 0 else [rest, code])
        out_ref[place, view, at] = code.astype(jnp.int16)


def fetch_scalars(pairs, sems):
    copies = [
        pltpu.make_async_copy(source, target, sems.at[i]) for i, (source, target) in enumerate(pairs)
    ]
    for copy in copies:
        copy.start()

    def wait():
        for copy in copies:
            copy.wait()

    return wait


def zero_outside(smooth, depth_index, n_depth, layers):
    @pl.when(depth_index == 0)
    def _():
        smooth[0] = jnp.zeros_like(smooth[0])

    @pl.when(depth_index == n_depth - 1)
    def _():
        smooth[layers - 1] = jnp.zeros_like(smooth[layers - 1])


def render_inner(live_slices, slopes, palette, owner, density, deep_odd, deep_even, n_depth):
    depth_cells, row_cells, columns = density.shape
    total_depth = depth_cells * n_depth
    extinct = 3.0 / total_depth
    tile_rows = row_cells // n_depth
    layers = depth_cells + 2
    rows = range(EDGE, row_cells - EDGE)
    height = len(rows)
    lead, span = EDGE, height + 2 * ROW_TILE

    def kernel(
        live_in, slopes_in, palette_in, owner_in, own_ref, odd_ref, even_ref,
        out_ref, deep, shear_ref, band_ref, triple, smooth, across, sheared,
        live_ref, slopes_ref, palette_ref, owner_ref, sems,
    ):
        wait_scalars = fetch_scalars(
            [
                (live_in, live_ref),
                (slopes_in, slopes_ref),
                (palette_in, palette_ref),
                (owner_in, owner_ref),
            ],
            sems,
        )
        depth_index = lax.axis_index("gz")
        row_index = lax.axis_index("xy")
        odd_depth = depth_index % 2 == 1

        low, high, word = [], [], 0
        for start in range(0, row_cells, ROW_TILE):
            while len(low) < HALO:
                even = [even_ref[word + k] for k in range(WORDS)]
                odd = [odd_ref[word + k] for k in range(WORDS)]
                low += unpack([jnp.where(odd_depth, e, o) for e, o in zip(even, odd)])
                high += unpack([jnp.where(odd_depth, o, e) for e, o in zip(even, odd)])
                word += WORDS
            own = [own_ref[i, pl.ds(start, ROW_TILE)] for i in range(depth_cells)]
            for z, total in enumerate(window_sums(low[:HALO] + own + high[:HALO], TAPS)):
                deep[z, pl.ds(ROW_TILE + start, ROW_TILE)] = total
            low, high = low[HALO:], high[HALO:]

        band = column_matrix(columns)
        band_ref[...] = band
        weights = jnp.concatenate([band, band, band], axis=0)
        for z in range(layers):
            triple[z] = (
                deep[z, pl.ds(lead - 4, span + ROW_TILE)]
                + deep[z, pl.ds(lead - 3, span + ROW_TILE)]
                + deep[z, pl.ds(lead - 2, span + ROW_TILE)]
            )
            total = (
                triple[z, pl.ds(0, span)] + triple[z, pl.ds(3, span)] + triple[z, pl.ds(6, span)]
            )
            if 1 <= z <= depth_cells:
                both = column_sums(total, weights)
                smooth[z] = both[:, :columns]
                across[z - 1] = both[ROW_TILE : ROW_TILE + height, columns:]
            else:
                smooth[z] = column_sums(total, weights[:, :columns])
        zero_outside(smooth, depth_index, n_depth, layers)

        wait_scalars()
        slab_start = (depth_index * depth_cells).astype(jnp.float32)
        for z in range(depth_cells):
            shear_ref[z] = shear_matrices(slopes_ref, slab_start + float(z), columns, total_depth)

        own_live = live_ref[depth_index, row_index]
        middle = pl.ds(ROW_TILE, height)
        for z in range(depth_cells):
            channels = shade(
                smooth[z + 1, middle],
                smooth[z + 2, middle] - smooth[z, middle],
                smooth[z + 1, pl.ds(ROW_TILE + 1, height)]
                - smooth[z + 1, pl.ds(ROW_TILE - 1, height)],
                across[z],
                z < own_live,
                palette_ref,
                extinct,
            )
            sheared[z] = jnp.dot(
                jnp.concatenate(channels), shear_ref[z], preferred_element_type=jnp.float32
            )
        row = rows.start
        while row < rows.stop:
            whole = tile_rows >= PACKED_ROWS and row % PACKED_ROWS == 0
            count = PACKED_ROWS if whole and row + PACKED_ROWS <= rows.stop else ROW_TILE
            at = row - rows.start
            for view in range(VIEWS):
                lanes = pl.ds(view * columns, columns)
                values = march(
                    lambda z, c: sheared[z, pl.ds(c * height + at, count), lanes],
                    depth_cells,
                    view,
                )
                place = owner_ref[view, row // tile_rows]
                codes = [encode(value) for value in values]
                store_codes(out_ref, place, view, codes, row % tile_rows, tile_rows)
            row += count

    vmem = pl.BlockSpec(memory_space=pltpu.VMEM)
    return pl.pallas_call(
        kernel,
        out_shape=(
            jax.ShapeDtypeStruct((n_depth, VIEWS, 4 * tile_rows, columns), jnp.int16),
            jax.ShapeDtypeStruct((layers, row_cells + 2 * ROW_TILE, columns), jnp.float32),
            jax.ShapeDtypeStruct((depth_cells, columns, VIEWS * columns), jnp.bfloat16),
            jax.ShapeDtypeStruct((columns, 2 * columns), jnp.bfloat16),
        ),
        in_specs=[vmem] * 7,
        out_specs=(vmem,) * 4,
        scratch_shapes=[
            pltpu.VMEM((layers, span + ROW_TILE, columns), jnp.float32),
            pltpu.VMEM((layers, span, columns), jnp.float32),
            pltpu.VMEM((depth_cells, height, columns), jnp.float32),
            pltpu.VMEM((depth_cells, 4 * height, VIEWS * columns), jnp.float32),
            pltpu.SMEM(live_slices.shape, jnp.int32),
            pltpu.SMEM(slopes.shape, jnp.float32),
            pltpu.SMEM(palette.shape, jnp.float32),
            pltpu.SMEM(owner.shape, jnp.int32),
            pltpu.SemaphoreType.DMA((4,)),
        ],
        compiler_params=pltpu.CompilerParams(vmem_limit_bytes=VMEM_BYTES),
        cost_estimate=pl.CostEstimate(
            flops=100 * depth_cells * row_cells * columns,
            bytes_accessed=16 * 4 * depth_cells * row_cells * columns,
            transcendentals=4 * depth_cells * row_cells * columns,
        ),
        name="render_inner",
    )(live_slices, slopes, palette, owner, density, deep_odd, deep_even)


def render_edges(
    live_slices, palette, owner, inner, deep, shear, band_weights,
    corner_odd, corner_even, row_even, row_odd, n_depth,
):
    layers, padded_rows, columns = deep.shape
    row_cells = padded_rows - 2 * ROW_TILE
    depth_cells = layers - 2
    n_rows = lax.axis_size("xy")
    extinct = 3.0 / (depth_cells * n_depth)
    tile_rows = row_cells // n_depth
    band = EDGE + 2 * ROW_TILE
    piece = 2 * ROW_TILE
    height = 2 * EDGE

    def kernel(
        live_in, palette_in, owner_in, inner_ref, deep_ref, shear_ref, band_ref,
        corner_odd_ref, corner_even_ref, row_even_ref, row_odd_ref,
        out_ref, halo, triple, split_sums, smooth, across, sheared,
        live_ref, palette_ref, owner_ref, sems,
    ):
        wait_scalars = fetch_scalars(
            [(live_in, live_ref), (palette_in, palette_ref), (owner_in, owner_ref)], sems
        )
        depth_index = lax.axis_index("gz")
        row_index = lax.axis_index("xy")
        odd_depth = depth_index % 2 == 1

        odd_row = row_index % 2 == 1
        from_even, from_odd = pl.ds(0, ROW_TILE), pl.ds(ROW_TILE, ROW_TILE)
        for side in range(2):
            take_even = odd_row if side == 0 else jnp.logical_not(odd_row)

            def facing_rows(ref, i):
                return jnp.where(take_even, ref[i, from_even], ref[i, from_odd])

            even = [facing_rows(corner_even_ref, i) for i in range(HALO)]
            odd = [facing_rows(corner_odd_ref, i) for i in range(HALO)]
            middle = [
                jnp.where(take_even, row_even_ref[i], row_odd_ref[i]) for i in range(depth_cells)
            ]
            low = [jnp.where(odd_depth, e, o) for e, o in zip(even, odd)]
            high = [jnp.where(odd_depth, o, e) for e, o in zip(even, odd)]
            outer = 0 if side == 0 else band - ROW_TILE
            inner_at = ROW_TILE if side == 0 else 0
            own_at = ROW_TILE if side == 0 else padded_rows - band
            sums = window_sums(low + middle + high, TAPS)
            for z in range(layers):
                halo[z, side, pl.ds(outer, ROW_TILE)] = sums[z]
                halo[z, side, pl.ds(inner_at, band - ROW_TILE)] = deep_ref[
                    z, pl.ds(own_at, band - ROW_TILE)
                ]

        span = band - ROW_TILE
        for z in range(layers):
            for side in range(2):
                triple[z, side, pl.ds(0, span)] = (
                    halo[z, side, pl.ds(3, span)]
                    + halo[z, side, pl.ds(4, span)]
                    + halo[z, side, pl.ds(5, span)]
                )
                split_sums[z, side] = (
                    triple[z, side, pl.ds(0, piece)]
                    + triple[z, side, pl.ds(3, piece)]
                    + triple[z, side, pl.ds(6, piece)]
                )
        weights = jnp.concatenate([band_ref[...]] * 3, axis=0)
        both = column_sums(split_sums[...].reshape(layers * 2 * piece, columns), weights)
        both = both.reshape(layers, 2, piece, 2 * columns)
        smooth[...] = both[..., :columns]
        across[...] = both[1:-1, :, :, columns:]

        @pl.when(row_index == 0)
        def _():
            smooth[:, 0, :1] = jnp.zeros((layers, 1, columns), jnp.float32)

        @pl.when(row_index == n_rows - 1)
        def _():
            smooth[:, 1, EDGE + 1 : EDGE + 2] = jnp.zeros((layers, 1, columns), jnp.float32)

        zero_outside(smooth, depth_index, n_depth, layers)

        wait_scalars()
        own_live = live_ref[depth_index, row_index]

        def both_sides(ref, z, start):
            return ref[z, :, pl.ds(start, EDGE)].reshape(height, columns)

        for z in range(depth_cells):
            channels = shade(
                both_sides(smooth, z + 1, 1),
                both_sides(smooth, z + 2, 1) - both_sides(smooth, z, 1),
                both_sides(smooth, z + 1, 2) - both_sides(smooth, z + 1, 0),
                both_sides(across, z, 1),
                z < own_live,
                palette_ref,
                extinct,
            )
            sheared[z] = jnp.dot(
                jnp.concatenate(channels), shear_ref[z], preferred_element_type=jnp.float32
            )
        out_ref[...] = inner_ref[...]
        for view in range(VIEWS):
            lanes = pl.ds(view * columns, columns)
            values = march(
                lambda z, c: sheared[z, pl.ds(c * height, height), lanes], depth_cells, view
            )
            codes = [encode(value) for value in values]
            for side, row in enumerate((0, row_cells - EDGE)):
                place = owner_ref[view, row // tile_rows]
                part = [code[side * EDGE : (side + 1) * EDGE] for code in codes]
                store_codes(out_ref, place, view, part, row % tile_rows, tile_rows, inner_ref)

    vmem = pl.BlockSpec(memory_space=pltpu.VMEM)
    return pl.pallas_call(
        kernel,
        out_shape=jax.ShapeDtypeStruct(inner.shape, inner.dtype),
        in_specs=[vmem] * 11,
        out_specs=vmem,
        scratch_shapes=[
            pltpu.VMEM((layers, 2, band, columns), jnp.float32),
            pltpu.VMEM((layers, 2, piece + ROW_TILE, columns), jnp.float32),
            pltpu.VMEM((layers, 2, piece, columns), jnp.float32),
            pltpu.VMEM((layers, 2, piece, columns), jnp.float32),
            pltpu.VMEM((depth_cells, 2, piece, columns), jnp.float32),
            pltpu.VMEM((depth_cells, 4 * height, VIEWS * columns), jnp.float32),
            pltpu.SMEM(live_slices.shape, jnp.int32),
            pltpu.SMEM(palette.shape, jnp.float32),
            pltpu.SMEM(owner.shape, jnp.int32),
            pltpu.SemaphoreType.DMA((3,)),
        ],
        compiler_params=pltpu.CompilerParams(vmem_limit_bytes=VMEM_BYTES),
        name="render_edges",
    )(
        live_slices, palette, owner, inner, deep, shear, band_weights,
        corner_odd, corner_even, row_even, row_odd,
    )


def cut_edges(density):
    depth_cells, row_cells, columns = density.shape

    places = [(i, start) for start in range(0, row_cells, ROW_TILE) for i in range(HALO)]
    words = len(places) // GROUP * WORDS

    def kernel(density_ref, row_even_ref, row_odd_ref, deep_even_ref, deep_odd_ref):
        row_bit = lax.axis_index("xy") % 2
        depth_bit = lax.axis_index("gz") % 2
        last_rows, last_deep = row_cells - ROW_TILE, depth_cells - HALO
        for ref, bit in ((deep_odd_ref, depth_bit), (deep_even_ref, 1 - depth_bit)):
            for group in range(len(places) // GROUP):
                values = [
                    density_ref[bit * last_deep + i, pl.ds(start, ROW_TILE)]
                    for i, start in places[group * GROUP : (group + 1) * GROUP]
                ]
                for k, word in enumerate(pack(values)):
                    ref[group * WORDS + k] = word
        for ref, bit in ((row_even_ref, 1 - row_bit), (row_odd_ref, row_bit)):
            start = pl.multiple_of(bit * last_rows, ROW_TILE)
            ref[...] = density_ref[:, pl.ds(start, ROW_TILE)]

    rows = jax.ShapeDtypeStruct((depth_cells, ROW_TILE, columns), jnp.float32)
    deep = jax.ShapeDtypeStruct((words, ROW_TILE, columns), jnp.int32)
    vmem = pl.BlockSpec(memory_space=pltpu.VMEM)
    return pl.pallas_call(
        kernel,
        out_shape=(rows, rows, deep, deep),
        in_specs=[vmem],
        out_specs=(vmem,) * 4,
        compiler_params=pltpu.CompilerParams(vmem_limit_bytes=VMEM_BYTES),
        name="cut_edges",
    )(density)


def composite_kernel(order_in, in_ref, out_ref, values, order_ref, sems):
    wait_scalars = fetch_scalars([(order_in, order_ref)], sems)
    count = in_ref.shape[0]
    rows = in_ref.shape[2] // 4
    for source in range(count):
        for view in range(VIEWS):
            values[source, view] = decode(in_ref[source, view])
    wait_scalars()
    for view in range(VIEWS):
        colour, transmit = None, None
        for k in range(count):
            source = order_ref[view, k]
            part = [values[source, view, pl.ds(c * rows, rows)] for c in range(4)]
            clear = 1.0 - part[3]
            if k == 0:
                colour, transmit = part[:3], clear
            else:
                colour = [colour[c] + transmit * part[c] for c in range(3)]
                transmit = transmit * clear
        for c, value in enumerate(colour + [1.0 - transmit]):
            out_ref[view, c, 0] = value


def body(density, live_slices, shear_slopes, palette, depth_order, tile_owner):
    depth_cells, row_cells, columns = density.shape
    n_depth = lax.axis_size("gz")
    edge = depth_cells - HALO
    odd_depth = lax.axis_index("gz") % 2 == 1

    def pairs(axis, first):
        count = lax.axis_size(axis)
        lower = range(first, count - 1, 2)
        return [(i, i + 1) for i in lower] + [(i + 1, i) for i in lower]

    row_even, row_odd, deep_even, deep_odd = cut_edges(density)
    row_even = lax.ppermute(row_even, "xy", pairs("xy", 0))
    row_odd = lax.ppermute(row_odd, "xy", pairs("xy", 1))
    deep_odd = lax.ppermute(deep_odd, "gz", pairs("gz", 1))
    deep_even = lax.ppermute(deep_even, "gz", pairs("gz", 0))
    rows = jnp.concatenate([row_even, row_odd], axis=1)
    facing = jnp.where(odd_depth, edge, 0)
    corner_odd = lax.ppermute(
        lax.dynamic_slice_in_dim(rows, facing, HALO), "gz", pairs("gz", 1)
    )
    corner_even = lax.ppermute(
        lax.dynamic_slice_in_dim(rows, edge - facing, HALO), "gz", pairs("gz", 0)
    )
    inner, deep, shear, band_weights = render_inner(
        live_slices, shear_slopes, palette, tile_owner, density, deep_odd, deep_even, n_depth
    )
    outgoing = render_edges(
        live_slices, palette, tile_owner, inner, deep, shear, band_weights,
        corner_odd, corner_even, row_even, row_odd, n_depth,
    )
    incoming = lax.all_to_all(outgoing, "gz", split_axis=0, concat_axis=0, tiled=True)
    tile_rows = row_cells // n_depth
    return pl.pallas_call(
        composite_kernel,
        out_shape=jax.ShapeDtypeStruct((VIEWS, 4, 1, tile_rows, columns), jnp.float32),
        in_specs=[pl.BlockSpec(memory_space=pltpu.VMEM)] * 2,
        out_specs=pl.BlockSpec(memory_space=pltpu.VMEM),
        scratch_shapes=[
            pltpu.VMEM(incoming.shape, jnp.float32),
            pltpu.SMEM(depth_order.shape, jnp.int32),
            pltpu.SemaphoreType.DMA((1,)),
        ],
        compiler_params=pltpu.CompilerParams(vmem_limit_bytes=VMEM_BYTES),
        name="composite",
    )(depth_order, incoming)


def solution(mesh):
    placed = (P("gz", "xy", None), P(), P(), P(), P(), P())
    return jax.shard_map(
        body, mesh=mesh, in_specs=placed, out_specs=P(None, None, "gz", "xy", None), check_vma=False
    )
```

```python
import math

import jax
import jax.numpy as jnp
from jax import lax
from jax.experimental import pallas as pl
from jax.experimental.pallas import tpu as pltpu
from jax.sharding import PartitionSpec as P

LIGHT = (0.48, 0.6, 0.64)
REACH = 4
HALO = REACH + 1
TAPS = 2 * REACH + 1
ROW_TILE = 8
PACKED_ROWS = 16
EDGE = 8
VIEWS = 2
TOP = 2.2
STEPS = 65535.0
MIDDLE = 32768
LEVELS_PER_UNIT = 5461.0
ZERO_LEVEL = 1 << 19
GROUP, WORDS = 8, 5
VMEM_BYTES = 40 * 1024 * 1024


def column_matrix(columns):
    source = lax.broadcasted_iota(jnp.int32, (columns, columns), 0)
    target = lax.broadcasted_iota(jnp.int32, (columns, columns), 1)

    def band(shift):
        at = target + shift
        inside = (jnp.abs(source - at) <= REACH) & (at >= 0) & (at < columns)
        return jnp.where(inside, 1.0, 0.0).astype(jnp.float32)

    return jnp.concatenate([band(0), band(1) - band(-1)], axis=1).astype(jnp.bfloat16)


def shear_matrices(slopes_ref, slice_depth, columns, total_depth):
    source = lax.broadcasted_iota(jnp.int32, (columns, columns), 0)
    target = lax.broadcasted_iota(jnp.int32, (columns, columns), 1)
    distance = (source - target).astype(jnp.float32)
    parts = []
    for view in range(VIEWS):
        shift = slopes_ref[view] * (slice_depth + 0.5 - 0.5 * total_depth)
        parts.append(jnp.maximum(0.0, 1.0 - jnp.abs(distance + shift)))
    return jnp.concatenate(parts, axis=1).astype(jnp.bfloat16)


def window_sums(layers, taps):
    sums, width = layers, 1
    while 2 * width < taps:
        sums = [sums[i] + sums[i + width] for i in range(len(sums) - width)]
        width *= 2
    return [sums[i] + layers[i + width] for i in range(len(layers) - width)]


def pack(values):
    v = [(x * LEVELS_PER_UNIT + (ZERO_LEVEL + 0.5)).astype(jnp.int32) for x in values]
    v = [(x - ZERO_LEVEL) & 0xFFFFF for x in v]
    upper = [
        v[5] & 0xFFF,
        (v[5] >> 12) | ((v[6] & 0xF) << 8),
        (v[6] >> 4) & 0xFFF,
        (v[6] >> 16) | ((v[7] & 0xFF) << 4),
        v[7] >> 8,
    ]
    return [v[i] | (upper[i] << 20) for i in range(WORDS)]


def unpack(words):
    upper = [lax.shift_right_logical(w, jnp.full_like(w, 20)) for w in words]
    levels = words + [
        upper[0] | ((upper[1] & 0xFF) << 12),
        (upper[1] >> 8) | (upper[2] << 4) | ((upper[3] & 0xF) << 16),
        (upper[3] >> 4) | (upper[4] << 8),
    ]
    levels = [(x << 12) >> 12 for x in levels]
    return [x.astype(jnp.float32) * (1.0 / LEVELS_PER_UNIT) for x in levels]


def encode(value):
    scale = math.log2(STEPS) - 0.125 * math.log2(TOP)
    root = jnp.exp2(0.125 * jnp.log2(jnp.maximum(value, 1e-30)) + scale)
    return (root + 0.5).astype(jnp.int32) - MIDDLE


def decode(code):
    root = (code.astype(jnp.int32) + MIDDLE).astype(jnp.float32) * (TOP**0.125 / STEPS)
    square = root * root
    fourth = square * square
    return fourth * fourth


def column_sums(total, weights):
    hi = total.astype(jnp.bfloat16)
    rest = total - hi.astype(jnp.float32)
    mid = rest.astype(jnp.bfloat16)
    lo = (rest - mid.astype(jnp.float32)).astype(jnp.bfloat16)
    split = jnp.concatenate([hi, mid, lo], axis=1)
    return jnp.dot(split, weights, preferred_element_type=jnp.float32)


def shade(center, diff_depth, diff_rows, diff_cols, live, palette_ref, extinct):
    cells = TAPS**3
    floor = 0.01 * (2.0 * cells) ** 2
    square = diff_depth * diff_depth + diff_rows * diff_rows + diff_cols * diff_cols + floor
    light = [0.75 * part for part in LIGHT]
    toward = light[0] * diff_depth + light[1] * diff_rows + light[2] * diff_cols
    facing = jnp.maximum(0.0, toward) * lax.rsqrt(square)
    t = center * (2.0 * math.log2(math.e) / cells)
    softplus = jnp.maximum(t, 0.0) + jnp.log2(1.0 + jnp.exp2(-jnp.abs(t)))
    opacity = 1.0 - jnp.exp2(jnp.where(live, -extinct, 0.0) * softplus)
    bright = opacity * (0.25 + facing)
    channels = [bright * palette_ref[c] for c in range(3)] + [opacity]
    return [channel.astype(jnp.bfloat16) for channel in channels]


def march(layer, depth_cells, view):
    colour, transmit = None, None
    for z in range(depth_cells):
        part = [layer(z, c) for c in range(4)]
        clear = 1.0 - part[3]
        if z == 0:
            colour, transmit = part[:3], clear
        elif view == 0:
            colour = [colour[c] + transmit * part[c] for c in range(3)]
            transmit = transmit * clear
        else:
            colour = [part[c] + clear * colour[c] for c in range(3)]
            transmit = transmit * clear
    return colour + [1.0 - transmit]


def store_codes(out_ref, place, view, codes, row, tile_rows, other=None):
    if tile_rows < PACKED_ROWS:
        for c in range(0, 4, 2):
            pair = jnp.concatenate(codes[c : c + 2])
            out_ref[place, view, pl.ds(c * tile_rows, PACKED_ROWS)] = pair.astype(jnp.int16)
        return
    for c in range(4):
        at = pl.ds(c * tile_rows + row // PACKED_ROWS * PACKED_ROWS, PACKED_ROWS)
        code = codes[c]
        if code.shape[0] < PACKED_ROWS:
            half = row % PACKED_ROWS
            rest = jnp.zeros_like(code)
            if other is not None:
                rest = other[place, view, at].astype(jnp.int32)
                rest = rest[ROW_TILE:] if half == 0 else rest[:ROW_TILE]
            code = jnp.concatenate([code, rest] if half == 0 else [rest, code])
        out_ref[place, view, at] = code.astype(jnp.int16)


def fetch_scalars(pairs, sems):
    copies = [
        pltpu.make_async_copy(source, target, sems.at[i]) for i, (source, target) in enumerate(pairs)
    ]
    for copy in copies:
        copy.start()

    def wait():
        for copy in copies:
            copy.wait()

    return wait


def zero_outside(smooth, depth_index, n_depth, layers):
    @pl.when(depth_index == 0)
    def _():
        smooth[0] = jnp.zeros_like(smooth[0])

    @pl.when(depth_index == n_depth - 1)
    def _():
        smooth[layers - 1] = jnp.zeros_like(smooth[layers - 1])


def render_inner(live_slices, slopes, palette, owner, density, deep_odd, deep_even, n_depth):
    depth_cells, row_cells, columns = density.shape
    total_depth = depth_cells * n_depth
    extinct = 3.0 / total_depth
    tile_rows = row_cells // n_depth
    layers = depth_cells + 2
    rows = range(EDGE, row_cells - EDGE)
    height = len(rows)
    lead, span = EDGE, height + 2 * ROW_TILE

    def kernel(
        live_in, slopes_in, palette_in, owner_in, own_ref, odd_ref, even_ref,
        out_ref, deep, shear_ref, band_ref, triple, smooth, across, sheared,
        live_ref, slopes_ref, palette_ref, owner_ref, sems,
    ):
        wait_scalars = fetch_scalars(
            [
                (live_in, live_ref),
                (slopes_in, slopes_ref),
                (palette_in, palette_ref),
                (owner_in, owner_ref),
            ],
            sems,
        )
        depth_index = lax.axis_index("gz")
        row_index = lax.axis_index("xy")
        odd_depth = depth_index % 2 == 1

        low, high, word = [], [], 0
        for start in range(0, row_cells, ROW_TILE):
            while len(low) < HALO:
                even = [even_ref[word + k] for k in range(WORDS)]
                odd = [odd_ref[word + k] for k in range(WORDS)]
                low += unpack([jnp.where(odd_depth, e, o) for e, o in zip(even, odd)])
                high += unpack([jnp.where(odd_depth, o, e) for e, o in zip(even, odd)])
                word += WORDS
            own = [own_ref[i, pl.ds(start, ROW_TILE)] for i in range(depth_cells)]
            for z, total in enumerate(window_sums(low[:HALO] + own + high[:HALO], TAPS)):
                deep[z, pl.ds(ROW_TILE + start, ROW_TILE)] = total
            low, high = low[HALO:], high[HALO:]

        band = column_matrix(columns)
        band_ref[...] = band
        weights = jnp.concatenate([band, band, band], axis=0)
        for z in range(layers):
            triple[z] = (
                deep[z, pl.ds(lead - 4, span + ROW_TILE)]
                + deep[z, pl.ds(lead - 3, span + ROW_TILE)]
                + deep[z, pl.ds(lead - 2, span + ROW_TILE)]
            )
            total = (
                triple[z, pl.ds(0, span)] + triple[z, pl.ds(3, span)] + triple[z, pl.ds(6, span)]
            )
            if 1 <= z <= depth_cells:
                both = column_sums(total, weights)
                smooth[z] = both[:, :columns]
                across[z - 1] = both[ROW_TILE : ROW_TILE + height, columns:]
            else:
                smooth[z] = column_sums(total, weights[:, :columns])
        zero_outside(smooth, depth_index, n_depth, layers)

        wait_scalars()
        slab_start = (depth_index * depth_cells).astype(jnp.float32)
        for z in range(depth_cells):
            shear_ref[z] = shear_matrices(slopes_ref, slab_start + float(z), columns, total_depth)

        own_live = live_ref[depth_index, row_index]
        middle = pl.ds(ROW_TILE, height)
        for z in range(depth_cells):
            channels = shade(
                smooth[z + 1, middle],
                smooth[z + 2, middle] - smooth[z, middle],
                smooth[z + 1, pl.ds(ROW_TILE + 1, height)]
                - smooth[z + 1, pl.ds(ROW_TILE - 1, height)],
                across[z],
                z < own_live,
                palette_ref,
                extinct,
            )
            sheared[z] = jnp.dot(
                jnp.concatenate(channels), shear_ref[z], preferred_element_type=jnp.float32
            )
        row = rows.start
        while row < rows.stop:
            whole = tile_rows >= PACKED_ROWS and row % PACKED_ROWS == 0
            count = PACKED_ROWS if whole and row + PACKED_ROWS <= rows.stop else ROW_TILE
            at = row - rows.start
            for view in range(VIEWS):
                lanes = pl.ds(view * columns, columns)
                values = march(
                    lambda z, c: sheared[z, pl.ds(c * height + at, count), lanes],
                    depth_cells,
                    view,
                )
                place = owner_ref[view, row // tile_rows]
                codes = [encode(value) for value in values]
                store_codes(out_ref, place, view, codes, row % tile_rows, tile_rows)
            row += count

    vmem = pl.BlockSpec(memory_space=pltpu.VMEM)
    return pl.pallas_call(
        kernel,
        out_shape=(
            jax.ShapeDtypeStruct((n_depth, VIEWS, 4 * tile_rows, columns), jnp.int16),
            jax.ShapeDtypeStruct((layers, row_cells + 2 * ROW_TILE, columns), jnp.float32),
            jax.ShapeDtypeStruct((depth_cells, columns, VIEWS * columns), jnp.bfloat16),
            jax.ShapeDtypeStruct((columns, 2 * columns), jnp.bfloat16),
        ),
        in_specs=[vmem] * 7,
        out_specs=(vmem,) * 4,
        scratch_shapes=[
            pltpu.VMEM((layers, span + ROW_TILE, columns), jnp.float32),
            pltpu.VMEM((layers, span, columns), jnp.float32),
            pltpu.VMEM((depth_cells, height, columns), jnp.float32),
            pltpu.VMEM((depth_cells, 4 * height, VIEWS * columns), jnp.float32),
            pltpu.SMEM(live_slices.shape, jnp.int32),
            pltpu.SMEM(slopes.shape, jnp.float32),
            pltpu.SMEM(palette.shape, jnp.float32),
            pltpu.SMEM(owner.shape, jnp.int32),
            pltpu.SemaphoreType.DMA((4,)),
        ],
        compiler_params=pltpu.CompilerParams(vmem_limit_bytes=VMEM_BYTES),
        cost_estimate=pl.CostEstimate(
            flops=100 * depth_cells * row_cells * columns,
            bytes_accessed=16 * 4 * depth_cells * row_cells * columns,
            transcendentals=4 * depth_cells * row_cells * columns,
        ),
        name="render_inner",
    )(live_slices, slopes, palette, owner, density, deep_odd, deep_even)


def render_edges(
    live_slices, palette, owner, inner, deep, shear, band_weights,
    corner_odd, corner_even, row_odd, row_even, n_depth,
):
    layers, padded_rows, columns = deep.shape
    row_cells = padded_rows - 2 * ROW_TILE
    depth_cells = layers - 2
    n_rows = lax.axis_size("xy")
    extinct = 3.0 / (depth_cells * n_depth)
    tile_rows = row_cells // n_depth
    band = EDGE + 2 * ROW_TILE
    piece = 2 * ROW_TILE
    height = 2 * EDGE

    def kernel(
        live_in, palette_in, owner_in, inner_ref, deep_ref, shear_ref, band_ref,
        corner_odd_ref, corner_even_ref, row_odd_ref, row_even_ref,
        out_ref, halo, triple, split_sums, smooth, across, sheared,
        live_ref, palette_ref, owner_ref, sems,
    ):
        wait_scalars = fetch_scalars(
            [(live_in, live_ref), (palette_in, palette_ref), (owner_in, owner_ref)], sems
        )
        depth_index = lax.axis_index("gz")
        row_index = lax.axis_index("xy")
        odd_depth = depth_index % 2 == 1

        odd_row = row_index % 2 == 1
        from_odd, from_even = pl.ds(0, ROW_TILE), pl.ds(ROW_TILE, ROW_TILE)
        for side in range(2):
            take_even = odd_row if side == 0 else jnp.logical_not(odd_row)

            def facing_rows(ref, i):
                return jnp.where(take_even, ref[i, from_even], ref[i, from_odd])

            even = [facing_rows(corner_even_ref, i) for i in range(HALO)]
            odd = [facing_rows(corner_odd_ref, i) for i in range(HALO)]
            middle = [
                jnp.where(take_even, row_even_ref[i], row_odd_ref[i]) for i in range(depth_cells)
            ]
            low = [jnp.where(odd_depth, e, o) for e, o in zip(even, odd)]
            high = [jnp.where(odd_depth, o, e) for e, o in zip(even, odd)]
            outer = 0 if side == 0 else band - ROW_TILE
            inner_at = ROW_TILE if side == 0 else 0
            own_at = ROW_TILE if side == 0 else padded_rows - band
            sums = window_sums(low + middle + high, TAPS)
            for z in range(layers):
                halo[z, side, pl.ds(outer, ROW_TILE)] = sums[z]
                halo[z, side, pl.ds(inner_at, band - ROW_TILE)] = deep_ref[
                    z, pl.ds(own_at, band - ROW_TILE)
                ]

        span = band - ROW_TILE
        for z in range(layers):
            for side in range(2):
                triple[z, side, pl.ds(0, span)] = (
                    halo[z, side, pl.ds(3, span)]
                    + halo[z, side, pl.ds(4, span)]
                    + halo[z, side, pl.ds(5, span)]
                )
                split_sums[z, side] = (
                    triple[z, side, pl.ds(0, piece)]
                    + triple[z, side, pl.ds(3, piece)]
                    + triple[z, side, pl.ds(6, piece)]
                )
        weights = jnp.concatenate([band_ref[...]] * 3, axis=0)
        both = column_sums(split_sums[...].reshape(layers * 2 * piece, columns), weights)
        both = both.reshape(layers, 2, piece, 2 * columns)
        smooth[...] = both[..., :columns]
        across[...] = both[1:-1, :, :, columns:]

        @pl.when(row_index == 0)
        def _():
            smooth[:, 0, :1] = jnp.zeros((layers, 1, columns), jnp.float32)

        @pl.when(row_index == n_rows - 1)
        def _():
            smooth[:, 1, EDGE + 1 : EDGE + 2] = jnp.zeros((layers, 1, columns), jnp.float32)

        zero_outside(smooth, depth_index, n_depth, layers)

        wait_scalars()
        own_live = live_ref[depth_index, row_index]

        def both_sides(ref, z, start):
            return ref[z, :, pl.ds(start, EDGE)].reshape(height, columns)

        for z in range(depth_cells):
            channels = shade(
                both_sides(smooth, z + 1, 1),
                both_sides(smooth, z + 2, 1) - both_sides(smooth, z, 1),
                both_sides(smooth, z + 1, 2) - both_sides(smooth, z + 1, 0),
                both_sides(across, z, 1),
                z < own_live,
                palette_ref,
                extinct,
            )
            sheared[z] = jnp.dot(
                jnp.concatenate(channels), shear_ref[z], preferred_element_type=jnp.float32
            )
        out_ref[...] = inner_ref[...]
        for view in range(VIEWS):
            lanes = pl.ds(view * columns, columns)
            values = march(
                lambda z, c: sheared[z, pl.ds(c * height, height), lanes], depth_cells, view
            )
            codes = [encode(value) for value in values]
            for side, row in enumerate((0, row_cells - EDGE)):
                place = owner_ref[view, row // tile_rows]
                part = [code[side * EDGE : (side + 1) * EDGE] for code in codes]
                store_codes(out_ref, place, view, part, row % tile_rows, tile_rows, inner_ref)

    vmem = pl.BlockSpec(memory_space=pltpu.VMEM)
    return pl.pallas_call(
        kernel,
        out_shape=jax.ShapeDtypeStruct(inner.shape, inner.dtype),
        in_specs=[vmem] * 11,
        out_specs=vmem,
        scratch_shapes=[
            pltpu.VMEM((layers, 2, band, columns), jnp.float32),
            pltpu.VMEM((layers, 2, piece + ROW_TILE, columns), jnp.float32),
            pltpu.VMEM((layers, 2, piece, columns), jnp.float32),
            pltpu.VMEM((layers, 2, piece, columns), jnp.float32),
            pltpu.VMEM((depth_cells, 2, piece, columns), jnp.float32),
            pltpu.VMEM((depth_cells, 4 * height, VIEWS * columns), jnp.float32),
            pltpu.SMEM(live_slices.shape, jnp.int32),
            pltpu.SMEM(palette.shape, jnp.float32),
            pltpu.SMEM(owner.shape, jnp.int32),
            pltpu.SemaphoreType.DMA((3,)),
        ],
        compiler_params=pltpu.CompilerParams(vmem_limit_bytes=VMEM_BYTES),
        name="render_edges",
    )(
        live_slices, palette, owner, inner, deep, shear, band_weights,
        corner_odd, corner_even, row_odd, row_even,
    )


def cut_edges(density):
    depth_cells, row_cells, columns = density.shape

    places = [(i, start) for start in range(0, row_cells, ROW_TILE) for i in range(HALO)]
    words = len(places) // GROUP * WORDS

    def kernel(density_ref, row_even_ref, row_odd_ref, deep_even_ref, deep_odd_ref):
        row_bit = lax.axis_index("xy") % 2
        depth_bit = lax.axis_index("gz") % 2
        last_rows, last_deep = row_cells - ROW_TILE, depth_cells - HALO
        for ref, bit in ((deep_odd_ref, depth_bit), (deep_even_ref, 1 - depth_bit)):
            for group in range(len(places) // GROUP):
                values = [
                    density_ref[bit * last_deep + i, pl.ds(start, ROW_TILE)]
                    for i, start in places[group * GROUP : (group + 1) * GROUP]
                ]
                for k, word in enumerate(pack(values)):
                    ref[group * WORDS + k] = word
        for ref, bit in ((row_even_ref, 1 - row_bit), (row_odd_ref, row_bit)):
            start = pl.multiple_of(bit * last_rows, ROW_TILE)
            ref[...] = density_ref[:, pl.ds(start, ROW_TILE)]

    rows = jax.ShapeDtypeStruct((depth_cells, ROW_TILE, columns), jnp.float32)
    deep = jax.ShapeDtypeStruct((words, ROW_TILE, columns), jnp.int32)
    vmem = pl.BlockSpec(memory_space=pltpu.VMEM)
    return pl.pallas_call(
        kernel,
        out_shape=(rows, rows, deep, deep),
        in_specs=[vmem],
        out_specs=(vmem,) * 4,
        compiler_params=pltpu.CompilerParams(vmem_limit_bytes=VMEM_BYTES),
        name="cut_edges",
    )(density)


def composite_kernel(order_in, in_ref, out_ref, values, order_ref, sems):
    wait_scalars = fetch_scalars([(order_in, order_ref)], sems)
    count = in_ref.shape[0]
    rows = in_ref.shape[2] // 4
    for source in range(count):
        for view in range(VIEWS):
            values[source, view] = decode(in_ref[source, view])
    wait_scalars()
    for view in range(VIEWS):
        colour, transmit = None, None
        for k in range(count):
            source = order_ref[view, k]
            part = [values[source, view, pl.ds(c * rows, rows)] for c in range(4)]
            clear = 1.0 - part[3]
            if k == 0:
                colour, transmit = part[:3], clear
            else:
                colour = [colour[c] + transmit * part[c] for c in range(3)]
                transmit = transmit * clear
        for c, value in enumerate(colour + [1.0 - transmit]):
            out_ref[view, c, 0] = value


def body(density, live_slices, shear_slopes, palette, depth_order, tile_owner):
    depth_cells, row_cells, columns = density.shape
    n_depth = lax.axis_size("gz")
    edge = depth_cells - HALO
    odd_depth = lax.axis_index("gz") % 2 == 1

    def pairs(axis, first):
        count = lax.axis_size(axis)
        lower = range(first, count - 1, 2)
        return [(i, i + 1) for i in lower] + [(i + 1, i) for i in lower]

    row_even, row_odd, deep_even, deep_odd = cut_edges(density)
    row_odd = lax.ppermute(row_odd, "xy", pairs("xy", 1))
    row_even = lax.ppermute(row_even, "xy", pairs("xy", 0))
    deep_odd = lax.ppermute(deep_odd, "gz", pairs("gz", 1))
    deep_even = lax.ppermute(deep_even, "gz", pairs("gz", 0))
    rows = jnp.concatenate([row_odd, row_even], axis=1)
    facing = jnp.where(odd_depth, edge, 0)
    corner_odd = lax.ppermute(
        lax.dynamic_slice_in_dim(rows, facing, HALO), "gz", pairs("gz", 1)
    )
    corner_even = lax.ppermute(
        lax.dynamic_slice_in_dim(rows, edge - facing, HALO), "gz", pairs("gz", 0)
    )
    inner, deep, shear, band_weights = render_inner(
        live_slices, shear_slopes, palette, tile_owner, density, deep_odd, deep_even, n_depth
    )
    outgoing = render_edges(
        live_slices, palette, tile_owner, inner, deep, shear, band_weights,
        corner_odd, corner_even, row_odd, row_even, n_depth,
    )
    incoming = lax.all_to_all(outgoing, "gz", split_axis=0, concat_axis=0, tiled=True)
    tile_rows = row_cells // n_depth
    return pl.pallas_call(
        composite_kernel,
        out_shape=jax.ShapeDtypeStruct((VIEWS, 4, 1, tile_rows, columns), jnp.float32),
        in_specs=[pl.BlockSpec(memory_space=pltpu.VMEM)] * 2,
        out_specs=pl.BlockSpec(memory_space=pltpu.VMEM),
        scratch_shapes=[
            pltpu.VMEM(incoming.shape, jnp.float32),
            pltpu.SMEM(depth_order.shape, jnp.int32),
            pltpu.SemaphoreType.DMA((1,)),
        ],
        compiler_params=pltpu.CompilerParams(vmem_limit_bytes=VMEM_BYTES),
        name="composite",
    )(depth_order, incoming)


def solution(mesh):
    placed = (P("gz", "xy", None), P(), P(), P(), P(), P())
    return jax.shard_map(
        body, mesh=mesh, in_specs=placed, out_specs=P(None, None, "gz", "xy", None), check_vma=False
    )
```

```python
import math

import jax
import jax.numpy as jnp
from jax import lax
from jax.experimental import pallas as pl
from jax.experimental.pallas import tpu as pltpu
from jax.sharding import PartitionSpec as P

LIGHT = (0.48, 0.6, 0.64)
REACH = 4
HALO = REACH + 1
TAPS = 2 * REACH + 1
ROW_TILE = 8
PACKED_ROWS = 16
EDGE = 8
VIEWS = 2
TOP = 2.2
STEPS = 65535.0
MIDDLE = 32768
LEVELS_PER_UNIT = 5461.0
ZERO_LEVEL = 1 << 19
GROUP, WORDS = 8, 5
VMEM_BYTES = 40 * 1024 * 1024


def column_matrix(columns):
    source = lax.broadcasted_iota(jnp.int32, (columns, columns), 0)
    target = lax.broadcasted_iota(jnp.int32, (columns, columns), 1)

    def band(shift):
        at = target + shift
        inside = (jnp.abs(source - at) <= REACH) & (at >= 0) & (at < columns)
        return jnp.where(inside, 1.0, 0.0).astype(jnp.float32)

    return jnp.concatenate([band(0), band(1) - band(-1)], axis=1).astype(jnp.bfloat16)


def shear_matrices(slopes_ref, slice_depth, columns, total_depth):
    source = lax.broadcasted_iota(jnp.int32, (columns, columns), 0)
    target = lax.broadcasted_iota(jnp.int32, (columns, columns), 1)
    distance = (source - target).astype(jnp.float32)
    parts = []
    for view in range(VIEWS):
        shift = slopes_ref[view] * (slice_depth + 0.5 - 0.5 * total_depth)
        parts.append(jnp.maximum(0.0, 1.0 - jnp.abs(distance + shift)))
    return jnp.concatenate(parts, axis=1).astype(jnp.bfloat16)


def window_sums(layers, taps):
    sums, width = layers, 1
    while 2 * width < taps:
        sums = [sums[i] + sums[i + width] for i in range(len(sums) - width)]
        width *= 2
    return [sums[i] + layers[i + width] for i in range(len(layers) - width)]


def pack(values):
    v = [(x * LEVELS_PER_UNIT + (ZERO_LEVEL + 0.5)).astype(jnp.int32) for x in values]
    v = [(x - ZERO_LEVEL) & 0xFFFFF for x in v]
    upper = [
        v[5] & 0xFFF,
        (v[5] >> 12) | ((v[6] & 0xF) << 8),
        (v[6] >> 4) & 0xFFF,
        (v[6] >> 16) | ((v[7] & 0xFF) << 4),
        v[7] >> 8,
    ]
    return [v[i] | (upper[i] << 20) for i in range(WORDS)]


def unpack(words):
    upper = [lax.shift_right_logical(w, jnp.full_like(w, 20)) for w in words]
    levels = words + [
        upper[0] | ((upper[1] & 0xFF) << 12),
        (upper[1] >> 8) | (upper[2] << 4) | ((upper[3] & 0xF) << 16),
        (upper[3] >> 4) | (upper[4] << 8),
    ]
    levels = [(x << 12) >> 12 for x in levels]
    return [x.astype(jnp.float32) * (1.0 / LEVELS_PER_UNIT) for x in levels]


def encode(value):
    scale = math.log2(STEPS) - 0.125 * math.log2(TOP)
    root = jnp.exp2(0.125 * jnp.log2(jnp.maximum(value, 1e-30)) + scale)
    return (root + 0.5).astype(jnp.int32) - MIDDLE


def decode(code):
    root = (code.astype(jnp.int32) + MIDDLE).astype(jnp.float32) * (TOP**0.125 / STEPS)
    square = root * root
    fourth = square * square
    return fourth * fourth


def column_sums(total, weights):
    hi = total.astype(jnp.bfloat16)
    rest = total - hi.astype(jnp.float32)
    mid = rest.astype(jnp.bfloat16)
    lo = (rest - mid.astype(jnp.float32)).astype(jnp.bfloat16)
    split = jnp.concatenate([hi, mid, lo], axis=1)
    return jnp.dot(split, weights, preferred_element_type=jnp.float32)


def shade(center, diff_depth, diff_rows, diff_cols, live, palette_ref, extinct):
    cells = TAPS**3
    floor = 0.01 * (2.0 * cells) ** 2
    square = diff_depth * diff_depth + diff_rows * diff_rows + diff_cols * diff_cols + floor
    light = [0.75 * part for part in LIGHT]
    toward = light[0] * diff_depth + light[1] * diff_rows + light[2] * diff_cols
    facing = jnp.maximum(0.0, toward) * lax.rsqrt(square)
    t = center * (2.0 * math.log2(math.e) / cells)
    softplus = jnp.maximum(t, 0.0) + jnp.log2(1.0 + jnp.exp2(-jnp.abs(t)))
    opacity = 1.0 - jnp.exp2(jnp.where(live, -extinct, 0.0) * softplus)
    bright = opacity * (0.25 + facing)
    channels = [bright * palette_ref[c] for c in range(3)] + [opacity]
    return [channel.astype(jnp.bfloat16) for channel in channels]


def march(layer, depth_cells, view):
    colour, transmit = None, None
    for z in range(depth_cells):
        part = [layer(z, c) for c in range(4)]
        clear = 1.0 - part[3]
        if z == 0:
            colour, transmit = part[:3], clear
        elif view == 0:
            colour = [colour[c] + transmit * part[c] for c in range(3)]
            transmit = transmit * clear
        else:
            colour = [part[c] + clear * colour[c] for c in range(3)]
            transmit = transmit * clear
    return colour + [1.0 - transmit]


def store_codes(out_ref, place, view, codes, row, tile_rows, other=None):
    if tile_rows < PACKED_ROWS:
        for c in range(0, 4, 2):
            pair = jnp.concatenate(codes[c : c + 2])
            out_ref[place, view, pl.ds(c * tile_rows, PACKED_ROWS)] = pair.astype(jnp.int16)
        return
    for c in range(4):
        at = pl.ds(c * tile_rows + row // PACKED_ROWS * PACKED_ROWS, PACKED_ROWS)
        code = codes[c]
        if code.shape[0] < PACKED_ROWS:
            half = row % PACKED_ROWS
            rest = jnp.zeros_like(code)
            if other is not None:
                rest = other[place, view, at].astype(jnp.int32)
                rest = rest[ROW_TILE:] if half == 0 else rest[:ROW_TILE]
            code = jnp.concatenate([code, rest] if half == 0 else [rest, code])
        out_ref[place, view, at] = code.astype(jnp.int16)


def fetch_scalars(pairs, sems):
    copies = [
        pltpu.make_async_copy(source, target, sems.at[i]) for i, (source, target) in enumerate(pairs)
    ]
    for copy in copies:
        copy.start()

    def wait():
        for copy in copies:
            copy.wait()

    return wait


def zero_outside(smooth, depth_index, n_depth, layers):
    @pl.when(depth_index == 0)
    def _():
        smooth[0] = jnp.zeros_like(smooth[0])

    @pl.when(depth_index == n_depth - 1)
    def _():
        smooth[layers - 1] = jnp.zeros_like(smooth[layers - 1])


def render_inner(live_slices, slopes, palette, owner, density, deep_odd, deep_even, n_depth):
    depth_cells, row_cells, columns = density.shape
    total_depth = depth_cells * n_depth
    extinct = 3.0 / total_depth
    tile_rows = row_cells // n_depth
    layers = depth_cells + 2
    rows = range(EDGE, row_cells - EDGE)
    height = len(rows)
    lead, span = EDGE, height + 2 * ROW_TILE

    def kernel(
        live_in, slopes_in, palette_in, owner_in, own_ref, odd_ref, even_ref,
        out_ref, deep, shear_ref, band_ref, triple, smooth, across, sheared,
        live_ref, slopes_ref, palette_ref, owner_ref, sems,
    ):
        wait_scalars = fetch_scalars(
            [
                (live_in, live_ref),
                (slopes_in, slopes_ref),
                (palette_in, palette_ref),
                (owner_in, owner_ref),
            ],
            sems,
        )
        depth_index = lax.axis_index("gz")
        row_index = lax.axis_index("xy")
        odd_depth = depth_index % 2 == 1

        low, high, word = [], [], 0
        for start in range(0, row_cells, ROW_TILE):
            while len(low) < HALO:
                even = [even_ref[word + k] for k in range(WORDS)]
                odd = [odd_ref[word + k] for k in range(WORDS)]
                low += unpack([jnp.where(odd_depth, e, o) for e, o in zip(even, odd)])
                high += unpack([jnp.where(odd_depth, o, e) for e, o in zip(even, odd)])
                word += WORDS
            own = [own_ref[i, pl.ds(start, ROW_TILE)] for i in range(depth_cells)]
            for z, total in enumerate(window_sums(low[:HALO] + own + high[:HALO], TAPS)):
                deep[z, pl.ds(ROW_TILE + start, ROW_TILE)] = total
            low, high = low[HALO:], high[HALO:]

        band = column_matrix(columns)
        band_ref[...] = band
        weights = jnp.concatenate([band, band, band], axis=0)
        for z in range(layers):
            triple[z] = (
                deep[z, pl.ds(lead - 4, span + ROW_TILE)]
                + deep[z, pl.ds(lead - 3, span + ROW_TILE)]
                + deep[z, pl.ds(lead - 2, span + ROW_TILE)]
            )
            total = (
                triple[z, pl.ds(0, span)] + triple[z, pl.ds(3, span)] + triple[z, pl.ds(6, span)]
            )
            if 1 <= z <= depth_cells:
                both = column_sums(total, weights)
                smooth[z] = both[:, :columns]
                across[z - 1] = both[ROW_TILE : ROW_TILE + height, columns:]
            else:
                smooth[z] = column_sums(total, weights[:, :columns])
        zero_outside(smooth, depth_index, n_depth, layers)

        wait_scalars()
        slab_start = (depth_index * depth_cells).astype(jnp.float32)
        for z in range(depth_cells):
            shear_ref[z] = shear_matrices(slopes_ref, slab_start + float(z), columns, total_depth)

        own_live = live_ref[depth_index, row_index]
        middle = pl.ds(ROW_TILE, height)
        for z in range(depth_cells):
            channels = shade(
                smooth[z + 1, middle],
                smooth[z + 2, middle] - smooth[z, middle],
                smooth[z + 1, pl.ds(ROW_TILE + 1, height)]
                - smooth[z + 1, pl.ds(ROW_TILE - 1, height)],
                across[z],
                z < own_live,
                palette_ref,
                extinct,
            )
            sheared[z] = jnp.dot(
                jnp.concatenate(channels), shear_ref[z], preferred_element_type=jnp.float32
            )
        row = rows.start
        while row < rows.stop:
            whole = tile_rows >= PACKED_ROWS and row % PACKED_ROWS == 0
            count = PACKED_ROWS if whole and row + PACKED_ROWS <= rows.stop else ROW_TILE
            at = row - rows.start
            for view in range(VIEWS):
                lanes = pl.ds(view * columns, columns)
                values = march(
                    lambda z, c: sheared[z, pl.ds(c * height + at, count), lanes],
                    depth_cells,
                    view,
                )
                place = owner_ref[view, row // tile_rows]
                codes = [encode(value) for value in values]
                store_codes(out_ref, place, view, codes, row % tile_rows, tile_rows)
            row += count

    vmem = pl.BlockSpec(memory_space=pltpu.VMEM)
    return pl.pallas_call(
        kernel,
        out_shape=(
            jax.ShapeDtypeStruct((n_depth, VIEWS, 4 * tile_rows, columns), jnp.int16),
            jax.ShapeDtypeStruct((layers, row_cells + 2 * ROW_TILE, columns), jnp.float32),
            jax.ShapeDtypeStruct((depth_cells, columns, VIEWS * columns), jnp.bfloat16),
            jax.ShapeDtypeStruct((columns, 2 * columns), jnp.bfloat16),
        ),
        in_specs=[vmem] * 7,
        out_specs=(vmem,) * 4,
        scratch_shapes=[
            pltpu.VMEM((layers, span + ROW_TILE, columns), jnp.float32),
            pltpu.VMEM((layers, span, columns), jnp.float32),
            pltpu.VMEM((depth_cells, height, columns), jnp.float32),
            pltpu.VMEM((depth_cells, 4 * height, VIEWS * columns), jnp.float32),
            pltpu.SMEM(live_slices.shape, jnp.int32),
            pltpu.SMEM(slopes.shape, jnp.float32),
            pltpu.SMEM(palette.shape, jnp.float32),
            pltpu.SMEM(owner.shape, jnp.int32),
            pltpu.SemaphoreType.DMA((4,)),
        ],
        compiler_params=pltpu.CompilerParams(vmem_limit_bytes=VMEM_BYTES),
        cost_estimate=pl.CostEstimate(
            flops=100 * depth_cells * row_cells * columns,
            bytes_accessed=16 * 4 * depth_cells * row_cells * columns,
            transcendentals=4 * depth_cells * row_cells * columns,
        ),
        name="render_inner",
    )(live_slices, slopes, palette, owner, density, deep_odd, deep_even)


def render_edges(
    live_slices, palette, owner, corner_odd, corner_even, row_even, row_odd,
    inner, deep, shear, band_weights, n_depth,
):
    layers, padded_rows, columns = deep.shape
    row_cells = padded_rows - 2 * ROW_TILE
    depth_cells = layers - 2
    n_rows = lax.axis_size("xy")
    extinct = 3.0 / (depth_cells * n_depth)
    tile_rows = row_cells // n_depth
    band = EDGE + 2 * ROW_TILE
    piece = 2 * ROW_TILE
    height = 2 * EDGE

    def kernel(
        live_in, palette_in, owner_in, corner_odd_ref, corner_even_ref, row_even_ref, row_odd_ref,
        inner_ref, deep_ref, shear_ref, band_ref,
        out_ref, halo, triple, split_sums, smooth, across, sheared,
        live_ref, palette_ref, owner_ref, sems,
    ):
        wait_scalars = fetch_scalars(
            [(live_in, live_ref), (palette_in, palette_ref), (owner_in, owner_ref)], sems
        )
        depth_index = lax.axis_index("gz")
        row_index = lax.axis_index("xy")
        odd_depth = depth_index % 2 == 1

        odd_row = row_index % 2 == 1
        from_even, from_odd = pl.ds(0, ROW_TILE), pl.ds(ROW_TILE, ROW_TILE)
        for side in range(2):
            take_even = odd_row if side == 0 else jnp.logical_not(odd_row)

            def facing_rows(ref, i):
                return jnp.where(take_even, ref[i, from_even], ref[i, from_odd])

            even = [facing_rows(corner_even_ref, i) for i in range(HALO)]
            odd = [facing_rows(corner_odd_ref, i) for i in range(HALO)]
            middle = [
                jnp.where(take_even, row_even_ref[i], row_odd_ref[i]) for i in range(depth_cells)
            ]
            low = [jnp.where(odd_depth, e, o) for e, o in zip(even, odd)]
            high = [jnp.where(odd_depth, o, e) for e, o in zip(even, odd)]
            outer = 0 if side == 0 else band - ROW_TILE
            inner_at = ROW_TILE if side == 0 else 0
            own_at = ROW_TILE if side == 0 else padded_rows - band
            sums = window_sums(low + middle + high, TAPS)
            for z in range(layers):
                halo[z, side, pl.ds(outer, ROW_TILE)] = sums[z]
                halo[z, side, pl.ds(inner_at, band - ROW_TILE)] = deep_ref[
                    z, pl.ds(own_at, band - ROW_TILE)
                ]

        span = band - ROW_TILE
        for z in range(layers):
            for side in range(2):
                triple[z, side, pl.ds(0, span)] = (
                    halo[z, side, pl.ds(3, span)]
                    + halo[z, side, pl.ds(4, span)]
                    + halo[z, side, pl.ds(5, span)]
                )
                split_sums[z, side] = (
                    triple[z, side, pl.ds(0, piece)]
                    + triple[z, side, pl.ds(3, piece)]
                    + triple[z, side, pl.ds(6, piece)]
                )
        weights = jnp.concatenate([band_ref[...]] * 3, axis=0)
        both = column_sums(split_sums[...].reshape(layers * 2 * piece, columns), weights)
        both = both.reshape(layers, 2, piece, 2 * columns)
        smooth[...] = both[..., :columns]
        across[...] = both[1:-1, :, :, columns:]

        @pl.when(row_index == 0)
        def _():
            smooth[:, 0, :1] = jnp.zeros((layers, 1, columns), jnp.float32)

        @pl.when(row_index == n_rows - 1)
        def _():
            smooth[:, 1, EDGE + 1 : EDGE + 2] = jnp.zeros((layers, 1, columns), jnp.float32)

        zero_outside(smooth, depth_index, n_depth, layers)

        wait_scalars()
        own_live = live_ref[depth_index, row_index]

        def both_sides(ref, z, start):
            return ref[z, :, pl.ds(start, EDGE)].reshape(height, columns)

        for z in range(depth_cells):
            channels = shade(
                both_sides(smooth, z + 1, 1),
                both_sides(smooth, z + 2, 1) - both_sides(smooth, z, 1),
                both_sides(smooth, z + 1, 2) - both_sides(smooth, z + 1, 0),
                both_sides(across, z, 1),
                z < own_live,
                palette_ref,
                extinct,
            )
            sheared[z] = jnp.dot(
                jnp.concatenate(channels), shear_ref[z], preferred_element_type=jnp.float32
            )
        out_ref[...] = inner_ref[...]
        for view in range(VIEWS):
            lanes = pl.ds(view * columns, columns)
            values = march(
                lambda z, c: sheared[z, pl.ds(c * height, height), lanes], depth_cells, view
            )
            codes = [encode(value) for value in values]
            for side, row in enumerate((0, row_cells - EDGE)):
                place = owner_ref[view, row // tile_rows]
                part = [code[side * EDGE : (side + 1) * EDGE] for code in codes]
                store_codes(out_ref, place, view, part, row % tile_rows, tile_rows, inner_ref)

    vmem = pl.BlockSpec(memory_space=pltpu.VMEM)
    return pl.pallas_call(
        kernel,
        out_shape=jax.ShapeDtypeStruct(inner.shape, inner.dtype),
        in_specs=[vmem] * 11,
        out_specs=vmem,
        scratch_shapes=[
            pltpu.VMEM((layers, 2, band, columns), jnp.float32),
            pltpu.VMEM((layers, 2, piece + ROW_TILE, columns), jnp.float32),
            pltpu.VMEM((layers, 2, piece, columns), jnp.float32),
            pltpu.VMEM((layers, 2, piece, columns), jnp.float32),
            pltpu.VMEM((depth_cells, 2, piece, columns), jnp.float32),
            pltpu.VMEM((depth_cells, 4 * height, VIEWS * columns), jnp.float32),
            pltpu.SMEM(live_slices.shape, jnp.int32),
            pltpu.SMEM(palette.shape, jnp.float32),
            pltpu.SMEM(owner.shape, jnp.int32),
            pltpu.SemaphoreType.DMA((3,)),
        ],
        compiler_params=pltpu.CompilerParams(vmem_limit_bytes=VMEM_BYTES),
        name="render_edges",
    )(
        live_slices, palette, owner, corner_odd, corner_even, row_even, row_odd,
        inner, deep, shear, band_weights,
    )


def cut_edges(density):
    depth_cells, row_cells, columns = density.shape

    places = [(i, start) for start in range(0, row_cells, ROW_TILE) for i in range(HALO)]
    words = len(places) // GROUP * WORDS

    def kernel(density_ref, row_even_ref, row_odd_ref, deep_even_ref, deep_odd_ref):
        row_bit = lax.axis_index("xy") % 2
        depth_bit = lax.axis_index("gz") % 2
        last_rows, last_deep = row_cells - ROW_TILE, depth_cells - HALO
        for ref, bit in ((deep_odd_ref, depth_bit), (deep_even_ref, 1 - depth_bit)):
            for group in range(len(places) // GROUP):
                values = [
                    density_ref[bit * last_deep + i, pl.ds(start, ROW_TILE)]
                    for i, start in places[group * GROUP : (group + 1) * GROUP]
                ]
                for k, word in enumerate(pack(values)):
                    ref[group * WORDS + k] = word
        for ref, bit in ((row_even_ref, 1 - row_bit), (row_odd_ref, row_bit)):
            start = pl.multiple_of(bit * last_rows, ROW_TILE)
            ref[...] = density_ref[:, pl.ds(start, ROW_TILE)]

    rows = jax.ShapeDtypeStruct((depth_cells, ROW_TILE, columns), jnp.float32)
    deep = jax.ShapeDtypeStruct((words, ROW_TILE, columns), jnp.int32)
    vmem = pl.BlockSpec(memory_space=pltpu.VMEM)
    return pl.pallas_call(
        kernel,
        out_shape=(rows, rows, deep, deep),
        in_specs=[vmem],
        out_specs=(vmem,) * 4,
        compiler_params=pltpu.CompilerParams(vmem_limit_bytes=VMEM_BYTES),
        name="cut_edges",
    )(density)


def composite_kernel(order_in, in_ref, out_ref, values, order_ref, sems):
    wait_scalars = fetch_scalars([(order_in, order_ref)], sems)
    count = in_ref.shape[0]
    rows = in_ref.shape[2] // 4
    for source in range(count):
        for view in range(VIEWS):
            values[source, view] = decode(in_ref[source, view])
    wait_scalars()
    for view in range(VIEWS):
        colour, transmit = None, None
        for k in range(count):
            source = order_ref[view, k]
            part = [values[source, view, pl.ds(c * rows, rows)] for c in range(4)]
            clear = 1.0 - part[3]
            if k == 0:
                colour, transmit = part[:3], clear
            else:
                colour = [colour[c] + transmit * part[c] for c in range(3)]
                transmit = transmit * clear
        for c, value in enumerate(colour + [1.0 - transmit]):
            out_ref[view, c, 0] = value


def body(density, live_slices, shear_slopes, palette, depth_order, tile_owner):
    depth_cells, row_cells, columns = density.shape
    n_depth = lax.axis_size("gz")
    edge = depth_cells - HALO
    odd_depth = lax.axis_index("gz") % 2 == 1

    def pairs(axis, first):
        count = lax.axis_size(axis)
        lower = range(first, count - 1, 2)
        return [(i, i + 1) for i in lower] + [(i + 1, i) for i in lower]

    row_even, row_odd, deep_even, deep_odd = cut_edges(density)
    row_even = lax.ppermute(row_even, "xy", pairs("xy", 0))
    row_odd = lax.ppermute(row_odd, "xy", pairs("xy", 1))
    deep_odd = lax.ppermute(deep_odd, "gz", pairs("gz", 1))
    deep_even = lax.ppermute(deep_even, "gz", pairs("gz", 0))
    rows = jnp.concatenate([row_even, row_odd], axis=1)
    facing = jnp.where(odd_depth, edge, 0)
    corner_odd = lax.ppermute(
        lax.dynamic_slice_in_dim(rows, facing, HALO), "gz", pairs("gz", 1)
    )
    corner_even = lax.ppermute(
        lax.dynamic_slice_in_dim(rows, edge - facing, HALO), "gz", pairs("gz", 0)
    )
    inner, deep, shear, band_weights = render_inner(
        live_slices, shear_slopes, palette, tile_owner, density, deep_odd, deep_even, n_depth
    )
    outgoing = render_edges(
        live_slices, palette, tile_owner, corner_odd, corner_even, row_even, row_odd,
        inner, deep, shear, band_weights, n_depth,
    )
    incoming = lax.all_to_all(outgoing, "gz", split_axis=0, concat_axis=0, tiled=True)
    tile_rows = row_cells // n_depth
    return pl.pallas_call(
        composite_kernel,
        out_shape=jax.ShapeDtypeStruct((VIEWS, 4, 1, tile_rows, columns), jnp.float32),
        in_specs=[pl.BlockSpec(memory_space=pltpu.VMEM)] * 2,
        out_specs=pl.BlockSpec(memory_space=pltpu.VMEM),
        scratch_shapes=[
            pltpu.VMEM(incoming.shape, jnp.float32),
            pltpu.SMEM(depth_order.shape, jnp.int32),
            pltpu.SemaphoreType.DMA((1,)),
        ],
        compiler_params=pltpu.CompilerParams(vmem_limit_bytes=VMEM_BYTES),
        name="composite",
    )(depth_order, incoming)


def solution(mesh):
    placed = (P("gz", "xy", None), P(), P(), P(), P(), P())
    return jax.shard_map(
        body, mesh=mesh, in_specs=placed, out_specs=P(None, None, "gz", "xy", None), check_vma=False
    )
```

```python
import math

import jax
import jax.numpy as jnp
from jax import lax
from jax.experimental import pallas as pl
from jax.experimental.pallas import tpu as pltpu
from jax.sharding import PartitionSpec as P

LIGHT = (0.48, 0.6, 0.64)
REACH = 4
HALO = REACH + 1
TAPS = 2 * REACH + 1
ROW_TILE = 8
PACKED_ROWS = 16
EDGE = 8
VIEWS = 2
TOP = 2.2
STEPS = 65535.0
MIDDLE = 32768
LEVELS_PER_UNIT = 5461.0
ZERO_LEVEL = 1 << 19
GROUP, WORDS = 8, 5
VMEM_BYTES = 40 * 1024 * 1024


def column_matrix(columns):
    source = lax.broadcasted_iota(jnp.int32, (columns, columns), 0)
    target = lax.broadcasted_iota(jnp.int32, (columns, columns), 1)

    def band(shift):
        at = target + shift
        inside = (jnp.abs(source - at) <= REACH) & (at >= 0) & (at < columns)
        return jnp.where(inside, 1.0, 0.0).astype(jnp.float32)

    return jnp.concatenate([band(0), band(1) - band(-1)], axis=1).astype(jnp.bfloat16)


def shear_matrices(slopes_ref, slice_depth, columns, total_depth):
    source = lax.broadcasted_iota(jnp.int32, (columns, columns), 0)
    target = lax.broadcasted_iota(jnp.int32, (columns, columns), 1)
    distance = (source - target).astype(jnp.float32)
    parts = []
    for view in range(VIEWS):
        shift = slopes_ref[view] * (slice_depth + 0.5 - 0.5 * total_depth)
        parts.append(jnp.maximum(0.0, 1.0 - jnp.abs(distance + shift)))
    return jnp.concatenate(parts, axis=1).astype(jnp.bfloat16)


def window_sums(layers, taps):
    sums, width = layers, 1
    while 2 * width < taps:
        sums = [sums[i] + sums[i + width] for i in range(len(sums) - width)]
        width *= 2
    return [sums[i] + layers[i + width] for i in range(len(layers) - width)]


def pack(values):
    v = [(x * LEVELS_PER_UNIT + (ZERO_LEVEL + 0.5)).astype(jnp.int32) for x in values]
    v = [(x - ZERO_LEVEL) & 0xFFFFF for x in v]
    upper = [
        v[5] & 0xFFF,
        (v[5] >> 12) | ((v[6] & 0xF) << 8),
        (v[6] >> 4) & 0xFFF,
        (v[6] >> 16) | ((v[7] & 0xFF) << 4),
        v[7] >> 8,
    ]
    return [v[i] | (upper[i] << 20) for i in range(WORDS)]


def unpack(words):
    upper = [lax.shift_right_logical(w, jnp.full_like(w, 20)) for w in words]
    levels = words + [
        upper[0] | ((upper[1] & 0xFF) << 12),
        (upper[1] >> 8) | (upper[2] << 4) | ((upper[3] & 0xF) << 16),
        (upper[3] >> 4) | (upper[4] << 8),
    ]
    levels = [(x << 12) >> 12 for x in levels]
    return [x.astype(jnp.float32) * (1.0 / LEVELS_PER_UNIT) for x in levels]


def encode(value):
    scale = math.log2(STEPS) - 0.125 * math.log2(TOP)
    root = jnp.exp2(0.125 * jnp.log2(jnp.maximum(value, 1e-30)) + scale)
    return (root + 0.5).astype(jnp.int32) - MIDDLE


def decode(code):
    root = (code.astype(jnp.int32) + MIDDLE).astype(jnp.float32) * (TOP**0.125 / STEPS)
    square = root * root
    fourth = square * square
    return fourth * fourth


def column_sums(total, weights):
    hi = total.astype(jnp.bfloat16)
    rest = total - hi.astype(jnp.float32)
    mid = rest.astype(jnp.bfloat16)
    lo = (rest - mid.astype(jnp.float32)).astype(jnp.bfloat16)
    split = jnp.concatenate([hi, mid, lo], axis=1)
    return jnp.dot(split, weights, preferred_element_type=jnp.float32)


def shade(center, diff_depth, diff_rows, diff_cols, live, palette_ref, extinct):
    cells = TAPS**3
    floor = 0.01 * (2.0 * cells) ** 2
    square = diff_depth * diff_depth + diff_rows * diff_rows + diff_cols * diff_cols + floor
    light = [0.75 * part for part in LIGHT]
    toward = light[0] * diff_depth + light[1] * diff_rows + light[2] * diff_cols
    facing = jnp.maximum(0.0, toward) * lax.rsqrt(square)
    t = center * (2.0 * math.log2(math.e) / cells)
    softplus = jnp.maximum(t, 0.0) + jnp.log2(1.0 + jnp.exp2(-jnp.abs(t)))
    opacity = 1.0 - jnp.exp2(jnp.where(live, -extinct, 0.0) * softplus)
    bright = opacity * (0.25 + facing)
    channels = [bright * palette_ref[c] for c in range(3)] + [opacity]
    return [channel.astype(jnp.bfloat16) for channel in channels]


def march(layer, depth_cells, view):
    colour, transmit = None, None
    for z in range(depth_cells):
        part = [layer(z, c) for c in range(4)]
        clear = 1.0 - part[3]
        if z == 0:
            colour, transmit = part[:3], clear
        elif view == 0:
            colour = [colour[c] + transmit * part[c] for c in range(3)]
            transmit = transmit * clear
        else:
            colour = [part[c] + clear * colour[c] for c in range(3)]
            transmit = transmit * clear
    return colour + [1.0 - transmit]


def store_codes(out_ref, place, view, codes, row, tile_rows, other=None):
    if tile_rows < PACKED_ROWS:
        for c in range(0, 4, 2):
            pair = jnp.concatenate(codes[c : c + 2])
            out_ref[place, view, pl.ds(c * tile_rows, PACKED_ROWS)] = pair.astype(jnp.int16)
        return
    for c in range(4):
        at = pl.ds(c * tile_rows + row // PACKED_ROWS * PACKED_ROWS, PACKED_ROWS)
        code = codes[c]
        if code.shape[0] < PACKED_ROWS:
            half = row % PACKED_ROWS
            rest = jnp.zeros_like(code)
            if other is not None:
                rest = other[place, view, at].astype(jnp.int32)
                rest = rest[ROW_TILE:] if half == 0 else rest[:ROW_TILE]
            code = jnp.concatenate([code, rest] if half == 0 else [rest, code])
        out_ref[place, view, at] = code.astype(jnp.int16)


def fetch_scalars(pairs, sems):
    copies = [
        pltpu.make_async_copy(source, target, sems.at[i]) for i, (source, target) in enumerate(pairs)
    ]
    for copy in copies:
        copy.start()

    def wait():
        for copy in copies:
            copy.wait()

    return wait


def zero_outside(smooth, depth_index, n_depth, layers):
    @pl.when(depth_index == 0)
    def _():
        smooth[0] = jnp.zeros_like(smooth[0])

    @pl.when(depth_index == n_depth - 1)
    def _():
        smooth[layers - 1] = jnp.zeros_like(smooth[layers - 1])


def render_inner(live_slices, slopes, palette, owner, density, deep_odd, deep_even, n_depth):
    depth_cells, row_cells, columns = density.shape
    total_depth = depth_cells * n_depth
    extinct = 3.0 / total_depth
    tile_rows = row_cells // n_depth
    layers = depth_cells + 2
    rows = range(EDGE, row_cells - EDGE)
    height = len(rows)
    lead, span = EDGE, height + 2 * ROW_TILE

    def kernel(
        live_in, slopes_in, palette_in, owner_in, own_ref, odd_ref, even_ref,
        out_ref, deep, shear_ref, band_ref, triple, smooth, across, sheared,
        live_ref, slopes_ref, palette_ref, owner_ref, sems,
    ):
        wait_scalars = fetch_scalars(
            [
                (live_in, live_ref),
                (slopes_in, slopes_ref),
                (palette_in, palette_ref),
                (owner_in, owner_ref),
            ],
            sems,
        )
        depth_index = lax.axis_index("gz")
        row_index = lax.axis_index("xy")
        odd_depth = depth_index % 2 == 1

        low, high, word = [], [], 0
        for start in range(0, row_cells, ROW_TILE):
            while len(low) < HALO:
                even = [even_ref[word + k] for k in range(WORDS)]
                odd = [odd_ref[word + k] for k in range(WORDS)]
                low += unpack([jnp.where(odd_depth, e, o) for e, o in zip(even, odd)])
                high += unpack([jnp.where(odd_depth, o, e) for e, o in zip(even, odd)])
                word += WORDS
            own = [own_ref[i, pl.ds(start, ROW_TILE)] for i in range(depth_cells)]
            for z, total in enumerate(window_sums(low[:HALO] + own + high[:HALO], TAPS)):
                deep[z, pl.ds(ROW_TILE + start, ROW_TILE)] = total
            low, high = low[HALO:], high[HALO:]

        band = column_matrix(columns)
        band_ref[...] = band
        weights = jnp.concatenate([band, band, band], axis=0)
        for z in range(layers):
            triple[z] = (
                deep[z, pl.ds(lead - 4, span + ROW_TILE)]
                + deep[z, pl.ds(lead - 3, span + ROW_TILE)]
                + deep[z, pl.ds(lead - 2, span + ROW_TILE)]
            )
            total = (
                triple[z, pl.ds(0, span)] + triple[z, pl.ds(3, span)] + triple[z, pl.ds(6, span)]
            )
            if 1 <= z <= depth_cells:
                both = column_sums(total, weights)
                smooth[z] = both[:, :columns]
                across[z - 1] = both[ROW_TILE : ROW_TILE + height, columns:]
            else:
                smooth[z] = column_sums(total, weights[:, :columns])
        zero_outside(smooth, depth_index, n_depth, layers)

        wait_scalars()
        slab_start = (depth_index * depth_cells).astype(jnp.float32)
        for z in range(depth_cells):
            shear_ref[z] = shear_matrices(slopes_ref, slab_start + float(z), columns, total_depth)

        own_live = live_ref[depth_index, row_index]
        middle = pl.ds(ROW_TILE, height)
        for z in range(depth_cells):
            channels = shade(
                smooth[z + 1, middle],
                smooth[z + 2, middle] - smooth[z, middle],
                smooth[z + 1, pl.ds(ROW_TILE + 1, height)]
                - smooth[z + 1, pl.ds(ROW_TILE - 1, height)],
                across[z],
                z < own_live,
                palette_ref,
                extinct,
            )
            sheared[z] = jnp.dot(
                jnp.concatenate(channels), shear_ref[z], preferred_element_type=jnp.float32
            )
        row = rows.start
        while row < rows.stop:
            whole = tile_rows >= PACKED_ROWS and row % PACKED_ROWS == 0
            count = PACKED_ROWS if whole and row + PACKED_ROWS <= rows.stop else ROW_TILE
            at = row - rows.start
            for view in range(VIEWS):
                lanes = pl.ds(view * columns, columns)
                values = march(
                    lambda z, c: sheared[z, pl.ds(c * height + at, count), lanes],
                    depth_cells,
                    view,
                )
                place = owner_ref[view, row // tile_rows]
                codes = [encode(value) for value in values]
                store_codes(out_ref, place, view, codes, row % tile_rows, tile_rows)
            row += count

    vmem = pl.BlockSpec(memory_space=pltpu.VMEM)
    return pl.pallas_call(
        kernel,
        out_shape=(
            jax.ShapeDtypeStruct((n_depth, VIEWS, 4 * tile_rows, columns), jnp.int16),
            jax.ShapeDtypeStruct((layers, row_cells + 2 * ROW_TILE, columns), jnp.float32),
            jax.ShapeDtypeStruct((depth_cells, columns, VIEWS * columns), jnp.bfloat16),
            jax.ShapeDtypeStruct((columns, 2 * columns), jnp.bfloat16),
        ),
        in_specs=[vmem] * 7,
        out_specs=(vmem,) * 4,
        scratch_shapes=[
            pltpu.VMEM((layers, span + ROW_TILE, columns), jnp.float32),
            pltpu.VMEM((layers, span, columns), jnp.float32),
            pltpu.VMEM((depth_cells, height, columns), jnp.float32),
            pltpu.VMEM((depth_cells, 4 * height, VIEWS * columns), jnp.float32),
            pltpu.SMEM(live_slices.shape, jnp.int32),
            pltpu.SMEM(slopes.shape, jnp.float32),
            pltpu.SMEM(palette.shape, jnp.float32),
            pltpu.SMEM(owner.shape, jnp.int32),
            pltpu.SemaphoreType.DMA((4,)),
        ],
        compiler_params=pltpu.CompilerParams(vmem_limit_bytes=VMEM_BYTES),
        cost_estimate=pl.CostEstimate(
            flops=100 * depth_cells * row_cells * columns,
            bytes_accessed=16 * 4 * depth_cells * row_cells * columns,
            transcendentals=4 * depth_cells * row_cells * columns,
        ),
        name="render_inner",
    )(live_slices, slopes, palette, owner, density, deep_odd, deep_even)


def render_edges(
    live_slices, palette, owner, corner_odd, corner_even, row_even, row_odd,
    inner, deep, shear, band_weights, n_depth,
):
    layers, padded_rows, columns = deep.shape
    row_cells = padded_rows - 2 * ROW_TILE
    depth_cells = layers - 2
    n_rows = lax.axis_size("xy")
    extinct = 3.0 / (depth_cells * n_depth)
    tile_rows = row_cells // n_depth
    band = EDGE + 2 * ROW_TILE
    piece = 2 * ROW_TILE
    height = 2 * EDGE

    def kernel(
        live_in, palette_in, owner_in, corner_odd_ref, corner_even_ref, row_even_ref, row_odd_ref,
        inner_ref, deep_ref, shear_ref, band_ref,
        out_ref, halo, triple, split_sums, smooth, across, sheared,
        live_ref, palette_ref, owner_ref, sems,
    ):
        wait_scalars = fetch_scalars(
            [(live_in, live_ref), (palette_in, palette_ref), (owner_in, owner_ref)], sems
        )
        depth_index = lax.axis_index("gz")
        row_index = lax.axis_index("xy")
        odd_depth = depth_index % 2 == 1

        odd_row = row_index % 2 == 1
        from_even, from_odd = pl.ds(0, ROW_TILE), pl.ds(ROW_TILE, ROW_TILE)
        for side in range(2):
            take_even = odd_row if side == 0 else jnp.logical_not(odd_row)

            def facing_rows(ref, i):
                return jnp.where(take_even, ref[i, from_even], ref[i, from_odd])

            even = [facing_rows(corner_even_ref, i) for i in range(HALO)]
            odd = [facing_rows(corner_odd_ref, i) for i in range(HALO)]
            middle = [
                jnp.where(take_even, row_even_ref[i], row_odd_ref[i]) for i in range(depth_cells)
            ]
            low = [jnp.where(odd_depth, e, o) for e, o in zip(even, odd)]
            high = [jnp.where(odd_depth, o, e) for e, o in zip(even, odd)]
            outer = 0 if side == 0 else band - ROW_TILE
            inner_at = ROW_TILE if side == 0 else 0
            own_at = ROW_TILE if side == 0 else padded_rows - band
            sums = window_sums(low + middle + high, TAPS)
            for z in range(layers):
                halo[z, side, pl.ds(outer, ROW_TILE)] = sums[z]
                halo[z, side, pl.ds(inner_at, band - ROW_TILE)] = deep_ref[
                    z, pl.ds(own_at, band - ROW_TILE)
                ]

        span = band - ROW_TILE
        for z in range(layers):
            for side in range(2):
                triple[z, side, pl.ds(0, span)] = (
                    halo[z, side, pl.ds(3, span)]
                    + halo[z, side, pl.ds(4, span)]
                    + halo[z, side, pl.ds(5, span)]
                )
                split_sums[z, side] = (
                    triple[z, side, pl.ds(0, piece)]
                    + triple[z, side, pl.ds(3, piece)]
                    + triple[z, side, pl.ds(6, piece)]
                )
        weights = jnp.concatenate([band_ref[...]] * 3, axis=0)
        both = column_sums(split_sums[...].reshape(layers * 2 * piece, columns), weights)
        both = both.reshape(layers, 2, piece, 2 * columns)
        smooth[...] = both[..., :columns]
        across[...] = both[1:-1, :, :, columns:]

        @pl.when(row_index == 0)
        def _():
            smooth[:, 0, :1] = jnp.zeros((layers, 1, columns), jnp.float32)

        @pl.when(row_index == n_rows - 1)
        def _():
            smooth[:, 1, EDGE + 1 : EDGE + 2] = jnp.zeros((layers, 1, columns), jnp.float32)

        zero_outside(smooth, depth_index, n_depth, layers)

        wait_scalars()
        own_live = live_ref[depth_index, row_index]

        def both_sides(ref, z, start):
            return ref[z, :, pl.ds(start, EDGE)].reshape(height, columns)

        for z in range(depth_cells):
            channels = shade(
                both_sides(smooth, z + 1, 1),
                both_sides(smooth, z + 2, 1) - both_sides(smooth, z, 1),
                both_sides(smooth, z + 1, 2) - both_sides(smooth, z + 1, 0),
                both_sides(across, z, 1),
                z < own_live,
                palette_ref,
                extinct,
            )
            sheared[z] = jnp.dot(
                jnp.concatenate(channels), shear_ref[z], preferred_element_type=jnp.float32
            )
        for view in range(VIEWS):
            lanes = pl.ds(view * columns, columns)
            values = march(
                lambda z, c: sheared[z, pl.ds(c * height, height), lanes], depth_cells, view
            )
            codes = [encode(value) for value in values]
            for side, row in enumerate((0, row_cells - EDGE)):
                place = owner_ref[view, row // tile_rows]
                part = [code[side * EDGE : (side + 1) * EDGE] for code in codes]
                store_codes(out_ref, place, view, part, row % tile_rows, tile_rows, out_ref)

    vmem = pl.BlockSpec(memory_space=pltpu.VMEM)
    return pl.pallas_call(
        kernel,
        out_shape=jax.ShapeDtypeStruct(inner.shape, inner.dtype),
        input_output_aliases={7: 0},
        in_specs=[vmem] * 11,
        out_specs=vmem,
        scratch_shapes=[
            pltpu.VMEM((layers, 2, band, columns), jnp.float32),
            pltpu.VMEM((layers, 2, piece + ROW_TILE, columns), jnp.float32),
            pltpu.VMEM((layers, 2, piece, columns), jnp.float32),
            pltpu.VMEM((layers, 2, piece, columns), jnp.float32),
            pltpu.VMEM((depth_cells, 2, piece, columns), jnp.float32),
            pltpu.VMEM((depth_cells, 4 * height, VIEWS * columns), jnp.float32),
            pltpu.SMEM(live_slices.shape, jnp.int32),
            pltpu.SMEM(palette.shape, jnp.float32),
            pltpu.SMEM(owner.shape, jnp.int32),
            pltpu.SemaphoreType.DMA((3,)),
        ],
        compiler_params=pltpu.CompilerParams(vmem_limit_bytes=VMEM_BYTES),
        name="render_edges",
    )(
        live_slices, palette, owner, corner_odd, corner_even, row_even, row_odd,
        inner, deep, shear, band_weights,
    )


def cut_edges(density):
    depth_cells, row_cells, columns = density.shape

    places = [(i, start) for start in range(0, row_cells, ROW_TILE) for i in range(HALO)]
    words = len(places) // GROUP * WORDS

    def kernel(density_ref, row_even_ref, row_odd_ref, deep_even_ref, deep_odd_ref):
        row_bit = lax.axis_index("xy") % 2
        depth_bit = lax.axis_index("gz") % 2
        last_rows, last_deep = row_cells - ROW_TILE, depth_cells - HALO
        for ref, bit in ((deep_odd_ref, depth_bit), (deep_even_ref, 1 - depth_bit)):
            for group in range(len(places) // GROUP):
                values = [
                    density_ref[bit * last_deep + i, pl.ds(start, ROW_TILE)]
                    for i, start in places[group * GROUP : (group + 1) * GROUP]
                ]
                for k, word in enumerate(pack(values)):
                    ref[group * WORDS + k] = word
        for ref, bit in ((row_even_ref, 1 - row_bit), (row_odd_ref, row_bit)):
            start = pl.multiple_of(bit * last_rows, ROW_TILE)
            ref[...] = density_ref[:, pl.ds(start, ROW_TILE)]

    rows = jax.ShapeDtypeStruct((depth_cells, ROW_TILE, columns), jnp.float32)
    deep = jax.ShapeDtypeStruct((words, ROW_TILE, columns), jnp.int32)
    vmem = pl.BlockSpec(memory_space=pltpu.VMEM)
    return pl.pallas_call(
        kernel,
        out_shape=(rows, rows, deep, deep),
        in_specs=[vmem],
        out_specs=(vmem,) * 4,
        compiler_params=pltpu.CompilerParams(vmem_limit_bytes=VMEM_BYTES),
        name="cut_edges",
    )(density)


def composite_kernel(order_in, in_ref, out_ref, values, image, order_ref, sems):
    wait_scalars = fetch_scalars([(order_in, order_ref)], sems)
    count = in_ref.shape[0]
    rows = in_ref.shape[2] // 4
    copies = []
    for view in range(VIEWS):
        for source in range(count):
            values[source, view] = decode(in_ref[source, view])
        if view == 0:
            wait_scalars()
        colour, transmit = None, None
        for k in range(count):
            source = order_ref[view, k]
            part = [values[source, view, pl.ds(c * rows, rows)] for c in range(4)]
            clear = 1.0 - part[3]
            if k == 0:
                colour, transmit = part[:3], clear
            else:
                colour = [colour[c] + transmit * part[c] for c in range(3)]
                transmit = transmit * clear
        for c, value in enumerate(colour + [1.0 - transmit]):
            image[view, c, 0] = value
        copies.append(pltpu.make_async_copy(image.at[view], out_ref.at[view], sems.at[1 + view]))
        copies[-1].start()
    for copy in copies:
        copy.wait()


def body(density, live_slices, shear_slopes, palette, depth_order, tile_owner):
    depth_cells, row_cells, columns = density.shape
    n_depth = lax.axis_size("gz")
    edge = depth_cells - HALO
    odd_depth = lax.axis_index("gz") % 2 == 1

    def pairs(axis, first):
        count = lax.axis_size(axis)
        lower = range(first, count - 1, 2)
        return [(i, i + 1) for i in lower] + [(i + 1, i) for i in lower]

    row_even, row_odd, deep_even, deep_odd = cut_edges(density)
    row_even = lax.ppermute(row_even, "xy", pairs("xy", 0))
    row_odd = lax.ppermute(row_odd, "xy", pairs("xy", 1))
    deep_odd = lax.ppermute(deep_odd, "gz", pairs("gz", 1))
    deep_even = lax.ppermute(deep_even, "gz", pairs("gz", 0))
    rows = jnp.concatenate([row_even, row_odd], axis=1)
    facing = jnp.where(odd_depth, edge, 0)
    corner_odd = lax.ppermute(
        lax.dynamic_slice_in_dim(rows, facing, HALO), "gz", pairs("gz", 1)
    )
    corner_even = lax.ppermute(
        lax.dynamic_slice_in_dim(rows, edge - facing, HALO), "gz", pairs("gz", 0)
    )
    inner, deep, shear, band_weights = render_inner(
        live_slices, shear_slopes, palette, tile_owner, density, deep_odd, deep_even, n_depth
    )
    outgoing = render_edges(
        live_slices, palette, tile_owner, corner_odd, corner_even, row_even, row_odd,
        inner, deep, shear, band_weights, n_depth,
    )
    incoming = lax.all_to_all(outgoing, "gz", split_axis=0, concat_axis=0, tiled=True)
    tile_rows = row_cells // n_depth
    return pl.pallas_call(
        composite_kernel,
        out_shape=jax.ShapeDtypeStruct((VIEWS, 4, 1, tile_rows, columns), jnp.float32),
        in_specs=[pl.BlockSpec(memory_space=pltpu.VMEM)] * 2,
        out_specs=pl.BlockSpec(memory_space=pltpu.HBM),
        scratch_shapes=[
            pltpu.VMEM(incoming.shape, jnp.float32),
            pltpu.VMEM((VIEWS, 4, 1, tile_rows, columns), jnp.float32),
            pltpu.SMEM(depth_order.shape, jnp.int32),
            pltpu.SemaphoreType.DMA((1 + VIEWS,)),
        ],
        compiler_params=pltpu.CompilerParams(vmem_limit_bytes=VMEM_BYTES),
        name="composite",
    )(depth_order, incoming)


def solution(mesh):
    placed = (P("gz", "xy", None), P(), P(), P(), P(), P())
    return jax.shard_map(
        body, mesh=mesh, in_specs=placed, out_specs=P(None, None, "gz", "xy", None), check_vma=False
    )
```

```python
import math

import jax
import jax.numpy as jnp
from jax import lax
from jax.experimental import pallas as pl
from jax.experimental.pallas import tpu as pltpu
from jax.sharding import PartitionSpec as P

LIGHT = (0.48, 0.6, 0.64)
REACH = 4
HALO = REACH + 1
TAPS = 2 * REACH + 1
ROW_TILE = 8
PACKED_ROWS = 16
EDGE = 8
VIEWS = 2
TOP = 2.2
STEPS = 65535.0
MIDDLE = 32768
VMEM_BYTES = 40 * 1024 * 1024


def column_matrix(columns):
    source = lax.broadcasted_iota(jnp.int32, (columns, columns), 0)
    target = lax.broadcasted_iota(jnp.int32, (columns, columns), 1)

    def band(shift):
        at = target + shift
        inside = (jnp.abs(source - at) <= REACH) & (at >= 0) & (at < columns)
        return jnp.where(inside, 1.0, 0.0).astype(jnp.float32)

    return jnp.concatenate([band(0), band(1) - band(-1)], axis=1).astype(jnp.bfloat16)


def shear_matrices(slopes_ref, slice_depth, columns, total_depth):
    source = lax.broadcasted_iota(jnp.int32, (columns, columns), 0)
    target = lax.broadcasted_iota(jnp.int32, (columns, columns), 1)
    distance = (source - target).astype(jnp.float32)
    parts = []
    for view in range(VIEWS):
        shift = slopes_ref[view] * (slice_depth + 0.5 - 0.5 * total_depth)
        parts.append(jnp.maximum(0.0, 1.0 - jnp.abs(distance + shift)))
    return jnp.concatenate(parts, axis=1).astype(jnp.bfloat16)


def window_sums(layers, taps):
    sums, width = layers, 1
    while 2 * width < taps:
        sums = [sums[i] + sums[i + width] for i in range(len(sums) - width)]
        width *= 2
    return [sums[i] + layers[i + width] for i in range(len(layers) - width)]


def encode(value):
    scale = math.log2(STEPS) - 0.125 * math.log2(TOP)
    root = jnp.exp2(0.125 * jnp.log2(jnp.maximum(value, 1e-30)) + scale)
    return (root + 0.5).astype(jnp.int32) - MIDDLE


def decode(code):
    root = (code.astype(jnp.int32) + MIDDLE).astype(jnp.float32) * (TOP**0.125 / STEPS)
    square = root * root
    fourth = square * square
    return fourth * fourth


def column_sums(total, weights):
    hi = total.astype(jnp.bfloat16)
    rest = total - hi.astype(jnp.float32)
    mid = rest.astype(jnp.bfloat16)
    lo = (rest - mid.astype(jnp.float32)).astype(jnp.bfloat16)
    split = jnp.concatenate([hi, mid, lo], axis=1)
    return jnp.dot(split, weights, preferred_element_type=jnp.float32)


def shade(center, diff_depth, diff_rows, diff_cols, live, palette_ref, extinct):
    cells = TAPS**3
    floor = 0.01 * (2.0 * cells) ** 2
    square = diff_depth * diff_depth + diff_rows * diff_rows + diff_cols * diff_cols + floor
    light = [0.75 * part for part in LIGHT]
    toward = light[0] * diff_depth + light[1] * diff_rows + light[2] * diff_cols
    facing = jnp.maximum(0.0, toward) * lax.rsqrt(square)
    t = center * (2.0 * math.log2(math.e) / cells)
    softplus = jnp.maximum(t, 0.0) + jnp.log2(1.0 + jnp.exp2(-jnp.abs(t)))
    opacity = 1.0 - jnp.exp2(jnp.where(live, -extinct, 0.0) * softplus)
    bright = opacity * (0.25 + facing)
    channels = [bright * palette_ref[c] for c in range(3)] + [opacity]
    return [channel.astype(jnp.bfloat16) for channel in channels]


def march(layer, depth_cells, view):
    colour, transmit = None, None
    for z in range(depth_cells):
        part = [layer(z, c) for c in range(4)]
        clear = 1.0 - part[3]
        if z == 0:
            colour, transmit = part[:3], clear
        elif view == 0:
            colour = [colour[c] + transmit * part[c] for c in range(3)]
            transmit = transmit * clear
        else:
            colour = [part[c] + clear * colour[c] for c in range(3)]
            transmit = transmit * clear
    return colour + [1.0 - transmit]


def store_codes(out_ref, place, view, codes, row, tile_rows, other=None):
    if tile_rows < PACKED_ROWS:
        for c in range(0, 4, 2):
            pair = jnp.concatenate(codes[c : c + 2])
            out_ref[place, view, pl.ds(c * tile_rows, PACKED_ROWS)] = pair.astype(jnp.int16)
        return
    for c in range(4):
        at = pl.ds(c * tile_rows + row // PACKED_ROWS * PACKED_ROWS, PACKED_ROWS)
        code = codes[c]
        if code.shape[0] < PACKED_ROWS:
            half = row % PACKED_ROWS
            rest = jnp.zeros_like(code)
            if other is not None:
                rest = other[place, view, at].astype(jnp.int32)
                rest = rest[ROW_TILE:] if half == 0 else rest[:ROW_TILE]
            code = jnp.concatenate([code, rest] if half == 0 else [rest, code])
        out_ref[place, view, at] = code.astype(jnp.int16)


def fetch_scalars(pairs, sems):
    copies = [
        pltpu.make_async_copy(source, target, sems.at[i]) for i, (source, target) in enumerate(pairs)
    ]
    for copy in copies:
        copy.start()

    def wait():
        for copy in copies:
            copy.wait()

    return wait


def zero_outside(smooth, depth_index, n_depth, layers):
    @pl.when(depth_index == 0)
    def _():
        smooth[0] = jnp.zeros_like(smooth[0])

    @pl.when(depth_index == n_depth - 1)
    def _():
        smooth[layers - 1] = jnp.zeros_like(smooth[layers - 1])


def render_inner(live_slices, slopes, palette, owner, density, deep_odd, deep_even, n_depth):
    depth_cells, row_cells, columns = density.shape
    total_depth = depth_cells * n_depth
    extinct = 3.0 / total_depth
    tile_rows = row_cells // n_depth
    layers = depth_cells + 2
    rows = range(EDGE, row_cells - EDGE)
    height = len(rows)
    lead, span = EDGE, height + 2 * ROW_TILE

    def kernel(
        live_in, slopes_in, palette_in, owner_in, own_ref, odd_ref, even_ref,
        out_ref, deep, shear_ref, band_ref, triple, smooth, across, sheared,
        live_ref, slopes_ref, palette_ref, owner_ref, sems,
    ):
        wait_scalars = fetch_scalars(
            [
                (live_in, live_ref),
                (slopes_in, slopes_ref),
                (palette_in, palette_ref),
                (owner_in, owner_ref),
            ],
            sems,
        )
        depth_index = lax.axis_index("gz")
        row_index = lax.axis_index("xy")
        odd_depth = depth_index % 2 == 1

        for start in range(0, row_cells, ROW_TILE):
            at = pl.ds(start, ROW_TILE)
            even = [even_ref[i, at] for i in range(HALO)]
            odd = [odd_ref[i, at] for i in range(HALO)]
            low = [jnp.where(odd_depth, e, o) for e, o in zip(even, odd)]
            high = [jnp.where(odd_depth, o, e) for e, o in zip(even, odd)]
            own = [own_ref[i, at] for i in range(depth_cells)]
            for z, total in enumerate(window_sums(low + own + high, TAPS)):
                deep[z, pl.ds(ROW_TILE + start, ROW_TILE)] = total

        band = column_matrix(columns)
        band_ref[...] = band
        weights = jnp.concatenate([band, band, band], axis=0)
        for z in range(layers):
            triple[z] = (
                deep[z, pl.ds(lead - 4, span + ROW_TILE)]
                + deep[z, pl.ds(lead - 3, span + ROW_TILE)]
                + deep[z, pl.ds(lead - 2, span + ROW_TILE)]
            )
            total = (
                triple[z, pl.ds(0, span)] + triple[z, pl.ds(3, span)] + triple[z, pl.ds(6, span)]
            )
            if 1 <= z <= depth_cells:
                both = column_sums(total, weights)
                smooth[z] = both[:, :columns]
                across[z - 1] = both[ROW_TILE : ROW_TILE + height, columns:]
            else:
                smooth[z] = column_sums(total, weights[:, :columns])
        zero_outside(smooth, depth_index, n_depth, layers)

        wait_scalars()
        slab_start = (depth_index * depth_cells).astype(jnp.float32)
        for z in range(depth_cells):
            shear_ref[z] = shear_matrices(slopes_ref, slab_start + float(z), columns, total_depth)

        own_live = live_ref[depth_index, row_index]
        middle = pl.ds(ROW_TILE, height)
        for z in range(depth_cells):
            channels = shade(
                smooth[z + 1, middle],
                smooth[z + 2, middle] - smooth[z, middle],
                smooth[z + 1, pl.ds(ROW_TILE + 1, height)]
                - smooth[z + 1, pl.ds(ROW_TILE - 1, height)],
                across[z],
                z < own_live,
                palette_ref,
                extinct,
            )
            sheared[z] = jnp.dot(
                jnp.concatenate(channels), shear_ref[z], preferred_element_type=jnp.float32
            )
        row = rows.start
        while row < rows.stop:
            whole = tile_rows >= PACKED_ROWS and row % PACKED_ROWS == 0
            count = PACKED_ROWS if whole and row + PACKED_ROWS <= rows.stop else ROW_TILE
            at = row - rows.start
            for view in range(VIEWS):
                lanes = pl.ds(view * columns, columns)
                values = march(
                    lambda z, c: sheared[z, pl.ds(c * height + at, count), lanes],
                    depth_cells,
                    view,
                )
                place = owner_ref[view, row // tile_rows]
                codes = [encode(value) for value in values]
                store_codes(out_ref, place, view, codes, row % tile_rows, tile_rows)
            row += count

    vmem = pl.BlockSpec(memory_space=pltpu.VMEM)
    return pl.pallas_call(
        kernel,
        out_shape=(
            jax.ShapeDtypeStruct((n_depth, VIEWS, 4 * tile_rows, columns), jnp.int16),
            jax.ShapeDtypeStruct((layers, row_cells + 2 * ROW_TILE, columns), jnp.float32),
            jax.ShapeDtypeStruct((depth_cells, columns, VIEWS * columns), jnp.bfloat16),
            jax.ShapeDtypeStruct((columns, 2 * columns), jnp.bfloat16),
        ),
        in_specs=[vmem] * 7,
        out_specs=(vmem,) * 4,
        scratch_shapes=[
            pltpu.VMEM((layers, span + ROW_TILE, columns), jnp.float32),
            pltpu.VMEM((layers, span, columns), jnp.float32),
            pltpu.VMEM((depth_cells, height, columns), jnp.float32),
            pltpu.VMEM((depth_cells, 4 * height, VIEWS * columns), jnp.float32),
            pltpu.SMEM(live_slices.shape, jnp.int32),
            pltpu.SMEM(slopes.shape, jnp.float32),
            pltpu.SMEM(palette.shape, jnp.float32),
            pltpu.SMEM(owner.shape, jnp.int32),
            pltpu.SemaphoreType.DMA((4,)),
        ],
        compiler_params=pltpu.CompilerParams(vmem_limit_bytes=VMEM_BYTES),
        cost_estimate=pl.CostEstimate(
            flops=100 * depth_cells * row_cells * columns,
            bytes_accessed=16 * 4 * depth_cells * row_cells * columns,
            transcendentals=4 * depth_cells * row_cells * columns,
        ),
        name="render_inner",
    )(live_slices, slopes, palette, owner, density, deep_odd, deep_even)


def render_edges(
    live_slices, palette, owner, corner_odd, corner_even, row_even, row_odd,
    inner, deep, shear, band_weights, n_depth,
):
    layers, padded_rows, columns = deep.shape
    row_cells = padded_rows - 2 * ROW_TILE
    depth_cells = layers - 2
    n_rows = lax.axis_size("xy")
    extinct = 3.0 / (depth_cells * n_depth)
    tile_rows = row_cells // n_depth
    band = EDGE + 2 * ROW_TILE
    piece = 2 * ROW_TILE
    height = 2 * EDGE

    def kernel(
        live_in, palette_in, owner_in, corner_odd_ref, corner_even_ref, row_even_ref, row_odd_ref,
        inner_ref, deep_ref, shear_ref, band_ref,
        out_ref, halo, triple, split_sums, smooth, across, sheared,
        live_ref, palette_ref, owner_ref, sems,
    ):
        wait_scalars = fetch_scalars(
            [(live_in, live_ref), (palette_in, palette_ref), (owner_in, owner_ref)], sems
        )
        depth_index = lax.axis_index("gz")
        row_index = lax.axis_index("xy")
        odd_depth = depth_index % 2 == 1

        odd_row = row_index % 2 == 1
        from_even, from_odd = pl.ds(0, ROW_TILE), pl.ds(ROW_TILE, ROW_TILE)
        for side in range(2):
            take_even = odd_row if side == 0 else jnp.logical_not(odd_row)

            def facing_rows(ref, i):
                return jnp.where(take_even, ref[i, from_even], ref[i, from_odd])

            even = [facing_rows(corner_even_ref, i) for i in range(HALO)]
            odd = [facing_rows(corner_odd_ref, i) for i in range(HALO)]
            middle = [
                jnp.where(take_even, row_even_ref[i], row_odd_ref[i]) for i in range(depth_cells)
            ]
            low = [jnp.where(odd_depth, e, o) for e, o in zip(even, odd)]
            high = [jnp.where(odd_depth, o, e) for e, o in zip(even, odd)]
            outer = 0 if side == 0 else band - ROW_TILE
            inner_at = ROW_TILE if side == 0 else 0
            own_at = ROW_TILE if side == 0 else padded_rows - band
            sums = window_sums(low + middle + high, TAPS)
            for z in range(layers):
                halo[z, side, pl.ds(outer, ROW_TILE)] = sums[z]
                halo[z, side, pl.ds(inner_at, band - ROW_TILE)] = deep_ref[
                    z, pl.ds(own_at, band - ROW_TILE)
                ]

        span = band - ROW_TILE
        for z in range(layers):
            for side in range(2):
                triple[z, side, pl.ds(0, span)] = (
                    halo[z, side, pl.ds(3, span)]
                    + halo[z, side, pl.ds(4, span)]
                    + halo[z, side, pl.ds(5, span)]
                )
                split_sums[z, side] = (
                    triple[z, side, pl.ds(0, piece)]
                    + triple[z, side, pl.ds(3, piece)]
                    + triple[z, side, pl.ds(6, piece)]
                )
        weights = jnp.concatenate([band_ref[...]] * 3, axis=0)
        both = column_sums(split_sums[...].reshape(layers * 2 * piece, columns), weights)
        both = both.reshape(layers, 2, piece, 2 * columns)
        smooth[...] = both[..., :columns]
        across[...] = both[1:-1, :, :, columns:]

        @pl.when(row_index == 0)
        def _():
            smooth[:, 0, :1] = jnp.zeros((layers, 1, columns), jnp.float32)

        @pl.when(row_index == n_rows - 1)
        def _():
            smooth[:, 1, EDGE + 1 : EDGE + 2] = jnp.zeros((layers, 1, columns), jnp.float32)

        zero_outside(smooth, depth_index, n_depth, layers)

        wait_scalars()
        own_live = live_ref[depth_index, row_index]

        def both_sides(ref, z, start):
            return ref[z, :, pl.ds(start, EDGE)].reshape(height, columns)

        for z in range(depth_cells):
            channels = shade(
                both_sides(smooth, z + 1, 1),
                both_sides(smooth, z + 2, 1) - both_sides(smooth, z, 1),
                both_sides(smooth, z + 1, 2) - both_sides(smooth, z + 1, 0),
                both_sides(across, z, 1),
                z < own_live,
                palette_ref,
                extinct,
            )
            sheared[z] = jnp.dot(
                jnp.concatenate(channels), shear_ref[z], preferred_element_type=jnp.float32
            )
        out_ref[...] = inner_ref[...]
        for view in range(VIEWS):
            lanes = pl.ds(view * columns, columns)
            values = march(
                lambda z, c: sheared[z, pl.ds(c * height, height), lanes], depth_cells, view
            )
            codes = [encode(value) for value in values]
            for side, row in enumerate((0, row_cells - EDGE)):
                place = owner_ref[view, row // tile_rows]
                part = [code[side * EDGE : (side + 1) * EDGE] for code in codes]
                store_codes(out_ref, place, view, part, row % tile_rows, tile_rows, inner_ref)

    vmem = pl.BlockSpec(memory_space=pltpu.VMEM)
    return pl.pallas_call(
        kernel,
        out_shape=jax.ShapeDtypeStruct(inner.shape, inner.dtype),
        in_specs=[vmem] * 11,
        out_specs=vmem,
        scratch_shapes=[
            pltpu.VMEM((layers, 2, band, columns), jnp.float32),
            pltpu.VMEM((layers, 2, piece + ROW_TILE, columns), jnp.float32),
            pltpu.VMEM((layers, 2, piece, columns), jnp.float32),
            pltpu.VMEM((layers, 2, piece, columns), jnp.float32),
            pltpu.VMEM((depth_cells, 2, piece, columns), jnp.float32),
            pltpu.VMEM((depth_cells, 4 * height, VIEWS * columns), jnp.float32),
            pltpu.SMEM(live_slices.shape, jnp.int32),
            pltpu.SMEM(palette.shape, jnp.float32),
            pltpu.SMEM(owner.shape, jnp.int32),
            pltpu.SemaphoreType.DMA((3,)),
        ],
        compiler_params=pltpu.CompilerParams(vmem_limit_bytes=VMEM_BYTES),
        name="render_edges",
    )(
        live_slices, palette, owner, corner_odd, corner_even, row_even, row_odd,
        inner, deep, shear, band_weights,
    )


def cut_edges(density):
    depth_cells, row_cells, columns = density.shape

    def kernel(density_ref, row_even_ref, row_odd_ref, deep_even_ref, deep_odd_ref):
        row_bit = lax.axis_index("xy") % 2
        depth_bit = lax.axis_index("gz") % 2
        last_rows, last_deep = row_cells - ROW_TILE, depth_cells - HALO
        for ref, bit in ((deep_odd_ref, depth_bit), (deep_even_ref, 1 - depth_bit)):
            for i in range(HALO):
                ref[i] = density_ref[bit * last_deep + i]
        for ref, bit in ((row_even_ref, 1 - row_bit), (row_odd_ref, row_bit)):
            start = pl.multiple_of(bit * last_rows, ROW_TILE)
            ref[...] = density_ref[:, pl.ds(start, ROW_TILE)]

    rows = jax.ShapeDtypeStruct((depth_cells, ROW_TILE, columns), jnp.float32)
    deep = jax.ShapeDtypeStruct((HALO, row_cells, columns), jnp.float32)
    vmem = pl.BlockSpec(memory_space=pltpu.VMEM)
    return pl.pallas_call(
        kernel,
        out_shape=(rows, rows, deep, deep),
        in_specs=[vmem],
        out_specs=(vmem,) * 4,
        compiler_params=pltpu.CompilerParams(vmem_limit_bytes=VMEM_BYTES),
        name="cut_edges",
    )(density)


def composite_kernel(order_in, in_ref, out_ref, values, order_ref, sems):
    wait_scalars = fetch_scalars([(order_in, order_ref)], sems)
    count = in_ref.shape[0]
    rows = in_ref.shape[2] // 4
    for source in range(count):
        for view in range(VIEWS):
            values[source, view] = decode(in_ref[source, view])
    wait_scalars()
    for view in range(VIEWS):
        colour, transmit = None, None
        for k in range(count):
            source = order_ref[view, k]
            part = [values[source, view, pl.ds(c * rows, rows)] for c in range(4)]
            clear = 1.0 - part[3]
            if k == 0:
                colour, transmit = part[:3], clear
            else:
                colour = [colour[c] + transmit * part[c] for c in range(3)]
                transmit = transmit * clear
        for c, value in enumerate(colour + [1.0 - transmit]):
            out_ref[view, c, 0] = value


def body(density, live_slices, shear_slopes, palette, depth_order, tile_owner):
    depth_cells, row_cells, columns = density.shape
    n_depth = lax.axis_size("gz")
    edge = depth_cells - HALO
    odd_depth = lax.axis_index("gz") % 2 == 1

    def pairs(axis, first):
        count = lax.axis_size(axis)
        lower = range(first, count - 1, 2)
        return [(i, i + 1) for i in lower] + [(i + 1, i) for i in lower]

    row_even, row_odd, deep_even, deep_odd = cut_edges(density)
    row_even = lax.ppermute(row_even, "xy", pairs("xy", 0))
    row_odd = lax.ppermute(row_odd, "xy", pairs("xy", 1))
    deep_odd = lax.ppermute(deep_odd, "gz", pairs("gz", 1))
    deep_even = lax.ppermute(deep_even, "gz", pairs("gz", 0))
    rows = jnp.concatenate([row_even, row_odd], axis=1)
    facing = jnp.where(odd_depth, edge, 0)
    corner_odd = lax.ppermute(
        lax.dynamic_slice_in_dim(rows, facing, HALO), "gz", pairs("gz", 1)
    )
    corner_even = lax.ppermute(
        lax.dynamic_slice_in_dim(rows, edge - facing, HALO), "gz", pairs("gz", 0)
    )
    inner, deep, shear, band_weights = render_inner(
        live_slices, shear_slopes, palette, tile_owner, density, deep_odd, deep_even, n_depth
    )
    outgoing = render_edges(
        live_slices, palette, tile_owner, corner_odd, corner_even, row_even, row_odd,
        inner, deep, shear, band_weights, n_depth,
    )
    incoming = lax.all_to_all(outgoing, "gz", split_axis=0, concat_axis=0, tiled=True)
    tile_rows = row_cells // n_depth
    return pl.pallas_call(
        composite_kernel,
        out_shape=jax.ShapeDtypeStruct((VIEWS, 4, 1, tile_rows, columns), jnp.float32),
        in_specs=[pl.BlockSpec(memory_space=pltpu.VMEM)] * 2,
        out_specs=pl.BlockSpec(memory_space=pltpu.VMEM),
        scratch_shapes=[
            pltpu.VMEM(incoming.shape, jnp.float32),
            pltpu.SMEM(depth_order.shape, jnp.int32),
            pltpu.SemaphoreType.DMA((1,)),
        ],
        compiler_params=pltpu.CompilerParams(vmem_limit_bytes=VMEM_BYTES),
        name="composite",
    )(depth_order, incoming)


def solution(mesh):
    placed = (P("gz", "xy", None), P(), P(), P(), P(), P())
    return jax.shard_map(
        body, mesh=mesh, in_specs=placed, out_specs=P(None, None, "gz", "xy", None), check_vma=False
    )
```

```python
import math

import jax
import jax.numpy as jnp
from jax import lax
from jax.experimental import pallas as pl
from jax.experimental.pallas import tpu as pltpu
from jax.sharding import PartitionSpec as P

LIGHT = (0.48, 0.6, 0.64)
REACH = 4
HALO = REACH + 1
TAPS = 2 * REACH + 1
ROW_TILE = 8
PACKED_ROWS = 16
EDGE = 8
VIEWS = 2
TOP = 2.2
STEPS = 65535.0
MIDDLE = 32768
LEVELS_PER_UNIT = float(1 << 17)
WORDS, SPARE = HALO - 1, 7
VMEM_BYTES = 40 * 1024 * 1024


def column_matrix(columns):
    source = lax.broadcasted_iota(jnp.int32, (columns, columns), 0)
    target = lax.broadcasted_iota(jnp.int32, (columns, columns), 1)

    def band(shift):
        at = target + shift
        inside = (jnp.abs(source - at) <= REACH) & (at >= 0) & (at < columns)
        return jnp.where(inside, 1.0, 0.0).astype(jnp.float32)

    return jnp.concatenate([band(0), band(1) - band(-1)], axis=1).astype(jnp.bfloat16)


def shear_matrices(slopes_ref, slice_depth, columns, total_depth):
    source = lax.broadcasted_iota(jnp.int32, (columns, columns), 0)
    target = lax.broadcasted_iota(jnp.int32, (columns, columns), 1)
    distance = (source - target).astype(jnp.float32)
    parts = []
    for view in range(VIEWS):
        shift = slopes_ref[view] * (slice_depth + 0.5 - 0.5 * total_depth)
        parts.append(jnp.maximum(0.0, 1.0 - jnp.abs(distance + shift)))
    return jnp.concatenate(parts, axis=1).astype(jnp.bfloat16)


def window_sums(layers, taps):
    sums, width = layers, 1
    while 2 * width < taps:
        sums = [sums[i] + sums[i + width] for i in range(len(sums) - width)]
        width *= 2
    return [sums[i] + layers[i + width] for i in range(len(layers) - width)]


def pack(values):
    levels = [jnp.floor(x * LEVELS_PER_UNIT + 0.5).astype(jnp.int32) for x in values]
    return [
        (levels[i] << SPARE) | ((levels[WORDS] >> (SPARE * i)) & 0x7F) for i in range(WORDS)
    ]


def unpack(words):
    last = words[0] & 0x7F
    for i in range(1, WORDS):
        last = last | ((words[i] & 0x7F) << (SPARE * i))
    levels = [word >> SPARE for word in words] + [(last << 4) >> 4]
    return [x.astype(jnp.float32) * (1.0 / LEVELS_PER_UNIT) for x in levels]


def encode(value):
    scale = math.log2(STEPS) - 0.125 * math.log2(TOP)
    root = jnp.exp2(0.125 * jnp.log2(jnp.maximum(value, 1e-30)) + scale)
    return (root + 0.5).astype(jnp.int32) - MIDDLE


def decode(code):
    root = (code.astype(jnp.int32) + MIDDLE).astype(jnp.float32) * (TOP**0.125 / STEPS)
    square = root * root
    fourth = square * square
    return fourth * fourth


def column_sums(total, weights):
    hi = total.astype(jnp.bfloat16)
    rest = total - hi.astype(jnp.float32)
    mid = rest.astype(jnp.bfloat16)
    lo = (rest - mid.astype(jnp.float32)).astype(jnp.bfloat16)
    split = jnp.concatenate([hi, mid, lo], axis=1)
    return jnp.dot(split, weights, preferred_element_type=jnp.float32)


def shade(center, diff_depth, diff_rows, diff_cols, live, palette_ref, extinct):
    cells = TAPS**3
    floor = 0.01 * (2.0 * cells) ** 2
    square = diff_depth * diff_depth + diff_rows * diff_rows + diff_cols * diff_cols + floor
    light = [0.75 * part for part in LIGHT]
    toward = light[0] * diff_depth + light[1] * diff_rows + light[2] * diff_cols
    facing = jnp.maximum(0.0, toward) * lax.rsqrt(square)
    t = center * (2.0 * math.log2(math.e) / cells)
    softplus = jnp.maximum(t, 0.0) + jnp.log2(1.0 + jnp.exp2(-jnp.abs(t)))
    opacity = 1.0 - jnp.exp2(jnp.where(live, -extinct, 0.0) * softplus)
    bright = opacity * (0.25 + facing)
    channels = [bright * palette_ref[c] for c in range(3)] + [opacity]
    return [channel.astype(jnp.bfloat16) for channel in channels]


def march(layer, depth_cells, view):
    colour, transmit = None, None
    for z in range(depth_cells):
        part = [layer(z, c) for c in range(4)]
        clear = 1.0 - part[3]
        if z == 0:
            colour, transmit = part[:3], clear
        elif view == 0:
            colour = [colour[c] + transmit * part[c] for c in range(3)]
            transmit = transmit * clear
        else:
            colour = [part[c] + clear * colour[c] for c in range(3)]
            transmit = transmit * clear
    return colour + [1.0 - transmit]


def store_codes(out_ref, place, view, codes, row, tile_rows, other=None):
    if tile_rows < PACKED_ROWS:
        for c in range(0, 4, 2):
            pair = jnp.concatenate(codes[c : c + 2])
            out_ref[place, view, pl.ds(c * tile_rows, PACKED_ROWS)] = pair.astype(jnp.int16)
        return
    for c in range(4):
        at = pl.ds(c * tile_rows + row // PACKED_ROWS * PACKED_ROWS, PACKED_ROWS)
        code = codes[c]
        if code.shape[0] < PACKED_ROWS:
            half = row % PACKED_ROWS
            rest = jnp.zeros_like(code)
            if other is not None:
                rest = other[place, view, at].astype(jnp.int32)
                rest = rest[ROW_TILE:] if half == 0 else rest[:ROW_TILE]
            code = jnp.concatenate([code, rest] if half == 0 else [rest, code])
        out_ref[place, view, at] = code.astype(jnp.int16)


def fetch_scalars(pairs, sems):
    copies = [
        pltpu.make_async_copy(source, target, sems.at[i]) for i, (source, target) in enumerate(pairs)
    ]
    for copy in copies:
        copy.start()

    def wait():
        for copy in copies:
            copy.wait()

    return wait


def zero_outside(smooth, depth_index, n_depth, layers):
    @pl.when(depth_index == 0)
    def _():
        smooth[0] = jnp.zeros_like(smooth[0])

    @pl.when(depth_index == n_depth - 1)
    def _():
        smooth[layers - 1] = jnp.zeros_like(smooth[layers - 1])


def render_inner(live_slices, slopes, palette, owner, density, deep_odd, deep_even, n_depth):
    depth_cells, row_cells, columns = density.shape
    total_depth = depth_cells * n_depth
    extinct = 3.0 / total_depth
    tile_rows = row_cells // n_depth
    layers = depth_cells + 2
    rows = range(EDGE, row_cells - EDGE)
    height = len(rows)
    lead, span = EDGE, height + 2 * ROW_TILE

    def kernel(
        live_in, slopes_in, palette_in, owner_in, own_ref, odd_ref, even_ref,
        out_ref, deep, shear_ref, band_ref, triple, smooth, across, sheared,
        live_ref, slopes_ref, palette_ref, owner_ref, sems,
    ):
        wait_scalars = fetch_scalars(
            [
                (live_in, live_ref),
                (slopes_in, slopes_ref),
                (palette_in, palette_ref),
                (owner_in, owner_ref),
            ],
            sems,
        )
        depth_index = lax.axis_index("gz")
        row_index = lax.axis_index("xy")
        odd_depth = depth_index % 2 == 1

        for start in range(0, row_cells, ROW_TILE):
            at = pl.ds(start, ROW_TILE)
            even = [even_ref[i, at] for i in range(WORDS)]
            odd = [odd_ref[i, at] for i in range(WORDS)]
            low = unpack([jnp.where(odd_depth, e, o) for e, o in zip(even, odd)])
            high = unpack([jnp.where(odd_depth, o, e) for e, o in zip(even, odd)])
            own = [own_ref[i, at] for i in range(depth_cells)]
            for z, total in enumerate(window_sums(low + own + high, TAPS)):
                deep[z, pl.ds(ROW_TILE + start, ROW_TILE)] = total

        band = column_matrix(columns)
        band_ref[...] = band
        weights = jnp.concatenate([band, band, band], axis=0)
        for z in range(layers):
            triple[z] = (
                deep[z, pl.ds(lead - 4, span + ROW_TILE)]
                + deep[z, pl.ds(lead - 3, span + ROW_TILE)]
                + deep[z, pl.ds(lead - 2, span + ROW_TILE)]
            )
            total = (
                triple[z, pl.ds(0, span)] + triple[z, pl.ds(3, span)] + triple[z, pl.ds(6, span)]
            )
            if 1 <= z <= depth_cells:
                both = column_sums(total, weights)
                smooth[z] = both[:, :columns]
                across[z - 1] = both[ROW_TILE : ROW_TILE + height, columns:]
            else:
                smooth[z] = column_sums(total, weights[:, :columns])
        zero_outside(smooth, depth_index, n_depth, layers)

        wait_scalars()
        slab_start = (depth_index * depth_cells).astype(jnp.float32)
        for z in range(depth_cells):
            shear_ref[z] = shear_matrices(slopes_ref, slab_start + float(z), columns, total_depth)

        own_live = live_ref[depth_index, row_index]
        middle = pl.ds(ROW_TILE, height)
        for z in range(depth_cells):
            channels = shade(
                smooth[z + 1, middle],
                smooth[z + 2, middle] - smooth[z, middle],
                smooth[z + 1, pl.ds(ROW_TILE + 1, height)]
                - smooth[z + 1, pl.ds(ROW_TILE - 1, height)],
                across[z],
                z < own_live,
                palette_ref,
                extinct,
            )
            sheared[z] = jnp.dot(
                jnp.concatenate(channels), shear_ref[z], preferred_element_type=jnp.float32
            )
        row = rows.start
        while row < rows.stop:
            whole = tile_rows >= PACKED_ROWS and row % PACKED_ROWS == 0
            count = PACKED_ROWS if whole and row + PACKED_ROWS <= rows.stop else ROW_TILE
            at = row - rows.start
            for view in range(VIEWS):
                lanes = pl.ds(view * columns, columns)
                values = march(
                    lambda z, c: sheared[z, pl.ds(c * height + at, count), lanes],
                    depth_cells,
                    view,
                )
                place = owner_ref[view, row // tile_rows]
                codes = [encode(value) for value in values]
                store_codes(out_ref, place, view, codes, row % tile_rows, tile_rows)
            row += count

    vmem = pl.BlockSpec(memory_space=pltpu.VMEM)
    return pl.pallas_call(
        kernel,
        out_shape=(
            jax.ShapeDtypeStruct((n_depth, VIEWS, 4 * tile_rows, columns), jnp.int16),
            jax.ShapeDtypeStruct((layers, row_cells + 2 * ROW_TILE, columns), jnp.float32),
            jax.ShapeDtypeStruct((depth_cells, columns, VIEWS * columns), jnp.bfloat16),
            jax.ShapeDtypeStruct((columns, 2 * columns), jnp.bfloat16),
        ),
        in_specs=[vmem] * 7,
        out_specs=(vmem,) * 4,
        scratch_shapes=[
            pltpu.VMEM((layers, span + ROW_TILE, columns), jnp.float32),
            pltpu.VMEM((layers, span, columns), jnp.float32),
            pltpu.VMEM((depth_cells, height, columns), jnp.float32),
            pltpu.VMEM((depth_cells, 4 * height, VIEWS * columns), jnp.float32),
            pltpu.SMEM(live_slices.shape, jnp.int32),
            pltpu.SMEM(slopes.shape, jnp.float32),
            pltpu.SMEM(palette.shape, jnp.float32),
            pltpu.SMEM(owner.shape, jnp.int32),
            pltpu.SemaphoreType.DMA((4,)),
        ],
        compiler_params=pltpu.CompilerParams(vmem_limit_bytes=VMEM_BYTES),
        cost_estimate=pl.CostEstimate(
            flops=100 * depth_cells * row_cells * columns,
            bytes_accessed=16 * 4 * depth_cells * row_cells * columns,
            transcendentals=4 * depth_cells * row_cells * columns,
        ),
        name="render_inner",
    )(live_slices, slopes, palette, owner, density, deep_odd, deep_even)


def render_edges(
    live_slices, palette, owner, corner_odd, corner_even, row_even, row_odd,
    inner, deep, shear, band_weights, n_depth,
):
    layers, padded_rows, columns = deep.shape
    row_cells = padded_rows - 2 * ROW_TILE
    depth_cells = layers - 2
    n_rows = lax.axis_size("xy")
    extinct = 3.0 / (depth_cells * n_depth)
    tile_rows = row_cells // n_depth
    band = EDGE + 2 * ROW_TILE
    piece = 2 * ROW_TILE
    height = 2 * EDGE

    def kernel(
        live_in, palette_in, owner_in, corner_odd_ref, corner_even_ref, row_even_ref, row_odd_ref,
        inner_ref, deep_ref, shear_ref, band_ref,
        out_ref, halo, triple, split_sums, smooth, across, sheared,
        live_ref, palette_ref, owner_ref, sems,
    ):
        wait_scalars = fetch_scalars(
            [(live_in, live_ref), (palette_in, palette_ref), (owner_in, owner_ref)], sems
        )
        depth_index = lax.axis_index("gz")
        row_index = lax.axis_index("xy")
        odd_depth = depth_index % 2 == 1

        odd_row = row_index % 2 == 1
        from_even, from_odd = pl.ds(0, ROW_TILE), pl.ds(ROW_TILE, ROW_TILE)
        for side in range(2):
            take_even = odd_row if side == 0 else jnp.logical_not(odd_row)

            def facing_rows(ref, i):
                return jnp.where(take_even, ref[i, from_even], ref[i, from_odd])

            even = [facing_rows(corner_even_ref, i) for i in range(HALO)]
            odd = [facing_rows(corner_odd_ref, i) for i in range(HALO)]
            middle = [
                jnp.where(take_even, row_even_ref[i], row_odd_ref[i]) for i in range(depth_cells)
            ]
            low = [jnp.where(odd_depth, e, o) for e, o in zip(even, odd)]
            high = [jnp.where(odd_depth, o, e) for e, o in zip(even, odd)]
            outer = 0 if side == 0 else band - ROW_TILE
            inner_at = ROW_TILE if side == 0 else 0
            own_at = ROW_TILE if side == 0 else padded_rows - band
            sums = window_sums(low + middle + high, TAPS)
            for z in range(layers):
                halo[z, side, pl.ds(outer, ROW_TILE)] = sums[z]
                halo[z, side, pl.ds(inner_at, band - ROW_TILE)] = deep_ref[
                    z, pl.ds(own_at, band - ROW_TILE)
                ]

        span = band - ROW_TILE
        for z in range(layers):
            for side in range(2):
                triple[z, side, pl.ds(0, span)] = (
                    halo[z, side, pl.ds(3, span)]
                    + halo[z, side, pl.ds(4, span)]
                    + halo[z, side, pl.ds(5, span)]
                )
                split_sums[z, side] = (
                    triple[z, side, pl.ds(0, piece)]
                    + triple[z, side, pl.ds(3, piece)]
                    + triple[z, side, pl.ds(6, piece)]
                )
        weights = jnp.concatenate([band_ref[...]] * 3, axis=0)
        both = column_sums(split_sums[...].reshape(layers * 2 * piece, columns), weights)
        both = both.reshape(layers, 2, piece, 2 * columns)
        smooth[...] = both[..., :columns]
        across[...] = both[1:-1, :, :, columns:]

        @pl.when(row_index == 0)
        def _():
            smooth[:, 0, :1] = jnp.zeros((layers, 1, columns), jnp.float32)

        @pl.when(row_index == n_rows - 1)
        def _():
            smooth[:, 1, EDGE + 1 : EDGE + 2] = jnp.zeros((layers, 1, columns), jnp.float32)

        zero_outside(smooth, depth_index, n_depth, layers)

        wait_scalars()
        own_live = live_ref[depth_index, row_index]

        def both_sides(ref, z, start):
            return ref[z, :, pl.ds(start, EDGE)].reshape(height, columns)

        for z in range(depth_cells):
            channels = shade(
                both_sides(smooth, z + 1, 1),
                both_sides(smooth, z + 2, 1) - both_sides(smooth, z, 1),
                both_sides(smooth, z + 1, 2) - both_sides(smooth, z + 1, 0),
                both_sides(across, z, 1),
                z < own_live,
                palette_ref,
                extinct,
            )
            sheared[z] = jnp.dot(
                jnp.concatenate(channels), shear_ref[z], preferred_element_type=jnp.float32
            )
        out_ref[...] = inner_ref[...]
        for view in range(VIEWS):
            lanes = pl.ds(view * columns, columns)
            values = march(
                lambda z, c: sheared[z, pl.ds(c * height, height), lanes], depth_cells, view
            )
            codes = [encode(value) for value in values]
            for side, row in enumerate((0, row_cells - EDGE)):
                place = owner_ref[view, row // tile_rows]
                part = [code[side * EDGE : (side + 1) * EDGE] for code in codes]
                store_codes(out_ref, place, view, part, row % tile_rows, tile_rows, inner_ref)

    vmem = pl.BlockSpec(memory_space=pltpu.VMEM)
    return pl.pallas_call(
        kernel,
        out_shape=jax.ShapeDtypeStruct(inner.shape, inner.dtype),
        in_specs=[vmem] * 11,
        out_specs=vmem,
        scratch_shapes=[
            pltpu.VMEM((layers, 2, band, columns), jnp.float32),
            pltpu.VMEM((layers, 2, piece + ROW_TILE, columns), jnp.float32),
            pltpu.VMEM((layers, 2, piece, columns), jnp.float32),
            pltpu.VMEM((layers, 2, piece, columns), jnp.float32),
            pltpu.VMEM((depth_cells, 2, piece, columns), jnp.float32),
            pltpu.VMEM((depth_cells, 4 * height, VIEWS * columns), jnp.float32),
            pltpu.SMEM(live_slices.shape, jnp.int32),
            pltpu.SMEM(palette.shape, jnp.float32),
            pltpu.SMEM(owner.shape, jnp.int32),
            pltpu.SemaphoreType.DMA((3,)),
        ],
        compiler_params=pltpu.CompilerParams(vmem_limit_bytes=VMEM_BYTES),
        name="render_edges",
    )(
        live_slices, palette, owner, corner_odd, corner_even, row_even, row_odd,
        inner, deep, shear, band_weights,
    )


def cut_edges(density):
    depth_cells, row_cells, columns = density.shape

    def kernel(density_ref, row_even_ref, row_odd_ref, deep_even_ref, deep_odd_ref):
        row_bit = lax.axis_index("xy") % 2
        depth_bit = lax.axis_index("gz") % 2
        last_rows, last_deep = row_cells - ROW_TILE, depth_cells - HALO
        for ref, bit in ((deep_odd_ref, depth_bit), (deep_even_ref, 1 - depth_bit)):
            for start in range(0, row_cells, ROW_TILE):
                at = pl.ds(start, ROW_TILE)
                layers = [density_ref[bit * last_deep + i, at] for i in range(HALO)]
                for i, word in enumerate(pack(layers)):
                    ref[i, at] = word
        for ref, bit in ((row_even_ref, 1 - row_bit), (row_odd_ref, row_bit)):
            start = pl.multiple_of(bit * last_rows, ROW_TILE)
            ref[...] = density_ref[:, pl.ds(start, ROW_TILE)]

    rows = jax.ShapeDtypeStruct((depth_cells, ROW_TILE, columns), jnp.float32)
    deep = jax.ShapeDtypeStruct((WORDS, row_cells, columns), jnp.int32)
    vmem = pl.BlockSpec(memory_space=pltpu.VMEM)
    return pl.pallas_call(
        kernel,
        out_shape=(rows, rows, deep, deep),
        in_specs=[vmem],
        out_specs=(vmem,) * 4,
        compiler_params=pltpu.CompilerParams(vmem_limit_bytes=VMEM_BYTES),
        name="cut_edges",
    )(density)


def composite_kernel(order_in, in_ref, out_ref, values, order_ref, sems):
    wait_scalars = fetch_scalars([(order_in, order_ref)], sems)
    count = in_ref.shape[0]
    rows = in_ref.shape[2] // 4
    for source in range(count):
        for view in range(VIEWS):
            values[source, view] = decode(in_ref[source, view])
    wait_scalars()
    for view in range(VIEWS):
        colour, transmit = None, None
        for k in range(count):
            source = order_ref[view, k]
            part = [values[source, view, pl.ds(c * rows, rows)] for c in range(4)]
            clear = 1.0 - part[3]
            if k == 0:
                colour, transmit = part[:3], clear
            else:
                colour = [colour[c] + transmit * part[c] for c in range(3)]
                transmit = transmit * clear
        for c, value in enumerate(colour + [1.0 - transmit]):
            out_ref[view, c, 0] = value


def body(density, live_slices, shear_slopes, palette, depth_order, tile_owner):
    depth_cells, row_cells, columns = density.shape
    n_depth = lax.axis_size("gz")
    edge = depth_cells - HALO
    odd_depth = lax.axis_index("gz") % 2 == 1

    def pairs(axis, first):
        count = lax.axis_size(axis)
        lower = range(first, count - 1, 2)
        return [(i, i + 1) for i in lower] + [(i + 1, i) for i in lower]

    row_even, row_odd, deep_even, deep_odd = cut_edges(density)
    row_even = lax.ppermute(row_even, "xy", pairs("xy", 0))
    row_odd = lax.ppermute(row_odd, "xy", pairs("xy", 1))
    deep_odd = lax.ppermute(deep_odd, "gz", pairs("gz", 1))
    deep_even = lax.ppermute(deep_even, "gz", pairs("gz", 0))
    rows = jnp.concatenate([row_even, row_odd], axis=1)
    facing = jnp.where(odd_depth, edge, 0)
    corner_odd = lax.ppermute(
        lax.dynamic_slice_in_dim(rows, facing, HALO), "gz", pairs("gz", 1)
    )
    corner_even = lax.ppermute(
        lax.dynamic_slice_in_dim(rows, edge - facing, HALO), "gz", pairs("gz", 0)
    )
    inner, deep, shear, band_weights = render_inner(
        live_slices, shear_slopes, palette, tile_owner, density, deep_odd, deep_even, n_depth
    )
    outgoing = render_edges(
        live_slices, palette, tile_owner, corner_odd, corner_even, row_even, row_odd,
        inner, deep, shear, band_weights, n_depth,
    )
    incoming = lax.all_to_all(outgoing, "gz", split_axis=0, concat_axis=0, tiled=True)
    tile_rows = row_cells // n_depth
    return pl.pallas_call(
        composite_kernel,
        out_shape=jax.ShapeDtypeStruct((VIEWS, 4, 1, tile_rows, columns), jnp.float32),
        in_specs=[pl.BlockSpec(memory_space=pltpu.VMEM)] * 2,
        out_specs=pl.BlockSpec(memory_space=pltpu.VMEM),
        scratch_shapes=[
            pltpu.VMEM(incoming.shape, jnp.float32),
            pltpu.SMEM(depth_order.shape, jnp.int32),
            pltpu.SemaphoreType.DMA((1,)),
        ],
        compiler_params=pltpu.CompilerParams(vmem_limit_bytes=VMEM_BYTES),
        name="composite",
    )(depth_order, incoming)


def solution(mesh):
    placed = (P("gz", "xy", None), P(), P(), P(), P(), P())
    return jax.shard_map(
        body, mesh=mesh, in_specs=placed, out_specs=P(None, None, "gz", "xy", None), check_vma=False
    )
```

```python
import math

import jax
import jax.numpy as jnp
from jax import lax
from jax.experimental import pallas as pl
from jax.experimental.pallas import tpu as pltpu
from jax.sharding import PartitionSpec as P

LIGHT = (0.48, 0.6, 0.64)
REACH = 4
HALO = REACH + 1
TAPS = 2 * REACH + 1
ROW_TILE = 8
PACKED_ROWS = 16
EDGE = 8
VIEWS = 2
TOP = 2.2
STEPS = 65535.0
MIDDLE = 32768
LEVELS_PER_UNIT = float(1 << 17)
WORDS, SPARE = HALO - 1, 7
VMEM_BYTES = 40 * 1024 * 1024


def column_matrix(columns):
    source = lax.broadcasted_iota(jnp.int32, (columns, columns), 0)
    target = lax.broadcasted_iota(jnp.int32, (columns, columns), 1)

    def band(shift):
        at = target + shift
        inside = (jnp.abs(source - at) <= REACH) & (at >= 0) & (at < columns)
        return jnp.where(inside, 1.0, 0.0).astype(jnp.float32)

    return jnp.concatenate([band(0), band(1) - band(-1)], axis=1).astype(jnp.bfloat16)


def shear_matrices(slopes_ref, slice_depth, columns, total_depth):
    source = lax.broadcasted_iota(jnp.int32, (columns, columns), 0)
    target = lax.broadcasted_iota(jnp.int32, (columns, columns), 1)
    distance = (source - target).astype(jnp.float32)
    parts = []
    for view in range(VIEWS):
        shift = slopes_ref[view] * (slice_depth + 0.5 - 0.5 * total_depth)
        parts.append(jnp.maximum(0.0, 1.0 - jnp.abs(distance + shift)))
    return jnp.concatenate(parts, axis=1).astype(jnp.bfloat16)


def window_sums(layers, taps):
    sums, width = layers, 1
    while 2 * width < taps:
        sums = [sums[i] + sums[i + width] for i in range(len(sums) - width)]
        width *= 2
    return [sums[i] + layers[i + width] for i in range(len(layers) - width)]


def pack(values):
    levels = [jnp.floor(x * LEVELS_PER_UNIT + 0.5).astype(jnp.int32) for x in values]
    return [
        (levels[i] << SPARE) | ((levels[WORDS] >> (SPARE * i)) & 0x7F) for i in range(WORDS)
    ]


def unpack(words):
    last = words[0] & 0x7F
    for i in range(1, WORDS):
        last = last | ((words[i] & 0x7F) << (SPARE * i))
    levels = [word >> SPARE for word in words] + [(last << 4) >> 4]
    return [x.astype(jnp.float32) * (1.0 / LEVELS_PER_UNIT) for x in levels]


def encode(value):
    scale = math.log2(STEPS) - 0.125 * math.log2(TOP)
    root = jnp.exp2(0.125 * jnp.log2(jnp.maximum(value, 1e-30)) + scale)
    return (root + 0.5).astype(jnp.int32) - MIDDLE


def decode(code):
    root = (code.astype(jnp.int32) + MIDDLE).astype(jnp.float32) * (TOP**0.125 / STEPS)
    square = root * root
    fourth = square * square
    return fourth * fourth


def column_sums(total, weights):
    hi = total.astype(jnp.bfloat16)
    rest = total - hi.astype(jnp.float32)
    mid = rest.astype(jnp.bfloat16)
    lo = (rest - mid.astype(jnp.float32)).astype(jnp.bfloat16)
    split = jnp.concatenate([hi, mid, lo], axis=1)
    return jnp.dot(split, weights, preferred_element_type=jnp.float32)


def shade(center, diff_depth, diff_rows, diff_cols, live, palette_ref, extinct):
    cells = TAPS**3
    floor = 0.01 * (2.0 * cells) ** 2
    square = diff_depth * diff_depth + diff_rows * diff_rows + diff_cols * diff_cols + floor
    light = [0.75 * part for part in LIGHT]
    toward = light[0] * diff_depth + light[1] * diff_rows + light[2] * diff_cols
    facing = jnp.maximum(0.0, toward) * lax.rsqrt(square)
    t = center * (2.0 * math.log2(math.e) / cells)
    softplus = jnp.maximum(t, 0.0) + jnp.log2(1.0 + jnp.exp2(-jnp.abs(t)))
    opacity = 1.0 - jnp.exp2(jnp.where(live, -extinct, 0.0) * softplus)
    bright = opacity * (0.25 + facing)
    channels = [bright * palette_ref[c] for c in range(3)] + [opacity]
    return [channel.astype(jnp.bfloat16) for channel in channels]


def march(layer, depth_cells, view):
    colour, transmit = None, None
    for z in range(depth_cells):
        part = [layer(z, c) for c in range(4)]
        clear = 1.0 - part[3]
        if z == 0:
            colour, transmit = part[:3], clear
        elif view == 0:
            colour = [colour[c] + transmit * part[c] for c in range(3)]
            transmit = transmit * clear
        else:
            colour = [part[c] + clear * colour[c] for c in range(3)]
            transmit = transmit * clear
    return colour + [1.0 - transmit]


def store_codes(out_ref, place, view, codes, row, tile_rows, other=None):
    if tile_rows < PACKED_ROWS:
        for c in range(0, 4, 2):
            pair = jnp.concatenate(codes[c : c + 2])
            out_ref[place, view, pl.ds(c * tile_rows, PACKED_ROWS)] = pair.astype(jnp.int16)
        return
    for c in range(4):
        at = pl.ds(c * tile_rows + row // PACKED_ROWS * PACKED_ROWS, PACKED_ROWS)
        code = codes[c]
        if code.shape[0] < PACKED_ROWS:
            half = row % PACKED_ROWS
            rest = jnp.zeros_like(code)
            if other is not None:
                rest = other[place, view, at].astype(jnp.int32)
                rest = rest[ROW_TILE:] if half == 0 else rest[:ROW_TILE]
            code = jnp.concatenate([code, rest] if half == 0 else [rest, code])
        out_ref[place, view, at] = code.astype(jnp.int16)


def fetch_scalars(pairs, sems):
    copies = [
        pltpu.make_async_copy(source, target, sems.at[i]) for i, (source, target) in enumerate(pairs)
    ]
    for copy in copies:
        copy.start()

    def wait():
        for copy in copies:
            copy.wait()

    return wait


def zero_outside(smooth, depth_index, n_depth, layers):
    @pl.when(depth_index == 0)
    def _():
        smooth[0] = jnp.zeros_like(smooth[0])

    @pl.when(depth_index == n_depth - 1)
    def _():
        smooth[layers - 1] = jnp.zeros_like(smooth[layers - 1])


def make_tables(slopes, depth_cells, columns, n_depth):
    def kernel(slopes_in, shear_ref, band_ref, slopes_ref, sems):
        wait_scalars = fetch_scalars([(slopes_in, slopes_ref)], sems)
        band_ref[...] = column_matrix(columns)
        slab_start = (lax.axis_index("gz") * depth_cells).astype(jnp.float32)
        wait_scalars()
        for z in range(depth_cells):
            shear_ref[z] = shear_matrices(
                slopes_ref, slab_start + float(z), columns, depth_cells * n_depth
            )

    vmem = pl.BlockSpec(memory_space=pltpu.VMEM)
    return pl.pallas_call(
        kernel,
        out_shape=(
            jax.ShapeDtypeStruct((depth_cells, columns, VIEWS * columns), jnp.bfloat16),
            jax.ShapeDtypeStruct((columns, 2 * columns), jnp.bfloat16),
        ),
        in_specs=[vmem],
        out_specs=(vmem,) * 2,
        scratch_shapes=[
            pltpu.SMEM(slopes.shape, jnp.float32),
            pltpu.SemaphoreType.DMA((1,)),
        ],
        compiler_params=pltpu.CompilerParams(vmem_limit_bytes=VMEM_BYTES),
        name="tables",
    )(slopes)


def render_inner(
    live_slices, palette, owner, density, deep_odd, deep_even, shear, band_weights, n_depth
):
    depth_cells, row_cells, columns = density.shape
    extinct = 3.0 / (depth_cells * n_depth)
    tile_rows = row_cells // n_depth
    layers = depth_cells + 2
    rows = range(EDGE, row_cells - EDGE)
    height = len(rows)
    lead, span = EDGE, height + 2 * ROW_TILE

    def kernel(
        live_in, palette_in, owner_in, own_ref, odd_ref, even_ref, shear_ref, band_ref,
        out_ref, deep, triple, smooth, across, sheared,
        live_ref, palette_ref, owner_ref, sems,
    ):
        wait_scalars = fetch_scalars(
            [(live_in, live_ref), (palette_in, palette_ref), (owner_in, owner_ref)], sems
        )
        depth_index = lax.axis_index("gz")
        row_index = lax.axis_index("xy")
        odd_depth = depth_index % 2 == 1

        for start in range(0, row_cells, ROW_TILE):
            at = pl.ds(start, ROW_TILE)
            even = [even_ref[i, at] for i in range(WORDS)]
            odd = [odd_ref[i, at] for i in range(WORDS)]
            low = unpack([jnp.where(odd_depth, e, o) for e, o in zip(even, odd)])
            high = unpack([jnp.where(odd_depth, o, e) for e, o in zip(even, odd)])
            own = [own_ref[i, at] for i in range(depth_cells)]
            for z, total in enumerate(window_sums(low + own + high, TAPS)):
                deep[z, pl.ds(ROW_TILE + start, ROW_TILE)] = total

        weights = jnp.concatenate([band_ref[...]] * 3, axis=0)
        for z in range(layers):
            triple[z] = (
                deep[z, pl.ds(lead - 4, span + ROW_TILE)]
                + deep[z, pl.ds(lead - 3, span + ROW_TILE)]
                + deep[z, pl.ds(lead - 2, span + ROW_TILE)]
            )
            total = (
                triple[z, pl.ds(0, span)] + triple[z, pl.ds(3, span)] + triple[z, pl.ds(6, span)]
            )
            if 1 <= z <= depth_cells:
                both = column_sums(total, weights)
                smooth[z] = both[:, :columns]
                across[z - 1] = both[ROW_TILE : ROW_TILE + height, columns:]
            else:
                smooth[z] = column_sums(total, weights[:, :columns])
        zero_outside(smooth, depth_index, n_depth, layers)

        wait_scalars()
        own_live = live_ref[depth_index, row_index]
        middle = pl.ds(ROW_TILE, height)
        for z in range(depth_cells):
            channels = shade(
                smooth[z + 1, middle],
                smooth[z + 2, middle] - smooth[z, middle],
                smooth[z + 1, pl.ds(ROW_TILE + 1, height)]
                - smooth[z + 1, pl.ds(ROW_TILE - 1, height)],
                across[z],
                z < own_live,
                palette_ref,
                extinct,
            )
            sheared[z] = jnp.dot(
                jnp.concatenate(channels), shear_ref[z], preferred_element_type=jnp.float32
            )
        row = rows.start
        while row < rows.stop:
            whole = tile_rows >= PACKED_ROWS and row % PACKED_ROWS == 0
            count = PACKED_ROWS if whole and row + PACKED_ROWS <= rows.stop else ROW_TILE
            at = row - rows.start
            for view in range(VIEWS):
                lanes = pl.ds(view * columns, columns)
                values = march(
                    lambda z, c: sheared[z, pl.ds(c * height + at, count), lanes],
                    depth_cells,
                    view,
                )
                place = owner_ref[view, row // tile_rows]
                codes = [encode(value) for value in values]
                store_codes(out_ref, place, view, codes, row % tile_rows, tile_rows)
            row += count

    vmem = pl.BlockSpec(memory_space=pltpu.VMEM)
    return pl.pallas_call(
        kernel,
        out_shape=(
            jax.ShapeDtypeStruct((n_depth, VIEWS, 4 * tile_rows, columns), jnp.int16),
            jax.ShapeDtypeStruct((layers, row_cells + 2 * ROW_TILE, columns), jnp.float32),
        ),
        in_specs=[vmem] * 8,
        out_specs=(vmem,) * 2,
        scratch_shapes=[
            pltpu.VMEM((layers, span + ROW_TILE, columns), jnp.float32),
            pltpu.VMEM((layers, span, columns), jnp.float32),
            pltpu.VMEM((depth_cells, height, columns), jnp.float32),
            pltpu.VMEM((depth_cells, 4 * height, VIEWS * columns), jnp.float32),
            pltpu.SMEM(live_slices.shape, jnp.int32),
            pltpu.SMEM(palette.shape, jnp.float32),
            pltpu.SMEM(owner.shape, jnp.int32),
            pltpu.SemaphoreType.DMA((3,)),
        ],
        compiler_params=pltpu.CompilerParams(vmem_limit_bytes=VMEM_BYTES),
        cost_estimate=pl.CostEstimate(
            flops=100 * depth_cells * row_cells * columns,
            bytes_accessed=16 * 4 * depth_cells * row_cells * columns,
            transcendentals=4 * depth_cells * row_cells * columns,
        ),
        name="render_inner",
    )(live_slices, palette, owner, density, deep_odd, deep_even, shear, band_weights)


def render_edges(
    live_slices, palette, owner, corner_odd, corner_even, row_even, row_odd,
    inner, deep, shear, band_weights, n_depth,
):
    layers, padded_rows, columns = deep.shape
    row_cells = padded_rows - 2 * ROW_TILE
    depth_cells = layers - 2
    n_rows = lax.axis_size("xy")
    extinct = 3.0 / (depth_cells * n_depth)
    tile_rows = row_cells // n_depth
    band = EDGE + 2 * ROW_TILE
    piece = 2 * ROW_TILE
    height = 2 * EDGE

    def kernel(
        live_in, palette_in, owner_in, corner_odd_ref, corner_even_ref, row_even_ref, row_odd_ref,
        inner_ref, deep_ref, shear_ref, band_ref,
        out_ref, halo, triple, split_sums, smooth, across, sheared,
        live_ref, palette_ref, owner_ref, sems,
    ):
        wait_scalars = fetch_scalars(
            [(live_in, live_ref), (palette_in, palette_ref), (owner_in, owner_ref)], sems
        )
        depth_index = lax.axis_index("gz")
        row_index = lax.axis_index("xy")
        odd_depth = depth_index % 2 == 1

        odd_row = row_index % 2 == 1
        from_even, from_odd = pl.ds(0, ROW_TILE), pl.ds(ROW_TILE, ROW_TILE)
        for side in range(2):
            take_even = odd_row if side == 0 else jnp.logical_not(odd_row)

            def facing_rows(ref, i):
                return jnp.where(take_even, ref[i, from_even], ref[i, from_odd])

            even = [facing_rows(corner_even_ref, i) for i in range(HALO)]
            odd = [facing_rows(corner_odd_ref, i) for i in range(HALO)]
            middle = [
                jnp.where(take_even, row_even_ref[i], row_odd_ref[i]) for i in range(depth_cells)
            ]
            low = [jnp.where(odd_depth, e, o) for e, o in zip(even, odd)]
            high = [jnp.where(odd_depth, o, e) for e, o in zip(even, odd)]
            outer = 0 if side == 0 else band - ROW_TILE
            inner_at = ROW_TILE if side == 0 else 0
            own_at = ROW_TILE if side == 0 else padded_rows - band
            sums = window_sums(low + middle + high, TAPS)
            for z in range(layers):
                halo[z, side, pl.ds(outer, ROW_TILE)] = sums[z]
                halo[z, side, pl.ds(inner_at, band - ROW_TILE)] = deep_ref[
                    z, pl.ds(own_at, band - ROW_TILE)
                ]

        span = band - ROW_TILE
        for z in range(layers):
            for side in range(2):
                triple[z, side, pl.ds(0, span)] = (
                    halo[z, side, pl.ds(3, span)]
                    + halo[z, side, pl.ds(4, span)]
                    + halo[z, side, pl.ds(5, span)]
                )
                split_sums[z, side] = (
                    triple[z, side, pl.ds(0, piece)]
                    + triple[z, side, pl.ds(3, piece)]
                    + triple[z, side, pl.ds(6, piece)]
                )
        weights = jnp.concatenate([band_ref[...]] * 3, axis=0)
        both = column_sums(split_sums[...].reshape(layers * 2 * piece, columns), weights)
        both = both.reshape(layers, 2, piece, 2 * columns)
        smooth[...] = both[..., :columns]
        across[...] = both[1:-1, :, :, columns:]

        @pl.when(row_index == 0)
        def _():
            smooth[:, 0, :1] = jnp.zeros((layers, 1, columns), jnp.float32)

        @pl.when(row_index == n_rows - 1)
        def _():
            smooth[:, 1, EDGE + 1 : EDGE + 2] = jnp.zeros((layers, 1, columns), jnp.float32)

        zero_outside(smooth, depth_index, n_depth, layers)

        wait_scalars()
        own_live = live_ref[depth_index, row_index]

        def both_sides(ref, z, start):
            return ref[z, :, pl.ds(start, EDGE)].reshape(height, columns)

        for z in range(depth_cells):
            channels = shade(
                both_sides(smooth, z + 1, 1),
                both_sides(smooth, z + 2, 1) - both_sides(smooth, z, 1),
                both_sides(smooth, z + 1, 2) - both_sides(smooth, z + 1, 0),
                both_sides(across, z, 1),
                z < own_live,
                palette_ref,
                extinct,
            )
            sheared[z] = jnp.dot(
                jnp.concatenate(channels), shear_ref[z], preferred_element_type=jnp.float32
            )
        out_ref[...] = inner_ref[...]
        for view in range(VIEWS):
            lanes = pl.ds(view * columns, columns)
            values = march(
                lambda z, c: sheared[z, pl.ds(c * height, height), lanes], depth_cells, view
            )
            codes = [encode(value) for value in values]
            for side, row in enumerate((0, row_cells - EDGE)):
                place = owner_ref[view, row // tile_rows]
                part = [code[side * EDGE : (side + 1) * EDGE] for code in codes]
                store_codes(out_ref, place, view, part, row % tile_rows, tile_rows, inner_ref)

    vmem = pl.BlockSpec(memory_space=pltpu.VMEM)
    return pl.pallas_call(
        kernel,
        out_shape=jax.ShapeDtypeStruct(inner.shape, inner.dtype),
        in_specs=[vmem] * 11,
        out_specs=vmem,
        scratch_shapes=[
            pltpu.VMEM((layers, 2, band, columns), jnp.float32),
            pltpu.VMEM((layers, 2, piece + ROW_TILE, columns), jnp.float32),
            pltpu.VMEM((layers, 2, piece, columns), jnp.float32),
            pltpu.VMEM((layers, 2, piece, columns), jnp.float32),
            pltpu.VMEM((depth_cells, 2, piece, columns), jnp.float32),
            pltpu.VMEM((depth_cells, 4 * height, VIEWS * columns), jnp.float32),
            pltpu.SMEM(live_slices.shape, jnp.int32),
            pltpu.SMEM(palette.shape, jnp.float32),
            pltpu.SMEM(owner.shape, jnp.int32),
            pltpu.SemaphoreType.DMA((3,)),
        ],
        compiler_params=pltpu.CompilerParams(vmem_limit_bytes=VMEM_BYTES),
        name="render_edges",
    )(
        live_slices, palette, owner, corner_odd, corner_even, row_even, row_odd,
        inner, deep, shear, band_weights,
    )


def cut_edges(density):
    depth_cells, row_cells, columns = density.shape

    def kernel(density_ref, row_even_ref, row_odd_ref, deep_even_ref, deep_odd_ref):
        row_bit = lax.axis_index("xy") % 2
        depth_bit = lax.axis_index("gz") % 2
        last_rows, last_deep = row_cells - ROW_TILE, depth_cells - HALO
        for ref, bit in ((deep_odd_ref, depth_bit), (deep_even_ref, 1 - depth_bit)):
            for start in range(0, row_cells, ROW_TILE):
                at = pl.ds(start, ROW_TILE)
                layers = [density_ref[bit * last_deep + i, at] for i in range(HALO)]
                for i, word in enumerate(pack(layers)):
                    ref[i, at] = word
        for ref, bit in ((row_even_ref, 1 - row_bit), (row_odd_ref, row_bit)):
            start = pl.multiple_of(bit * last_rows, ROW_TILE)
            ref[...] = density_ref[:, pl.ds(start, ROW_TILE)]

    rows = jax.ShapeDtypeStruct((depth_cells, ROW_TILE, columns), jnp.float32)
    deep = jax.ShapeDtypeStruct((WORDS, row_cells, columns), jnp.int32)
    vmem = pl.BlockSpec(memory_space=pltpu.VMEM)
    return pl.pallas_call(
        kernel,
        out_shape=(rows, rows, deep, deep),
        in_specs=[vmem],
        out_specs=(vmem,) * 4,
        compiler_params=pltpu.CompilerParams(vmem_limit_bytes=VMEM_BYTES),
        name="cut_edges",
    )(density)


def composite_kernel(order_in, in_ref, out_ref, values, order_ref, sems):
    wait_scalars = fetch_scalars([(order_in, order_ref)], sems)
    count = in_ref.shape[0]
    rows = in_ref.shape[2] // 4
    for source in range(count):
        for view in range(VIEWS):
            values[source, view] = decode(in_ref[source, view])
    wait_scalars()
    for view in range(VIEWS):
        colour, transmit = None, None
        for k in range(count):
            source = order_ref[view, k]
            part = [values[source, view, pl.ds(c * rows, rows)] for c in range(4)]
            clear = 1.0 - part[3]
            if k == 0:
                colour, transmit = part[:3], clear
            else:
                colour = [colour[c] + transmit * part[c] for c in range(3)]
                transmit = transmit * clear
        for c, value in enumerate(colour + [1.0 - transmit]):
            out_ref[view, c, 0] = value


def body(density, live_slices, shear_slopes, palette, depth_order, tile_owner):
    depth_cells, row_cells, columns = density.shape
    n_depth = lax.axis_size("gz")
    edge = depth_cells - HALO
    odd_depth = lax.axis_index("gz") % 2 == 1

    def pairs(axis, first):
        count = lax.axis_size(axis)
        lower = range(first, count - 1, 2)
        return [(i, i + 1) for i in lower] + [(i + 1, i) for i in lower]

    row_even, row_odd, deep_even, deep_odd = cut_edges(density)
    row_even = lax.ppermute(row_even, "xy", pairs("xy", 0))
    row_odd = lax.ppermute(row_odd, "xy", pairs("xy", 1))
    deep_odd = lax.ppermute(deep_odd, "gz", pairs("gz", 1))
    deep_even = lax.ppermute(deep_even, "gz", pairs("gz", 0))
    rows = jnp.concatenate([row_even, row_odd], axis=1)
    facing = jnp.where(odd_depth, edge, 0)
    corner_odd = lax.ppermute(
        lax.dynamic_slice_in_dim(rows, facing, HALO), "gz", pairs("gz", 1)
    )
    corner_even = lax.ppermute(
        lax.dynamic_slice_in_dim(rows, edge - facing, HALO), "gz", pairs("gz", 0)
    )
    shear, band_weights = make_tables(shear_slopes, depth_cells, columns, n_depth)
    inner, deep = render_inner(
        live_slices, palette, tile_owner, density, deep_odd, deep_even, shear, band_weights, n_depth
    )
    outgoing = render_edges(
        live_slices, palette, tile_owner, corner_odd, corner_even, row_even, row_odd,
        inner, deep, shear, band_weights, n_depth,
    )
    incoming = lax.all_to_all(outgoing, "gz", split_axis=0, concat_axis=0, tiled=True)
    tile_rows = row_cells // n_depth
    return pl.pallas_call(
        composite_kernel,
        out_shape=jax.ShapeDtypeStruct((VIEWS, 4, 1, tile_rows, columns), jnp.float32),
        in_specs=[pl.BlockSpec(memory_space=pltpu.VMEM)] * 2,
        out_specs=pl.BlockSpec(memory_space=pltpu.VMEM),
        scratch_shapes=[
            pltpu.VMEM(incoming.shape, jnp.float32),
            pltpu.SMEM(depth_order.shape, jnp.int32),
            pltpu.SemaphoreType.DMA((1,)),
        ],
        compiler_params=pltpu.CompilerParams(vmem_limit_bytes=VMEM_BYTES),
        name="composite",
    )(depth_order, incoming)


def solution(mesh):
    placed = (P("gz", "xy", None), P(), P(), P(), P(), P())
    return jax.shard_map(
        body, mesh=mesh, in_specs=placed, out_specs=P(None, None, "gz", "xy", None), check_vma=False
    )
```

```python
import math

import jax
import jax.numpy as jnp
from jax import lax
from jax.experimental import pallas as pl
from jax.experimental.pallas import tpu as pltpu
from jax.sharding import PartitionSpec as P

LIGHT = (0.48, 0.6, 0.64)
REACH = 4
HALO = REACH + 1
TAPS = 2 * REACH + 1
ROW_TILE = 8
PACKED_ROWS = 16
EDGE = 8
VIEWS = 2
TOP = 2.2
STEPS = 65535.0
MIDDLE = 32768
LEVELS_PER_UNIT = float(1 << 17)
WORDS, SPARE = HALO - 1, 7
VMEM_BYTES = 40 * 1024 * 1024


def column_matrix(columns):
    source = lax.broadcasted_iota(jnp.int32, (columns, columns), 0)
    target = lax.broadcasted_iota(jnp.int32, (columns, columns), 1)

    def band(shift):
        at = target + shift
        inside = (jnp.abs(source - at) <= REACH) & (at >= 0) & (at < columns)
        return jnp.where(inside, 1.0, 0.0).astype(jnp.float32)

    return jnp.concatenate([band(0), band(1) - band(-1)], axis=1).astype(jnp.bfloat16)


def shear_matrices(slopes_ref, slice_depth, columns, total_depth):
    source = lax.broadcasted_iota(jnp.int32, (columns, columns), 0)
    target = lax.broadcasted_iota(jnp.int32, (columns, columns), 1)
    distance = (source - target).astype(jnp.float32)
    parts = []
    for view in range(VIEWS):
        shift = slopes_ref[view] * (slice_depth + 0.5 - 0.5 * total_depth)
        parts.append(jnp.maximum(0.0, 1.0 - jnp.abs(distance + shift)))
    return jnp.concatenate(parts, axis=1).astype(jnp.bfloat16)


def window_sums(layers, taps):
    sums, width = layers, 1
    while 2 * width < taps:
        sums = [sums[i] + sums[i + width] for i in range(len(sums) - width)]
        width *= 2
    return [sums[i] + layers[i + width] for i in range(len(layers) - width)]


def pack(values):
    levels = [jnp.floor(x * LEVELS_PER_UNIT + 0.5).astype(jnp.int32) for x in values]
    return [
        (levels[i] << SPARE) | ((levels[WORDS] >> (SPARE * i)) & 0x7F) for i in range(WORDS)
    ]


def unpack(words):
    last = words[0] & 0x7F
    for i in range(1, WORDS):
        last = last | ((words[i] & 0x7F) << (SPARE * i))
    levels = [word >> SPARE for word in words] + [(last << 4) >> 4]
    return [x.astype(jnp.float32) * (1.0 / LEVELS_PER_UNIT) for x in levels]


def encode(value):
    scale = math.log2(STEPS) - 0.125 * math.log2(TOP)
    root = jnp.exp2(0.125 * jnp.log2(jnp.maximum(value, 1e-30)) + scale)
    return (root + 0.5).astype(jnp.int32) - MIDDLE


def decode(code):
    root = (code.astype(jnp.int32) + MIDDLE).astype(jnp.float32) * (TOP**0.125 / STEPS)
    square = root * root
    fourth = square * square
    return fourth * fourth


def column_sums(total, weights):
    hi = total.astype(jnp.bfloat16)
    rest = total - hi.astype(jnp.float32)
    mid = rest.astype(jnp.bfloat16)
    lo = (rest - mid.astype(jnp.float32)).astype(jnp.bfloat16)
    split = jnp.concatenate([hi, mid, lo], axis=1)
    return jnp.dot(split, weights, preferred_element_type=jnp.float32)


def shade(center, diff_depth, diff_rows, diff_cols, live, palette_ref, extinct):
    cells = TAPS**3
    floor = 0.01 * (2.0 * cells) ** 2
    square = diff_depth * diff_depth + diff_rows * diff_rows + diff_cols * diff_cols + floor
    light = [0.75 * part for part in LIGHT]
    toward = light[0] * diff_depth + light[1] * diff_rows + light[2] * diff_cols
    facing = jnp.maximum(0.0, toward) * lax.rsqrt(square)
    t = center * (2.0 * math.log2(math.e) / cells)
    softplus = jnp.maximum(t, 0.0) + jnp.log2(1.0 + jnp.exp2(-jnp.abs(t)))
    opacity = 1.0 - jnp.exp2(jnp.where(live, -extinct, 0.0) * softplus)
    bright = opacity * (0.25 + facing)
    channels = [bright * palette_ref[c] for c in range(3)] + [opacity]
    return [channel.astype(jnp.bfloat16) for channel in channels]


def march(layer, depth_cells, view):
    colour, transmit = None, None
    for z in range(depth_cells):
        part = [layer(z, c) for c in range(4)]
        clear = 1.0 - part[3]
        if z == 0:
            colour, transmit = part[:3], clear
        elif view == 0:
            colour = [colour[c] + transmit * part[c] for c in range(3)]
            transmit = transmit * clear
        else:
            colour = [part[c] + clear * colour[c] for c in range(3)]
            transmit = transmit * clear
    return colour + [1.0 - transmit]


def store_codes(out_ref, place, view, codes, row, tile_rows, other=None):
    if tile_rows < PACKED_ROWS:
        for c in range(0, 4, 2):
            pair = jnp.concatenate(codes[c : c + 2])
            out_ref[place, view, pl.ds(c * tile_rows, PACKED_ROWS)] = pair.astype(jnp.int16)
        return
    for c in range(4):
        at = pl.ds(c * tile_rows + row // PACKED_ROWS * PACKED_ROWS, PACKED_ROWS)
        code = codes[c]
        if code.shape[0] < PACKED_ROWS:
            half = row % PACKED_ROWS
            rest = jnp.zeros_like(code)
            if other is not None:
                rest = other[place, view, at].astype(jnp.int32)
                rest = rest[ROW_TILE:] if half == 0 else rest[:ROW_TILE]
            code = jnp.concatenate([code, rest] if half == 0 else [rest, code])
        out_ref[place, view, at] = code.astype(jnp.int16)


def fetch_scalars(pairs, sems):
    copies = [
        pltpu.make_async_copy(source, target, sems.at[i]) for i, (source, target) in enumerate(pairs)
    ]
    for copy in copies:
        copy.start()

    def wait():
        for copy in copies:
            copy.wait()

    return wait


def zero_outside(smooth, depth_index, n_depth, layers):
    @pl.when(depth_index == 0)
    def _():
        smooth[0] = jnp.zeros_like(smooth[0])

    @pl.when(depth_index == n_depth - 1)
    def _():
        smooth[layers - 1] = jnp.zeros_like(smooth[layers - 1])


def render_inner(live_slices, slopes, palette, owner, density, deep_odd, deep_even, n_depth):
    depth_cells, row_cells, columns = density.shape
    total_depth = depth_cells * n_depth
    extinct = 3.0 / total_depth
    tile_rows = row_cells // n_depth
    layers = depth_cells + 2
    rows = range(EDGE, row_cells - EDGE)
    height = len(rows)
    lead, span = EDGE, height + 2 * ROW_TILE

    def kernel(
        live_in, slopes_in, palette_in, owner_in, own_ref, odd_ref, even_ref,
        out_ref, deep, shear_ref, band_ref, triple, smooth, across, sheared,
        live_ref, slopes_ref, palette_ref, owner_ref, sems,
    ):
        wait_scalars = fetch_scalars(
            [
                (live_in, live_ref),
                (slopes_in, slopes_ref),
                (palette_in, palette_ref),
                (owner_in, owner_ref),
            ],
            sems,
        )
        depth_index = lax.axis_index("gz")
        row_index = lax.axis_index("xy")
        odd_depth = depth_index % 2 == 1

        for start in range(0, row_cells, ROW_TILE):
            at = pl.ds(start, ROW_TILE)
            even = [even_ref[i, at] for i in range(WORDS)]
            odd = [odd_ref[i, at] for i in range(WORDS)]
            low = unpack([jnp.where(odd_depth, e, o) for e, o in zip(even, odd)])
            high = unpack([jnp.where(odd_depth, o, e) for e, o in zip(even, odd)])
            own = [own_ref[i, at] for i in range(depth_cells)]
            for z, total in enumerate(window_sums(low + own + high, TAPS)):
                deep[z, pl.ds(ROW_TILE + start, ROW_TILE)] = total

        band = column_matrix(columns)
        band_ref[...] = band
        weights = jnp.concatenate([band, band, band], axis=0)
        for z in range(layers):
            triple[z] = (
                deep[z, pl.ds(lead - 4, span + ROW_TILE)]
                + deep[z, pl.ds(lead - 3, span + ROW_TILE)]
                + deep[z, pl.ds(lead - 2, span + ROW_TILE)]
            )
            total = (
                triple[z, pl.ds(0, span)] + triple[z, pl.ds(3, span)] + triple[z, pl.ds(6, span)]
            )
            if 1 <= z <= depth_cells:
                both = column_sums(total, weights)
                smooth[z] = both[:, :columns]
                across[z - 1] = both[ROW_TILE : ROW_TILE + height, columns:]
            else:
                smooth[z] = column_sums(total, weights[:, :columns])
        zero_outside(smooth, depth_index, n_depth, layers)

        wait_scalars()
        slab_start = (depth_index * depth_cells).astype(jnp.float32)
        for z in range(depth_cells):
            shear_ref[z] = shear_matrices(slopes_ref, slab_start + float(z), columns, total_depth)

        own_live = live_ref[depth_index, row_index]
        middle = pl.ds(ROW_TILE, height)
        for z in range(depth_cells):
            channels = shade(
                smooth[z + 1, middle],
                smooth[z + 2, middle] - smooth[z, middle],
                smooth[z + 1, pl.ds(ROW_TILE + 1, height)]
                - smooth[z + 1, pl.ds(ROW_TILE - 1, height)],
                across[z],
                z < own_live,
                palette_ref,
                extinct,
            )
            sheared[z] = jnp.dot(
                jnp.concatenate(channels), shear_ref[z], preferred_element_type=jnp.float32
            )
        row = rows.start
        while row < rows.stop:
            whole = tile_rows >= PACKED_ROWS and row % PACKED_ROWS == 0
            count = PACKED_ROWS if whole and row + PACKED_ROWS <= rows.stop else ROW_TILE
            at = row - rows.start
            for view in range(VIEWS):
                lanes = pl.ds(view * columns, columns)
                values = march(
                    lambda z, c: sheared[z, pl.ds(c * height + at, count), lanes],
                    depth_cells,
                    view,
                )
                place = owner_ref[view, row // tile_rows]
                codes = [encode(value) for value in values]
                store_codes(out_ref, place, view, codes, row % tile_rows, tile_rows)
            row += count

    vmem = pl.BlockSpec(memory_space=pltpu.VMEM)
    return pl.pallas_call(
        kernel,
        out_shape=(
            jax.ShapeDtypeStruct((n_depth, VIEWS, 4 * tile_rows, columns), jnp.int16),
            jax.ShapeDtypeStruct((layers, row_cells + 2 * ROW_TILE, columns), jnp.float32),
            jax.ShapeDtypeStruct((depth_cells, columns, VIEWS * columns), jnp.bfloat16),
            jax.ShapeDtypeStruct((columns, 2 * columns), jnp.bfloat16),
        ),
        in_specs=[vmem] * 7,
        out_specs=(vmem,) * 4,
        scratch_shapes=[
            pltpu.VMEM((layers, span + ROW_TILE, columns), jnp.float32),
            pltpu.VMEM((layers, span, columns), jnp.float32),
            pltpu.VMEM((depth_cells, height, columns), jnp.float32),
            pltpu.VMEM((depth_cells, 4 * height, VIEWS * columns), jnp.float32),
            pltpu.SMEM(live_slices.shape, jnp.int32),
            pltpu.SMEM(slopes.shape, jnp.float32),
            pltpu.SMEM(palette.shape, jnp.float32),
            pltpu.SMEM(owner.shape, jnp.int32),
            pltpu.SemaphoreType.DMA((4,)),
        ],
        compiler_params=pltpu.CompilerParams(vmem_limit_bytes=VMEM_BYTES),
        cost_estimate=pl.CostEstimate(
            flops=100 * depth_cells * row_cells * columns,
            bytes_accessed=16 * 4 * depth_cells * row_cells * columns,
            transcendentals=4 * depth_cells * row_cells * columns,
        ),
        name="render_inner",
    )(live_slices, slopes, palette, owner, density, deep_odd, deep_even)


def render_edges(
    live_slices, palette, owner, corner_even, corner_odd, row_even, row_odd,
    inner, deep, shear, band_weights, n_depth,
):
    layers, padded_rows, columns = deep.shape
    row_cells = padded_rows - 2 * ROW_TILE
    depth_cells = layers - 2
    n_rows = lax.axis_size("xy")
    extinct = 3.0 / (depth_cells * n_depth)
    tile_rows = row_cells // n_depth
    band = EDGE + 2 * ROW_TILE
    piece = 2 * ROW_TILE
    height = 2 * EDGE

    def kernel(
        live_in, palette_in, owner_in, corner_even_ref, corner_odd_ref, row_even_ref, row_odd_ref,
        inner_ref, deep_ref, shear_ref, band_ref,
        out_ref, halo, triple, split_sums, smooth, across, sheared,
        live_ref, palette_ref, owner_ref, sems,
    ):
        wait_scalars = fetch_scalars(
            [(live_in, live_ref), (palette_in, palette_ref), (owner_in, owner_ref)], sems
        )
        depth_index = lax.axis_index("gz")
        row_index = lax.axis_index("xy")
        odd_depth = depth_index % 2 == 1

        odd_row = row_index % 2 == 1
        from_even, from_odd = pl.ds(0, ROW_TILE), pl.ds(ROW_TILE, ROW_TILE)
        for side in range(2):
            take_even = odd_row if side == 0 else jnp.logical_not(odd_row)

            def facing_rows(ref, i):
                return jnp.where(take_even, ref[i, from_even], ref[i, from_odd])

            even = [facing_rows(corner_even_ref, i) for i in range(HALO)]
            odd = [facing_rows(corner_odd_ref, i) for i in range(HALO)]
            middle = [
                jnp.where(take_even, row_even_ref[i], row_odd_ref[i]) for i in range(depth_cells)
            ]
            low = [jnp.where(odd_depth, e, o) for e, o in zip(even, odd)]
            high = [jnp.where(odd_depth, o, e) for e, o in zip(even, odd)]
            outer = 0 if side == 0 else band - ROW_TILE
            inner_at = ROW_TILE if side == 0 else 0
            own_at = ROW_TILE if side == 0 else padded_rows - band
            sums = window_sums(low + middle + high, TAPS)
            for z in range(layers):
                halo[z, side, pl.ds(outer, ROW_TILE)] = sums[z]
                halo[z, side, pl.ds(inner_at, band - ROW_TILE)] = deep_ref[
                    z, pl.ds(own_at, band - ROW_TILE)
                ]

        span = band - ROW_TILE
        for z in range(layers):
            for side in range(2):
                triple[z, side, pl.ds(0, span)] = (
                    halo[z, side, pl.ds(3, span)]
                    + halo[z, side, pl.ds(4, span)]
                    + halo[z, side, pl.ds(5, span)]
                )
                split_sums[z, side] = (
                    triple[z, side, pl.ds(0, piece)]
                    + triple[z, side, pl.ds(3, piece)]
                    + triple[z, side, pl.ds(6, piece)]
                )
        weights = jnp.concatenate([band_ref[...]] * 3, axis=0)
        both = column_sums(split_sums[...].reshape(layers * 2 * piece, columns), weights)
        both = both.reshape(layers, 2, piece, 2 * columns)
        smooth[...] = both[..., :columns]
        across[...] = both[1:-1, :, :, columns:]

        @pl.when(row_index == 0)
        def _():
            smooth[:, 0, :1] = jnp.zeros((layers, 1, columns), jnp.float32)

        @pl.when(row_index == n_rows - 1)
        def _():
            smooth[:, 1, EDGE + 1 : EDGE + 2] = jnp.zeros((layers, 1, columns), jnp.float32)

        zero_outside(smooth, depth_index, n_depth, layers)

        wait_scalars()
        own_live = live_ref[depth_index, row_index]

        def both_sides(ref, z, start):
            return ref[z, :, pl.ds(start, EDGE)].reshape(height, columns)

        for z in range(depth_cells):
            channels = shade(
                both_sides(smooth, z + 1, 1),
                both_sides(smooth, z + 2, 1) - both_sides(smooth, z, 1),
                both_sides(smooth, z + 1, 2) - both_sides(smooth, z + 1, 0),
                both_sides(across, z, 1),
                z < own_live,
                palette_ref,
                extinct,
            )
            sheared[z] = jnp.dot(
                jnp.concatenate(channels), shear_ref[z], preferred_element_type=jnp.float32
            )
        out_ref[...] = inner_ref[...]
        for view in range(VIEWS):
            lanes = pl.ds(view * columns, columns)
            values = march(
                lambda z, c: sheared[z, pl.ds(c * height, height), lanes], depth_cells, view
            )
            codes = [encode(value) for value in values]
            for side, row in enumerate((0, row_cells - EDGE)):
                place = owner_ref[view, row // tile_rows]
                part = [code[side * EDGE : (side + 1) * EDGE] for code in codes]
                store_codes(out_ref, place, view, part, row % tile_rows, tile_rows, inner_ref)

    vmem = pl.BlockSpec(memory_space=pltpu.VMEM)
    return pl.pallas_call(
        kernel,
        out_shape=jax.ShapeDtypeStruct(inner.shape, inner.dtype),
        in_specs=[vmem] * 11,
        out_specs=vmem,
        scratch_shapes=[
            pltpu.VMEM((layers, 2, band, columns), jnp.float32),
            pltpu.VMEM((layers, 2, piece + ROW_TILE, columns), jnp.float32),
            pltpu.VMEM((layers, 2, piece, columns), jnp.float32),
            pltpu.VMEM((layers, 2, piece, columns), jnp.float32),
            pltpu.VMEM((depth_cells, 2, piece, columns), jnp.float32),
            pltpu.VMEM((depth_cells, 4 * height, VIEWS * columns), jnp.float32),
            pltpu.SMEM(live_slices.shape, jnp.int32),
            pltpu.SMEM(palette.shape, jnp.float32),
            pltpu.SMEM(owner.shape, jnp.int32),
            pltpu.SemaphoreType.DMA((3,)),
        ],
        compiler_params=pltpu.CompilerParams(vmem_limit_bytes=VMEM_BYTES),
        name="render_edges",
    )(
        live_slices, palette, owner, corner_even, corner_odd, row_even, row_odd,
        inner, deep, shear, band_weights,
    )


def cut_edges(density):
    depth_cells, row_cells, columns = density.shape

    def kernel(density_ref, row_even_ref, row_odd_ref, deep_even_ref, deep_odd_ref):
        row_bit = lax.axis_index("xy") % 2
        depth_bit = lax.axis_index("gz") % 2
        last_rows, last_deep = row_cells - ROW_TILE, depth_cells - HALO
        for ref, bit in ((deep_odd_ref, depth_bit), (deep_even_ref, 1 - depth_bit)):
            for start in range(0, row_cells, ROW_TILE):
                at = pl.ds(start, ROW_TILE)
                layers = [density_ref[bit * last_deep + i, at] for i in range(HALO)]
                for i, word in enumerate(pack(layers)):
                    ref[i, at] = word
        for ref, bit in ((row_even_ref, 1 - row_bit), (row_odd_ref, row_bit)):
            start = pl.multiple_of(bit * last_rows, ROW_TILE)
            ref[...] = density_ref[:, pl.ds(start, ROW_TILE)]

    rows = jax.ShapeDtypeStruct((depth_cells, ROW_TILE, columns), jnp.float32)
    deep = jax.ShapeDtypeStruct((WORDS, row_cells, columns), jnp.int32)
    vmem = pl.BlockSpec(memory_space=pltpu.VMEM)
    return pl.pallas_call(
        kernel,
        out_shape=(rows, rows, deep, deep),
        in_specs=[vmem],
        out_specs=(vmem,) * 4,
        compiler_params=pltpu.CompilerParams(vmem_limit_bytes=VMEM_BYTES),
        name="cut_edges",
    )(density)


def composite_kernel(order_in, in_ref, out_ref, values, order_ref, sems):
    wait_scalars = fetch_scalars([(order_in, order_ref)], sems)
    count = in_ref.shape[0]
    rows = in_ref.shape[2] // 4
    for source in range(count):
        for view in range(VIEWS):
            values[source, view] = decode(in_ref[source, view])
    wait_scalars()
    for view in range(VIEWS):
        colour, transmit = None, None
        for k in range(count):
            source = order_ref[view, k]
            part = [values[source, view, pl.ds(c * rows, rows)] for c in range(4)]
            clear = 1.0 - part[3]
            if k == 0:
                colour, transmit = part[:3], clear
            else:
                colour = [colour[c] + transmit * part[c] for c in range(3)]
                transmit = transmit * clear
        for c, value in enumerate(colour + [1.0 - transmit]):
            out_ref[view, c, 0] = value


def body(density, live_slices, shear_slopes, palette, depth_order, tile_owner):
    depth_cells, row_cells, columns = density.shape
    n_depth = lax.axis_size("gz")
    edge = depth_cells - HALO
    odd_depth = lax.axis_index("gz") % 2 == 1

    def pairs(axis, first):
        count = lax.axis_size(axis)
        lower = range(first, count - 1, 2)
        return [(i, i + 1) for i in lower] + [(i + 1, i) for i in lower]

    row_even, row_odd, deep_even, deep_odd = cut_edges(density)
    row_even = lax.ppermute(row_even, "xy", pairs("xy", 0))
    row_odd = lax.ppermute(row_odd, "xy", pairs("xy", 1))
    deep_odd = lax.ppermute(deep_odd, "gz", pairs("gz", 1))
    deep_even = lax.ppermute(deep_even, "gz", pairs("gz", 0))
    rows = jnp.concatenate([row_even, row_odd], axis=1)
    facing = jnp.where(odd_depth, edge, 0)
    corner_odd = lax.ppermute(
        lax.dynamic_slice_in_dim(rows, facing, HALO), "gz", pairs("gz", 1)
    )
    corner_even = lax.ppermute(
        lax.dynamic_slice_in_dim(rows, edge - facing, HALO), "gz", pairs("gz", 0)
    )
    inner, deep, shear, band_weights = render_inner(
        live_slices, shear_slopes, palette, tile_owner, density, deep_odd, deep_even, n_depth
    )
    outgoing = render_edges(
        live_slices, palette, tile_owner, corner_even, corner_odd, row_even, row_odd,
        inner, deep, shear, band_weights, n_depth,
    )
    incoming = lax.all_to_all(outgoing, "gz", split_axis=0, concat_axis=0, tiled=True)
    tile_rows = row_cells // n_depth
    return pl.pallas_call(
        composite_kernel,
        out_shape=jax.ShapeDtypeStruct((VIEWS, 4, 1, tile_rows, columns), jnp.float32),
        in_specs=[pl.BlockSpec(memory_space=pltpu.VMEM)] * 2,
        out_specs=pl.BlockSpec(memory_space=pltpu.VMEM),
        scratch_shapes=[
            pltpu.VMEM(incoming.shape, jnp.float32),
            pltpu.SMEM(depth_order.shape, jnp.int32),
            pltpu.SemaphoreType.DMA((1,)),
        ],
        compiler_params=pltpu.CompilerParams(vmem_limit_bytes=VMEM_BYTES),
        name="composite",
    )(depth_order, incoming)


def solution(mesh):
    placed = (P("gz", "xy", None), P(), P(), P(), P(), P())
    return jax.shard_map(
        body, mesh=mesh, in_specs=placed, out_specs=P(None, None, "gz", "xy", None), check_vma=False
    )
```

```python
import math

import jax
import jax.numpy as jnp
from jax import lax
from jax.experimental import pallas as pl
from jax.experimental.pallas import tpu as pltpu
from jax.sharding import PartitionSpec as P

LIGHT = (0.48, 0.6, 0.64)
REACH = 4
HALO = REACH + 1
TAPS = 2 * REACH + 1
ROW_TILE = 8
PACKED_ROWS = 16
EDGE = 8
VIEWS = 2
TOP = 2.2
STEPS = 65535.0
MIDDLE = 32768
LEVELS_PER_UNIT = float(1 << 17)
WORDS, SPARE = HALO - 1, 7
VMEM_BYTES = 40 * 1024 * 1024


def column_matrix(columns):
    source = lax.broadcasted_iota(jnp.int32, (columns, columns), 0)
    target = lax.broadcasted_iota(jnp.int32, (columns, columns), 1)

    def band(shift):
        at = target + shift
        inside = (jnp.abs(source - at) <= REACH) & (at >= 0) & (at < columns)
        return jnp.where(inside, 1.0, 0.0).astype(jnp.float32)

    return jnp.concatenate([band(0), band(1) - band(-1)], axis=1).astype(jnp.bfloat16)


def shear_matrices(slopes_ref, slice_depth, columns, total_depth):
    source = lax.broadcasted_iota(jnp.int32, (columns, columns), 0)
    target = lax.broadcasted_iota(jnp.int32, (columns, columns), 1)
    distance = (source - target).astype(jnp.float32)
    parts = []
    for view in range(VIEWS):
        shift = slopes_ref[view] * (slice_depth + 0.5 - 0.5 * total_depth)
        parts.append(jnp.maximum(0.0, 1.0 - jnp.abs(distance + shift)))
    return jnp.concatenate(parts, axis=1).astype(jnp.bfloat16)


def window_sums(layers, taps):
    sums, width = layers, 1
    while 2 * width < taps:
        sums = [sums[i] + sums[i + width] for i in range(len(sums) - width)]
        width *= 2
    return [sums[i] + layers[i + width] for i in range(len(layers) - width)]


def pack(values):
    levels = [jnp.floor(x * LEVELS_PER_UNIT + 0.5).astype(jnp.int32) for x in values]
    return [
        (levels[i] << SPARE) | ((levels[WORDS] >> (SPARE * i)) & 0x7F) for i in range(WORDS)
    ]


def unpack(words):
    last = words[0] & 0x7F
    for i in range(1, WORDS):
        last = last | ((words[i] & 0x7F) << (SPARE * i))
    levels = [word >> SPARE for word in words] + [(last << 4) >> 4]
    return [x.astype(jnp.float32) * (1.0 / LEVELS_PER_UNIT) for x in levels]


def encode(value):
    scale = math.log2(STEPS) - 0.125 * math.log2(TOP)
    root = jnp.exp2(0.125 * jnp.log2(jnp.maximum(value, 1e-30)) + scale)
    return (root + 0.5).astype(jnp.int32) - MIDDLE


def decode(code):
    root = (code.astype(jnp.int32) + MIDDLE).astype(jnp.float32) * (TOP**0.125 / STEPS)
    square = root * root
    fourth = square * square
    return fourth * fourth


def column_sums(total, weights):
    hi = total.astype(jnp.bfloat16)
    rest = total - hi.astype(jnp.float32)
    mid = rest.astype(jnp.bfloat16)
    lo = (rest - mid.astype(jnp.float32)).astype(jnp.bfloat16)
    split = jnp.concatenate([hi, mid, lo], axis=1)
    return jnp.dot(split, weights, preferred_element_type=jnp.float32)


def shade(center, diff_depth, diff_rows, diff_cols, live, palette_ref, extinct):
    cells = TAPS**3
    floor = 0.01 * (2.0 * cells) ** 2
    square = diff_depth * diff_depth + diff_rows * diff_rows + diff_cols * diff_cols + floor
    light = [0.75 * part for part in LIGHT]
    toward = light[0] * diff_depth + light[1] * diff_rows + light[2] * diff_cols
    facing = jnp.maximum(0.0, toward) * lax.rsqrt(square)
    t = center * (2.0 * math.log2(math.e) / cells)
    softplus = jnp.maximum(t, 0.0) + jnp.log2(1.0 + jnp.exp2(-jnp.abs(t)))
    opacity = 1.0 - jnp.exp2(jnp.where(live, -extinct, 0.0) * softplus)
    bright = opacity * (0.25 + facing)
    channels = [bright * palette_ref[c] for c in range(3)] + [opacity]
    return [channel.astype(jnp.bfloat16) for channel in channels]


def march(layer, depth_cells, view):
    colour, transmit = None, None
    for z in range(depth_cells):
        part = [layer(z, c) for c in range(4)]
        clear = 1.0 - part[3]
        if z == 0:
            colour, transmit = part[:3], clear
        elif view == 0:
            colour = [colour[c] + transmit * part[c] for c in range(3)]
            transmit = transmit * clear
        else:
            colour = [part[c] + clear * colour[c] for c in range(3)]
            transmit = transmit * clear
    return colour + [1.0 - transmit]


def store_codes(out_ref, place, view, codes, row, tile_rows, other=None):
    if tile_rows < PACKED_ROWS:
        for c in range(0, 4, 2):
            pair = jnp.concatenate(codes[c : c + 2])
            out_ref[place, view, pl.ds(c * tile_rows, PACKED_ROWS)] = pair.astype(jnp.int16)
        return
    for c in range(4):
        at = pl.ds(c * tile_rows + row // PACKED_ROWS * PACKED_ROWS, PACKED_ROWS)
        code = codes[c]
        if code.shape[0] < PACKED_ROWS:
            half = row % PACKED_ROWS
            rest = jnp.zeros_like(code)
            if other is not None:
                rest = other[place, view, at].astype(jnp.int32)
                rest = rest[ROW_TILE:] if half == 0 else rest[:ROW_TILE]
            code = jnp.concatenate([code, rest] if half == 0 else [rest, code])
        out_ref[place, view, at] = code.astype(jnp.int16)


def fetch_scalars(pairs, sems):
    copies = [
        pltpu.make_async_copy(source, target, sems.at[i]) for i, (source, target) in enumerate(pairs)
    ]
    for copy in copies:
        copy.start()

    def wait():
        for copy in copies:
            copy.wait()

    return wait


def zero_outside(smooth, depth_index, n_depth, layers):
    @pl.when(depth_index == 0)
    def _():
        smooth[0] = jnp.zeros_like(smooth[0])

    @pl.when(depth_index == n_depth - 1)
    def _():
        smooth[layers - 1] = jnp.zeros_like(smooth[layers - 1])


def render_inner(live_slices, slopes, palette, owner, density, deep_odd, deep_even, n_depth):
    depth_cells, row_cells, columns = density.shape
    total_depth = depth_cells * n_depth
    extinct = 3.0 / total_depth
    tile_rows = row_cells // n_depth
    layers = depth_cells + 2
    rows = range(EDGE, row_cells - EDGE)
    height = len(rows)
    lead, span = EDGE, height + 2 * ROW_TILE

    def kernel(
        live_in, slopes_in, palette_in, owner_in, own_ref, odd_ref, even_ref,
        out_ref, deep, shear_ref, band_ref, triple, smooth, across, sheared,
        live_ref, slopes_ref, palette_ref, owner_ref, sems,
    ):
        wait_scalars = fetch_scalars(
            [
                (live_in, live_ref),
                (slopes_in, slopes_ref),
                (palette_in, palette_ref),
                (owner_in, owner_ref),
            ],
            sems,
        )
        depth_index = lax.axis_index("gz")
        row_index = lax.axis_index("xy")
        odd_depth = depth_index % 2 == 1

        for start in range(0, row_cells, ROW_TILE):
            at = pl.ds(start, ROW_TILE)
            even = [even_ref[i, at] for i in range(WORDS)]
            odd = [odd_ref[i, at] for i in range(WORDS)]
            low = unpack([jnp.where(odd_depth, e, o) for e, o in zip(even, odd)])
            high = unpack([jnp.where(odd_depth, o, e) for e, o in zip(even, odd)])
            own = [own_ref[i, at] for i in range(depth_cells)]
            for z, total in enumerate(window_sums(low + own + high, TAPS)):
                deep[z, pl.ds(ROW_TILE + start, ROW_TILE)] = total

        band = column_matrix(columns)
        band_ref[...] = band
        weights = jnp.concatenate([band, band, band], axis=0)
        for z in range(layers):
            triple[z] = (
                deep[z, pl.ds(lead - 4, span + ROW_TILE)]
                + deep[z, pl.ds(lead - 3, span + ROW_TILE)]
                + deep[z, pl.ds(lead - 2, span + ROW_TILE)]
            )
            total = (
                triple[z, pl.ds(0, span)] + triple[z, pl.ds(3, span)] + triple[z, pl.ds(6, span)]
            )
            if 1 <= z <= depth_cells:
                both = column_sums(total, weights)
                smooth[z] = both[:, :columns]
                across[z - 1] = both[ROW_TILE : ROW_TILE + height, columns:]
            else:
                smooth[z] = column_sums(total, weights[:, :columns])
        zero_outside(smooth, depth_index, n_depth, layers)

        wait_scalars()
        slab_start = (depth_index * depth_cells).astype(jnp.float32)
        for z in range(depth_cells):
            shear_ref[z] = shear_matrices(slopes_ref, slab_start + float(z), columns, total_depth)

        own_live = live_ref[depth_index, row_index]
        middle = pl.ds(ROW_TILE, height)
        for z in range(depth_cells):
            channels = shade(
                smooth[z + 1, middle],
                smooth[z + 2, middle] - smooth[z, middle],
                smooth[z + 1, pl.ds(ROW_TILE + 1, height)]
                - smooth[z + 1, pl.ds(ROW_TILE - 1, height)],
                across[z],
                z < own_live,
                palette_ref,
                extinct,
            )
            sheared[z] = jnp.dot(
                jnp.concatenate(channels), shear_ref[z], preferred_element_type=jnp.float32
            )
        row = rows.start
        while row < rows.stop:
            whole = tile_rows >= PACKED_ROWS and row % PACKED_ROWS == 0
            count = PACKED_ROWS if whole and row + PACKED_ROWS <= rows.stop else ROW_TILE
            at = row - rows.start
            for view in range(VIEWS):
                lanes = pl.ds(view * columns, columns)
                values = march(
                    lambda z, c: sheared[z, pl.ds(c * height + at, count), lanes],
                    depth_cells,
                    view,
                )
                place = owner_ref[view, row // tile_rows]
                codes = [encode(value) for value in values]
                store_codes(out_ref, place, view, codes, row % tile_rows, tile_rows)
            row += count

    vmem = pl.BlockSpec(memory_space=pltpu.VMEM)
    return pl.pallas_call(
        kernel,
        out_shape=(
            jax.ShapeDtypeStruct((n_depth, VIEWS, 4 * tile_rows, columns), jnp.int16),
            jax.ShapeDtypeStruct((layers, row_cells + 2 * ROW_TILE, columns), jnp.float32),
            jax.ShapeDtypeStruct((depth_cells, columns, VIEWS * columns), jnp.bfloat16),
            jax.ShapeDtypeStruct((columns, 2 * columns), jnp.bfloat16),
        ),
        in_specs=[vmem] * 7,
        out_specs=(vmem,) * 4,
        scratch_shapes=[
            pltpu.VMEM((layers, span + ROW_TILE, columns), jnp.float32),
            pltpu.VMEM((layers, span, columns), jnp.float32),
            pltpu.VMEM((depth_cells, height, columns), jnp.float32),
            pltpu.VMEM((depth_cells, 4 * height, VIEWS * columns), jnp.float32),
            pltpu.SMEM(live_slices.shape, jnp.int32),
            pltpu.SMEM(slopes.shape, jnp.float32),
            pltpu.SMEM(palette.shape, jnp.float32),
            pltpu.SMEM(owner.shape, jnp.int32),
            pltpu.SemaphoreType.DMA((4,)),
        ],
        compiler_params=pltpu.CompilerParams(vmem_limit_bytes=VMEM_BYTES),
        cost_estimate=pl.CostEstimate(
            flops=100 * depth_cells * row_cells * columns,
            bytes_accessed=16 * 4 * depth_cells * row_cells * columns,
            transcendentals=4 * depth_cells * row_cells * columns,
        ),
        name="render_inner",
    )(live_slices, slopes, palette, owner, density, deep_odd, deep_even)


def render_edges(
    live_slices, palette, owner, corner_odd, corner_even, row_even, row_odd,
    inner, deep, shear, band_weights, n_depth,
):
    layers, padded_rows, columns = deep.shape
    row_cells = padded_rows - 2 * ROW_TILE
    depth_cells = layers - 2
    n_rows = lax.axis_size("xy")
    extinct = 3.0 / (depth_cells * n_depth)
    tile_rows = row_cells // n_depth
    band = EDGE + 2 * ROW_TILE
    piece = 2 * ROW_TILE
    height = 2 * EDGE

    def kernel(
        live_in, palette_in, owner_in, corner_odd_ref, corner_even_ref, row_even_ref, row_odd_ref,
        inner_ref, deep_ref, shear_ref, band_ref,
        out_ref, halo, triple, split_sums, smooth, across, sheared,
        live_ref, palette_ref, owner_ref, sems,
    ):
        wait_scalars = fetch_scalars(
            [(live_in, live_ref), (palette_in, palette_ref), (owner_in, owner_ref)], sems
        )
        depth_index = lax.axis_index("gz")
        row_index = lax.axis_index("xy")
        odd_depth = depth_index % 2 == 1

        odd_row = row_index % 2 == 1
        from_even, from_odd = pl.ds(0, ROW_TILE), pl.ds(ROW_TILE, ROW_TILE)
        for side in range(2):
            take_even = odd_row if side == 0 else jnp.logical_not(odd_row)

            def facing_rows(ref, i):
                return jnp.where(take_even, ref[i, from_even], ref[i, from_odd])

            even = [facing_rows(corner_even_ref, i) for i in range(HALO)]
            odd = [facing_rows(corner_odd_ref, i) for i in range(HALO)]
            middle = [
                jnp.where(take_even, row_even_ref[i], row_odd_ref[i]) for i in range(depth_cells)
            ]
            low = [jnp.where(odd_depth, e, o) for e, o in zip(even, odd)]
            high = [jnp.where(odd_depth, o, e) for e, o in zip(even, odd)]
            outer = 0 if side == 0 else band - ROW_TILE
            inner_at = ROW_TILE if side == 0 else 0
            own_at = ROW_TILE if side == 0 else padded_rows - band
            sums = window_sums(low + middle + high, TAPS)
            for z in range(layers):
                halo[z, side, pl.ds(outer, ROW_TILE)] = sums[z]
                halo[z, side, pl.ds(inner_at, band - ROW_TILE)] = deep_ref[
                    z, pl.ds(own_at, band - ROW_TILE)
                ]

        span = band - ROW_TILE
        for z in range(layers):
            for side in range(2):
                triple[z, side, pl.ds(0, span)] = (
                    halo[z, side, pl.ds(3, span)]
                    + halo[z, side, pl.ds(4, span)]
                    + halo[z, side, pl.ds(5, span)]
                )
                split_sums[z, side] = (
                    triple[z, side, pl.ds(0, piece)]
                    + triple[z, side, pl.ds(3, piece)]
                    + triple[z, side, pl.ds(6, piece)]
                )
        weights = jnp.concatenate([band_ref[...]] * 3, axis=0)
        both = column_sums(split_sums[...].reshape(layers * 2 * piece, columns), weights)
        both = both.reshape(layers, 2, piece, 2 * columns)
        smooth[...] = both[..., :columns]
        across[...] = both[1:-1, :, :, columns:]

        @pl.when(row_index == 0)
        def _():
            smooth[:, 0, :1] = jnp.zeros((layers, 1, columns), jnp.float32)

        @pl.when(row_index == n_rows - 1)
        def _():
            smooth[:, 1, EDGE + 1 : EDGE + 2] = jnp.zeros((layers, 1, columns), jnp.float32)

        zero_outside(smooth, depth_index, n_depth, layers)

        wait_scalars()
        own_live = live_ref[depth_index, row_index]

        def both_sides(ref, z, start):
            return ref[z, :, pl.ds(start, EDGE)].reshape(height, columns)

        for z in range(depth_cells):
            channels = shade(
                both_sides(smooth, z + 1, 1),
                both_sides(smooth, z + 2, 1) - both_sides(smooth, z, 1),
                both_sides(smooth, z + 1, 2) - both_sides(smooth, z + 1, 0),
                both_sides(across, z, 1),
                z < own_live,
                palette_ref,
                extinct,
            )
            sheared[z] = jnp.dot(
                jnp.concatenate(channels), shear_ref[z], preferred_element_type=jnp.float32
            )
        for view in range(VIEWS):
            lanes = pl.ds(view * columns, columns)
            values = march(
                lambda z, c: sheared[z, pl.ds(c * height, height), lanes], depth_cells, view
            )
            codes = [encode(value) for value in values]
            for side, row in enumerate((0, row_cells - EDGE)):
                place = owner_ref[view, row // tile_rows]
                part = [code[side * EDGE : (side + 1) * EDGE] for code in codes]
                store_codes(out_ref, place, view, part, row % tile_rows, tile_rows, out_ref)

    vmem = pl.BlockSpec(memory_space=pltpu.VMEM)
    return pl.pallas_call(
        kernel,
        out_shape=jax.ShapeDtypeStruct(inner.shape, inner.dtype),
        input_output_aliases={7: 0},
        in_specs=[vmem] * 11,
        out_specs=vmem,
        scratch_shapes=[
            pltpu.VMEM((layers, 2, band, columns), jnp.float32),
            pltpu.VMEM((layers, 2, piece + ROW_TILE, columns), jnp.float32),
            pltpu.VMEM((layers, 2, piece, columns), jnp.float32),
            pltpu.VMEM((layers, 2, piece, columns), jnp.float32),
            pltpu.VMEM((depth_cells, 2, piece, columns), jnp.float32),
            pltpu.VMEM((depth_cells, 4 * height, VIEWS * columns), jnp.float32),
            pltpu.SMEM(live_slices.shape, jnp.int32),
            pltpu.SMEM(palette.shape, jnp.float32),
            pltpu.SMEM(owner.shape, jnp.int32),
            pltpu.SemaphoreType.DMA((3,)),
        ],
        compiler_params=pltpu.CompilerParams(vmem_limit_bytes=VMEM_BYTES),
        name="render_edges",
    )(
        live_slices, palette, owner, corner_odd, corner_even, row_even, row_odd,
        inner, deep, shear, band_weights,
    )


def cut_edges(density):
    depth_cells, row_cells, columns = density.shape

    def kernel(density_ref, row_even_ref, row_odd_ref, deep_even_ref, deep_odd_ref):
        row_bit = lax.axis_index("xy") % 2
        depth_bit = lax.axis_index("gz") % 2
        last_rows, last_deep = row_cells - ROW_TILE, depth_cells - HALO
        for ref, bit in ((deep_odd_ref, depth_bit), (deep_even_ref, 1 - depth_bit)):
            for start in range(0, row_cells, ROW_TILE):
                at = pl.ds(start, ROW_TILE)
                layers = [density_ref[bit * last_deep + i, at] for i in range(HALO)]
                for i, word in enumerate(pack(layers)):
                    ref[i, at] = word
        for ref, bit in ((row_even_ref, 1 - row_bit), (row_odd_ref, row_bit)):
            start = pl.multiple_of(bit * last_rows, ROW_TILE)
            ref[...] = density_ref[:, pl.ds(start, ROW_TILE)]

    rows = jax.ShapeDtypeStruct((depth_cells, ROW_TILE, columns), jnp.float32)
    deep = jax.ShapeDtypeStruct((WORDS, row_cells, columns), jnp.int32)
    vmem = pl.BlockSpec(memory_space=pltpu.VMEM)
    return pl.pallas_call(
        kernel,
        out_shape=(rows, rows, deep, deep),
        in_specs=[vmem],
        out_specs=(vmem,) * 4,
        compiler_params=pltpu.CompilerParams(vmem_limit_bytes=VMEM_BYTES),
        name="cut_edges",
    )(density)


def composite_kernel(order_in, in_ref, out_ref, values, order_ref, sems):
    wait_scalars = fetch_scalars([(order_in, order_ref)], sems)
    count = in_ref.shape[0]
    rows = in_ref.shape[2] // 4
    for source in range(count):
        for view in range(VIEWS):
            values[source, view] = decode(in_ref[source, view])
    wait_scalars()
    for view in range(VIEWS):
        colour, transmit = None, None
        for k in range(count):
            source = order_ref[view, k]
            part = [values[source, view, pl.ds(c * rows, rows)] for c in range(4)]
            clear = 1.0 - part[3]
            if k == 0:
                colour, transmit = part[:3], clear
            else:
                colour = [colour[c] + transmit * part[c] for c in range(3)]
                transmit = transmit * clear
        for c, value in enumerate(colour + [1.0 - transmit]):
            out_ref[view, c, 0] = value


def body(density, live_slices, shear_slopes, palette, depth_order, tile_owner):
    depth_cells, row_cells, columns = density.shape
    n_depth = lax.axis_size("gz")
    edge = depth_cells - HALO
    odd_depth = lax.axis_index("gz") % 2 == 1

    def pairs(axis, first):
        count = lax.axis_size(axis)
        lower = range(first, count - 1, 2)
        return [(i, i + 1) for i in lower] + [(i + 1, i) for i in lower]

    row_even, row_odd, deep_even, deep_odd = cut_edges(density)
    row_even = lax.ppermute(row_even, "xy", pairs("xy", 0))
    row_odd = lax.ppermute(row_odd, "xy", pairs("xy", 1))
    deep_odd = lax.ppermute(deep_odd, "gz", pairs("gz", 1))
    deep_even = lax.ppermute(deep_even, "gz", pairs("gz", 0))
    rows = jnp.concatenate([row_even, row_odd], axis=1)
    facing = jnp.where(odd_depth, edge, 0)
    corner_odd = lax.ppermute(
        lax.dynamic_slice_in_dim(rows, facing, HALO), "gz", pairs("gz", 1)
    )
    corner_even = lax.ppermute(
        lax.dynamic_slice_in_dim(rows, edge - facing, HALO), "gz", pairs("gz", 0)
    )
    inner, deep, shear, band_weights = render_inner(
        live_slices, shear_slopes, palette, tile_owner, density, deep_odd, deep_even, n_depth
    )
    outgoing = render_edges(
        live_slices, palette, tile_owner, corner_odd, corner_even, row_even, row_odd,
        inner, deep, shear, band_weights, n_depth,
    )
    incoming = lax.all_to_all(outgoing, "gz", split_axis=0, concat_axis=0, tiled=True)
    tile_rows = row_cells // n_depth
    return pl.pallas_call(
        composite_kernel,
        out_shape=jax.ShapeDtypeStruct((VIEWS, 4, 1, tile_rows, columns), jnp.float32),
        in_specs=[pl.BlockSpec(memory_space=pltpu.VMEM)] * 2,
        out_specs=pl.BlockSpec(memory_space=pltpu.VMEM),
        scratch_shapes=[
            pltpu.VMEM(incoming.shape, jnp.float32),
            pltpu.SMEM(depth_order.shape, jnp.int32),
            pltpu.SemaphoreType.DMA((1,)),
        ],
        compiler_params=pltpu.CompilerParams(vmem_limit_bytes=VMEM_BYTES),
        name="composite",
    )(depth_order, incoming)


def solution(mesh):
    placed = (P("gz", "xy", None), P(), P(), P(), P(), P())
    return jax.shard_map(
        body, mesh=mesh, in_specs=placed, out_specs=P(None, None, "gz", "xy", None), check_vma=False
    )
```
